32 devices in a mesh: groups: 2 (over x), dp: 8 (over z, y), tensor: 2 (over core).
Axes of the slice: x: 2, y: 2, z: 4, core: 2. Of those that a mesh axis runs over, the one named last changes fastest.
Arguments:
- tokens: bfloat16 [6144, 8192], P(('groups', 'dp'), 'tensor'), parts along dimension 0, may hold values from -6 to 6
- base_key: bfloat16 [8192, 1024], P('tensor'), may hold values from -0.0625 to 0.0625
- adapter_down: bfloat16 [16, 8192, 64], P('dp', 'tensor'), may hold values from -0.0625 to 0.0625
- adapter_up: bfloat16 [16, 64, 1024], P('dp', None, 'tensor'), may hold values from -0.75 to 0.75
- adapter_ids: int32 [48, 1], P(('groups', 'dp')), parts along dimension 0, may hold values from 0 to 15
- owner_slot: int32 [16], replicated, may hold values from 0 to 15, each once
- lengths: int32 [48], P(('groups', 'dp')), parts along dimension 0, may hold values from 1 to 128, 2304 in all
Outputs:
- keys: bfloat16 [6144, 1024], P(('groups', 'dp'), 'tensor'), parts along dimension 0
The draws below stay inside these ranges and needn't reach their ends.
There are 2 independent parts, one for each index of `groups`. The reference program is written for one: setup_inputs(seed, part) draws one part's arguments, and reference() takes and returns one part's arrays. A program takes and returns all parts, laid end to end along the dimension named above; an argument that names none is the same for every part. Nothing has to cross between parts.
Inputs may be any that keep to these rules, and one draw needn't show every extreme that they name: `adapter_ids`: every adapter is named by some block. `owner_slot`: each slot holds exactly one adapter. `lengths`: some block is full.
All inputs are finite; a program needn't handle non-finite values.
Results may differ from the reference program's by a relative error of at most 0.0039.
Values may be sent and summed in bfloat16 or wider, within the bound.
No kernel may reach another device: no remote copies, remote signals or barrier semaphores. Data moves between devices by JAX's collectives and lax.ppermute only.
A program may use at most 128 MiB of HBM per device.

```python
import math
import jax
import jax.numpy as jnp
import numpy as np
from jax import lax

D = 8192
KV = 1024
R = 64
BLOCK = 128
BLOCKS = 24
TOKENS = 3072
ADAPT = 16


def levels(rng, dims, cuts, least, high):
    def one(dim, parts):
        steps = jax.random.uniform(jax.random.fold_in(jax.random.fold_in(rng, 6), dim), (parts,), jnp.float32, least / len(cuts), high / len(cuts))
        return jnp.repeat(jnp.exp(steps), dims[dim] // parts).reshape((-1,) + (1,) * (len(dims) - dim - 1))

    level = one(*cuts[0])
    for cut in cuts[1:]:
        level = level * one(*cut)
    return level


def distinct(key, rows, amount, top, lift):
    order = jax.random.permutation(jax.random.fold_in(key, 1), amount)
    pull = order
    for power in range(3):
        pull = pull * pull // amount
    pull = pull * lift // amount
    lots = jax.random.randint(jax.random.fold_in(key, 2), (rows, amount), 0, 4096) + pull
    fixed_rows = jax.random.permutation(jax.random.fold_in(key, 3), rows)[jnp.arange(amount) % rows]
    lots = jnp.where(jnp.arange(rows)[:, None] == fixed_rows[None, :], 1 << 14, lots)
    score = lots * amount + jnp.arange(amount)
    return lax.top_k(score.astype(jnp.int32), top)[1].astype(jnp.int32)


def profile(count, total, bound, skew):
    portions = [(1 << 20) // math.isqrt(rank ** skew) + 1 for rank in range(2, count + 1)]
    surplus, counts = total - bound - (count - 1), [1] * (count - 1)
    while surplus > 0:
        candidates = [i for i in range(count - 1) if counts[i] < bound]
        whole, budget = sum([portions[i] for i in candidates]), surplus
        for i in candidates:
            extra = min(bound - counts[i], max(1, budget * portions[i] // whole), surplus)
            counts[i] = counts[i] + extra
            surplus = surplus - extra
    return np.array([bound] + counts)


def uneven(own_key, amount, total, bound, lean):
    if amount == 2:
        one = jax.random.randint(own_key, (), max(1, total - bound), min(bound, total - 1) + 1)
        return jnp.stack([one, total - one])
    sizes = jnp.asarray(profile(amount, total, bound, lean), jnp.int32)
    couples = (amount - 1) // 2
    source_of, taker = sizes[1:1 + 2 * couples:2], sizes[2:2 + 2 * couples:2]
    slack = jnp.minimum(source_of - 1, bound - taker)
    shifted = jax.random.randint(jax.random.fold_in(own_key, 1), (couples,), 0, 1 << 20) % (slack + 1)
    sizes = sizes.at[1:1 + 2 * couples:2].set(source_of - shifted).at[2:2 + 2 * couples:2].set(taker + shifted)
    return sizes[jax.random.permutation(jax.random.fold_in(own_key, 2), amount)]


def scatter_about(stream_key, extent, width, limit, pieces=(), held_as=jnp.bfloat16):
    result = width * jax.random.normal(stream_key, extent, jnp.float32)
    if pieces:
        result = result * levels(stream_key, extent, pieces, -0.22, 0.18)
    return jnp.clip(result, -limit, limit).astype(held_as)


def setup_inputs(seed: int = 0, part: int = 0) -> dict:
    splits = jax.random.split(jax.random.key(seed), 8)
    own_keys = jax.random.split(jax.random.fold_in(splits[7], part), 8)
    return {
        "tokens": scatter_about(own_keys[0], (TOKENS, D), 1.0, 6.0, ((0, 8), (1, 2))),
        "base_key": scatter_about(splits[1], (D, KV), D ** -0.5, 0.0625, ((0, 2),)),
        "adapter_down": scatter_about(splits[2], (ADAPT, D, R), D ** -0.5, 0.0625, ((0, 8), (1, 2))),
        "adapter_up": scatter_about(splits[3], (ADAPT, R, KV), R ** -0.5, 0.75, ((0, 8), (2, 2))),
        "adapter_ids": distinct(own_keys[4], BLOCKS, ADAPT, 1, 1024),
        "owner_slot": jax.random.permutation(splits[5], ADAPT).astype(jnp.int32),
        "lengths": uneven(own_keys[6], BLOCKS, BLOCKS * BLOCK * 3 // 4, BLOCK, 1).astype(jnp.int32),
    }


def reference(tokens, base_key, adapter_down, adapter_up, adapter_ids, owner_slot, lengths):
    base = jnp.dot(tokens, base_key, preferred_element_type=jnp.float32)
    slots = owner_slot[adapter_ids[:, 0].astype(jnp.int32)].astype(jnp.int32)
    grouped = tokens.reshape(BLOCKS, BLOCK, D)

    def one_block(item):
        block_rows, slot = item
        down = lax.dynamic_index_in_dim(adapter_down, slot, 0, keepdims=False)
        upper = lax.dynamic_index_in_dim(adapter_up, slot, 0, keepdims=False)
        shrunk = jnp.dot(block_rows, down, preferred_element_type=jnp.float32).astype(jnp.bfloat16)
        return jnp.dot(shrunk, upper, preferred_element_type=jnp.float32)

    delta = lax.map(one_block, (grouped, slots))
    positions = lax.broadcasted_iota(jnp.int32, (BLOCKS, BLOCK), 1)
    inside = positions < lengths[:, None].astype(jnp.int32)
    total = base.reshape(BLOCKS, BLOCK, KV) + delta
    keys = jnp.where(inside[:, :, None], total, jnp.zeros_like(total))
    return keys.reshape(TOKENS, KV).astype(jnp.bfloat16)
```

```python
import functools

import jax
import jax.numpy as jnp
from jax import lax
from jax.experimental import pallas as pl
from jax.experimental.pallas import tpu as pltpu
from jax.sharding import PartitionSpec as P

LANES = 128
ANY = pl.BlockSpec(memory_space=pl.ANY)
SMEM = pl.BlockSpec(memory_space=pltpu.SMEM)
BIG = pltpu.CompilerParams(vmem_limit_bytes=32 * 1024 * 1024)


def pack_kernel(where, *refs):
    ways = (len(refs) - 1) // 2
    downs, up_ref, outs = refs[:ways], refs[ways], refs[ways + 1 :]
    for way in range(ways):
        down_ref, out_ref = downs[way], outs[way]
        share = where[way]
        adapters, feats, rank = down_ref.shape
        half = feats // 2
        wide = up_ref.shape[2] // LANES
        up_rows = (out_ref.shape[1] - half) // wide
        for a in range(adapters):
            out_ref[a, :half, :] = jnp.concatenate([down_ref[a, :half, :], down_ref[a, half:, :]], axis=1)
            row = pl.multiple_of(share * up_rows, up_rows)
            part = up_ref[a, pl.ds(row, up_rows), :]
            part = jnp.concatenate([part[:, c * LANES : (c + 1) * LANES] for c in range(wide)], axis=0)
            out_ref[a, half:, :] = part.astype(out_ref.dtype)


def pack(down, up, shares, share_of):
    adapters, feats, rank = down.shape
    step = feats // shares
    ways = len(share_of)
    rows = step // 2 + rank * up.shape[2] // shares // LANES

    def at(way):
        return lambda i, s: (0, s[way], 0)

    return pl.pallas_call(
        pack_kernel,
        grid_spec=pltpu.PrefetchScalarGridSpec(
            num_scalar_prefetch=1,
            grid=(1,),
            in_specs=[pl.BlockSpec((adapters, step, rank), at(w)) for w in range(ways)]
            + [pl.BlockSpec(up.shape, lambda i, s: (0, 0, 0))],
            out_specs=[pl.BlockSpec((adapters, rows, LANES), lambda i, s: (0, 0, 0)) for _ in range(ways)],
        ),
        out_shape=[jax.ShapeDtypeStruct((adapters, rows, LANES), down.dtype) for _ in range(ways)],
        compiler_params=BIG,
        name="pack",
    )(jnp.stack(share_of).astype(jnp.int32), *([down] * ways), up.astype(jnp.float32))


def pick_kernel(targets, ring, pair, *refs):
    here, owner = refs[0], refs[1]
    ids = refs[2 : 2 + targets]
    pieces = refs[2 + targets : 2 + targets + ring * pair]
    outs = refs[2 + targets + ring * pair : -1]
    sems = refs[-1]
    blocks = outs[0].shape[0]
    per = pieces[0].shape[0]
    for k in range(targets):
        for b in range(blocks):
            slot = owner[ids[k][b, 0]]
            chip = slot // per
            local = slot - chip * per
            dz = lax.rem(chip // pair - here[0] + ring, ring)
            dy = lax.rem(lax.rem(chip, pair) - here[1] + pair, pair)
            piece = dz * pair + dy
            for j in range(ring * pair):

                @pl.when(piece == j)
                def _():
                    pltpu.make_async_copy(pieces[j].at[local], outs[k].at[b], sems.at[k, b]).start()

    for k in range(targets):
        for b in range(blocks):
            pltpu.make_async_copy(pieces[0].at[0], outs[k].at[b], sems.at[k, b]).wait()


def pick(here, owner, ids, pieces, ring, pair):
    targets = len(ids)
    blocks = ids[0].shape[0]
    shape = (blocks,) + pieces[0].shape[1:]
    return pl.pallas_call(
        functools.partial(pick_kernel, targets, ring, pair),
        in_specs=[SMEM] * (2 + targets) + [ANY] * len(pieces),
        out_specs=[ANY] * targets,
        out_shape=[jax.ShapeDtypeStruct(shape, pieces[0].dtype)] * targets,
        scratch_shapes=[pltpu.SemaphoreType.DMA((targets, blocks))],
        name="pick",
    )(here, owner, *ids, *pieces)


def base_kernel(side, tok_ref, key_ref, out_ref):
    part = jnp.dot(tok_ref[...], key_ref[...], preferred_element_type=jnp.float32)

    @pl.when(pl.program_id(0) == 0)
    def _():
        out_ref[...] = part

    @pl.when(pl.program_id(0) > 0)
    def _():
        out_ref[...] += part


def base_half(tokens, base_key, side, sides):
    rows, depth = tokens.shape
    wide = base_key.shape[1] // sides
    step = 1024
    return pl.pallas_call(
        base_kernel,
        grid_spec=pltpu.PrefetchScalarGridSpec(
            num_scalar_prefetch=1,
            grid=(depth // step,),
            in_specs=[
                pl.BlockSpec((rows, step), lambda i, s: (0, i)),
                pl.BlockSpec((step, wide), lambda i, s: (i, s[0])),
            ],
            out_specs=pl.BlockSpec((rows, wide), lambda i, s: (0, 0)),
        ),
        out_shape=jax.ShapeDtypeStruct((rows, wide), jnp.float32),
        compiler_params=BIG,
        cost_estimate=pl.CostEstimate(
            flops=2 * rows * depth * wide, bytes_accessed=2 * depth * (rows + wide) + 4 * rows * wide, transcendentals=0
        ),
        name="base",
    )(side.reshape(1), tokens, base_key)


def rank_kernel(where, tok_ref, *refs):
    parts, (sum_ref, up_ref, up_acc) = refs[:-3], refs[-3:]
    shares = len(parts)
    step = tok_ref.shape[1] // shares
    half = step // 2
    rank = sum_ref.shape[1]
    wide = up_ref.shape[2] // LANES
    up_rows = rank // shares
    low = high = None
    for k in range(shares):
        start = where[k] * step
        one = tok_ref[:, pl.ds(pl.multiple_of(start, LANES), half)]
        two = tok_ref[:, pl.ds(pl.multiple_of(start + half, LANES), half)]
        down = parts[k][0, :half, :]
        first = jnp.dot(one, down, preferred_element_type=jnp.float32)
        second = jnp.dot(two, down, preferred_element_type=jnp.float32)
        low = first if low is None else low + first
        high = second if high is None else high + second
        up = parts[k][0, half:, :].astype(jnp.float32)
        for c in range(wide):
            row = pl.multiple_of(where[k] * up_rows, up_rows)
            up_acc[pl.ds(row, up_rows), c * LANES : (c + 1) * LANES] = up[c * up_rows : (c + 1) * up_rows, :]
    sum_ref[...] = low[:, :rank] + high[:, rank:]
    up_ref[0] = up_acc[...].astype(up_ref.dtype)


def rank_sums(tokens, parts, share_of, rank, up_wide):
    rows, feats = tokens.shape
    blocks = parts[0].shape[0]
    block = rows // blocks
    return pl.pallas_call(
        rank_kernel,
        grid_spec=pltpu.PrefetchScalarGridSpec(
            num_scalar_prefetch=1,
            grid=(blocks,),
            in_specs=[pl.BlockSpec((block, feats), lambda i, s: (i, 0))]
            + [pl.BlockSpec((1,) + p.shape[1:], lambda i, s: (i, 0, 0)) for p in parts],
            out_specs=[
                pl.BlockSpec((block, rank), lambda i, s: (i, 0)),
                pl.BlockSpec((1, rank, up_wide), lambda i, s: (i, 0, 0)),
            ],
            scratch_shapes=[pltpu.VMEM((rank, up_wide), jnp.float32)],
        ),
        out_shape=[
            jax.ShapeDtypeStruct((rows, rank), jnp.float32),
            jax.ShapeDtypeStruct((blocks, rank, up_wide), tokens.dtype),
        ],
        compiler_params=BIG,
        cost_estimate=pl.CostEstimate(
            flops=4 * rows * feats * rank, bytes_accessed=2 * rows * feats + 2 * len(parts) * parts[0].size, transcendentals=0
        ),
        name="rank",
    )(jnp.stack(share_of).astype(jnp.int32), tokens, *parts)


def final_kernel(lengths, mine, theirs, up_ref, base_a, base_b, out_ref):
    shrunk = (mine[...] + theirs[...]).astype(jnp.bfloat16)
    delta = jnp.dot(shrunk, up_ref[0], preferred_element_type=jnp.float32)
    total = base_a[...] + base_b[...] + delta
    rows = lax.broadcasted_iota(jnp.int32, total.shape, 0)
    out_ref[...] = jnp.where(rows < lengths[pl.program_id(0)], total, 0.0).astype(out_ref.dtype)


def final(lengths, mine, theirs, up, base_a, base_b, dtype):
    blocks, rank, wide = up.shape
    block = mine.shape[0] // blocks
    row = lambda i, s: (i, 0)
    return pl.pallas_call(
        final_kernel,
        grid_spec=pltpu.PrefetchScalarGridSpec(
            num_scalar_prefetch=1,
            grid=(blocks,),
            in_specs=[
                pl.BlockSpec((block, rank), row),
                pl.BlockSpec((block, rank), row),
                pl.BlockSpec((1, rank, wide), lambda i, s: (i, 0, 0)),
                pl.BlockSpec((block, wide), row),
                pl.BlockSpec((block, wide), row),
            ],
            out_specs=pl.BlockSpec((block, wide), row),
        ),
        out_shape=jax.ShapeDtypeStruct((blocks * block, wide), dtype),
        name="final",
    )(lengths, mine, theirs, up, base_a, base_b)


def body(tokens, base_key, adapter_down, adapter_up, adapter_ids, owner_slot, lengths):
    groups, dp, sides = lax.axis_size("groups"), lax.axis_size("dp"), lax.axis_size("tensor")
    pair = 2 if dp % 2 == 0 else 1
    ring = dp // pair
    shares = groups * pair
    g, d, t = lax.axis_index("groups"), lax.axis_index("dp"), lax.axis_index("tensor")
    z, y = d // pair, d % pair
    rank, up_wide = adapter_up.shape[1:]

    def along_ring(x, step):
        return lax.ppermute(
            x, "dp", [(a * pair + b, (a + step) % ring * pair + b) for a in range(ring) for b in range(pair)]
        )

    def in_plane(x, kg, ky):
        pairs = []
        for a in range(groups):
            for c in range(ring):
                for b in range(pair):
                    to = (a + kg) % groups * dp + c * pair + (b + ky) % pair
                    pairs.append((a * dp + c * pair + b, to))
        return lax.ppermute(x, ("groups", "dp"), pairs)

    def across(x):
        return lax.ppermute(x, "tensor", [(i, (i + 1) % sides) for i in range(sides)])

    offsets = [(k // pair, k % pair) for k in range(shares)]
    ids = [adapter_ids] + [in_plane(adapter_ids, -kg, -ky) for kg, ky in offsets[1:]]

    packed = pack(adapter_down, adapter_up, shares, [g * pair + (y + w) % pair for w in range(pair)])
    pieces = {(0, 0): packed[0]}
    for w in range(1, pair):
        pieces[0, pair - w] = in_plane(packed[w], 0, w)
    for k in range(1, ring // 2 + 1):
        last = 2 * k == ring
        for w in range(pair):
            if not last or w == 0:
                pieces[ring - k, w] = along_ring(pieces[(ring - k + 1) % ring, w], 1)
            if not last or w > 0:
                pieces[k, w] = along_ring(pieces[k - 1, w], -1)
    pieces = [pieces[a, w] for a in range(ring) for w in range(pair)]

    base_out = base_half(tokens, base_key, (t + 1) % sides, sides)
    base_in = across(base_out)
    base_mine = base_half(tokens, base_key, t, sides)

    here = jnp.stack([z, y]).astype(jnp.int32)
    picked = pick(here, owner_slot, ids, pieces, ring, pair)
    parts = [picked[0]] + [in_plane(picked[k], *offsets[k]) for k in range(1, shares)]
    share_of = [(g - kg) % groups * pair + (y - ky) % pair for kg, ky in offsets]
    mine, up = rank_sums(tokens, parts, share_of, rank, up_wide)
    theirs = across(mine)
    return final(lengths, mine, theirs, up, base_mine, base_in, tokens.dtype)


def solution(mesh):
    placed = (
        P(("groups", "dp"), "tensor"),
        P("tensor", None),
        P("dp", "tensor", None),
        P("dp", None, "tensor"),
        P(("groups", "dp"), None),
        P(),
        P(("groups", "dp")),
    )
    return jax.shard_map(
        body, mesh=mesh, in_specs=placed, out_specs=P(("groups", "dp"), "tensor"), check_vma=False
    )
```

```python
import functools

import jax
import jax.numpy as jnp
from jax import lax
from jax.experimental import pallas as pl
from jax.experimental.pallas import tpu as pltpu
from jax.sharding import Mesh
from jax.sharding import PartitionSpec as P

LANES = 128
ANY = pl.BlockSpec(memory_space=pl.ANY)
SMEM = pl.BlockSpec(memory_space=pltpu.SMEM)
VMEM = pl.BlockSpec(memory_space=pltpu.VMEM)
BIG = pltpu.CompilerParams(vmem_limit_bytes=32 * 1024 * 1024)
PLANE = ("groups", "pair")
WHOLE = ("groups", "ring", "pair")


def pack_kernel(where, *refs):
    ways = (len(refs)) // 3
    for way in range(ways):
        down_ref, up_ref, out_ref = refs[way], refs[ways + way], refs[2 * ways + way]
        feats = down_ref.shape[2]
        out_ref[:, :, :feats] = down_ref[...]
        out_ref[:, :, feats:] = up_ref[...]


def pack(down, up, shares, share_of):
    adapters, rank, feats = down.shape
    step = feats // shares
    tiles = up.shape[2] // LANES
    ways = len(share_of)

    def down_at(way):
        return lambda i, s: (0, 0, s[way])

    def up_at(way):
        return lambda i, s: (0, 0, s[way] % tiles)

    shape = (adapters, rank, step + LANES)
    return pl.pallas_call(
        pack_kernel,
        grid_spec=pltpu.PrefetchScalarGridSpec(
            num_scalar_prefetch=1,
            grid=(1,),
            in_specs=[pl.BlockSpec((adapters, rank, step), down_at(w)) for w in range(ways)]
            + [pl.BlockSpec((adapters, rank, LANES), up_at(w)) for w in range(ways)],
            out_specs=[pl.BlockSpec(shape, lambda i, s: (0, 0, 0)) for _ in range(ways)],
        ),
        out_shape=[jax.ShapeDtypeStruct(shape, down.dtype) for _ in range(ways)],
        compiler_params=BIG,
        name="pack",
    )(jnp.stack(share_of).astype(jnp.int32), *([down] * ways), *([up] * ways))


def spread_kernel(in_ref, out_ref):
    out_ref[0] = in_ref[...]


def spread(tokens, shares):
    rows, feats = tokens.shape
    step = feats // shares
    return pl.pallas_call(
        spread_kernel,
        grid=(shares,),
        in_specs=[pl.BlockSpec((rows, step), lambda i: (0, i))],
        out_specs=pl.BlockSpec((1, rows, step), lambda i: (i, 0, 0)),
        out_shape=jax.ShapeDtypeStruct((shares, rows, step), tokens.dtype),
        compiler_params=BIG,
        name="spread",
    )(tokens)


def base_kernel(side, tok_ref, key_ref, after, out_ref):
    part = jnp.dot(tok_ref[...], key_ref[...], preferred_element_type=jnp.float32)

    @pl.when(pl.program_id(0) == 0)
    def _():
        out_ref[...] = part

    @pl.when(pl.program_id(0) > 0)
    def _():
        out_ref[...] += part


def base_half(tokens, base_key, side, sides, after):
    rows, depth = tokens.shape
    wide = base_key.shape[1] // sides
    step = 1024
    return pl.pallas_call(
        base_kernel,
        grid_spec=pltpu.PrefetchScalarGridSpec(
            num_scalar_prefetch=1,
            grid=(depth // step,),
            in_specs=[
                pl.BlockSpec((rows, step), lambda i, s: (0, i)),
                pl.BlockSpec((step, wide), lambda i, s: (i, s[0])),
                ANY,
            ],
            out_specs=pl.BlockSpec((rows, wide), lambda i, s: (0, 0)),
        ),
        out_shape=jax.ShapeDtypeStruct((rows, wide), jnp.float32),
        compiler_params=BIG,
        cost_estimate=pl.CostEstimate(
            flops=2 * rows * depth * wide, bytes_accessed=2 * depth * (rows + wide) + 4 * rows * wide, transcendentals=0
        ),
        name="base",
    )(side.reshape(1), tokens, base_key, after)


def rank_kernel(place, pair, ids, owner, here, tok_ref, *refs):
    pieces = refs[:-4]
    after, out_ref, held, sems = refs[-4:]
    per, rank = pieces[0].shape[:2]
    blocks = out_ref.shape[1]
    feats = tok_ref.shape[2]
    block = tok_ref.shape[1] // blocks
    mate = pl.program_id(0)

    @pl.when(mate == 0)
    def _():
        copies = [
            pltpu.make_async_copy(piece, held.at[pl.ds(j * per, per)], sems.at[j]) for j, piece in enumerate(pieces)
        ]
        for copy in copies:
            copy.start()
        for copy in copies:
            copy.wait()

    for b in range(blocks):
        slot = owner[ids[mate * blocks + b]]
        chip = slot // per
        at = place(chip // pair, chip % pair, here[0], here[1]) * per + slot % per
        tok = tok_ref[0, b * block : (b + 1) * block, :]
        part = lax.dot_general(
            tok, held[at, :, :feats], (((1,), (1,)), ((), ())), preferred_element_type=jnp.float32
        )
        half = block // 2
        part = jnp.concatenate([part[:half], part[half:]], axis=1)
        out_ref[0, b, :half, :] = part.astype(out_ref.dtype)
        out_ref[0, b, half:, :] = held[at, :, feats:]


def rank_parts(ids, owner, here, tok, pieces, place, pair, blocks, after):
    shares, rows, feats = tok.shape
    per, rank, wide = pieces[0].shape
    tall = rows // blocks // 2 + rank
    return pl.pallas_call(
        functools.partial(rank_kernel, place, pair),
        grid=(shares,),
        in_specs=[SMEM, SMEM, SMEM, pl.BlockSpec((1, rows, feats), lambda i: (i, 0, 0))] + [ANY] * (len(pieces) + 1),
        out_specs=pl.BlockSpec((1, blocks, tall, LANES), lambda i: (i, 0, 0, 0)),
        out_shape=jax.ShapeDtypeStruct((shares, blocks, tall, LANES), tok.dtype),
        scratch_shapes=[
            pltpu.VMEM((len(pieces) * per, rank, wide), tok.dtype),
            pltpu.SemaphoreType.DMA((len(pieces),)),
        ],
        compiler_params=BIG,
        cost_estimate=pl.CostEstimate(
            flops=2 * shares * rows * feats * rank, bytes_accessed=2 * tok.size, transcendentals=0
        ),
        name="rank",
    )(ids, owner, here, tok, *pieces, after)


def sum_kernel(in_ref, out_ref):
    shares, blocks = in_ref.shape[:2]
    block, rank = out_ref.shape[0] // blocks, out_ref.shape[1]
    half = block // 2
    for b in range(blocks):
        total = in_ref[0, b, :half, :].astype(jnp.float32)
        for s in range(1, shares):
            total += in_ref[s, b, :half, :].astype(jnp.float32)
        out_ref[b * block : b * block + half, :] = total[:, :rank]
        out_ref[b * block + half : (b + 1) * block, :] = total[:, rank:]


def rank_sums(parts, rows, rank):
    return pl.pallas_call(
        sum_kernel,
        in_specs=[VMEM],
        out_specs=VMEM,
        out_shape=jax.ShapeDtypeStruct((rows, rank), jnp.float32),
        name="sums",
    )(parts)


def final_kernel(lengths, mine, theirs, parts, base, out_ref):
    shares, blocks = parts.shape[:2]
    block = out_ref.shape[0] // blocks
    rank = mine.shape[1]
    wide = out_ref.shape[1]
    shrunk = (mine[...] + theirs[...]).astype(jnp.bfloat16)
    rows = lax.broadcasted_iota(jnp.int32, (block, wide), 0)
    for b in range(blocks):
        here = slice(b * block, (b + 1) * block)
        up = jnp.concatenate([parts[s, b, block // 2 :, :] for s in range(wide // LANES)], axis=1)
        delta = jnp.dot(shrunk[here], up, preferred_element_type=jnp.float32)
        out_ref[here, :] = jnp.where(rows < lengths[b], base[here, :] + delta, 0.0).astype(out_ref.dtype)


def final(lengths, mine, theirs, parts, base, dtype):
    return pl.pallas_call(
        final_kernel,
        in_specs=[SMEM, VMEM, VMEM, VMEM, VMEM],
        out_specs=VMEM,
        out_shape=jax.ShapeDtypeStruct(base.shape, dtype),
        compiler_params=BIG,
        name="final",
    )(lengths, mine, theirs, parts, base)


def line_of_four(x):
    two = lax.ppermute(x, "ring", [(0, 2), (1, 3), (2, 0), (3, 1)])
    up = lax.ppermute(x, "ring", [(0, 1), (1, 2), (2, 3)])
    down = lax.ppermute(x, "ring", [(1, 0), (2, 1), (3, 2)])
    three = lax.ppermute(two, "ring", [(1, 0), (2, 3)])
    return [x, up, down, two, three]


def place_in_four(z_from, z):
    away = jnp.abs(z_from - z)
    near = jnp.where(z_from < z, 1, 2)
    return jnp.where(away == 0, 0, jnp.where(away == 1, near, jnp.where(away == 2, 3, 4)))


def any_ring(x, ring):
    held = {0: x}
    for k in range(1, ring // 2 + 1):
        held[ring - k] = lax.ppermute(held[(ring - k + 1) % ring], "ring", [(a, (a + 1) % ring) for a in range(ring)])
        if 2 * k < ring:
            held[k] = lax.ppermute(held[k - 1], "ring", [(a, (a - 1) % ring) for a in range(ring)])
    return [held[k] for k in range(ring)]


def body(tokens, base_key, adapter_down, adapter_up, adapter_ids, owner_slot, lengths):
    groups, ring, pair = lax.axis_size("groups"), lax.axis_size("ring"), lax.axis_size("pair")
    sides = lax.axis_size("tensor")
    shares = groups * pair
    g, z, y, t = (lax.axis_index(name) for name in ("groups", "ring", "pair", "tensor"))
    rows = tokens.shape[0]
    blocks = lengths.shape[0]
    rank = adapter_up.shape[1]

    def across(x):
        return lax.ppermute(x, "tensor", [(i, (i + 1) % sides) for i in range(sides)])

    def to_plane(x):
        return lax.all_to_all(x, PLANE, split_axis=0, concat_axis=0, tiled=True)

    gather = line_of_four if ring == 4 else functools.partial(any_ring, ring=ring)
    each = 5 if ring == 4 else ring

    def place(z_from, y_from, z_here, y_here):
        at = place_in_four(z_from, z_here) if ring == 4 else lax.rem(z_from - z_here + ring, ring)
        return lax.rem(y_from - y_here + pair, pair) * each + at

    packed = pack(jnp.swapaxes(adapter_down, 1, 2), adapter_up, shares, [g * pair + (y + w) % pair for w in range(pair)])
    swapped = [
        lax.ppermute(packed[w], "pair", [(a, (a + w) % pair) for a in range(pair)]) for w in range(1, pair)
    ]
    pieces = gather(packed[0])
    for w in range(1, pair):
        pieces = pieces + gather(swapped[pair - 1 - w])

    tok = to_plane(spread(tokens, shares))
    ids = to_plane(jnp.broadcast_to(adapter_ids[:, 0], (shares, blocks))).reshape(-1)

    base_out = base_half(tokens, base_key, (t + 1) % sides, sides, pieces[-4])
    base_in = across(base_out)
    base_mine = base_half(tokens, base_key, t, sides, base_out)
    base = base_mine + base_in

    here = jnp.stack([z, y]).astype(jnp.int32)
    parts = to_plane(rank_parts(ids, owner_slot, here, tok, pieces, place, pair, blocks, base))
    mine = rank_sums(parts, rows, rank)
    return final(lengths, mine, across(mine), parts, base, tokens.dtype)


def solution(mesh):
    groups, dp, sides = (mesh.shape[name] for name in ("groups", "dp", "tensor"))
    pair = 2 if dp % 2 == 0 else 1
    cut = Mesh(mesh.devices.reshape(groups, dp // pair, pair, sides), ("groups", "ring", "pair", "tensor"))
    stored = ("ring", "pair")
    placed = (
        P(WHOLE, "tensor"),
        P("tensor", None),
        P(stored, "tensor", None),
        P(stored, None, "tensor"),
        P(WHOLE, None),
        P(),
        P(WHOLE),
    )
    return jax.shard_map(body, mesh=cut, in_specs=placed, out_specs=P(WHOLE, "tensor"), check_vma=False)
```

```python
import functools

import jax
import jax.numpy as jnp
from jax import lax
from jax.experimental import pallas as pl
from jax.experimental.pallas import tpu as pltpu
from jax.sharding import Mesh
from jax.sharding import PartitionSpec as P

LANES = 128
ANY = pl.BlockSpec(memory_space=pl.ANY)
SMEM = pl.BlockSpec(memory_space=pltpu.SMEM)
VMEM = pl.BlockSpec(memory_space=pltpu.VMEM)
BIG = pltpu.CompilerParams(vmem_limit_bytes=32 * 1024 * 1024)
PLANE = ("groups", "pair")
WHOLE = ("groups", "ring", "pair")


def pack_kernel(where, *refs):
    ways = (len(refs)) // 3
    for way in range(ways):
        down_ref, up_ref, out_ref = refs[way], refs[ways + way], refs[2 * ways + way]
        feats = down_ref.shape[2]
        out_ref[:, :, :feats] = down_ref[...]
        out_ref[:, :, feats:] = up_ref[...]


def pack(down, up, shares, share_of):
    adapters, rank, feats = down.shape
    step = feats // shares
    tiles = up.shape[2] // LANES
    ways = len(share_of)

    def down_at(way):
        return lambda i, s: (0, 0, s[way])

    def up_at(way):
        return lambda i, s: (0, 0, s[way] % tiles)

    shape = (adapters, rank, step + LANES)
    return pl.pallas_call(
        pack_kernel,
        grid_spec=pltpu.PrefetchScalarGridSpec(
            num_scalar_prefetch=1,
            grid=(1,),
            in_specs=[pl.BlockSpec((adapters, rank, step), down_at(w)) for w in range(ways)]
            + [pl.BlockSpec((adapters, rank, LANES), up_at(w)) for w in range(ways)],
            out_specs=[pl.BlockSpec(shape, lambda i, s: (0, 0, 0)) for _ in range(ways)],
        ),
        out_shape=[jax.ShapeDtypeStruct(shape, down.dtype) for _ in range(ways)],
        compiler_params=BIG,
        name="pack",
    )(jnp.stack(share_of).astype(jnp.int32), *([down] * ways), *([up] * ways))


def spread_kernel(lengths, ids, in_ref, after, out_ref):
    blocks = lengths.shape[0]
    rows, step = in_ref.shape
    block = rows // blocks
    row = lax.broadcasted_iota(jnp.int32, (block, step), 0)
    for b in range(blocks):
        part = in_ref[b * block : (b + 1) * block, :]
        out_ref[0, b * block : (b + 1) * block, :] = jnp.where(row < lengths[b], part, jnp.zeros_like(part))
    extra = out_ref.shape[1] - rows
    lane = lax.broadcasted_iota(jnp.int32, (extra, step), 1)
    named = jnp.zeros((extra, step), jnp.float32)
    for b in range(blocks):
        named = jnp.where(lane == b, ids[b, 0].astype(jnp.float32), named)
    out_ref[0, rows:, :] = named.astype(out_ref.dtype)


def spread(tokens, lengths, ids, shares, after):
    rows, feats = tokens.shape
    step = feats // shares
    return pl.pallas_call(
        spread_kernel,
        grid=(shares,),
        in_specs=[SMEM, SMEM, pl.BlockSpec((rows, step), lambda i: (0, i)), ANY],
        out_specs=pl.BlockSpec((1, rows + 16, step), lambda i: (i, 0, 0)),
        out_shape=jax.ShapeDtypeStruct((shares, rows + 16, step), tokens.dtype),
        compiler_params=BIG,
        name="spread",
    )(lengths, ids, tokens, after)


def base_kernel(side, tok_ref, key_ref, after, out_ref):
    part = jnp.dot(tok_ref[0, : out_ref.shape[0], :], key_ref[...], preferred_element_type=jnp.float32)

    @pl.when(pl.program_id(0) == 0)
    def _():
        out_ref[...] = part

    @pl.when(pl.program_id(0) > 0)
    def _():
        out_ref[...] += part


def base_half(slabs, base_key, side, sides, rows, after):
    shares, tall, step = slabs.shape
    depth = shares * step
    wide = base_key.shape[1] // sides
    return pl.pallas_call(
        base_kernel,
        grid_spec=pltpu.PrefetchScalarGridSpec(
            num_scalar_prefetch=1,
            grid=(shares,),
            in_specs=[
                pl.BlockSpec((1, tall, step), lambda i, s: (i, 0, 0)),
                pl.BlockSpec((step, wide), lambda i, s: (i, s[0])),
                ANY,
            ],
            out_specs=pl.BlockSpec((rows, wide), lambda i, s: (0, 0)),
        ),
        out_shape=jax.ShapeDtypeStruct((rows, wide), jnp.float32),
        compiler_params=BIG,
        cost_estimate=pl.CostEstimate(
            flops=2 * rows * depth * wide, bytes_accessed=2 * depth * (rows + wide) + 4 * rows * wide, transcendentals=0
        ),
        name="base",
    )(side.reshape(1), slabs, base_key, after)


def rank_kernel(pair, per, ids, owner, here, tok_ref, *refs):
    pieces = refs[:-4]
    after, out_ref, held, sems = refs[-4:]
    count, rank = pieces[0].shape[:2]
    blocks = out_ref.shape[1]
    feats = tok_ref.shape[2]
    block = out_ref.shape[3]
    mate = pl.program_id(0)

    @pl.when(mate == 0)
    def _():
        copies = [
            pltpu.make_async_copy(piece, held.at[pl.ds(j * count, count)], sems.at[j])
            for j, piece in enumerate(pieces)
        ]
        for copy in copies:
            copy.start()
        for copy in copies:
            copy.wait()

    for b in range(blocks):
        slot = owner[ids[mate * blocks + b]]
        chip = slot // per
        way = lax.rem(lax.rem(chip, pair) - here[0] + pair, pair)
        at = way * count + chip // pair * per + lax.rem(slot, per)
        tok = tok_ref[0, b * block : (b + 1) * block, :]
        part = lax.dot_general(
            held[at, :, :feats], tok, (((1,), (1,)), ((), ())), preferred_element_type=jnp.float32
        )
        out_ref[0, b, :rank, :] = part.astype(out_ref.dtype)
        out_ref[0, b, rank:, :] = held[at, :, feats:]


def rank_parts(ids, owner, here, tok, pieces, pair, per, blocks, after):
    shares, tall, feats = tok.shape
    block = tall // blocks // LANES * LANES
    count, rank, wide = pieces[0].shape
    shape = (shares, blocks, 2 * rank, block)
    return pl.pallas_call(
        functools.partial(rank_kernel, pair, per),
        grid=(shares,),
        in_specs=[SMEM, SMEM, SMEM, pl.BlockSpec((1, tall, feats), lambda i: (i, 0, 0))] + [ANY] * (len(pieces) + 1),
        out_specs=pl.BlockSpec((1,) + shape[1:], lambda i: (i, 0, 0, 0)),
        out_shape=jax.ShapeDtypeStruct(shape, tok.dtype),
        scratch_shapes=[
            pltpu.VMEM((len(pieces) * count, rank, wide), tok.dtype),
            pltpu.SemaphoreType.DMA((len(pieces),)),
        ],
        compiler_params=BIG,
        cost_estimate=pl.CostEstimate(
            flops=2 * tok.size * rank, bytes_accessed=2 * tok.size, transcendentals=0
        ),
        name="rank",
    )(ids, owner, here, tok, *pieces, after)


def final_kernel(mine, theirs, base, out_ref):
    shares, blocks, tall, block = mine.shape
    rank = tall // 2
    wide = out_ref.shape[1]
    for b in range(blocks):
        here = slice(b * block, (b + 1) * block)
        total = mine[0, b, :rank, :].astype(jnp.float32) + theirs[0, b, :rank, :].astype(jnp.float32)
        for s in range(1, shares):
            total += mine[s, b, :rank, :].astype(jnp.float32) + theirs[s, b, :rank, :].astype(jnp.float32)
        up = jnp.concatenate([mine[s, b, rank:, :] for s in range(wide // LANES)], axis=1)
        delta = lax.dot_general(
            total.astype(jnp.bfloat16), up, (((0,), (0,)), ((), ())), preferred_element_type=jnp.float32
        )
        out_ref[here, :] = (base[here, :] + delta).astype(out_ref.dtype)


def final(mine, theirs, base, dtype):
    return pl.pallas_call(
        final_kernel,
        in_specs=[VMEM, VMEM, VMEM],
        out_specs=VMEM,
        out_shape=jax.ShapeDtypeStruct(base.shape, dtype),
        compiler_params=BIG,
        name="final",
    )(mine, theirs, base)


def body(tokens, base_key, adapter_down, adapter_up, adapter_ids, owner_slot, lengths):
    groups, pair = lax.axis_size("groups"), lax.axis_size("pair")
    sides = lax.axis_size("tensor")
    shares = groups * pair
    g, y, t = (lax.axis_index(name) for name in ("groups", "pair", "tensor"))
    rows = tokens.shape[0]
    blocks = lengths.shape[0]
    per = adapter_down.shape[0]

    def across(x):
        return lax.ppermute(x, "tensor", [(i, (i + 1) % sides) for i in range(sides)])

    def to_plane(x):
        return lax.all_to_all(x, PLANE, split_axis=0, concat_axis=0, tiled=True)

    packed = pack(jnp.swapaxes(adapter_down, 1, 2), adapter_up, shares, [g * pair + (y + w) % pair for w in range(pair)])
    slabs = spread(tokens, lengths, adapter_ids, shares, packed[0])
    pieces = [packed[0]]
    for w in range(1, pair):
        pieces.append(lax.ppermute(packed[pair - w], "pair", [(a, (a - w) % pair) for a in range(pair)]))
    swapped = pieces[-1]
    pieces = [lax.all_gather(piece, "ring", axis=0, tiled=True) for piece in pieces]

    tok = to_plane(slabs)
    ids = tok[:, rows, :blocks].astype(jnp.int32).reshape(-1)

    base_out = base_half(slabs, base_key, (t + 1) % sides, sides, rows, swapped)
    base_in = across(base_out)
    base_mine = base_half(slabs, base_key, t, sides, rows, base_out)
    base = base_mine + base_in

    mine = to_plane(rank_parts(ids, owner_slot, y.reshape(1), tok, pieces, pair, per, blocks, base))
    return final(mine, across(mine), base, tokens.dtype)


def solution(mesh):
    groups, dp, sides = (mesh.shape[name] for name in ("groups", "dp", "tensor"))
    pair = 2 if dp % 2 == 0 else 1
    cut = Mesh(mesh.devices.reshape(groups, dp // pair, pair, sides), ("groups", "ring", "pair", "tensor"))
    stored = ("ring", "pair")
    placed = (
        P(WHOLE, "tensor"),
        P("tensor", None),
        P(stored, "tensor", None),
        P(stored, None, "tensor"),
        P(WHOLE, None),
        P(),
        P(WHOLE),
    )
    return jax.shard_map(body, mesh=cut, in_specs=placed, out_specs=P(WHOLE, "tensor"), check_vma=False)
```

```python
import functools

import jax
import jax.numpy as jnp
from jax import lax
from jax.experimental import pallas as pl
from jax.experimental.pallas import tpu as pltpu
from jax.sharding import Mesh
from jax.sharding import PartitionSpec as P

LANES = 128
ANY = pl.BlockSpec(memory_space=pl.ANY)
SMEM = pl.BlockSpec(memory_space=pltpu.SMEM)
VMEM = pl.BlockSpec(memory_space=pltpu.VMEM)
HBM = pl.BlockSpec(memory_space=pltpu.HBM)
BIG = pltpu.CompilerParams(vmem_limit_bytes=32 * 1024 * 1024)
PLANE = ("groups", "pair")
WHOLE = ("groups", "ring", "pair")


def hand_kernel(*refs):
    pass


def hand_on(x, *after):
    return pl.pallas_call(
        hand_kernel,
        in_specs=[ANY] * (1 + len(after)),
        out_specs=ANY,
        out_shape=jax.ShapeDtypeStruct(x.shape, x.dtype),
        input_output_aliases={0: 0},
        name="hand",
    )(x, *after)


def pack_kernel(where, down, up, *refs):
    outs, sems = refs[:-1], refs[-1]
    feats = outs[0].shape[2] - LANES
    copies = []
    for way, out in enumerate(outs):
        start = pl.multiple_of(where[way] * feats, LANES)
        tile = pl.multiple_of(lax.rem(where[way], up.shape[2] // LANES) * LANES, LANES)
        copies.append(pltpu.make_async_copy(down.at[:, :, pl.ds(start, feats)], out.at[:, :, :feats], sems.at[way, 0]))
        copies.append(pltpu.make_async_copy(up.at[:, :, pl.ds(tile, LANES)], out.at[:, :, feats:], sems.at[way, 1]))
    for copy in copies:
        copy.start()
    for copy in copies:
        copy.wait()


def pack(down, up, shares, share_of):
    adapters, rank, feats = down.shape
    ways = len(share_of)
    shape = jax.ShapeDtypeStruct((adapters, rank, feats // shares + LANES), down.dtype)
    return pl.pallas_call(
        pack_kernel,
        in_specs=[SMEM, HBM, HBM],
        out_specs=[VMEM] * ways,
        out_shape=[shape] * ways,
        scratch_shapes=[pltpu.SemaphoreType.DMA((ways, 2))],
        compiler_params=BIG,
        name="pack",
    )(jnp.stack(share_of).astype(jnp.int32), down, up)


def spread_kernel(lengths, ids, in_ref, out_ref):
    blocks = lengths.shape[0]
    rows, step = in_ref.shape
    block = rows // blocks
    row = lax.broadcasted_iota(jnp.int32, (block, step), 0)
    for b in range(blocks):
        part = in_ref[b * block : (b + 1) * block, :]
        out_ref[0, b * block : (b + 1) * block, :] = jnp.where(row < lengths[b], part, jnp.zeros_like(part))
    extra = out_ref.shape[1] - rows
    lane = lax.broadcasted_iota(jnp.int32, (extra, step), 1)
    named = jnp.zeros((extra, step), jnp.float32)
    for b in range(blocks):
        named = jnp.where(lane == b, ids[b, 0].astype(jnp.float32), named)
    out_ref[0, rows:, :] = named.astype(out_ref.dtype)


def spread(tokens, lengths, ids, shares):
    rows, feats = tokens.shape
    step = feats // shares
    return pl.pallas_call(
        spread_kernel,
        grid=(shares,),
        in_specs=[SMEM, SMEM, pl.BlockSpec((rows, step), lambda i: (0, i))],
        out_specs=pl.BlockSpec((1, rows + 16, step), lambda i: (i, 0, 0)),
        out_shape=jax.ShapeDtypeStruct((shares, rows + 16, step), tokens.dtype),
        compiler_params=BIG,
        name="spread",
    )(lengths, ids, tokens)


def base_kernel(side, lengths, tok_ref, key_ref, *refs):
    out_ref = refs[-1]
    part = jnp.dot(tok_ref[...], key_ref[...], preferred_element_type=jnp.float32)
    step = pl.program_id(0)

    @pl.when(step == 0)
    def _():
        out_ref[...] = part

    @pl.when(step > 0)
    def _():
        out_ref[...] += part

    @pl.when(step == pl.num_programs(0) - 1)
    def _():
        blocks = lengths.shape[0]
        block = out_ref.shape[0] // blocks
        row = lax.broadcasted_iota(jnp.int32, (block, out_ref.shape[1]), 0)
        for b in range(blocks):
            here = slice(b * block, (b + 1) * block)
            out_ref[here, :] = jnp.where(row < lengths[b], out_ref[here, :], 0.0)


def base_half(tokens, base_key, side, sides, lengths, *after):
    rows, depth = tokens.shape
    wide = base_key.shape[1] // sides
    step = 1024
    return pl.pallas_call(
        base_kernel,
        grid_spec=pltpu.PrefetchScalarGridSpec(
            num_scalar_prefetch=2,
            grid=(depth // step,),
            in_specs=[
                pl.BlockSpec((rows, step), lambda i, s, n: (0, i)),
                pl.BlockSpec((step, wide), lambda i, s, n: (i, s[0])),
            ]
            + [ANY] * len(after),
            out_specs=pl.BlockSpec((rows, wide), lambda i, s, n: (0, 0)),
        ),
        out_shape=jax.ShapeDtypeStruct((rows, wide), jnp.float32),
        compiler_params=BIG,
        cost_estimate=pl.CostEstimate(
            flops=2 * rows * depth * wide, bytes_accessed=2 * depth * (rows + wide) + 4 * rows * wide, transcendentals=0
        ),
        name="base",
    )(side.reshape(1), lengths, tokens, base_key, *after)


def rank_kernel(ring, pair, ids, owner, here, tok_ref, *refs):
    pieces = refs[:-4]
    after, out_ref, held, sems = refs[-4:]
    per, rank = pieces[0].shape[:2]
    blocks = out_ref.shape[1]
    feats = tok_ref.shape[2]
    block = out_ref.shape[3]
    mate = pl.program_id(0)

    @pl.when(mate == 0)
    def _():
        copies = [
            pltpu.make_async_copy(piece, held.at[pl.ds(j * per, per)], sems.at[j])
            for j, piece in enumerate(pieces)
        ]
        for copy in copies:
            copy.start()
        for copy in copies:
            copy.wait()

    for b in range(blocks):
        slot = owner[ids[mate * blocks + b]]
        chip = slot // per
        away = lax.rem(chip // pair - here[0] + ring, ring)
        way = lax.rem(lax.rem(chip, pair) - here[1] + pair, pair)
        at = (way * ring + away) * per + lax.rem(slot, per)
        tok = tok_ref[0, b * block : (b + 1) * block, :]
        part = lax.dot_general(
            held[at, :, :feats], tok, (((1,), (1,)), ((), ())), preferred_element_type=jnp.float32
        )
        out_ref[0, b, :rank, :] = part.astype(out_ref.dtype)
        out_ref[0, b, rank:, :] = held[at, :, feats:]


def rank_parts(ids, owner, here, tok, pieces, ring, pair, blocks, after):
    shares, tall, feats = tok.shape
    block = tall // blocks // LANES * LANES
    per, rank, wide = pieces[0].shape
    shape = (shares, blocks, 2 * rank, block)
    return pl.pallas_call(
        functools.partial(rank_kernel, ring, pair),
        grid=(shares,),
        in_specs=[SMEM, SMEM, SMEM, pl.BlockSpec((1, tall, feats), lambda i: (i, 0, 0))] + [ANY] * (len(pieces) + 1),
        out_specs=pl.BlockSpec((1,) + shape[1:], lambda i: (i, 0, 0, 0)),
        out_shape=jax.ShapeDtypeStruct(shape, tok.dtype),
        scratch_shapes=[
            pltpu.VMEM((len(pieces) * per, rank, wide), tok.dtype),
            pltpu.SemaphoreType.DMA((len(pieces),)),
        ],
        compiler_params=BIG,
        cost_estimate=pl.CostEstimate(
            flops=2 * tok.size * rank, bytes_accessed=2 * tok.size, transcendentals=0
        ),
        name="rank",
    )(ids, owner, here, tok, *pieces, after)


def final_kernel(mine, theirs, base, out_ref):
    shares, blocks, tall, block = mine.shape
    rank = tall // 2
    wide = out_ref.shape[1]
    for b in range(blocks):
        here = slice(b * block, (b + 1) * block)
        total = mine[0, b, :rank, :].astype(jnp.float32) + theirs[0, b, :rank, :].astype(jnp.float32)
        for s in range(1, shares):
            total += mine[s, b, :rank, :].astype(jnp.float32) + theirs[s, b, :rank, :].astype(jnp.float32)
        up = jnp.concatenate([mine[s, b, rank:, :] for s in range(wide // LANES)], axis=1)
        delta = lax.dot_general(
            total.astype(jnp.bfloat16), up, (((0,), (0,)), ((), ())), preferred_element_type=jnp.float32
        )
        out_ref[here, :] = (base[here, :] + delta).astype(out_ref.dtype)


def final(mine, theirs, base, dtype):
    return pl.pallas_call(
        final_kernel,
        in_specs=[VMEM, VMEM, VMEM],
        out_specs=VMEM,
        out_shape=jax.ShapeDtypeStruct(base.shape, dtype),
        compiler_params=BIG,
        name="final",
    )(mine, theirs, base)


def body(tokens, base_key, adapter_down, adapter_up, adapter_ids, owner_slot, lengths):
    groups, ring, pair = lax.axis_size("groups"), lax.axis_size("ring"), lax.axis_size("pair")
    sides = lax.axis_size("tensor")
    shares = groups * pair
    g, z, y, t = (lax.axis_index(name) for name in ("groups", "ring", "pair", "tensor"))
    rows = tokens.shape[0]
    blocks = lengths.shape[0]

    def across(x):
        return lax.ppermute(x, "tensor", [(i, (i + 1) % sides) for i in range(sides)])

    def to_plane(x):
        return lax.all_to_all(x, PLANE, split_axis=0, concat_axis=0, tiled=True)

    def along(x, step):
        return lax.ppermute(x, "ring", [(a, (a + step) % ring) for a in range(ring)])

    def first_hops(x):
        return {0: x, ring - 1: along(x, 1), **({1: along(x, -1)} if ring > 2 else {})}

    def more_hops(held, way):
        for k in range(2, ring // 2 + 1):
            if 2 * k < ring or way % 2 == 0:
                held[ring - k] = along(held[ring - k + 1], 1)
            if 2 * k < ring or way % 2 == 1:
                held[k] = along(held[k - 1], -1)
        return [held[k] for k in range(ring)]

    packed = pack(jnp.swapaxes(adapter_down, 1, 2), adapter_up, shares, [g * pair + (y + w) % pair for w in range(pair)])
    slabs = spread(tokens, lengths, adapter_ids, shares)
    swapped = [
        lax.ppermute(packed[pair - w], "pair", [(a, (a - w) % pair) for a in range(pair)]) for w in range(1, pair)
    ]
    own = first_hops(packed[0])
    near = [own[k] for k in own if k > 0]
    others = [first_hops(hand_on(piece, *near)) for piece in swapped]
    tok = to_plane(hand_on(slabs, *swapped))
    ids = tok[:, rows, :blocks].astype(jnp.int32).reshape(-1)

    next_near = [held[k] for held in others for k in held if k > 0]
    base_out = base_half(tokens, base_key, (t + 1) % sides, sides, lengths, *next_near)
    pieces = [more_hops(held, way) for way, held in enumerate([own] + others)]
    base_in = across(base_out)
    base_mine = base_half(tokens, base_key, t, sides, lengths, base_out, pieces[0][ring // 2])
    base = base_mine + base_in

    here = jnp.stack([z, y]).astype(jnp.int32)
    flat = [piece for way in pieces for piece in way]
    mine = to_plane(rank_parts(ids, owner_slot, here, tok, flat, ring, pair, blocks, base))
    return final(mine, across(mine), base, tokens.dtype)


def solution(mesh):
    groups, dp, sides = (mesh.shape[name] for name in ("groups", "dp", "tensor"))
    pair = 2 if dp % 2 == 0 else 1
    cut = Mesh(mesh.devices.reshape(groups, dp // pair, pair, sides), ("groups", "ring", "pair", "tensor"))
    stored = ("ring", "pair")
    placed = (
        P(WHOLE, "tensor"),
        P("tensor", None),
        P(stored, "tensor", None),
        P(stored, None, "tensor"),
        P(WHOLE, None),
        P(),
        P(WHOLE),
    )
    return jax.shard_map(body, mesh=cut, in_specs=placed, out_specs=P(WHOLE, "tensor"), check_vma=False)
```

```python
import functools

import jax
import jax.numpy as jnp
from jax import lax
from jax.experimental import pallas as pl
from jax.experimental.pallas import tpu as pltpu
from jax.sharding import Mesh
from jax.sharding import PartitionSpec as P

LANES = 128
ANY = pl.BlockSpec(memory_space=pl.ANY)
SMEM = pl.BlockSpec(memory_space=pltpu.SMEM)
VMEM = pl.BlockSpec(memory_space=pltpu.VMEM)
HBM = pl.BlockSpec(memory_space=pltpu.HBM)
BIG = pltpu.CompilerParams(vmem_limit_bytes=32 * 1024 * 1024)
PLANE = ("groups", "pair")
WHOLE = ("groups", "ring", "pair")


def hand_kernel(*refs):
    pass


def hand_on(x, *after):
    return pl.pallas_call(
        hand_kernel,
        in_specs=[ANY] * (1 + len(after)),
        out_specs=ANY,
        out_shape=jax.ShapeDtypeStruct(x.shape, x.dtype),
        input_output_aliases={0: 0},
        name="hand",
    )(x, *after)


def pack_kernel(where, down, up, *refs):
    outs, sems = refs[:-1], refs[-1]
    feats = outs[0].shape[2] - LANES
    copies = []
    for way, out in enumerate(outs):
        start = pl.multiple_of(where[way] * feats, LANES)
        tile = pl.multiple_of(lax.rem(where[way], up.shape[2] // LANES) * LANES, LANES)
        copies.append(pltpu.make_async_copy(down.at[:, :, pl.ds(start, feats)], out.at[:, :, :feats], sems.at[way, 0]))
        copies.append(pltpu.make_async_copy(up.at[:, :, pl.ds(tile, LANES)], out.at[:, :, feats:], sems.at[way, 1]))
    for copy in copies:
        copy.start()
    for copy in copies:
        copy.wait()


def pack(down, up, shares, share_of):
    adapters, rank, feats = down.shape
    ways = len(share_of)
    shape = jax.ShapeDtypeStruct((adapters, rank, feats // shares + LANES), down.dtype)
    return pl.pallas_call(
        pack_kernel,
        in_specs=[SMEM, HBM, HBM],
        out_specs=[VMEM] * ways,
        out_shape=[shape] * ways,
        scratch_shapes=[pltpu.SemaphoreType.DMA((ways, 2))],
        name="pack",
    )(jnp.stack(share_of).astype(jnp.int32), down, up)


def spread_kernel(lengths, ids, in_ref, out_ref):
    blocks = lengths.shape[0]
    rows, step = in_ref.shape
    block = rows // blocks
    row = lax.broadcasted_iota(jnp.int32, (block, step), 0)
    for b in range(blocks):
        part = in_ref[b * block : (b + 1) * block, :]
        out_ref[0, b * block : (b + 1) * block, :] = jnp.where(row < lengths[b], part, jnp.zeros_like(part))
    extra = out_ref.shape[1] - rows
    lane = lax.broadcasted_iota(jnp.int32, (extra, step), 1)
    named = jnp.zeros((extra, step), jnp.float32)
    for b in range(blocks):
        named = jnp.where(lane == b, ids[b, 0].astype(jnp.float32), named)
    out_ref[0, rows:, :] = named.astype(out_ref.dtype)


def spread(tokens, lengths, ids, shares):
    rows, feats = tokens.shape
    step = feats // shares
    return pl.pallas_call(
        spread_kernel,
        grid=(shares,),
        in_specs=[SMEM, SMEM, pl.BlockSpec((rows, step), lambda i: (0, i))],
        out_specs=pl.BlockSpec((1, rows + 16, step), lambda i: (i, 0, 0)),
        out_shape=jax.ShapeDtypeStruct((shares, rows + 16, step), tokens.dtype),
        name="spread",
    )(lengths, ids, tokens)


def base_kernel(side, lengths, tok_ref, key_ref, *refs):
    out_ref = refs[-1]
    part = jnp.dot(tok_ref[...], key_ref[...], preferred_element_type=jnp.float32)
    step = pl.program_id(0)

    @pl.when(step == 0)
    def _():
        out_ref[...] = part

    @pl.when(step > 0)
    def _():
        out_ref[...] += part

    @pl.when(step == pl.num_programs(0) - 1)
    def _():
        blocks = lengths.shape[0]
        block = out_ref.shape[0] // blocks
        row = lax.broadcasted_iota(jnp.int32, (block, out_ref.shape[1]), 0)
        for b in range(blocks):
            here = slice(b * block, (b + 1) * block)
            out_ref[here, :] = jnp.where(row < lengths[b], out_ref[here, :], 0.0)


def base_half(tokens, base_key, side, sides, lengths, *after):
    rows, depth = tokens.shape
    wide = base_key.shape[1] // sides
    step = 1024
    return pl.pallas_call(
        base_kernel,
        grid_spec=pltpu.PrefetchScalarGridSpec(
            num_scalar_prefetch=2,
            grid=(depth // step,),
            in_specs=[
                pl.BlockSpec((rows, step), lambda i, s, n: (0, i)),
                pl.BlockSpec((step, wide), lambda i, s, n: (i, s[0])),
            ]
            + [ANY] * len(after),
            out_specs=pl.BlockSpec((rows, wide), lambda i, s, n: (0, 0)),
        ),
        out_shape=jax.ShapeDtypeStruct((rows, wide), jnp.float32),
        cost_estimate=pl.CostEstimate(
            flops=2 * rows * depth * wide, bytes_accessed=2 * depth * (rows + wide) + 4 * rows * wide, transcendentals=0
        ),
        name="base",
    )(side.reshape(1), lengths, tokens, base_key, *after)


def rank_kernel(ring, pair, ids, owner, here, tok_ref, *refs):
    pieces = refs[:-4]
    after, out_ref, held, sems = refs[-4:]
    per, rank = pieces[0].shape[:2]
    blocks = out_ref.shape[1]
    feats = tok_ref.shape[2]
    block = out_ref.shape[3]
    mate = pl.program_id(0)

    @pl.when(mate == 0)
    def _():
        copies = [
            pltpu.make_async_copy(piece, held.at[pl.ds(j * per, per)], sems.at[j])
            for j, piece in enumerate(pieces)
        ]
        for copy in copies:
            copy.start()
        for copy in copies:
            copy.wait()

    for b in range(blocks):
        slot = owner[ids[mate * blocks + b]]
        chip = slot // per
        away = lax.rem(chip // pair - here[0] + ring, ring)
        way = lax.rem(lax.rem(chip, pair) - here[1] + pair, pair)
        at = (way * ring + away) * per + lax.rem(slot, per)
        tok = tok_ref[0, b * block : (b + 1) * block, :]
        part = lax.dot_general(
            held[at, :, :feats], tok, (((1,), (1,)), ((), ())), preferred_element_type=jnp.float32
        )
        out_ref[0, b, :rank, :] = part.astype(out_ref.dtype)
        out_ref[0, b, rank:, :] = held[at, :, feats:]


def rank_parts(ids, owner, here, tok, pieces, ring, pair, blocks, after):
    shares, tall, feats = tok.shape
    block = tall // blocks // LANES * LANES
    per, rank, wide = pieces[0].shape
    shape = (shares, blocks, 2 * rank, block)
    return pl.pallas_call(
        functools.partial(rank_kernel, ring, pair),
        grid=(shares,),
        in_specs=[SMEM, SMEM, SMEM, pl.BlockSpec((1, tall, feats), lambda i: (i, 0, 0))] + [ANY] * (len(pieces) + 1),
        out_specs=pl.BlockSpec((1,) + shape[1:], lambda i: (i, 0, 0, 0)),
        out_shape=jax.ShapeDtypeStruct(shape, tok.dtype),
        scratch_shapes=[
            pltpu.VMEM((len(pieces) * per, rank, wide), tok.dtype),
            pltpu.SemaphoreType.DMA((len(pieces),)),
        ],
        cost_estimate=pl.CostEstimate(
            flops=2 * tok.size * rank, bytes_accessed=2 * tok.size, transcendentals=0
        ),
        name="rank",
    )(ids, owner, here, tok, *pieces, after)


def final_kernel(mine, theirs, base, out_ref):
    shares, blocks, tall, block = mine.shape
    rank = tall // 2
    wide = out_ref.shape[1]
    for b in range(blocks):
        here = slice(b * block, (b + 1) * block)
        total = mine[0, b, :rank, :].astype(jnp.float32) + theirs[0, b, :rank, :].astype(jnp.float32)
        for s in range(1, shares):
            total += mine[s, b, :rank, :].astype(jnp.float32) + theirs[s, b, :rank, :].astype(jnp.float32)
        up = jnp.concatenate([mine[s, b, rank:, :] for s in range(wide // LANES)], axis=1)
        delta = lax.dot_general(
            total.astype(jnp.bfloat16), up, (((0,), (0,)), ((), ())), preferred_element_type=jnp.float32
        )
        out_ref[here, :] = (base[here, :] + delta).astype(out_ref.dtype)


def final(mine, theirs, base, dtype):
    return pl.pallas_call(
        final_kernel,
        in_specs=[VMEM, VMEM, VMEM],
        out_specs=VMEM,
        out_shape=jax.ShapeDtypeStruct(base.shape, dtype),
        compiler_params=BIG,
        name="final",
    )(mine, theirs, base)


def body(tokens, base_key, adapter_down, adapter_up, adapter_ids, owner_slot, lengths):
    groups, ring, pair = lax.axis_size("groups"), lax.axis_size("ring"), lax.axis_size("pair")
    sides = lax.axis_size("tensor")
    shares = groups * pair
    g, z, y, t = (lax.axis_index(name) for name in ("groups", "ring", "pair", "tensor"))
    rows = tokens.shape[0]
    blocks = lengths.shape[0]

    def across(x):
        return lax.ppermute(x, "tensor", [(i, (i + 1) % sides) for i in range(sides)])

    def to_plane(x):
        return lax.all_to_all(x, PLANE, split_axis=0, concat_axis=0, tiled=True)

    def along(x, step):
        return lax.ppermute(x, "ring", [(a, (a + step) % ring) for a in range(ring)])

    def first_hops(x):
        return {0: x, ring - 1: along(x, 1), **({1: along(x, -1)} if ring > 2 else {})}

    def more_hops(held, way, after):
        for k in range(2, ring // 2 + 1):
            if 2 * k < ring or way % 2 == 0:
                if k == 2:
                    held[ring - 1] = hand_on(held[ring - 1], after)
                held[ring - k] = along(held[ring - k + 1], 1)
            if 2 * k < ring or way % 2 == 1:
                if k == 2:
                    held[1] = hand_on(held[1], after)
                held[k] = along(held[k - 1], -1)
        return [held[k] for k in range(ring)]

    packed = pack(jnp.swapaxes(adapter_down, 1, 2), adapter_up, shares, [g * pair + (y + w) % pair for w in range(pair)])
    slabs = spread(tokens, lengths, adapter_ids, shares)
    swapped = [
        lax.ppermute(packed[pair - w], "pair", [(a, (a - w) % pair) for a in range(pair)]) for w in range(1, pair)
    ]
    firsts = [first_hops(piece) for piece in [packed[0]] + swapped]
    tok = to_plane(hand_on(slabs, *swapped))
    ids = tok[:, rows, :blocks].astype(jnp.int32).reshape(-1)

    base_out = base_half(tokens, base_key, (t + 1) % sides, sides, lengths)
    base_in = across(base_out)
    base_mine = base_half(tokens, base_key, t, sides, lengths, base_out)
    base = base_mine + base_in
    pieces = [more_hops(held, way, base_out if way == 0 else base_mine) for way, held in enumerate(firsts)]

    here = jnp.stack([z, y]).astype(jnp.int32)
    flat = [piece for way in pieces for piece in way]
    mine = to_plane(rank_parts(ids, owner_slot, here, tok, flat, ring, pair, blocks, base))
    return final(mine, across(mine), base, tokens.dtype)


def solution(mesh):
    groups, dp, sides = (mesh.shape[name] for name in ("groups", "dp", "tensor"))
    pair = 2 if dp % 2 == 0 else 1
    cut = Mesh(mesh.devices.reshape(groups, dp // pair, pair, sides), ("groups", "ring", "pair", "tensor"))
    stored = ("ring", "pair")
    placed = (
        P(WHOLE, "tensor"),
        P("tensor", None),
        P(stored, "tensor", None),
        P(stored, None, "tensor"),
        P(WHOLE, None),
        P(),
        P(WHOLE),
    )
    return jax.shard_map(body, mesh=cut, in_specs=placed, out_specs=P(WHOLE, "tensor"), check_vma=False)
```

```python
import functools

import jax
import jax.numpy as jnp
from jax import lax
from jax.experimental import pallas as pl
from jax.experimental.pallas import tpu as pltpu
from jax.sharding import Mesh
from jax.sharding import PartitionSpec as P

LANES = 128
ANY = pl.BlockSpec(memory_space=pl.ANY)
SMEM = pl.BlockSpec(memory_space=pltpu.SMEM)
VMEM = pl.BlockSpec(memory_space=pltpu.VMEM)
HBM = pl.BlockSpec(memory_space=pltpu.HBM)
BIG = pltpu.CompilerParams(vmem_limit_bytes=55 * 1024 * 1024)
PLANE = ("groups", "pair")
WHOLE = ("groups", "ring", "pair")


def hand_kernel(*refs):
    pass


def hand_on(x, *after):
    return pl.pallas_call(
        hand_kernel,
        in_specs=[ANY] * (1 + len(after)),
        out_specs=ANY,
        out_shape=jax.ShapeDtypeStruct(x.shape, x.dtype),
        input_output_aliases={0: 0},
        compiler_params=BIG,
        name="hand",
    )(x, *after)


def pack_kernel(where, down, up, *refs):
    outs, sems = refs[:-1], refs[-1]
    feats = outs[0].shape[2] - LANES
    copies = []
    for way, out in enumerate(outs):
        start = pl.multiple_of(where[way] * feats, LANES)
        tile = pl.multiple_of(lax.rem(where[way], up.shape[2] // LANES) * LANES, LANES)
        copies.append(pltpu.make_async_copy(down.at[:, :, pl.ds(start, feats)], out.at[:, :, :feats], sems.at[way, 0]))
        copies.append(pltpu.make_async_copy(up.at[:, :, pl.ds(tile, LANES)], out.at[:, :, feats:], sems.at[way, 1]))
    for copy in copies:
        copy.start()
    for copy in copies:
        copy.wait()


def pack(down, up, shares, share_of):
    adapters, rank, feats = down.shape
    ways = len(share_of)
    shape = jax.ShapeDtypeStruct((adapters, rank, feats // shares + LANES), down.dtype)
    return pl.pallas_call(
        pack_kernel,
        in_specs=[SMEM, HBM, HBM],
        out_specs=[VMEM] * ways,
        out_shape=[shape] * ways,
        scratch_shapes=[pltpu.SemaphoreType.DMA((ways, 2))],
        compiler_params=BIG,
        name="pack",
    )(jnp.stack(share_of).astype(jnp.int32), down, up)


def spread_kernel(lengths, ids, in_ref, out_ref):
    blocks = lengths.shape[0]
    rows, step = in_ref.shape
    block = rows // blocks
    row = lax.broadcasted_iota(jnp.int32, (block, step), 0)
    for b in range(blocks):
        part = in_ref[b * block : (b + 1) * block, :]
        out_ref[0, b * block : (b + 1) * block, :] = jnp.where(row < lengths[b], part, jnp.zeros_like(part))
    extra = out_ref.shape[1] - rows
    lane = lax.broadcasted_iota(jnp.int32, (extra, step), 1)
    named = jnp.zeros((extra, step), jnp.float32)
    for b in range(blocks):
        named = jnp.where(lane == b, ids[b, 0].astype(jnp.float32), named)
    out_ref[0, rows:, :] = named.astype(out_ref.dtype)


def spread(tokens, lengths, ids, shares):
    rows, feats = tokens.shape
    step = feats // shares
    return pl.pallas_call(
        spread_kernel,
        grid=(shares,),
        in_specs=[SMEM, SMEM, pl.BlockSpec((rows, step), lambda i: (0, i))],
        out_specs=pl.BlockSpec((1, rows + 16, step), lambda i: (i, 0, 0)),
        out_shape=jax.ShapeDtypeStruct((shares, rows + 16, step), tokens.dtype),
        compiler_params=BIG,
        name="spread",
    )(lengths, ids, tokens)


def base_kernel(side, lengths, tok_ref, key_ref, *refs):
    out_ref = refs[-1]
    part = jnp.dot(tok_ref[...], key_ref[...], preferred_element_type=jnp.float32)
    step = pl.program_id(0)

    @pl.when(step == 0)
    def _():
        out_ref[...] = part

    @pl.when(step > 0)
    def _():
        out_ref[...] += part

    @pl.when(step == pl.num_programs(0) - 1)
    def _():
        blocks = lengths.shape[0]
        block = out_ref.shape[0] // blocks
        row = lax.broadcasted_iota(jnp.int32, (block, out_ref.shape[1]), 0)
        for b in range(blocks):
            here = slice(b * block, (b + 1) * block)
            out_ref[here, :] = jnp.where(row < lengths[b], out_ref[here, :], 0.0)


def base_half(tokens, base_key, side, sides, lengths, *after):
    rows, depth = tokens.shape
    wide = base_key.shape[1] // sides
    step = 1024
    return pl.pallas_call(
        base_kernel,
        grid_spec=pltpu.PrefetchScalarGridSpec(
            num_scalar_prefetch=2,
            grid=(depth // step,),
            in_specs=[
                pl.BlockSpec((rows, step), lambda i, s, n: (0, i)),
                pl.BlockSpec((step, wide), lambda i, s, n: (i, s[0])),
            ]
            + [ANY] * len(after),
            out_specs=pl.BlockSpec((rows, wide), lambda i, s, n: (0, 0)),
        ),
        out_shape=jax.ShapeDtypeStruct((rows, wide), jnp.float32),
        cost_estimate=pl.CostEstimate(
            flops=0, bytes_accessed=0, transcendentals=0
        ),
        compiler_params=BIG,
        name="base",
    )(side.reshape(1), lengths, tokens, base_key, *after)


def rank_kernel(ring, pair, ids, owner, here, tok_ref, *refs):
    pieces = refs[:-4]
    after, out_ref, held, sems = refs[-4:]
    per, rank = pieces[0].shape[:2]
    blocks = out_ref.shape[1]
    feats = tok_ref.shape[2]
    block = out_ref.shape[3]
    mate = pl.program_id(0)

    @pl.when(mate == 0)
    def _():
        copies = [
            pltpu.make_async_copy(piece, held.at[pl.ds(j * per, per)], sems.at[j])
            for j, piece in enumerate(pieces)
        ]
        for copy in copies:
            copy.start()
        for copy in copies:
            copy.wait()

    for b in range(blocks):
        slot = owner[ids[mate * blocks + b]]
        chip = slot // per
        away = lax.rem(chip // pair - here[0] + ring, ring)
        way = lax.rem(lax.rem(chip, pair) - here[1] + pair, pair)
        at = (way * ring + away) * per + lax.rem(slot, per)
        tok = tok_ref[0, b * block : (b + 1) * block, :]
        part = lax.dot_general(
            held[at, :, :feats], tok, (((1,), (1,)), ((), ())), preferred_element_type=jnp.float32
        )
        out_ref[0, b, :rank, :] = part.astype(out_ref.dtype)
        out_ref[0, b, rank:, :] = held[at, :, feats:]


def rank_parts(ids, owner, here, tok, pieces, ring, pair, blocks, after):
    shares, tall, feats = tok.shape
    block = tall // blocks // LANES * LANES
    per, rank, wide = pieces[0].shape
    shape = (shares, blocks, 2 * rank, block)
    return pl.pallas_call(
        functools.partial(rank_kernel, ring, pair),
        grid=(shares,),
        in_specs=[SMEM, SMEM, SMEM, pl.BlockSpec((1, tall, feats), lambda i: (i, 0, 0))] + [ANY] * (len(pieces) + 1),
        out_specs=pl.BlockSpec((1,) + shape[1:], lambda i: (i, 0, 0, 0)),
        out_shape=jax.ShapeDtypeStruct(shape, tok.dtype),
        scratch_shapes=[
            pltpu.VMEM((len(pieces) * per, rank, wide), tok.dtype),
            pltpu.SemaphoreType.DMA((len(pieces),)),
        ],
        cost_estimate=pl.CostEstimate(
            flops=2 * tok.size * rank, bytes_accessed=2 * tok.size, transcendentals=0
        ),
        compiler_params=BIG,
        name="rank",
    )(ids, owner, here, tok, *pieces, after)


def final_kernel(mine, theirs, base, out_ref):
    shares, blocks, tall, block = mine.shape
    rank = tall // 2
    wide = out_ref.shape[1]
    for b in range(blocks):
        here = slice(b * block, (b + 1) * block)
        total = mine[0, b, :rank, :].astype(jnp.float32) + theirs[0, b, :rank, :].astype(jnp.float32)
        for s in range(1, shares):
            total += mine[s, b, :rank, :].astype(jnp.float32) + theirs[s, b, :rank, :].astype(jnp.float32)
        up = jnp.concatenate([mine[s, b, rank:, :] for s in range(wide // LANES)], axis=1)
        delta = lax.dot_general(
            total.astype(jnp.bfloat16), up, (((0,), (0,)), ((), ())), preferred_element_type=jnp.float32
        )
        out_ref[here, :] = (base[here, :] + delta).astype(out_ref.dtype)


def final(mine, theirs, base, dtype):
    return pl.pallas_call(
        final_kernel,
        in_specs=[VMEM, VMEM, VMEM],
        out_specs=VMEM,
        out_shape=jax.ShapeDtypeStruct(base.shape, dtype),
        compiler_params=BIG,
        name="final",
    )(mine, theirs, base)


def body(tokens, base_key, adapter_down, adapter_up, adapter_ids, owner_slot, lengths):
    groups, ring, pair = lax.axis_size("groups"), lax.axis_size("ring"), lax.axis_size("pair")
    sides = lax.axis_size("tensor")
    shares = groups * pair
    g, z, y, t = (lax.axis_index(name) for name in ("groups", "ring", "pair", "tensor"))
    rows = tokens.shape[0]
    blocks = lengths.shape[0]

    def across(x):
        return lax.ppermute(x, "tensor", [(i, (i + 1) % sides) for i in range(sides)])

    def to_plane(x):
        return lax.all_to_all(x, PLANE, split_axis=0, concat_axis=0, tiled=True)

    def along(x, step):
        return lax.ppermute(x, "ring", [(a, (a + step) % ring) for a in range(ring)])

    def first_hops(x):
        return {0: x, ring - 1: along(x, 1), **({1: along(x, -1)} if ring > 2 else {})}

    def more_hops(held, way, after):
        for k in range(2, ring // 2 + 1):
            if 2 * k < ring or way % 2 == 0:
                if k == 2:
                    held[ring - 1] = hand_on(held[ring - 1], after)
                held[ring - k] = along(held[ring - k + 1], 1)
            if 2 * k < ring or way % 2 == 1:
                if k == 2:
                    held[1] = hand_on(held[1], after)
                held[k] = along(held[k - 1], -1)
        return [held[k] for k in range(ring)]

    packed = pack(jnp.swapaxes(adapter_down, 1, 2), adapter_up, shares, [g * pair + (y + w) % pair for w in range(pair)])
    slabs = spread(tokens, lengths, adapter_ids, shares)
    swapped = [
        lax.ppermute(packed[pair - w], "pair", [(a, (a - w) % pair) for a in range(pair)]) for w in range(1, pair)
    ]
    firsts = [first_hops(piece) for piece in [packed[0]] + swapped]
    tok = to_plane(hand_on(slabs, *swapped))
    ids = tok[:, rows, :blocks].astype(jnp.int32).reshape(-1)

    base_out = base_half(tokens, base_key, (t + 1) % sides, sides, lengths)
    base_in = across(base_out)
    base_mine = base_half(tokens, base_key, t, sides, lengths, base_out)
    base = base_mine + base_in
    pieces = [more_hops(held, way, base_out if way == 0 else base_mine) for way, held in enumerate(firsts)]

    here = jnp.stack([z, y]).astype(jnp.int32)
    flat = [piece for way in pieces for piece in way]
    mine = to_plane(rank_parts(ids, owner_slot, here, tok, flat, ring, pair, blocks, base))
    return final(mine, across(mine), base, tokens.dtype)


def solution(mesh):
    groups, dp, sides = (mesh.shape[name] for name in ("groups", "dp", "tensor"))
    pair = 2 if dp % 2 == 0 else 1
    cut = Mesh(mesh.devices.reshape(groups, dp // pair, pair, sides), ("groups", "ring", "pair", "tensor"))
    stored = ("ring", "pair")
    placed = (
        P(WHOLE, "tensor"),
        P("tensor", None),
        P(stored, "tensor", None),
        P(stored, None, "tensor"),
        P(WHOLE, None),
        P(),
        P(WHOLE),
    )
    return jax.shard_map(body, mesh=cut, in_specs=placed, out_specs=P(WHOLE, "tensor"), check_vma=False)
```

```python
import functools

import jax
import jax.numpy as jnp
from jax import lax
from jax.experimental import pallas as pl
from jax.experimental.pallas import tpu as pltpu
from jax.sharding import Mesh
from jax.sharding import PartitionSpec as P

LANES = 128
ANY = pl.BlockSpec(memory_space=pl.ANY)
SMEM = pl.BlockSpec(memory_space=pltpu.SMEM)
VMEM = pl.BlockSpec(memory_space=pltpu.VMEM)
HBM = pl.BlockSpec(memory_space=pltpu.HBM)
BIG = pltpu.CompilerParams(vmem_limit_bytes=32 * 1024 * 1024)
PLANE = ("groups", "pair")
WHOLE = ("groups", "ring", "pair")


def hand_kernel(*refs):
    pass


def hand_on(x, *after):
    return pl.pallas_call(
        hand_kernel,
        in_specs=[ANY] * (1 + len(after)),
        out_specs=ANY,
        out_shape=jax.ShapeDtypeStruct(x.shape, x.dtype),
        input_output_aliases={0: 0},
        name="hand",
    )(x, *after)


def pack_kernel(down, up, *refs):
    outs, sems = refs[:-1], refs[-1]
    feats = outs[0].shape[2] - LANES
    copies = []
    for way, out in enumerate(outs):
        share = lax.axis_index("groups") * len(outs) + lax.rem(lax.axis_index("pair") + way, len(outs))
        start = pl.multiple_of(share * feats, LANES)
        tile = pl.multiple_of(lax.rem(share, up.shape[2] // LANES) * LANES, LANES)
        copies.append(pltpu.make_async_copy(down.at[:, :, pl.ds(start, feats)], out.at[:, :, :feats], sems.at[way, 0]))
        copies.append(pltpu.make_async_copy(up.at[:, :, pl.ds(tile, LANES)], out.at[:, :, feats:], sems.at[way, 1]))
    for copy in copies:
        copy.start()
    for copy in copies:
        copy.wait()


def pack(down, up, shares, ways):
    adapters, rank, feats = down.shape
    shape = jax.ShapeDtypeStruct((adapters, rank, feats // shares + LANES), down.dtype)
    return pl.pallas_call(
        pack_kernel,
        in_specs=[HBM, HBM],
        out_specs=[VMEM] * ways,
        out_shape=[shape] * ways,
        scratch_shapes=[pltpu.SemaphoreType.DMA((ways, 2))],
        name="pack",
    )(down, up)


def spread_kernel(lengths, ids, in_ref, out_ref):
    blocks = lengths.shape[0]
    rows, step = in_ref.shape
    block = rows // blocks
    row = lax.broadcasted_iota(jnp.int32, (block, step), 0)
    for b in range(blocks):
        part = in_ref[b * block : (b + 1) * block, :]
        out_ref[0, b * block : (b + 1) * block, :] = jnp.where(row < lengths[b], part, jnp.zeros_like(part))
    extra = out_ref.shape[1] - rows
    lane = lax.broadcasted_iota(jnp.int32, (extra, step), 1)
    named = jnp.zeros((extra, step), jnp.float32)
    for b in range(blocks):
        named = jnp.where(lane == b, ids[b, 0].astype(jnp.float32), named)
    out_ref[0, rows:, :] = named.astype(out_ref.dtype)


def spread(tokens, lengths, ids, shares):
    rows, feats = tokens.shape
    step = feats // shares
    return pl.pallas_call(
        spread_kernel,
        grid=(shares,),
        in_specs=[SMEM, SMEM, pl.BlockSpec((rows, step), lambda i: (0, i))],
        out_specs=pl.BlockSpec((1, rows + 16, step), lambda i: (i, 0, 0)),
        out_shape=jax.ShapeDtypeStruct((shares, rows + 16, step), tokens.dtype),
        name="spread",
    )(lengths, ids, tokens)


def base_kernel(side, lengths, tok_ref, key_ref, *refs):
    out_ref = refs[-1]
    part = jnp.dot(tok_ref[...], key_ref[...], preferred_element_type=jnp.float32)
    step = pl.program_id(0)

    @pl.when(step == 0)
    def _():
        out_ref[...] = part

    @pl.when(step > 0)
    def _():
        out_ref[...] += part

    @pl.when(step == pl.num_programs(0) - 1)
    def _():
        blocks = lengths.shape[0]
        block = out_ref.shape[0] // blocks
        row = lax.broadcasted_iota(jnp.int32, (block, out_ref.shape[1]), 0)
        for b in range(blocks):
            here = slice(b * block, (b + 1) * block)
            out_ref[here, :] = jnp.where(row < lengths[b], out_ref[here, :], 0.0)


def base_half(tokens, base_key, side, sides, lengths, *after):
    rows, depth = tokens.shape
    wide = base_key.shape[1] // sides
    step = 1024
    return pl.pallas_call(
        base_kernel,
        grid_spec=pltpu.PrefetchScalarGridSpec(
            num_scalar_prefetch=2,
            grid=(depth // step,),
            in_specs=[
                pl.BlockSpec((rows, step), lambda i, s, n: (0, i)),
                pl.BlockSpec((step, wide), lambda i, s, n: (i, s[0])),
            ]
            + [ANY] * len(after),
            out_specs=pl.BlockSpec((rows, wide), lambda i, s, n: (0, 0)),
        ),
        out_shape=jax.ShapeDtypeStruct((rows, wide), jnp.float32),
        cost_estimate=pl.CostEstimate(
            flops=0, bytes_accessed=0, transcendentals=0
        ),
        name="base",
    )(side.reshape(1), lengths, tokens, base_key, *after)


def mate_at(k, sign, groups, pair):
    kg, ky = k // pair, k % pair
    g = lax.rem(lax.axis_index("groups") + sign * kg + groups, groups)
    y = lax.rem(lax.axis_index("pair") + sign * ky + pair, pair)
    return g * pair + y


def rank_kernel(groups, ring, pair, ids, owner, tok, *refs):
    shares = groups * pair
    tok_held, held, tok_sems, sems = refs[-4:]
    outs = refs[-4 - shares : -4]
    pieces = refs[: ring * pair]
    per, rank = pieces[0].shape[:2]
    blocks, _, block = outs[0].shape
    feats = tok.shape[2]
    z, y = lax.axis_index("ring"), lax.axis_index("pair")
    mates = [mate_at(k, 1, groups, pair) for k in range(shares)]
    copies = [pltpu.make_async_copy(piece, held.at[pl.ds(j * per, per)], sems.at[j]) for j, piece in enumerate(pieces)]
    tok_copies = [
        pltpu.make_async_copy(tok.at[mates[k], : blocks * block, :], tok_held.at[k], tok_sems.at[k])
        for k in range(shares)
    ]
    for copy in copies + tok_copies:
        copy.start()
    for copy in copies:
        copy.wait()
    for k in range(shares):
        tok_copies[k].wait()
        for b in range(blocks):
            slot = owner[ids[mates[k] * blocks + b]]
            chip = slot // per
            away = lax.rem(chip // pair - z + ring, ring)
            way = lax.rem(lax.rem(chip, pair) - y + pair, pair)
            at = (way * ring + away) * per + lax.rem(slot, per)
            part = lax.dot_general(
                held[at, :, :feats],
                tok_held[k, b * block : (b + 1) * block, :],
                (((1,), (1,)), ((), ())),
                preferred_element_type=jnp.float32,
            )
            outs[k][b, :rank, :] = part.astype(outs[k].dtype)
            outs[k][b, rank:, :] = held[at, :, feats:]


def rank_parts(ids, owner, tok, pieces, groups, ring, pair, blocks, after):
    shares, tall, feats = tok.shape
    block = tall // blocks // LANES * LANES
    per, rank, wide = pieces[0].shape
    return pl.pallas_call(
        functools.partial(rank_kernel, groups, ring, pair),
        in_specs=[SMEM, SMEM, ANY] + [ANY] * (len(pieces) + 1),
        out_specs=[VMEM] * shares,
        out_shape=[jax.ShapeDtypeStruct((blocks, 2 * rank, block), tok.dtype)] * shares,
        scratch_shapes=[
            pltpu.VMEM((shares, blocks * block, feats), tok.dtype),
            pltpu.VMEM((len(pieces) * per, rank, wide), tok.dtype),
            pltpu.SemaphoreType.DMA((shares,)),
            pltpu.SemaphoreType.DMA((len(pieces),)),
        ],
        compiler_params=BIG,
        cost_estimate=pl.CostEstimate(flops=2 * tok.size * rank, bytes_accessed=2 * tok.size, transcendentals=0),
        name="rank",
    )(ids, owner, tok, *pieces, after)


def final_kernel(groups, pair, base, *refs):
    shares = groups * pair
    mine, theirs, out_ref, up = refs[:shares], refs[shares : 2 * shares], refs[-2], refs[-1]
    blocks, tall, block = mine[0].shape
    rank = tall // 2
    tiles = out_ref.shape[1] // LANES
    for b in range(blocks):
        here = slice(b * block, (b + 1) * block)
        total = mine[0][b, :rank, :].astype(jnp.float32)
        for part in mine[1:] + theirs:
            total += part[b, :rank, :].astype(jnp.float32)
        for k in range(shares):
            tile = lax.rem(mate_at(k, -1, groups, pair), tiles)
            up[b, :, pl.ds(pl.multiple_of(tile * LANES, LANES), LANES)] = mine[k][b, rank:, :]
        delta = lax.dot_general(
            total.astype(jnp.bfloat16), up[b], (((0,), (0,)), ((), ())), preferred_element_type=jnp.float32
        )
        out_ref[here, :] = (base[here, :] + delta).astype(out_ref.dtype)


def final(mine, theirs, base, groups, pair, dtype):
    blocks, tall, _ = mine[0].shape
    return pl.pallas_call(
        functools.partial(final_kernel, groups, pair),
        in_specs=[VMEM] * (1 + 2 * len(mine)),
        out_specs=VMEM,
        out_shape=jax.ShapeDtypeStruct(base.shape, dtype),
        scratch_shapes=[pltpu.VMEM((blocks, tall // 2, base.shape[1]), mine[0].dtype)],
        compiler_params=BIG,
        name="final",
    )(base, *mine, *theirs)


def body(tokens, base_key, adapter_down, adapter_up, adapter_ids, owner_slot, lengths):
    groups, ring, pair = lax.axis_size("groups"), lax.axis_size("ring"), lax.axis_size("pair")
    sides = lax.axis_size("tensor")
    shares = groups * pair
    t = lax.axis_index("tensor")
    rows = tokens.shape[0]
    blocks = lengths.shape[0]

    def across(x):
        return lax.ppermute(x, "tensor", [(i, (i + 1) % sides) for i in range(sides)])

    def to_plane(x):
        return lax.all_to_all(x, PLANE, split_axis=0, concat_axis=0, tiled=True)

    def along(x, step):
        return lax.ppermute(x, "ring", [(a, (a + step) % ring) for a in range(ring)])

    def first_hops(x):
        return {0: x, ring - 1: along(x, 1), **({1: along(x, -1)} if ring > 2 else {})}

    def in_plane(x, kg, ky):
        pairs = []
        for a in range(groups):
            for b in range(pair):
                pairs.append((a * pair + b, (a + kg) % groups * pair + (b + ky) % pair))
        return lax.ppermute(x, PLANE, pairs)

    def more_hops(held, way, *after):
        for k in range(2, ring // 2 + 1):
            if 2 * k < ring or way % 2 == 0:
                if k == 2:
                    held[ring - 1] = hand_on(held[ring - 1], *after)
                held[ring - k] = along(held[ring - k + 1], 1)
            if 2 * k < ring or way % 2 == 1:
                if k == 2:
                    held[1] = hand_on(held[1], *after)
                held[k] = along(held[k - 1], -1)
        return [held[k] for k in range(ring)]

    packed = pack(jnp.swapaxes(adapter_down, 1, 2), adapter_up, shares, pair)
    slabs = spread(tokens, lengths, adapter_ids, shares)
    swapped = [
        lax.ppermute(packed[pair - w], "pair", [(a, (a - w) % pair) for a in range(pair)]) for w in range(1, pair)
    ]
    firsts = [first_hops(piece) for piece in [packed[0]] + swapped]
    tok = to_plane(hand_on(slabs, *swapped))
    ids = tok[:, rows, :blocks].astype(jnp.int32).reshape(-1)

    near = [firsts[0][k] for k in firsts[0] if k > 0]
    base_out = base_half(tokens, base_key, (t + 1) % sides, sides, lengths, *near)
    base_in = across(base_out)
    base_mine = base_half(tokens, base_key, t, sides, lengths)
    base = base_mine + base_in
    pieces = [
        more_hops(held, way, base_out, *([held[ring - 1]] if way % 2 and ring > 2 else [])) for way, held in enumerate(firsts)
    ]

    flat = [piece for way in pieces for piece in way]
    parts = rank_parts(ids, owner_slot, tok, flat, groups, ring, pair, blocks, base)
    mine = [parts[0]] + [in_plane(parts[k], k // pair, k % pair) for k in range(1, shares)]
    theirs = [across(part) for part in mine]
    return final(mine, theirs, base, groups, pair, tokens.dtype)


def solution(mesh):
    groups, dp, sides = (mesh.shape[name] for name in ("groups", "dp", "tensor"))
    pair = 2 if dp % 2 == 0 else 1
    cut = Mesh(mesh.devices.reshape(groups, dp // pair, pair, sides), ("groups", "ring", "pair", "tensor"))
    stored = ("ring", "pair")
    placed = (
        P(WHOLE, "tensor"),
        P("tensor", None),
        P(stored, "tensor", None),
        P(stored, None, "tensor"),
        P(WHOLE, None),
        P(),
        P(WHOLE),
    )
    return jax.shard_map(body, mesh=cut, in_specs=placed, out_specs=P(WHOLE, "tensor"), check_vma=False)
```

```python
import functools

import jax
import jax.numpy as jnp
from jax import lax
from jax.experimental import pallas as pl
from jax.experimental.pallas import tpu as pltpu
from jax.sharding import Mesh
from jax.sharding import PartitionSpec as P

LANES = 128
ANY = pl.BlockSpec(memory_space=pl.ANY)
SMEM = pl.BlockSpec(memory_space=pltpu.SMEM)
VMEM = pl.BlockSpec(memory_space=pltpu.VMEM)
HBM = pl.BlockSpec(memory_space=pltpu.HBM)
BIG = pltpu.CompilerParams(vmem_limit_bytes=32 * 1024 * 1024)
PLANE = ("groups", "pair")
WHOLE = ("groups", "ring", "pair")


def hand_kernel(*refs):
    pass


def hand_on(x, *after):
    return pl.pallas_call(
        hand_kernel,
        in_specs=[ANY] * (1 + len(after)),
        out_specs=ANY,
        out_shape=jax.ShapeDtypeStruct(x.shape, x.dtype),
        input_output_aliases={0: 0},
        name="hand",
    )(x, *after)


def pack_kernel(down, up, *refs):
    outs, sems = refs[:-1], refs[-1]
    feats = outs[0].shape[2] - LANES
    copies = []
    for way, out in enumerate(outs):
        share = lax.axis_index("groups") * len(outs) + lax.rem(lax.axis_index("pair") + way, len(outs))
        start = pl.multiple_of(share * feats, LANES)
        tile = pl.multiple_of(lax.rem(share, up.shape[2] // LANES) * LANES, LANES)
        copies.append(pltpu.make_async_copy(down.at[:, :, pl.ds(start, feats)], out.at[:, :, :feats], sems.at[way, 0]))
        copies.append(pltpu.make_async_copy(up.at[:, :, pl.ds(tile, LANES)], out.at[:, :, feats:], sems.at[way, 1]))
    for copy in copies:
        copy.start()
    for copy in copies:
        copy.wait()


def pack(down, up, shares, ways):
    adapters, rank, feats = down.shape
    shape = jax.ShapeDtypeStruct((adapters, rank, feats // shares + LANES), down.dtype)
    return pl.pallas_call(
        pack_kernel,
        in_specs=[HBM, HBM],
        out_specs=[VMEM] * ways,
        out_shape=[shape] * ways,
        scratch_shapes=[pltpu.SemaphoreType.DMA((ways, 2))],
        name="pack",
    )(down, up)


def spread_kernel(lengths, ids, in_ref, out_ref):
    blocks = lengths.shape[0]
    rows, step = in_ref.shape
    block = rows // blocks
    row = lax.broadcasted_iota(jnp.int32, (block, step), 0)
    for b in range(blocks):
        part = in_ref[b * block : (b + 1) * block, :]
        out_ref[0, b * block : (b + 1) * block, :] = jnp.where(row < lengths[b], part, jnp.zeros_like(part))
    extra = out_ref.shape[1] - rows
    lane = lax.broadcasted_iota(jnp.int32, (extra, step), 1)
    named = jnp.zeros((extra, step), jnp.float32)
    for b in range(blocks):
        named = jnp.where(lane == b, ids[b, 0].astype(jnp.float32), named)
    out_ref[0, rows:, :] = named.astype(out_ref.dtype)


def spread(tokens, lengths, ids, shares):
    rows, feats = tokens.shape
    step = feats // shares
    return pl.pallas_call(
        spread_kernel,
        grid=(shares,),
        in_specs=[SMEM, SMEM, pl.BlockSpec((rows, step), lambda i: (0, i))],
        out_specs=pl.BlockSpec((1, rows + 16, step), lambda i: (i, 0, 0)),
        out_shape=jax.ShapeDtypeStruct((shares, rows + 16, step), tokens.dtype),
        name="spread",
    )(lengths, ids, tokens)


def base_kernel(side, lengths, tok_ref, key_ref, *refs):
    out_ref = refs[-1]
    part = jnp.dot(tok_ref[...], key_ref[...], preferred_element_type=jnp.float32)
    step = pl.program_id(0)

    @pl.when(step == 0)
    def _():
        out_ref[...] = part

    @pl.when(step > 0)
    def _():
        out_ref[...] += part

    @pl.when(step == pl.num_programs(0) - 1)
    def _():
        blocks = lengths.shape[0]
        block = out_ref.shape[0] // blocks
        row = lax.broadcasted_iota(jnp.int32, (block, out_ref.shape[1]), 0)
        for b in range(blocks):
            here = slice(b * block, (b + 1) * block)
            out_ref[here, :] = jnp.where(row < lengths[b], out_ref[here, :], 0.0)


def base_half(tokens, base_key, side, sides, lengths, *after):
    rows, depth = tokens.shape
    wide = base_key.shape[1] // sides
    step = 1024
    return pl.pallas_call(
        base_kernel,
        grid_spec=pltpu.PrefetchScalarGridSpec(
            num_scalar_prefetch=2,
            grid=(depth // step,),
            in_specs=[
                pl.BlockSpec((rows, step), lambda i, s, n: (0, i)),
                pl.BlockSpec((step, wide), lambda i, s, n: (i, s[0])),
            ]
            + [ANY] * len(after),
            out_specs=pl.BlockSpec((rows, wide), lambda i, s, n: (0, 0)),
        ),
        out_shape=jax.ShapeDtypeStruct((rows, wide), jnp.float32),
        cost_estimate=pl.CostEstimate(
            flops=0, bytes_accessed=0, transcendentals=0
        ),
        name="base",
    )(side.reshape(1), lengths, tokens, base_key, *after)


def mate_at(k, sign, groups, pair):
    kg, ky = k // pair, k % pair
    g = lax.rem(lax.axis_index("groups") + sign * kg + groups, groups)
    y = lax.rem(lax.axis_index("pair") + sign * ky + pair, pair)
    return g * pair + y


def rank_kernel(groups, ring, pair, ids, owner, tok, *refs):
    shares = groups * pair
    tok_held, held, tok_sems, sems = refs[-4:]
    outs = refs[-4 - shares : -4]
    pieces = refs[: len(refs) - 5 - shares]
    per, rank = owner.shape[0] // (ring * pair), pieces[0].shape[1]
    blocks, _, block = outs[0].shape
    feats = tok.shape[2]
    z, y = lax.axis_index("ring"), lax.axis_index("pair")
    mates = [mate_at(k, 1, groups, pair) for k in range(shares)]
    copies, start = [], 0
    for j, piece in enumerate(pieces):
        copies.append(pltpu.make_async_copy(piece, held.at[pl.ds(start, piece.shape[0])], sems.at[j]))
        start += piece.shape[0]
    tok_copies = [
        pltpu.make_async_copy(tok.at[mates[k], : blocks * block, :], tok_held.at[k], tok_sems.at[k])
        for k in range(shares)
    ]
    for copy in copies + tok_copies:
        copy.start()
    for copy in copies:
        copy.wait()
    for k in range(shares):
        tok_copies[k].wait()
        for b in range(blocks):
            slot = owner[ids[mates[k] * blocks + b]]
            chip = slot // per
            away = lax.rem(chip // pair - z + ring, ring)
            way = lax.rem(lax.rem(chip, pair) - y + pair, pair)
            at = (away * pair + way) * per + lax.rem(slot, per)
            part = lax.dot_general(
                held[at, :, :feats],
                tok_held[k, b * block : (b + 1) * block, :],
                (((1,), (1,)), ((), ())),
                preferred_element_type=jnp.float32,
            )
            outs[k][b, :rank, :] = part.astype(outs[k].dtype)
            outs[k][b, rank:, :] = held[at, :, feats:]


def rank_parts(ids, owner, tok, pieces, groups, ring, pair, blocks, after):
    shares, tall, feats = tok.shape
    block = tall // blocks // LANES * LANES
    _, rank, wide = pieces[0].shape
    return pl.pallas_call(
        functools.partial(rank_kernel, groups, ring, pair),
        in_specs=[SMEM, SMEM, ANY] + [ANY] * (len(pieces) + 1),
        out_specs=[VMEM] * shares,
        out_shape=[jax.ShapeDtypeStruct((blocks, 2 * rank, block), tok.dtype)] * shares,
        scratch_shapes=[
            pltpu.VMEM((shares, blocks * block, feats), tok.dtype),
            pltpu.VMEM((owner.shape[0], rank, wide), tok.dtype),
            pltpu.SemaphoreType.DMA((shares,)),
            pltpu.SemaphoreType.DMA((len(pieces),)),
        ],
        cost_estimate=pl.CostEstimate(flops=2 * tok.size * rank, bytes_accessed=2 * tok.size, transcendentals=0),
        name="rank",
    )(ids, owner, tok, *pieces, after)


def final_kernel(groups, pair, base, *refs):
    shares = groups * pair
    mine, theirs, out_ref, up = refs[:shares], refs[shares : 2 * shares], refs[-2], refs[-1]
    blocks, tall, block = mine[0].shape
    rank = tall // 2
    tiles = out_ref.shape[1] // LANES
    for b in range(blocks):
        here = slice(b * block, (b + 1) * block)
        total = mine[0][b, :rank, :].astype(jnp.float32)
        for part in mine[1:] + theirs:
            total += part[b, :rank, :].astype(jnp.float32)
        for k in range(shares):
            tile = lax.rem(mate_at(k, -1, groups, pair), tiles)
            up[b, :, pl.ds(pl.multiple_of(tile * LANES, LANES), LANES)] = mine[k][b, rank:, :]
        delta = lax.dot_general(
            total.astype(jnp.bfloat16), up[b], (((0,), (0,)), ((), ())), preferred_element_type=jnp.float32
        )
        out_ref[here, :] = (base[here, :] + delta).astype(out_ref.dtype)


def final(mine, theirs, base, groups, pair, dtype):
    blocks, tall, _ = mine[0].shape
    return pl.pallas_call(
        functools.partial(final_kernel, groups, pair),
        in_specs=[VMEM] * (1 + 2 * len(mine)),
        out_specs=VMEM,
        out_shape=jax.ShapeDtypeStruct(base.shape, dtype),
        scratch_shapes=[pltpu.VMEM((blocks, tall // 2, base.shape[1]), mine[0].dtype)],
        compiler_params=BIG,
        name="final",
    )(base, *mine, *theirs)


def body(tokens, base_key, adapter_down, adapter_up, adapter_ids, owner_slot, lengths):
    groups, ring, pair = lax.axis_size("groups"), lax.axis_size("ring"), lax.axis_size("pair")
    sides = lax.axis_size("tensor")
    shares = groups * pair
    t = lax.axis_index("tensor")
    rows = tokens.shape[0]
    blocks = lengths.shape[0]

    def across(x):
        return lax.ppermute(x, "tensor", [(i, (i + 1) % sides) for i in range(sides)])

    def to_plane(x):
        return lax.all_to_all(x, PLANE, split_axis=0, concat_axis=0, tiled=True)

    def along(x, step):
        return lax.ppermute(x, "ring", [(a, (a + step) % ring) for a in range(ring)])

    def in_plane(x, kg, ky):
        pairs = []
        for a in range(groups):
            for b in range(pair):
                pairs.append((a * pair + b, (a + kg) % groups * pair + (b + ky) % pair))
        return lax.ppermute(x, PLANE, pairs)

    packed = pack(jnp.swapaxes(adapter_down, 1, 2), adapter_up, shares, pair)
    slabs = spread(tokens, lengths, adapter_ids, shares)
    swapped = [
        lax.ppermute(packed[pair - w], "pair", [(a, (a - w) % pair) for a in range(pair)]) for w in range(1, pair)
    ]
    held = {0: jnp.concatenate([packed[0]] + swapped)}
    tok = to_plane(hand_on(slabs, *swapped))
    ids = tok[:, rows, :blocks].astype(jnp.int32).reshape(-1)
    held[ring - 1] = along(held[0], 1)
    if ring > 2:
        held[1] = along(held[0], -1)

    base_out = base_half(tokens, base_key, (t + 1) % sides, sides, lengths, *swapped)
    base_in = across(base_out)
    base_mine = base_half(tokens, base_key, t, sides, lengths, *swapped)
    base = base_mine + base_in

    for k in range(2, ring // 2 + 1):
        if k == 2:
            held[ring - 1] = hand_on(held[ring - 1], base_out, base_mine, held[1])
            held[1] = hand_on(held[1], base_out, base_mine, held[ring - 1])
        if 2 * k < ring:
            held[ring - k] = along(held[ring - k + 1], 1)
            held[k] = along(held[k - 1], -1)
        else:
            half = held[0].shape[0] // 2
            one = along(lax.slice_in_dim(held[k + 1], 0, half), 1)
            two = along(lax.slice_in_dim(held[k - 1], half, 2 * half), -1)
    pieces = [held[k] for k in range(ring // 2)] + [one, two] + [held[k] for k in range(ring // 2 + 1, ring)]
    parts = rank_parts(ids, owner_slot, tok, pieces, groups, ring, pair, blocks, base)
    mine = [parts[0]] + [in_plane(parts[k], k // pair, k % pair) for k in range(1, shares)]
    theirs = [across(part) for part in mine]
    return final(mine, theirs, base, groups, pair, tokens.dtype)


def solution(mesh):
    groups, dp, sides = (mesh.shape[name] for name in ("groups", "dp", "tensor"))
    pair = 2 if dp % 2 == 0 else 1
    cut = Mesh(mesh.devices.reshape(groups, dp // pair, pair, sides), ("groups", "ring", "pair", "tensor"))
    stored = ("ring", "pair")
    placed = (
        P(WHOLE, "tensor"),
        P("tensor", None),
        P(stored, "tensor", None),
        P(stored, None, "tensor"),
        P(WHOLE, None),
        P(),
        P(WHOLE),
    )
    return jax.shard_map(body, mesh=cut, in_specs=placed, out_specs=P(WHOLE, "tensor"), check_vma=False)
```

```python
import functools

import jax
import jax.numpy as jnp
from jax import lax
from jax.experimental import pallas as pl
from jax.experimental.pallas import tpu as pltpu
from jax.sharding import Mesh
from jax.sharding import PartitionSpec as P

LANES = 128
ANY = pl.BlockSpec(memory_space=pl.ANY)
SMEM = pl.BlockSpec(memory_space=pltpu.SMEM)
VMEM = pl.BlockSpec(memory_space=pltpu.VMEM)
HBM = pl.BlockSpec(memory_space=pltpu.HBM)
BIG = pltpu.CompilerParams(vmem_limit_bytes=32 * 1024 * 1024)
PLANE = ("groups", "pair")
WHOLE = ("groups", "ring", "pair")


def hand_kernel(*refs):
    pass


def hand_on(x, *after):
    return pl.pallas_call(
        hand_kernel,
        in_specs=[ANY] * (1 + len(after)),
        out_specs=ANY,
        out_shape=jax.ShapeDtypeStruct(x.shape, x.dtype),
        input_output_aliases={0: 0},
        name="hand",
    )(x, *after)


def pack_kernel(down, up, *refs):
    outs, sems = refs[:-1], refs[-1]
    feats = outs[0].shape[2] - LANES
    copies = []
    for way, out in enumerate(outs):
        share = lax.axis_index("groups") * len(outs) + lax.rem(lax.axis_index("pair") + way, len(outs))
        start = pl.multiple_of(share * feats, LANES)
        tile = pl.multiple_of(lax.rem(share, up.shape[2] // LANES) * LANES, LANES)
        copies.append(pltpu.make_async_copy(down.at[:, :, pl.ds(start, feats)], out.at[:, :, :feats], sems.at[way, 0]))
        copies.append(pltpu.make_async_copy(up.at[:, :, pl.ds(tile, LANES)], out.at[:, :, feats:], sems.at[way, 1]))
    for copy in copies:
        copy.start()
    for copy in copies:
        copy.wait()


def pack(down, up, shares, ways):
    adapters, rank, feats = down.shape
    shape = jax.ShapeDtypeStruct((adapters, rank, feats // shares + LANES), down.dtype)
    return pl.pallas_call(
        pack_kernel,
        in_specs=[HBM, HBM],
        out_specs=[VMEM] * ways,
        out_shape=[shape] * ways,
        scratch_shapes=[pltpu.SemaphoreType.DMA((ways, 2))],
        name="pack",
    )(down, up)


def spread_kernel(lengths, ids, in_ref, out_ref):
    blocks = lengths.shape[0]
    rows, step = in_ref.shape
    block = rows // blocks
    row = lax.broadcasted_iota(jnp.int32, (block, step), 0)
    for b in range(blocks):
        part = in_ref[b * block : (b + 1) * block, :]
        out_ref[0, b * block : (b + 1) * block, :] = jnp.where(row < lengths[b], part, jnp.zeros_like(part))
    extra = out_ref.shape[1] - rows
    lane = lax.broadcasted_iota(jnp.int32, (extra, step), 1)
    named = jnp.zeros((extra, step), jnp.float32)
    for b in range(blocks):
        named = jnp.where(lane == b, ids[b].astype(jnp.float32), named)
    out_ref[0, rows:, :] = named.astype(out_ref.dtype)


def spread(tokens, lengths, ids, shares):
    rows, feats = tokens.shape
    step = feats // shares
    return pl.pallas_call(
        spread_kernel,
        grid=(shares,),
        in_specs=[SMEM, SMEM, pl.BlockSpec((rows, step), lambda i: (0, i))],
        out_specs=pl.BlockSpec((1, rows + 16, step), lambda i: (i, 0, 0)),
        out_shape=jax.ShapeDtypeStruct((shares, rows + 16, step), tokens.dtype),
        name="spread",
    )(lengths, ids, tokens)


def base_kernel(side, lengths, tok_ref, key_ref, *refs):
    out_ref = refs[-1]
    part = jnp.dot(tok_ref[...], key_ref[...], preferred_element_type=jnp.float32)
    step = pl.program_id(0)

    @pl.when(step == 0)
    def _():
        out_ref[...] = part

    @pl.when(step > 0)
    def _():
        out_ref[...] += part

    @pl.when(step == pl.num_programs(0) - 1)
    def _():
        blocks = lengths.shape[0]
        block = out_ref.shape[0] // blocks
        row = lax.broadcasted_iota(jnp.int32, (block, out_ref.shape[1]), 0)
        for b in range(blocks):
            here = slice(b * block, (b + 1) * block)
            out_ref[here, :] = jnp.where(row < lengths[b], out_ref[here, :], 0.0)


def base_half(tokens, base_key, side, sides, lengths, *after):
    rows, depth = tokens.shape
    wide = base_key.shape[1] // sides
    step = 1024
    return pl.pallas_call(
        base_kernel,
        grid_spec=pltpu.PrefetchScalarGridSpec(
            num_scalar_prefetch=2,
            grid=(depth // step,),
            in_specs=[
                pl.BlockSpec((rows, step), lambda i, s, n: (0, i)),
                pl.BlockSpec((step, wide), lambda i, s, n: (i, s[0])),
            ]
            + [ANY] * len(after),
            out_specs=pl.BlockSpec((rows, wide), lambda i, s, n: (0, 0)),
        ),
        out_shape=jax.ShapeDtypeStruct((rows, wide), jnp.float32),
        cost_estimate=pl.CostEstimate(
            flops=0, bytes_accessed=0, transcendentals=0
        ),
        name="base",
    )(side.reshape(1), lengths, tokens, base_key, *after)


def mate_at(k, sign, groups, pair):
    kg, ky = k // pair, k % pair
    g = lax.rem(lax.axis_index("groups") + sign * kg + groups, groups)
    y = lax.rem(lax.axis_index("pair") + sign * ky + pair, pair)
    return g * pair + y


def rank_kernel(groups, ring, pair, ids, owner, tok, *refs):
    shares = groups * pair
    tok_held, held, tok_sems, sems = refs[-4:]
    outs = refs[-4 - shares : -4]
    pieces = refs[: ring * pair]
    per, rank = pieces[0].shape[:2]
    blocks, _, block = outs[0].shape
    feats = tok.shape[2]
    z, y = lax.axis_index("ring"), lax.axis_index("pair")
    mates = [mate_at(k, 1, groups, pair) for k in range(shares)]
    copies = [pltpu.make_async_copy(piece, held.at[pl.ds(j * per, per)], sems.at[j]) for j, piece in enumerate(pieces)]
    tok_copies = [
        pltpu.make_async_copy(tok.at[mates[k], : blocks * block, :], tok_held.at[k], tok_sems.at[k])
        for k in range(shares)
    ]
    for copy in copies + tok_copies:
        copy.start()
    for copy in copies:
        copy.wait()
    for k in range(shares):
        tok_copies[k].wait()
        for b in range(blocks):
            slot = owner[ids[mates[k] * blocks + b]]
            chip = slot // per
            away = lax.rem(chip // pair - z + ring, ring)
            way = lax.rem(lax.rem(chip, pair) - y + pair, pair)
            at = (way * ring + away) * per + lax.rem(slot, per)
            part = lax.dot_general(
                held[at, :, :feats],
                tok_held[k, b * block : (b + 1) * block, :],
                (((1,), (1,)), ((), ())),
                preferred_element_type=jnp.float32,
            )
            outs[k][b, :rank, :] = part.astype(outs[k].dtype)
            outs[k][b, rank:, :] = held[at, :, feats:]


def rank_parts(ids, owner, tok, pieces, groups, ring, pair, blocks):
    shares, tall, feats = tok.shape
    block = tall // blocks // LANES * LANES
    per, rank, wide = pieces[0].shape
    return pl.pallas_call(
        functools.partial(rank_kernel, groups, ring, pair),
        in_specs=[SMEM, SMEM, ANY] + [ANY] * len(pieces),
        out_specs=[VMEM] * shares,
        out_shape=[jax.ShapeDtypeStruct((blocks, 2 * rank, block), tok.dtype)] * shares,
        scratch_shapes=[
            pltpu.VMEM((shares, blocks * block, feats), tok.dtype),
            pltpu.VMEM((len(pieces) * per, rank, wide), tok.dtype),
            pltpu.SemaphoreType.DMA((shares,)),
            pltpu.SemaphoreType.DMA((len(pieces),)),
        ],
        cost_estimate=pl.CostEstimate(flops=2 * tok.size * rank, bytes_accessed=2 * tok.size, transcendentals=0),
        name="rank",
    )(ids, owner, tok, *pieces)


def final_kernel(groups, pair, base_a, base_b, *refs):
    shares = groups * pair
    mine, theirs, out_ref, up = refs[:shares], refs[shares : 2 * shares], refs[-2], refs[-1]
    blocks, tall, block = mine[0].shape
    rank = tall // 2
    tiles = out_ref.shape[1] // LANES
    for b in range(blocks):
        here = slice(b * block, (b + 1) * block)
        total = mine[0][b, :rank, :].astype(jnp.float32)
        for part in mine[1:] + theirs:
            total += part[b, :rank, :].astype(jnp.float32)
        for k in range(shares):
            tile = lax.rem(mate_at(k, -1, groups, pair), tiles)
            up[b, :, pl.ds(pl.multiple_of(tile * LANES, LANES), LANES)] = mine[k][b, rank:, :]
        delta = lax.dot_general(
            total.astype(jnp.bfloat16), up[b], (((0,), (0,)), ((), ())), preferred_element_type=jnp.float32
        )
        out_ref[here, :] = (base_a[here, :] + base_b[here, :] + delta).astype(out_ref.dtype)


def final(mine, theirs, base, groups, pair, dtype):
    blocks, tall, _ = mine[0].shape
    return pl.pallas_call(
        functools.partial(final_kernel, groups, pair),
        in_specs=[VMEM] * (2 + 2 * len(mine)),
        out_specs=VMEM,
        out_shape=jax.ShapeDtypeStruct(base[0].shape, dtype),
        scratch_shapes=[pltpu.VMEM((blocks, tall // 2, base[0].shape[1]), mine[0].dtype)],
        compiler_params=BIG,
        name="final",
    )(*base, *mine, *theirs)


def body(tokens, base_key, adapter_down, adapter_up, adapter_ids, owner_slot, lengths):
    groups, ring, pair = lax.axis_size("groups"), lax.axis_size("ring"), lax.axis_size("pair")
    sides = lax.axis_size("tensor")
    shares = groups * pair
    t = lax.axis_index("tensor")
    rows = tokens.shape[0]
    blocks = lengths.shape[0]

    def across(x):
        return lax.ppermute(x, "tensor", [(i, (i + 1) % sides) for i in range(sides)])

    def to_plane(x):
        return lax.all_to_all(x, PLANE, split_axis=0, concat_axis=0, tiled=True)

    def along(x, step):
        return lax.ppermute(x, "ring", [(a, (a + step) % ring) for a in range(ring)])

    def first_hops(x):
        return {0: x, ring - 1: along(x, 1), **({1: along(x, -1)} if ring > 2 else {})}

    def in_plane(x, kg, ky):
        pairs = []
        for a in range(groups):
            for b in range(pair):
                pairs.append((a * pair + b, (a + kg) % groups * pair + (b + ky) % pair))
        return lax.ppermute(x, PLANE, pairs)

    def more_hops(held, way, *after):
        for k in range(2, ring // 2 + 1):
            if 2 * k < ring or way % 2 == 0:
                if k == 2:
                    held[ring - 1] = hand_on(held[ring - 1], held[1], *after)
                held[ring - k] = along(held[ring - k + 1], 1)
            if 2 * k < ring or way % 2 == 1:
                if k == 2:
                    held[1] = hand_on(held[1], held[ring - 1], *after)
                held[k] = along(held[k - 1], -1)
        return [held[k] for k in range(ring)]

    packed = pack(jnp.swapaxes(adapter_down, 1, 2), adapter_up, shares, pair)
    slabs = spread(tokens, lengths, adapter_ids.reshape(-1), shares)
    swapped = [
        lax.ppermute(packed[pair - w], "pair", [(a, (a - w) % pair) for a in range(pair)]) for w in range(1, pair)
    ]
    firsts = [first_hops(piece) for piece in [packed[0]] + swapped]
    tok = to_plane(hand_on(slabs, *swapped))
    ids = tok[:, rows, :blocks].astype(jnp.int32).reshape(-1)

    base_out = base_half(tokens, base_key, (t + 1) % sides, sides, lengths, *swapped)
    base_mine = base_half(tokens, base_key, t, sides, lengths, *swapped)
    pieces = [
        more_hops(held, way, base_out, base_mine)
        for way, held in enumerate(firsts)
    ]

    flat = [piece for way in pieces for piece in way]
    parts = rank_parts(ids, owner_slot, tok, flat, groups, ring, pair, blocks)
    mine = [parts[0]] + [in_plane(parts[k], k // pair, k % pair) for k in range(1, shares)]
    theirs = [across(part) for part in mine]
    base_in = across(hand_on(base_out, parts[0]))
    return final(mine, theirs, [base_mine, base_in], groups, pair, tokens.dtype)


def solution(mesh):
    groups, dp, sides = (mesh.shape[name] for name in ("groups", "dp", "tensor"))
    pair = 2 if dp % 2 == 0 else 1
    cut = Mesh(mesh.devices.reshape(groups, dp // pair, pair, sides), ("groups", "ring", "pair", "tensor"))
    stored = ("ring", "pair")
    placed = (
        P(WHOLE, "tensor"),
        P("tensor", None),
        P(stored, "tensor", None),
        P(stored, None, "tensor"),
        P(WHOLE, None),
        P(),
        P(WHOLE),
    )
    return jax.shard_map(body, mesh=cut, in_specs=placed, out_specs=P(WHOLE, "tensor"), check_vma=False)
```

```python
import functools

import jax
import jax.numpy as jnp
from jax import lax
from jax.experimental import pallas as pl
from jax.experimental.pallas import tpu as pltpu
from jax.sharding import Mesh
from jax.sharding import PartitionSpec as P

LANES = 128
ANY = pl.BlockSpec(memory_space=pl.ANY)
SMEM = pl.BlockSpec(memory_space=pltpu.SMEM)
VMEM = pl.BlockSpec(memory_space=pltpu.VMEM)
HBM = pl.BlockSpec(memory_space=pltpu.HBM)
BIG = pltpu.CompilerParams(vmem_limit_bytes=32 * 1024 * 1024)
PLANE = ("groups", "pair")
WHOLE = ("groups", "ring", "pair")


def hand_kernel(*refs):
    pass


def hand_on(x, *after):
    return pl.pallas_call(
        hand_kernel,
        in_specs=[ANY] * (1 + len(after)),
        out_specs=ANY,
        out_shape=jax.ShapeDtypeStruct(x.shape, x.dtype),
        input_output_aliases={0: 0},
        name="hand",
    )(x, *after)


def go_kernel(*refs):
    refs[-1][...] = jnp.zeros(refs[-1].shape, refs[-1].dtype)


def go_after(*arrays):
    return pl.pallas_call(
        go_kernel,
        in_specs=[ANY] * len(arrays),
        out_specs=VMEM,
        out_shape=jax.ShapeDtypeStruct((16, LANES), jnp.bfloat16),
        name="go",
    )(*arrays)


def pack_kernel(ways, down, up, *refs):
    outs, sems = refs[:-1], refs[-1]
    feats = outs[0].shape[2] - LANES
    adapters = down.shape[0]
    copies = []
    for way in range(ways):
        share = lax.axis_index("groups") * ways + lax.rem(lax.axis_index("pair") + way, ways)
        start = pl.multiple_of(share * feats, LANES)
        tile = pl.multiple_of(lax.rem(share, up.shape[2] // LANES) * LANES, LANES)
        for a in range(adapters):
            if way == 0:
                to = outs[0].at[a]
            else:
                to = outs[1 + (way - 1) * adapters + a].at[0]
            sem = sems.at[way, a]
            copies.append(pltpu.make_async_copy(down.at[a, :, pl.ds(start, feats)], to.at[:, :feats], sem.at[0]))
            copies.append(pltpu.make_async_copy(up.at[a, :, pl.ds(tile, LANES)], to.at[:, feats:], sem.at[1]))
    for copy in copies:
        copy.start()
    for copy in copies:
        copy.wait()


def pack(down, up, shares, ways):
    adapters, rank, feats = down.shape
    wide = feats // shares + LANES
    shapes = [(adapters, rank, wide)] + [(1, rank, wide)] * (adapters * (ways - 1))
    outs = pl.pallas_call(
        functools.partial(pack_kernel, ways),
        in_specs=[HBM, HBM],
        out_specs=[VMEM] * len(shapes),
        out_shape=[jax.ShapeDtypeStruct(shape, down.dtype) for shape in shapes],
        scratch_shapes=[pltpu.SemaphoreType.DMA((ways, adapters, 2))],
        name="pack",
    )(down, up)
    return outs[0], [outs[1 + w * adapters : 1 + (w + 1) * adapters] for w in range(ways - 1)]


def spread_kernel(lengths, ids, in_ref, out_ref):
    blocks = lengths.shape[0]
    rows, step = in_ref.shape
    block = rows // blocks
    row = lax.broadcasted_iota(jnp.int32, (block, step), 0)
    for b in range(blocks):
        part = in_ref[b * block : (b + 1) * block, :]
        out_ref[0, b * block : (b + 1) * block, :] = jnp.where(row < lengths[b], part, jnp.zeros_like(part))
    extra = out_ref.shape[1] - rows
    lane = lax.broadcasted_iota(jnp.int32, (extra, step), 1)
    named = jnp.zeros((extra, step), jnp.float32)
    for b in range(blocks):
        named = jnp.where(lane == b, ids[b].astype(jnp.float32), named)
    out_ref[0, rows:, :] = named.astype(out_ref.dtype)


def spread(tokens, lengths, ids, shares):
    rows, feats = tokens.shape
    step = feats // shares
    return pl.pallas_call(
        spread_kernel,
        grid=(shares,),
        in_specs=[SMEM, SMEM, pl.BlockSpec((rows, step), lambda i: (0, i))],
        out_specs=pl.BlockSpec((1, rows + 16, step), lambda i: (i, 0, 0)),
        out_shape=jax.ShapeDtypeStruct((shares, rows + 16, step), tokens.dtype),
        name="spread",
    )(lengths, ids, tokens)


def base_kernel(side, lengths, tok_ref, key_ref, *refs):
    out_ref = refs[-1]
    part = jnp.dot(tok_ref[...], key_ref[...], preferred_element_type=jnp.float32)
    step = pl.program_id(0)

    @pl.when(step == 0)
    def _():
        out_ref[...] = part

    @pl.when(step > 0)
    def _():
        out_ref[...] += part

    @pl.when(step == pl.num_programs(0) - 1)
    def _():
        blocks = lengths.shape[0]
        block = out_ref.shape[0] // blocks
        row = lax.broadcasted_iota(jnp.int32, (block, out_ref.shape[1]), 0)
        for b in range(blocks):
            here = slice(b * block, (b + 1) * block)
            out_ref[here, :] = jnp.where(row < lengths[b], out_ref[here, :], 0.0)


def base_half(tokens, base_key, side, sides, lengths, *after):
    rows, depth = tokens.shape
    wide = base_key.shape[1] // sides
    step = 1024
    return pl.pallas_call(
        base_kernel,
        grid_spec=pltpu.PrefetchScalarGridSpec(
            num_scalar_prefetch=2,
            grid=(depth // step,),
            in_specs=[
                pl.BlockSpec((rows, step), lambda i, s, n: (0, i)),
                pl.BlockSpec((step, wide), lambda i, s, n: (i, s[0])),
            ]
            + [ANY] * len(after),
            out_specs=pl.BlockSpec((rows, wide), lambda i, s, n: (0, 0)),
        ),
        out_shape=jax.ShapeDtypeStruct((rows, wide), jnp.float32),
        cost_estimate=pl.CostEstimate(
            flops=0, bytes_accessed=0, transcendentals=0
        ),
        name="base",
    )(side.reshape(1), lengths, tokens, base_key, *after)


def mate_at(k, sign, groups, pair):
    kg, ky = k // pair, k % pair
    g = lax.rem(lax.axis_index("groups") + sign * kg + groups, groups)
    y = lax.rem(lax.axis_index("pair") + sign * ky + pair, pair)
    return g * pair + y


def rank_kernel(groups, ring, pair, ids, owner, tok, *refs):
    shares = groups * pair
    tok_held, held, tok_sems, sems = refs[-4:]
    outs = refs[-4 - shares : -4]
    pieces = refs[: ring * pair]
    per, rank = pieces[0].shape[:2]
    blocks, _, block = outs[0].shape
    feats = tok.shape[2]
    z, y = lax.axis_index("ring"), lax.axis_index("pair")
    mates = [mate_at(k, 1, groups, pair) for k in range(shares)]
    copies = [pltpu.make_async_copy(piece, held.at[pl.ds(j * per, per)], sems.at[j]) for j, piece in enumerate(pieces)]
    tok_copies = [
        pltpu.make_async_copy(tok.at[mates[k], : blocks * block, :], tok_held.at[k], tok_sems.at[k])
        for k in range(shares)
    ]
    for copy in copies + tok_copies:
        copy.start()
    for copy in copies:
        copy.wait()
    for k in range(shares):
        tok_copies[k].wait()
        for b in range(blocks):
            slot = owner[ids[mates[k] * blocks + b]]
            chip = slot // per
            away = lax.rem(chip // pair - z + ring, ring)
            way = lax.rem(lax.rem(chip, pair) - y + pair, pair)
            at = (way * ring + away) * per + lax.rem(slot, per)
            part = lax.dot_general(
                held[at, :, :feats],
                tok_held[k, b * block : (b + 1) * block, :],
                (((1,), (1,)), ((), ())),
                preferred_element_type=jnp.float32,
            )
            outs[k][b, :rank, :] = part.astype(outs[k].dtype)
            outs[k][b, rank:, :] = held[at, :, feats:]


def rank_parts(ids, owner, tok, pieces, groups, ring, pair, blocks):
    shares, tall, feats = tok.shape
    block = tall // blocks // LANES * LANES
    per, rank, wide = pieces[0].shape
    return pl.pallas_call(
        functools.partial(rank_kernel, groups, ring, pair),
        in_specs=[SMEM, SMEM, ANY] + [ANY] * len(pieces),
        out_specs=[VMEM] * shares,
        out_shape=[jax.ShapeDtypeStruct((blocks, 2 * rank, block), tok.dtype)] * shares,
        scratch_shapes=[
            pltpu.VMEM((shares, blocks * block, feats), tok.dtype),
            pltpu.VMEM((len(pieces) * per, rank, wide), tok.dtype),
            pltpu.SemaphoreType.DMA((shares,)),
            pltpu.SemaphoreType.DMA((len(pieces),)),
        ],
        cost_estimate=pl.CostEstimate(flops=2 * tok.size * rank, bytes_accessed=2 * tok.size, transcendentals=0),
        name="rank",
    )(ids, owner, tok, *pieces)


def final_kernel(groups, pair, base_a, base_b, *refs):
    shares = groups * pair
    mine, theirs, out_ref, up = refs[:shares], refs[shares : 2 * shares], refs[-2], refs[-1]
    blocks, tall, block = mine[0].shape
    rank = tall // 2
    tiles = out_ref.shape[1] // LANES
    for b in range(blocks):
        here = slice(b * block, (b + 1) * block)
        total = mine[0][b, :rank, :].astype(jnp.float32)
        for part in mine[1:] + theirs:
            total += part[b, :rank, :].astype(jnp.float32)
        for k in range(shares):
            tile = lax.rem(mate_at(k, -1, groups, pair), tiles)
            up[b, :, pl.ds(pl.multiple_of(tile * LANES, LANES), LANES)] = mine[k][b, rank:, :]
        delta = lax.dot_general(
            total.astype(jnp.bfloat16), up[b], (((0,), (0,)), ((), ())), preferred_element_type=jnp.float32
        )
        out_ref[here, :] = (base_a[here, :] + base_b[here, :] + delta).astype(out_ref.dtype)


def final(mine, theirs, base, groups, pair, dtype):
    blocks, tall, _ = mine[0].shape
    return pl.pallas_call(
        functools.partial(final_kernel, groups, pair),
        in_specs=[VMEM] * (2 + 2 * len(mine)),
        out_specs=VMEM,
        out_shape=jax.ShapeDtypeStruct(base[0].shape, dtype),
        scratch_shapes=[pltpu.VMEM((blocks, tall // 2, base[0].shape[1]), mine[0].dtype)],
        compiler_params=BIG,
        name="final",
    )(*base, *mine, *theirs)


def body(tokens, base_key, adapter_down, adapter_up, adapter_ids, owner_slot, lengths):
    groups, ring, pair = lax.axis_size("groups"), lax.axis_size("ring"), lax.axis_size("pair")
    sides = lax.axis_size("tensor")
    shares = groups * pair
    t = lax.axis_index("tensor")
    rows = tokens.shape[0]
    blocks = lengths.shape[0]

    def across(x):
        return lax.ppermute(x, "tensor", [(i, (i + 1) % sides) for i in range(sides)])

    def to_plane(x):
        return lax.all_to_all(x, PLANE, split_axis=0, concat_axis=0, tiled=True)

    def along(x, step):
        return lax.ppermute(x, "ring", [(a, (a + step) % ring) for a in range(ring)])

    def first_hops(x):
        return {0: x, ring - 1: along(x, 1), **({1: along(x, -1)} if ring > 2 else {})}

    def in_plane(x, kg, ky):
        pairs = []
        for a in range(groups):
            for b in range(pair):
                pairs.append((a * pair + b, (a + kg) % groups * pair + (b + ky) % pair))
        return lax.ppermute(x, PLANE, pairs)

    def more_hops(held, way, *after):
        for k in range(2, ring // 2 + 1):
            if 2 * k < ring or way % 2 == 0:
                if k == 2:
                    held[ring - 1] = hand_on(held[ring - 1], held[1], *after)
                held[ring - k] = along(held[ring - k + 1], 1)
            if 2 * k < ring or way % 2 == 1:
                if k == 2:
                    held[1] = hand_on(held[1], held[ring - 1], *after)
                held[k] = along(held[k - 1], -1)
        return [held[k] for k in range(ring)]

    own, others = pack(jnp.swapaxes(adapter_down, 1, 2), adapter_up, shares, pair)
    slabs = spread(tokens, lengths, adapter_ids.reshape(-1), shares)
    swapped, first_in = [], []
    for w in range(1, pair):
        back = [(a, (a - w) % pair) for a in range(pair)]
        halves = [lax.ppermute(piece, "pair", back) for piece in others[pair - w - 1]]
        swapped.append(jnp.concatenate(halves))
        first_in.append(halves[0])
    firsts = [first_hops(piece) for piece in [own] + swapped]
    go = across(go_after(*(firsts[0][k] for k in firsts[0] if k > 0)))
    tok = to_plane(hand_on(slabs, *first_in))
    ids = tok[:, rows, :blocks].astype(jnp.int32).reshape(-1)

    base_out = base_half(tokens, base_key, (t + 1) % sides, sides, lengths, *swapped)
    base_mine = base_half(tokens, base_key, t, sides, lengths, *swapped)
    pieces = [
        more_hops(held, way, go, base_out, base_mine)
        for way, held in enumerate(firsts)
    ]

    flat = [piece for way in pieces for piece in way]
    parts = rank_parts(ids, owner_slot, tok, flat, groups, ring, pair, blocks)
    mine = [parts[0]] + [in_plane(parts[k], k // pair, k % pair) for k in range(1, shares)]
    theirs = [across(part) for part in mine]
    base_in = across(hand_on(base_out, parts[0]))
    return final(mine, theirs, [base_mine, base_in], groups, pair, tokens.dtype)


def solution(mesh):
    groups, dp, sides = (mesh.shape[name] for name in ("groups", "dp", "tensor"))
    pair = 2 if dp % 2 == 0 else 1
    cut = Mesh(mesh.devices.reshape(groups, dp // pair, pair, sides), ("groups", "ring", "pair", "tensor"))
    stored = ("ring", "pair")
    placed = (
        P(WHOLE, "tensor"),
        P("tensor", None),
        P(stored, "tensor", None),
        P(stored, None, "tensor"),
        P(WHOLE, None),
        P(),
        P(WHOLE),
    )
    return jax.shard_map(body, mesh=cut, in_specs=placed, out_specs=P(WHOLE, "tensor"), check_vma=False)
```

```python
import functools

import jax
import jax.numpy as jnp
from jax import lax
from jax.experimental import pallas as pl
from jax.experimental.pallas import tpu as pltpu
from jax.sharding import Mesh
from jax.sharding import PartitionSpec as P

LANES = 128
ANY = pl.BlockSpec(memory_space=pl.ANY)
SMEM = pl.BlockSpec(memory_space=pltpu.SMEM)
VMEM = pl.BlockSpec(memory_space=pltpu.VMEM)
HBM = pl.BlockSpec(memory_space=pltpu.HBM)
BIG = pltpu.CompilerParams(vmem_limit_bytes=32 * 1024 * 1024)
PLANE = ("groups", "pair")
WHOLE = ("groups", "ring", "pair")


def hand_kernel(*refs):
    pass


def hand_on(x, *after):
    return pl.pallas_call(
        hand_kernel,
        in_specs=[ANY] * (1 + len(after)),
        out_specs=ANY,
        out_shape=jax.ShapeDtypeStruct(x.shape, x.dtype),
        input_output_aliases={0: 0},
        name="hand",
    )(x, *after)


def pack_kernel(ways, down, up, *refs):
    outs, sems = refs[:-1], refs[-1]
    feats = outs[0].shape[2] - LANES
    adapters = down.shape[0]
    copies = []
    for way in range(ways):
        share = lax.axis_index("groups") * ways + lax.rem(lax.axis_index("pair") + way, ways)
        start = pl.multiple_of(share * feats, LANES)
        tile = pl.multiple_of(lax.rem(share, up.shape[2] // LANES) * LANES, LANES)
        for a in range(adapters):
            to = outs[adapters + way - 1].at[a] if way else outs[a].at[0]
            sem = sems.at[way, a]
            copies.append(pltpu.make_async_copy(down.at[a, :, pl.ds(start, feats)], to.at[:, :feats], sem.at[0]))
            copies.append(pltpu.make_async_copy(up.at[a, :, pl.ds(tile, LANES)], to.at[:, feats:], sem.at[1]))
    for copy in copies:
        copy.start()
    for copy in copies:
        copy.wait()


def pack(down, up, shares, ways):
    adapters, rank, feats = down.shape
    wide = feats // shares + LANES
    shapes = [(1, rank, wide)] * adapters + [(adapters, rank, wide)] * (ways - 1)
    outs = pl.pallas_call(
        functools.partial(pack_kernel, ways),
        in_specs=[HBM, HBM],
        out_specs=[VMEM] * len(shapes),
        out_shape=[jax.ShapeDtypeStruct(shape, down.dtype) for shape in shapes],
        scratch_shapes=[pltpu.SemaphoreType.DMA((ways, adapters, 2))],
        name="pack",
    )(down, up)
    return outs[:adapters], outs[adapters:]


def spread_kernel(lengths, ids, in_ref, out_ref):
    blocks = lengths.shape[0]
    rows, step = in_ref.shape
    block = rows // blocks
    row = lax.broadcasted_iota(jnp.int32, (block, step), 0)
    for b in range(blocks):
        part = in_ref[b * block : (b + 1) * block, :]
        out_ref[0, b * block : (b + 1) * block, :] = jnp.where(row < lengths[b], part, jnp.zeros_like(part))
    extra = out_ref.shape[1] - rows
    lane = lax.broadcasted_iota(jnp.int32, (extra, step), 1)
    named = jnp.zeros((extra, step), jnp.float32)
    for b in range(blocks):
        named = jnp.where(lane == b, ids[b].astype(jnp.float32), named)
    out_ref[0, rows:, :] = named.astype(out_ref.dtype)


def spread(tokens, lengths, ids, shares):
    rows, feats = tokens.shape
    step = feats // shares
    return pl.pallas_call(
        spread_kernel,
        grid=(shares,),
        in_specs=[SMEM, SMEM, pl.BlockSpec((rows, step), lambda i: (0, i))],
        out_specs=pl.BlockSpec((1, rows + 16, step), lambda i: (i, 0, 0)),
        out_shape=jax.ShapeDtypeStruct((shares, rows + 16, step), tokens.dtype),
        name="spread",
    )(lengths, ids, tokens)


def base_kernel(side, lengths, tok_ref, key_ref, *refs):
    out_ref = refs[-1]
    part = jnp.dot(tok_ref[...], key_ref[...], preferred_element_type=jnp.float32)
    step = pl.program_id(0)

    @pl.when(step == 0)
    def _():
        out_ref[...] = part

    @pl.when(step > 0)
    def _():
        out_ref[...] += part

    @pl.when(step == pl.num_programs(0) - 1)
    def _():
        blocks = lengths.shape[0]
        block = out_ref.shape[0] // blocks
        row = lax.broadcasted_iota(jnp.int32, (block, out_ref.shape[1]), 0)
        for b in range(blocks):
            here = slice(b * block, (b + 1) * block)
            out_ref[here, :] = jnp.where(row < lengths[b], out_ref[here, :], 0.0)


def base_half(tokens, base_key, side, sides, lengths, *after):
    rows, depth = tokens.shape
    wide = base_key.shape[1] // sides
    step = 1024
    return pl.pallas_call(
        base_kernel,
        grid_spec=pltpu.PrefetchScalarGridSpec(
            num_scalar_prefetch=2,
            grid=(depth // step,),
            in_specs=[
                pl.BlockSpec((rows, step), lambda i, s, n: (0, i)),
                pl.BlockSpec((step, wide), lambda i, s, n: (i, s[0])),
            ]
            + [ANY] * len(after),
            out_specs=pl.BlockSpec((rows, wide), lambda i, s, n: (0, 0)),
        ),
        out_shape=jax.ShapeDtypeStruct((rows, wide), jnp.float32),
        cost_estimate=pl.CostEstimate(
            flops=0, bytes_accessed=0, transcendentals=0
        ),
        name="base",
    )(side.reshape(1), lengths, tokens, base_key, *after)


def mate_at(k, sign, groups, pair):
    kg, ky = k // pair, k % pair
    g = lax.rem(lax.axis_index("groups") + sign * kg + groups, groups)
    y = lax.rem(lax.axis_index("pair") + sign * ky + pair, pair)
    return g * pair + y


def rank_kernel(groups, ring, pair, ids, owner, tok, *refs):
    shares = groups * pair
    tok_held, held, tok_sems, sems = refs[-4:]
    outs = refs[-4 - shares : -4]
    pieces = refs[: len(refs) - 4 - shares]
    per, rank = owner.shape[0] // (ring * pair), pieces[0].shape[1]
    blocks, _, block = outs[0].shape
    feats = tok.shape[2]
    z, y = lax.axis_index("ring"), lax.axis_index("pair")
    mates = [mate_at(k, 1, groups, pair) for k in range(shares)]
    copies, start = [], 0
    for j, piece in enumerate(pieces):
        copies.append(pltpu.make_async_copy(piece, held.at[pl.ds(start, piece.shape[0])], sems.at[j]))
        start += piece.shape[0]
    tok_copies = [
        pltpu.make_async_copy(tok.at[mates[k], : blocks * block, :], tok_held.at[k], tok_sems.at[k])
        for k in range(shares)
    ]
    for copy in copies + tok_copies:
        copy.start()
    for copy in copies:
        copy.wait()
    for k in range(shares):
        tok_copies[k].wait()
        for b in range(blocks):
            slot = owner[ids[mates[k] * blocks + b]]
            chip = slot // per
            away = lax.rem(chip // pair - z + ring, ring)
            way = lax.rem(lax.rem(chip, pair) - y + pair, pair)
            at = (way * ring + away) * per + lax.rem(slot, per)
            part = lax.dot_general(
                held[at, :, :feats],
                tok_held[k, b * block : (b + 1) * block, :],
                (((1,), (1,)), ((), ())),
                preferred_element_type=jnp.float32,
            )
            outs[k][b, :rank, :] = part.astype(outs[k].dtype)
            outs[k][b, rank:, :] = held[at, :, feats:]


def rank_parts(ids, owner, tok, pieces, groups, ring, pair, blocks):
    shares, tall, feats = tok.shape
    block = tall // blocks // LANES * LANES
    _, rank, wide = pieces[0].shape
    return pl.pallas_call(
        functools.partial(rank_kernel, groups, ring, pair),
        in_specs=[SMEM, SMEM, ANY] + [ANY] * len(pieces),
        out_specs=[VMEM] * shares,
        out_shape=[jax.ShapeDtypeStruct((blocks, 2 * rank, block), tok.dtype)] * shares,
        scratch_shapes=[
            pltpu.VMEM((shares, blocks * block, feats), tok.dtype),
            pltpu.VMEM((owner.shape[0], rank, wide), tok.dtype),
            pltpu.SemaphoreType.DMA((shares,)),
            pltpu.SemaphoreType.DMA((len(pieces),)),
        ],
        cost_estimate=pl.CostEstimate(flops=2 * tok.size * rank, bytes_accessed=2 * tok.size, transcendentals=0),
        name="rank",
    )(ids, owner, tok, *pieces)


def final_kernel(groups, pair, base_a, base_b, *refs):
    shares = groups * pair
    mine, theirs, out_ref, up = refs[:shares], refs[shares : 2 * shares], refs[-2], refs[-1]
    blocks, tall, block = mine[0].shape
    rank = tall // 2
    tiles = out_ref.shape[1] // LANES
    for b in range(blocks):
        here = slice(b * block, (b + 1) * block)
        total = mine[0][b, :rank, :].astype(jnp.float32)
        for part in mine[1:] + theirs:
            total += part[b, :rank, :].astype(jnp.float32)
        for k in range(shares):
            tile = lax.rem(mate_at(k, -1, groups, pair), tiles)
            up[b, :, pl.ds(pl.multiple_of(tile * LANES, LANES), LANES)] = mine[k][b, rank:, :]
        delta = lax.dot_general(
            total.astype(jnp.bfloat16), up[b], (((0,), (0,)), ((), ())), preferred_element_type=jnp.float32
        )
        out_ref[here, :] = (base_a[here, :] + base_b[here, :] + delta).astype(out_ref.dtype)


def final(mine, theirs, base, groups, pair, dtype):
    blocks, tall, _ = mine[0].shape
    return pl.pallas_call(
        functools.partial(final_kernel, groups, pair),
        in_specs=[VMEM] * (2 + 2 * len(mine)),
        out_specs=VMEM,
        out_shape=jax.ShapeDtypeStruct(base[0].shape, dtype),
        scratch_shapes=[pltpu.VMEM((blocks, tall // 2, base[0].shape[1]), mine[0].dtype)],
        compiler_params=BIG,
        name="final",
    )(*base, *mine, *theirs)


def body(tokens, base_key, adapter_down, adapter_up, adapter_ids, owner_slot, lengths):
    groups, ring, pair = lax.axis_size("groups"), lax.axis_size("ring"), lax.axis_size("pair")
    sides = lax.axis_size("tensor")
    shares = groups * pair
    t = lax.axis_index("tensor")
    rows = tokens.shape[0]
    blocks = lengths.shape[0]

    def across(x):
        return lax.ppermute(x, "tensor", [(i, (i + 1) % sides) for i in range(sides)])

    def to_plane(x):
        return lax.all_to_all(x, PLANE, split_axis=0, concat_axis=0, tiled=True)

    def along(x, step):
        return lax.ppermute(x, "ring", [(a, (a + step) % ring) for a in range(ring)])

    def first_hops(x):
        return {0: x, ring - 1: along(x, 1), **({1: along(x, -1)} if ring > 2 else {})}

    def in_plane(x, kg, ky):
        pairs = []
        for a in range(groups):
            for b in range(pair):
                pairs.append((a * pair + b, (a + kg) % groups * pair + (b + ky) % pair))
        return lax.ppermute(x, PLANE, pairs)

    def more_hops(held, way, *after):
        for k in range(2, ring // 2 + 1):
            if 2 * k < ring or way % 2 == 0:
                if k == 2:
                    held[ring - 1] = hand_on(held[ring - 1], held[1], *after)
                held[ring - k] = along(held[ring - k + 1], 1)
            if 2 * k < ring or way % 2 == 1:
                if k == 2:
                    held[1] = hand_on(held[1], held[ring - 1], *after)
                held[k] = along(held[k - 1], -1)
        return [held[k] for k in range(ring)]

    own, others = pack(jnp.swapaxes(adapter_down, 1, 2), adapter_up, shares, pair)
    slabs = spread(tokens, lengths, adapter_ids.reshape(-1), shares)
    swapped = [lax.ppermute(others[pair - w - 1], "pair", [(a, (a - w) % pair) for a in range(pair)]) for w in range(1, pair)]
    own_firsts = [first_hops(piece) for piece in own]
    firsts = [first_hops(piece) for piece in swapped]
    tok = to_plane(hand_on(slabs, *swapped, *(own_firsts[0][k] for k in own_firsts[0] if k > 0)))
    ids = tok[:, rows, :blocks].astype(jnp.int32).reshape(-1)

    base_out = base_half(tokens, base_key, (t + 1) % sides, sides, lengths, *swapped)
    base_mine = base_half(tokens, base_key, t, sides, lengths, *swapped)
    own_pieces = [more_hops(held, 0, base_out, base_mine) for held in own_firsts]
    pieces = [more_hops(held, 1 + way, base_out, base_mine) for way, held in enumerate(firsts)]
    flat = [piece for same in zip(*own_pieces) for piece in same] + [piece for way in pieces for piece in way]
    parts = rank_parts(ids, owner_slot, tok, flat, groups, ring, pair, blocks)
    mine = [parts[0]] + [in_plane(parts[k], k // pair, k % pair) for k in range(1, shares)]
    theirs = [across(part) for part in mine]
    base_in = across(hand_on(base_out, parts[0]))
    return final(mine, theirs, [base_mine, base_in], groups, pair, tokens.dtype)


def solution(mesh):
    groups, dp, sides = (mesh.shape[name] for name in ("groups", "dp", "tensor"))
    pair = 2 if dp % 2 == 0 else 1
    cut = Mesh(mesh.devices.reshape(groups, dp // pair, pair, sides), ("groups", "ring", "pair", "tensor"))
    stored = ("ring", "pair")
    placed = (
        P(WHOLE, "tensor"),
        P("tensor", None),
        P(stored, "tensor", None),
        P(stored, None, "tensor"),
        P(WHOLE, None),
        P(),
        P(WHOLE),
    )
    return jax.shard_map(body, mesh=cut, in_specs=placed, out_specs=P(WHOLE, "tensor"), check_vma=False)
```

```python
import functools

import jax
import jax.numpy as jnp
from jax import lax
from jax.experimental import pallas as pl
from jax.experimental.pallas import tpu as pltpu
from jax.sharding import Mesh
from jax.sharding import PartitionSpec as P

LANES = 128
ANY = pl.BlockSpec(memory_space=pl.ANY)
SMEM = pl.BlockSpec(memory_space=pltpu.SMEM)
VMEM = pl.BlockSpec(memory_space=pltpu.VMEM)
HBM = pl.BlockSpec(memory_space=pltpu.HBM)
BIG = pltpu.CompilerParams(vmem_limit_bytes=32 * 1024 * 1024)
PLANE = ("groups", "pair")
WHOLE = ("groups", "ring", "pair")


def hand_kernel(*refs):
    pass


def hand_on(x, *after):
    return pl.pallas_call(
        hand_kernel,
        in_specs=[ANY] * (1 + len(after)),
        out_specs=ANY,
        out_shape=jax.ShapeDtypeStruct(x.shape, x.dtype),
        input_output_aliases={0: 0},
        compiler_params=BIG,
        name="hand",
    )(x, *after)


def pack_kernel(ways, down, up, *refs):
    outs, sems = refs[:-1], refs[-1]
    feats = outs[0].shape[2] - LANES
    adapters = down.shape[0]
    copies = []
    for way in range(ways):
        share = lax.axis_index("groups") * ways + lax.rem(lax.axis_index("pair") + way, ways)
        start = pl.multiple_of(share * feats, LANES)
        tile = pl.multiple_of(lax.rem(share, up.shape[2] // LANES) * LANES, LANES)
        for a in range(adapters):
            to = outs[adapters + way - 1].at[a] if way else outs[a].at[0]
            sem = sems.at[way, a]
            copies.append(pltpu.make_async_copy(down.at[a, :, pl.ds(start, feats)], to.at[:, :feats], sem.at[0]))
            copies.append(pltpu.make_async_copy(up.at[a, :, pl.ds(tile, LANES)], to.at[:, feats:], sem.at[1]))
    for copy in copies:
        copy.start()
    for copy in copies:
        copy.wait()


def pack(down, up, shares, ways):
    adapters, rank, feats = down.shape
    wide = feats // shares + LANES
    shapes = [(1, rank, wide)] * adapters + [(adapters, rank, wide)] * (ways - 1)
    outs = pl.pallas_call(
        functools.partial(pack_kernel, ways),
        in_specs=[HBM, HBM],
        out_specs=[VMEM] * len(shapes),
        out_shape=[jax.ShapeDtypeStruct(shape, down.dtype) for shape in shapes],
        scratch_shapes=[pltpu.SemaphoreType.DMA((ways, adapters, 2))],
        compiler_params=BIG,
        name="pack",
    )(down, up)
    return outs[:adapters], outs[adapters:]


def spread_kernel(lengths, ids, tok, out, held, in_sems, out_sems):
    blocks = lengths.shape[0]
    shares, tall, step = held.shape
    rows = tok.shape[0]
    block = rows // blocks

    def read(k, b):
        here = pl.ds(b * block, block)
        return pltpu.make_async_copy(tok.at[here, pl.ds(k * step, step)], held.at[k, here, :], in_sems.at[k, b])

    for k in range(shares):
        for b in range(blocks):
            read(k, b).start()
    lane = lax.broadcasted_iota(jnp.int32, (tall - rows, step), 1)
    named = jnp.zeros((tall - rows, step), jnp.float32)
    for b in range(blocks):
        named = jnp.where(lane == b, ids[b].astype(jnp.float32), named)
    named = named.astype(held.dtype)
    writes = [pltpu.make_async_copy(held.at[k], out.at[k], out_sems.at[k]) for k in range(shares)]
    for k in range(shares):
        held[k, rows:, :] = named
        for b in range(blocks):
            read(k, b).wait()

            @pl.when(lengths[b] < block)
            def _():
                here = slice(b * block, (b + 1) * block)
                row = lax.broadcasted_iota(jnp.int32, (block, step), 0)
                part = held[k, here, :]
                held[k, here, :] = jnp.where(row < lengths[b], part, jnp.zeros_like(part))

        writes[k].start()
    for write in writes:
        write.wait()


def spread(tokens, lengths, ids, shares):
    rows, feats = tokens.shape
    shape = (shares, rows + 16, feats // shares)
    return pl.pallas_call(
        spread_kernel,
        in_specs=[SMEM, SMEM, ANY],
        out_specs=ANY,
        out_shape=jax.ShapeDtypeStruct(shape, tokens.dtype),
        scratch_shapes=[
            pltpu.VMEM(shape, tokens.dtype),
            pltpu.SemaphoreType.DMA((shares, lengths.shape[0])),
            pltpu.SemaphoreType.DMA((shares,)),
        ],
        name="spread",
    )(lengths, ids, tokens)


def base_kernel(side, lengths, tok_ref, key_ref, out_ref, flag_ref):
    part = jnp.dot(tok_ref[...], key_ref[...], preferred_element_type=jnp.float32)
    step = pl.program_id(0)

    @pl.when(step == 0)
    def _():
        out_ref[...] = part

    @pl.when(step > 0)
    def _():
        out_ref[...] += part

    @pl.when(step == pl.num_programs(0) - 1)
    def _():
        flag_ref[...] = jnp.zeros_like(flag_ref)
        blocks = lengths.shape[0]
        block = out_ref.shape[0] // blocks
        row = lax.broadcasted_iota(jnp.int32, (block, out_ref.shape[1]), 0)
        for b in range(blocks):
            here = slice(b * block, (b + 1) * block)
            out_ref[here, :] = jnp.where(row < lengths[b], out_ref[here, :], 0.0)


def base_half(tokens, base_key, side, sides, lengths):
    rows, depth = tokens.shape
    wide = base_key.shape[1] // sides
    step = 1024
    return pl.pallas_call(
        base_kernel,
        grid_spec=pltpu.PrefetchScalarGridSpec(
            num_scalar_prefetch=2,
            grid=(depth // step,),
            in_specs=[
                pl.BlockSpec((rows, step), lambda i, s, n: (0, i)),
                pl.BlockSpec((step, wide), lambda i, s, n: (i, s[0])),
            ],
            out_specs=[
                pl.BlockSpec((rows, wide), lambda i, s, n: (0, 0)),
                pl.BlockSpec((8, LANES), lambda i, s, n: (0, 0)),
            ],
        ),
        out_shape=[jax.ShapeDtypeStruct((rows, wide), jnp.float32), jax.ShapeDtypeStruct((8, LANES), jnp.float32)],
        cost_estimate=pl.CostEstimate(
            flops=0, bytes_accessed=0, transcendentals=0
        ),
        name="base",
    )(side.reshape(1), lengths, tokens, base_key)


def mate_at(k, sign, groups, pair):
    kg, ky = k // pair, k % pair
    g = lax.rem(lax.axis_index("groups") + sign * kg + groups, groups)
    y = lax.rem(lax.axis_index("pair") + sign * ky + pair, pair)
    return g * pair + y


def rank_kernel(groups, ring, pair, rows, owner, tok, *refs):
    shares = groups * pair
    held, sems = refs[-2:]
    outs = refs[-2 - shares : -2]
    pieces = refs[: len(refs) - 2 - shares]
    per, rank = owner.shape[0] // (ring * pair), pieces[0].shape[1]
    blocks, _, block = outs[0].shape
    feats = tok.shape[2]
    z, y = lax.axis_index("ring"), lax.axis_index("pair")
    mates = [mate_at(k, 1, groups, pair) for k in range(shares)]
    copies, start = [], 0
    for j, piece in enumerate(pieces):
        copies.append(pltpu.make_async_copy(piece, held.at[pl.ds(start, piece.shape[0])], sems.at[j]))
        start += piece.shape[0]
    for copy in copies:
        copy.start()
    lane = lax.broadcasted_iota(jnp.int32, (16, LANES), 1)
    row = lax.broadcasted_iota(jnp.int32, (16, LANES), 0)
    slots = []
    for k in range(shares):
        named = tok[mates[k], rows:, :LANES].astype(jnp.float32)
        ids = [jnp.sum(jnp.where((lane == b) & (row == 0), named, 0.0)).astype(jnp.int32) for b in range(blocks)]
        slots.append([owner[i] for i in ids])
    for copy in copies:
        copy.wait()
    for k in range(shares):
        for b in range(blocks):
            slot = slots[k][b]
            chip = slot // per
            away = lax.rem(chip // pair - z + ring, ring)
            way = lax.rem(lax.rem(chip, pair) - y + pair, pair)
            at = (way * ring + away) * per + lax.rem(slot, per)
            part = lax.dot_general(
                held[at, :, :feats],
                tok[mates[k], b * block : (b + 1) * block, :],
                (((1,), (1,)), ((), ())),
                preferred_element_type=jnp.float32,
            )
            outs[k][b, :rank, :] = part.astype(outs[k].dtype)
            outs[k][b, rank:, :] = held[at, :, feats:]


def rank_parts(owner, tok, pieces, groups, ring, pair, rows, blocks):
    shares, tall, feats = tok.shape
    block = rows // blocks
    _, rank, wide = pieces[0].shape
    return pl.pallas_call(
        functools.partial(rank_kernel, groups, ring, pair, rows),
        in_specs=[SMEM, VMEM] + [ANY] * len(pieces),
        out_specs=[VMEM] * shares,
        out_shape=[jax.ShapeDtypeStruct((blocks, 2 * rank, block), tok.dtype)] * shares,
        scratch_shapes=[
            pltpu.VMEM((owner.shape[0], rank, wide), tok.dtype),
            pltpu.SemaphoreType.DMA((len(pieces),)),
        ],
        cost_estimate=pl.CostEstimate(flops=2 * tok.size * rank, bytes_accessed=2 * tok.size, transcendentals=0),
        compiler_params=BIG,
        name="rank",
    )(owner, tok, *pieces)


def final_kernel(groups, pair, base_a, base_b, *refs):
    shares = groups * pair
    mine, theirs, out_ref, up = refs[:shares], refs[shares : 2 * shares], refs[-2], refs[-1]
    blocks, tall, block = mine[0].shape
    rank = tall // 2
    tiles = out_ref.shape[1] // LANES
    for b in range(blocks):
        here = slice(b * block, (b + 1) * block)
        total = mine[0][b, :rank, :].astype(jnp.float32)
        for part in mine[1:] + theirs:
            total += part[b, :rank, :].astype(jnp.float32)
        for k in range(shares):
            tile = lax.rem(mate_at(k, -1, groups, pair), tiles)
            up[b, :, pl.ds(pl.multiple_of(tile * LANES, LANES), LANES)] = mine[k][b, rank:, :]
        delta = lax.dot_general(
            total.astype(jnp.bfloat16), up[b], (((0,), (0,)), ((), ())), preferred_element_type=jnp.float32
        )
        out_ref[here, :] = (base_a[here, :] + base_b[here, :] + delta).astype(out_ref.dtype)


def final(mine, theirs, base, groups, pair, dtype):
    blocks, tall, _ = mine[0].shape
    return pl.pallas_call(
        functools.partial(final_kernel, groups, pair),
        in_specs=[VMEM] * (2 + 2 * len(mine)),
        out_specs=VMEM,
        out_shape=jax.ShapeDtypeStruct(base[0].shape, dtype),
        scratch_shapes=[pltpu.VMEM((blocks, tall // 2, base[0].shape[1]), mine[0].dtype)],
        compiler_params=BIG,
        name="final",
    )(*base, *mine, *theirs)


def body(tokens, base_key, adapter_down, adapter_up, adapter_ids, owner_slot, lengths):
    groups, ring, pair = lax.axis_size("groups"), lax.axis_size("ring"), lax.axis_size("pair")
    sides = lax.axis_size("tensor")
    shares = groups * pair
    t = lax.axis_index("tensor")
    rows = tokens.shape[0]
    blocks = lengths.shape[0]

    def across(x):
        return lax.ppermute(x, "tensor", [(i, (i + 1) % sides) for i in range(sides)])

    def to_plane(x):
        return lax.all_to_all(x, PLANE, split_axis=0, concat_axis=0, tiled=True)

    def along(x, step):
        return lax.ppermute(x, "ring", [(a, (a + step) % ring) for a in range(ring)])

    def first_hops(x):
        return {0: x, ring - 1: along(x, 1), **({1: along(x, -1)} if ring > 2 else {})}

    def in_plane(x, kg, ky):
        pairs = []
        for a in range(groups):
            for b in range(pair):
                pairs.append((a * pair + b, (a + kg) % groups * pair + (b + ky) % pair))
        return lax.ppermute(x, PLANE, pairs)

    def more_hops(held, way, *after):
        for k in range(2, ring // 2 + 1):
            if 2 * k < ring or way % 2 == 0:
                if k == 2:
                    held[ring - 1] = hand_on(held[ring - 1], held[1], *after)
                held[ring - k] = along(held[ring - k + 1], 1)
            if 2 * k < ring or way % 2 == 1:
                if k == 2:
                    held[1] = hand_on(held[1], held[ring - 1], *after)
                held[k] = along(held[k - 1], -1)
        return [held[k] for k in range(ring)]

    own, others = pack(jnp.swapaxes(adapter_down, 1, 2), adapter_up, shares, pair)
    slabs = spread(tokens, lengths, adapter_ids.reshape(-1), shares)
    swapped = [lax.ppermute(others[pair - w - 1], "pair", [(a, (a - w) % pair) for a in range(pair)]) for w in range(1, pair)]
    own_firsts = [first_hops(piece) for piece in own]
    firsts = [first_hops(piece) for piece in swapped]
    tok = to_plane(hand_on(slabs, *swapped, *(own_firsts[0][k] for k in own_firsts[0] if k > 0)))

    base_out, flag_out = base_half(tokens, base_key, (t + 1) % sides, sides, lengths)
    base_mine, flag_mine = base_half(tokens, base_key, t, sides, lengths)
    own_pieces = [more_hops(held, 0, flag_out, flag_mine) for held in own_firsts]
    pieces = [more_hops(held, 1 + way, flag_out, flag_mine) for way, held in enumerate(firsts)]
    flat = [piece for same in zip(*own_pieces) for piece in same] + [piece for way in pieces for piece in way]
    parts = rank_parts(owner_slot, tok, flat, groups, ring, pair, rows, blocks)
    mine = [parts[0]] + [in_plane(parts[k], k // pair, k % pair) for k in range(1, shares)]
    theirs = [across(part) for part in mine]
    base_in = across(hand_on(base_out, parts[0]))
    return final(mine, theirs, [base_mine, base_in], groups, pair, tokens.dtype)


def solution(mesh):
    groups, dp, sides = (mesh.shape[name] for name in ("groups", "dp", "tensor"))
    pair = 2 if dp % 2 == 0 else 1
    cut = Mesh(mesh.devices.reshape(groups, dp // pair, pair, sides), ("groups", "ring", "pair", "tensor"))
    stored = ("ring", "pair")
    placed = (
        P(WHOLE, "tensor"),
        P("tensor", None),
        P(stored, "tensor", None),
        P(stored, None, "tensor"),
        P(WHOLE, None),
        P(),
        P(WHOLE),
    )
    return jax.shard_map(body, mesh=cut, in_specs=placed, out_specs=P(WHOLE, "tensor"), check_vma=False)
```

```python
import functools

import jax
import jax.numpy as jnp
from jax import lax
from jax.experimental import pallas as pl
from jax.experimental.pallas import tpu as pltpu
from jax.sharding import Mesh
from jax.sharding import PartitionSpec as P

LANES = 128
ANY = pl.BlockSpec(memory_space=pl.ANY)
SMEM = pl.BlockSpec(memory_space=pltpu.SMEM)
VMEM = pl.BlockSpec(memory_space=pltpu.VMEM)
HBM = pl.BlockSpec(memory_space=pltpu.HBM)
ROOM = pltpu.CompilerParams(vmem_limit_bytes=32 * 1024 * 1024)
FULL = pltpu.CompilerParams(vmem_limit_bytes=60 * 1024 * 1024)
PLANE = ("groups", "pair")
WHOLE = ("groups", "ring", "pair")


def hand_kernel(*refs):
    pass


def hand_on(x, *after):
    return pl.pallas_call(
        hand_kernel,
        in_specs=[ANY] * (1 + len(after)),
        out_specs=ANY,
        out_shape=jax.ShapeDtypeStruct(x.shape, x.dtype),
        input_output_aliases={0: 0},
        compiler_params=FULL,
        name="hand",
    )(x, *after)


def pack_kernel(down, up, *refs):
    outs, sems = refs[:-1], refs[-1]
    feats = outs[0].shape[2] - LANES
    copies = []
    for way, out in enumerate(outs):
        share = lax.axis_index("groups") * len(outs) + lax.rem(lax.axis_index("pair") + way, len(outs))
        start = pl.multiple_of(share * feats, LANES)
        tile = pl.multiple_of(lax.rem(share, up.shape[2] // LANES) * LANES, LANES)
        copies.append(pltpu.make_async_copy(down.at[:, :, pl.ds(start, feats)], out.at[:, :, :feats], sems.at[way, 0]))
        copies.append(pltpu.make_async_copy(up.at[:, :, pl.ds(tile, LANES)], out.at[:, :, feats:], sems.at[way, 1]))
    for copy in copies:
        copy.start()
    for copy in copies:
        copy.wait()


def pack(down, up, shares, ways):
    adapters, rank, feats = down.shape
    shape = jax.ShapeDtypeStruct((adapters, rank, feats // shares + LANES), down.dtype)
    return pl.pallas_call(
        pack_kernel,
        in_specs=[HBM, HBM],
        out_specs=[VMEM] * ways,
        out_shape=[shape] * ways,
        scratch_shapes=[pltpu.SemaphoreType.DMA((ways, 2))],
        compiler_params=FULL,
        name="pack",
    )(down, up)


def spread_kernel(lengths, ids, tok, out, held, in_sems, out_sems):
    blocks = lengths.shape[0]
    shares, tall, step = held.shape
    rows = tok.shape[0]
    block = rows // blocks

    def read(k, b):
        here = pl.ds(b * block, block)
        return pltpu.make_async_copy(tok.at[here, pl.ds(k * step, step)], held.at[k, here, :], in_sems.at[k, b])

    for k in range(shares):
        for b in range(blocks):
            read(k, b).start()
    lane = lax.broadcasted_iota(jnp.int32, (tall - rows, step), 1)
    named = jnp.zeros((tall - rows, step), jnp.float32)
    for b in range(blocks):
        named = jnp.where(lane == b, ids[b].astype(jnp.float32), named)
    named = named.astype(held.dtype)
    writes = [pltpu.make_async_copy(held.at[k], out.at[k], out_sems.at[k]) for k in range(shares)]
    for k in range(shares):
        held[k, rows:, :] = named
        for b in range(blocks):
            read(k, b).wait()

            @pl.when(lengths[b] < block)
            def _():
                here = slice(b * block, (b + 1) * block)
                row = lax.broadcasted_iota(jnp.int32, (block, step), 0)
                part = held[k, here, :]
                held[k, here, :] = jnp.where(row < lengths[b], part, jnp.zeros_like(part))

        writes[k].start()
    for write in writes:
        write.wait()


def spread(tokens, lengths, ids, shares):
    rows, feats = tokens.shape
    shape = (shares, rows + 16, feats // shares)
    return pl.pallas_call(
        spread_kernel,
        in_specs=[SMEM, SMEM, ANY],
        out_specs=ANY,
        out_shape=jax.ShapeDtypeStruct(shape, tokens.dtype),
        scratch_shapes=[
            pltpu.VMEM(shape, tokens.dtype),
            pltpu.SemaphoreType.DMA((shares, lengths.shape[0])),
            pltpu.SemaphoreType.DMA((shares,)),
        ],
        compiler_params=FULL,
        name="spread",
    )(lengths, ids, tokens)


def base_kernel(side, lengths, tok_ref, key_ref, *refs):
    out_ref = refs[-1]
    part = jnp.dot(tok_ref[...], key_ref[...], preferred_element_type=jnp.float32)
    step = pl.program_id(0)

    @pl.when(step == 0)
    def _():
        out_ref[...] = part

    @pl.when(step > 0)
    def _():
        out_ref[...] += part

    @pl.when(step == pl.num_programs(0) - 1)
    def _():
        blocks = lengths.shape[0]
        block = out_ref.shape[0] // blocks
        row = lax.broadcasted_iota(jnp.int32, (block, out_ref.shape[1]), 0)
        for b in range(blocks):
            here = slice(b * block, (b + 1) * block)
            out_ref[here, :] = jnp.where(row < lengths[b], out_ref[here, :], 0.0)


def base_half(tokens, base_key, side, sides, lengths, *after):
    rows, depth = tokens.shape
    wide = base_key.shape[1] // sides
    step = 1024
    return pl.pallas_call(
        base_kernel,
        grid_spec=pltpu.PrefetchScalarGridSpec(
            num_scalar_prefetch=2,
            grid=(depth // step,),
            in_specs=[
                pl.BlockSpec((rows, step), lambda i, s, n: (0, i)),
                pl.BlockSpec((step, wide), lambda i, s, n: (i, s[0])),
            ]
            + [ANY] * len(after),
            out_specs=pl.BlockSpec((rows, wide), lambda i, s, n: (0, 0)),
        ),
        out_shape=jax.ShapeDtypeStruct((rows, wide), jnp.float32),
        cost_estimate=pl.CostEstimate(
            flops=0, bytes_accessed=0, transcendentals=0
        ),
        compiler_params=FULL,
        name="base",
    )(side.reshape(1), lengths, tokens, base_key, *after)


def mate_at(k, sign, groups, pair):
    kg, ky = k // pair, k % pair
    g = lax.rem(lax.axis_index("groups") + sign * kg + groups, groups)
    y = lax.rem(lax.axis_index("pair") + sign * ky + pair, pair)
    return g * pair + y


def rank_kernel(groups, ring, pair, rows, owner, tok, *refs):
    shares = groups * pair
    tok_held, held, tok_sems, sems = refs[-4:]
    outs = refs[-4 - shares : -4]
    pieces = refs[: ring * pair]
    per, rank = pieces[0].shape[:2]
    blocks, _, block = outs[0].shape
    feats = tok.shape[2]
    z, y = lax.axis_index("ring"), lax.axis_index("pair")
    mates = [mate_at(k, 1, groups, pair) for k in range(shares)]
    copies = [pltpu.make_async_copy(piece, held.at[pl.ds(j * per, per)], sems.at[j]) for j, piece in enumerate(pieces)]
    tok_copies = [
        pltpu.make_async_copy(tok.at[mates[k]], tok_held.at[k], tok_sems.at[k])
        for k in range(shares)
    ]
    for copy in copies + tok_copies:
        copy.start()
    for copy in copies:
        copy.wait()
    lane = lax.broadcasted_iota(jnp.int32, (16, LANES), 1)
    row = lax.broadcasted_iota(jnp.int32, (16, LANES), 0)
    for k in range(shares):
        tok_copies[k].wait()
        named = tok_held[k, rows:, :LANES].astype(jnp.float32)
        ids = [jnp.sum(jnp.where((lane == b) & (row == 0), named, 0.0)).astype(jnp.int32) for b in range(blocks)]
        for b in range(blocks):
            slot = owner[ids[b]]
            chip = slot // per
            away = lax.rem(chip // pair - z + ring, ring)
            way = lax.rem(lax.rem(chip, pair) - y + pair, pair)
            at = (way * ring + away) * per + lax.rem(slot, per)
            part = lax.dot_general(
                held[at, :, :feats],
                tok_held[k, b * block : (b + 1) * block, :],
                (((1,), (1,)), ((), ())),
                preferred_element_type=jnp.float32,
            )
            outs[k][b, :rank, :] = part.astype(outs[k].dtype)
            outs[k][b, rank:, :] = held[at, :, feats:]


def rank_parts(owner, tok, pieces, groups, ring, pair, rows, blocks):
    shares, tall, feats = tok.shape
    block = rows // blocks
    per, rank, wide = pieces[0].shape
    return pl.pallas_call(
        functools.partial(rank_kernel, groups, ring, pair, rows),
        in_specs=[SMEM, ANY] + [ANY] * len(pieces),
        out_specs=[VMEM] * shares,
        out_shape=[jax.ShapeDtypeStruct((blocks, 2 * rank, block), tok.dtype)] * shares,
        scratch_shapes=[
            pltpu.VMEM(tok.shape, tok.dtype),
            pltpu.VMEM((len(pieces) * per, rank, wide), tok.dtype),
            pltpu.SemaphoreType.DMA((shares,)),
            pltpu.SemaphoreType.DMA((len(pieces),)),
        ],
        cost_estimate=pl.CostEstimate(flops=2 * tok.size * rank, bytes_accessed=2 * tok.size, transcendentals=0),
        compiler_params=FULL,
        name="rank",
    )(owner, tok, *pieces)


def final_kernel(groups, pair, base_a, base_b, *refs):
    shares = groups * pair
    mine, theirs, out_ref, up = refs[:shares], refs[shares : 2 * shares], refs[-2], refs[-1]
    blocks, tall, block = mine[0].shape
    rank = tall // 2
    tiles = out_ref.shape[1] // LANES
    for b in range(blocks):
        here = slice(b * block, (b + 1) * block)
        total = mine[0][b, :rank, :].astype(jnp.float32)
        for part in mine[1:] + theirs:
            total += part[b, :rank, :].astype(jnp.float32)
        for k in range(shares):
            tile = lax.rem(mate_at(k, -1, groups, pair), tiles)
            up[b, :, pl.ds(pl.multiple_of(tile * LANES, LANES), LANES)] = mine[k][b, rank:, :]
        delta = lax.dot_general(
            total.astype(jnp.bfloat16), up[b], (((0,), (0,)), ((), ())), preferred_element_type=jnp.float32
        )
        out_ref[here, :] = (base_a[here, :] + base_b[here, :] + delta).astype(out_ref.dtype)


def final(mine, theirs, base, groups, pair, dtype):
    blocks, tall, _ = mine[0].shape
    return pl.pallas_call(
        functools.partial(final_kernel, groups, pair),
        in_specs=[VMEM] * (2 + 2 * len(mine)),
        out_specs=VMEM,
        out_shape=jax.ShapeDtypeStruct(base[0].shape, dtype),
        scratch_shapes=[pltpu.VMEM((blocks, tall // 2, base[0].shape[1]), mine[0].dtype)],
        compiler_params=ROOM,
        name="final",
    )(*base, *mine, *theirs)


def body(tokens, base_key, adapter_down, adapter_up, adapter_ids, owner_slot, lengths):
    groups, ring, pair = lax.axis_size("groups"), lax.axis_size("ring"), lax.axis_size("pair")
    sides = lax.axis_size("tensor")
    shares = groups * pair
    t = lax.axis_index("tensor")
    rows = tokens.shape[0]
    blocks = lengths.shape[0]

    def across(x):
        return lax.ppermute(x, "tensor", [(i, (i + 1) % sides) for i in range(sides)])

    def to_plane(x):
        return lax.all_to_all(x, PLANE, split_axis=0, concat_axis=0, tiled=True)

    def along(x, step):
        return lax.ppermute(x, "ring", [(a, (a + step) % ring) for a in range(ring)])

    def first_hops(x):
        return {0: x, ring - 1: along(x, 1), **({1: along(x, -1)} if ring > 2 else {})}

    def in_plane(x, kg, ky):
        pairs = []
        for a in range(groups):
            for b in range(pair):
                pairs.append((a * pair + b, (a + kg) % groups * pair + (b + ky) % pair))
        return lax.ppermute(x, PLANE, pairs)

    def more_hops(held, way, *after):
        for k in range(2, ring // 2 + 1):
            if 2 * k < ring or way % 2 == 0:
                if k == 2:
                    held[ring - 1] = hand_on(held[ring - 1], held[1], *after)
                held[ring - k] = along(held[ring - k + 1], 1)
            if 2 * k < ring or way % 2 == 1:
                if k == 2:
                    held[1] = hand_on(held[1], held[ring - 1], *after)
                held[k] = along(held[k - 1], -1)
        return [held[k] for k in range(ring)]

    packed = pack(jnp.swapaxes(adapter_down, 1, 2), adapter_up, shares, pair)
    slabs = spread(tokens, lengths, adapter_ids.reshape(-1), shares)
    swapped = [
        lax.ppermute(packed[pair - w], "pair", [(a, (a - w) % pair) for a in range(pair)]) for w in range(1, pair)
    ]
    firsts = [first_hops(piece) for piece in [packed[0]] + swapped]
    tok = to_plane(hand_on(slabs, *swapped, firsts[0][ring - 1]))

    base_out = base_half(tokens, base_key, (t + 1) % sides, sides, lengths)
    base_mine = base_half(tokens, base_key, t, sides, lengths)
    pieces = [
        more_hops(held, way, base_out, base_mine)
        for way, held in enumerate(firsts)
    ]

    flat = [piece for way in pieces for piece in way]
    parts = rank_parts(owner_slot, tok, flat, groups, ring, pair, rows, blocks)
    mine = [parts[0]] + [in_plane(parts[k], k // pair, k % pair) for k in range(1, shares)]
    theirs = [across(part) for part in mine]
    base_in = across(hand_on(base_out, parts[0]))
    return final(mine, theirs, [base_mine, base_in], groups, pair, tokens.dtype)


def solution(mesh):
    groups, dp, sides = (mesh.shape[name] for name in ("groups", "dp", "tensor"))
    pair = 2 if dp % 2 == 0 else 1
    cut = Mesh(mesh.devices.reshape(groups, dp // pair, pair, sides), ("groups", "ring", "pair", "tensor"))
    stored = ("ring", "pair")
    placed = (
        P(WHOLE, "tensor"),
        P("tensor", None),
        P(stored, "tensor", None),
        P(stored, None, "tensor"),
        P(WHOLE, None),
        P(),
        P(WHOLE),
    )
    return jax.shard_map(body, mesh=cut, in_specs=placed, out_specs=P(WHOLE, "tensor"), check_vma=False)
```

```python
import functools

import jax
import jax.numpy as jnp
from jax import lax
from jax.experimental import pallas as pl
from jax.experimental.pallas import tpu as pltpu
from jax.sharding import Mesh
from jax.sharding import PartitionSpec as P

LANES = 128
ANY = pl.BlockSpec(memory_space=pl.ANY)
SMEM = pl.BlockSpec(memory_space=pltpu.SMEM)
VMEM = pl.BlockSpec(memory_space=pltpu.VMEM)
HBM = pl.BlockSpec(memory_space=pltpu.HBM)
ROOM = pltpu.CompilerParams(vmem_limit_bytes=32 * 1024 * 1024)
FULL = pltpu.CompilerParams(vmem_limit_bytes=60 * 1024 * 1024)
PLANE = ("groups", "pair")
WHOLE = ("groups", "ring", "pair")


def hand_kernel(*refs):
    pass


def hand_on(x, *after):
    return pl.pallas_call(
        hand_kernel,
        in_specs=[ANY] * (1 + len(after)),
        out_specs=ANY,
        out_shape=jax.ShapeDtypeStruct(x.shape, x.dtype),
        input_output_aliases={0: 0},
        compiler_params=FULL,
        name="hand",
    )(x, *after)


def pack_kernel(down, up, *refs):
    outs, sems = refs[:-1], refs[-1]
    feats = outs[0].shape[2] - LANES
    copies = []
    for way, out in enumerate(outs):
        share = lax.axis_index("groups") * len(outs) + lax.rem(lax.axis_index("pair") + way, len(outs))
        start = pl.multiple_of(share * feats, LANES)
        tile = pl.multiple_of(lax.rem(share, up.shape[2] // LANES) * LANES, LANES)
        copies.append(pltpu.make_async_copy(down.at[:, :, pl.ds(start, feats)], out.at[:, :, :feats], sems.at[way, 0]))
        copies.append(pltpu.make_async_copy(up.at[:, :, pl.ds(tile, LANES)], out.at[:, :, feats:], sems.at[way, 1]))
    for copy in copies:
        copy.start()
    for copy in copies:
        copy.wait()


def pack(down, up, shares, ways):
    adapters, rank, feats = down.shape
    shape = jax.ShapeDtypeStruct((adapters, rank, feats // shares + LANES), down.dtype)
    return pl.pallas_call(
        pack_kernel,
        in_specs=[HBM, HBM],
        out_specs=[VMEM] * ways,
        out_shape=[shape] * ways,
        scratch_shapes=[pltpu.SemaphoreType.DMA((ways, 2))],
        compiler_params=FULL,
        name="pack",
    )(down, up)


def spread_kernel(lengths, ids, tok, out, held, in_sems, out_sems):
    blocks = lengths.shape[0]
    shares, tall, step = held.shape
    rows = tok.shape[0]
    block = rows // blocks

    def read(k, b):
        here = pl.ds(b * block, block)
        return pltpu.make_async_copy(tok.at[here, pl.ds(k * step, step)], held.at[k, here, :], in_sems.at[k, b])

    for k in range(shares):
        for b in range(blocks):
            read(k, b).start()
    lane = lax.broadcasted_iota(jnp.int32, (tall - rows, step), 1)
    named = jnp.zeros((tall - rows, step), jnp.float32)
    for b in range(blocks):
        named = jnp.where(lane == b, ids[b].astype(jnp.float32), named)
    named = named.astype(held.dtype)
    writes = [pltpu.make_async_copy(held.at[k], out.at[k], out_sems.at[k]) for k in range(shares)]
    for k in range(shares):
        held[k, rows:, :] = named
        for b in range(blocks):
            read(k, b).wait()

            @pl.when(lengths[b] < block)
            def _():
                here = slice(b * block, (b + 1) * block)
                row = lax.broadcasted_iota(jnp.int32, (block, step), 0)
                part = held[k, here, :]
                held[k, here, :] = jnp.where(row < lengths[b], part, jnp.zeros_like(part))

        writes[k].start()
    for write in writes:
        write.wait()


def spread(tokens, lengths, ids, shares):
    rows, feats = tokens.shape
    shape = (shares, rows + 16, feats // shares)
    return pl.pallas_call(
        spread_kernel,
        in_specs=[SMEM, SMEM, ANY],
        out_specs=ANY,
        out_shape=jax.ShapeDtypeStruct(shape, tokens.dtype),
        scratch_shapes=[
            pltpu.VMEM(shape, tokens.dtype),
            pltpu.SemaphoreType.DMA((shares, lengths.shape[0])),
            pltpu.SemaphoreType.DMA((shares,)),
        ],
        compiler_params=FULL,
        name="spread",
    )(lengths, ids, tokens)


def base_kernel(sides, lengths, tok_ref, key_ref, mine, other, flag_ref, total):
    step = pl.program_id(0)
    part = jnp.dot(tok_ref[...], key_ref[...], preferred_element_type=jnp.float32)

    @pl.when(step == 0)
    def _():
        total[...] = part

    @pl.when(step > 0)
    def _():
        total[...] += part

    @pl.when(step == pl.num_programs(0) - 1)
    def _():
        flag_ref[...] = jnp.zeros_like(flag_ref)
        blocks = lengths.shape[0]
        rows, wide = mine.shape
        block = rows // blocks
        row = lax.broadcasted_iota(jnp.int32, (block, wide), 0)
        t = lax.axis_index("tensor")
        for out, side in ((mine, t), (other, lax.rem(t + 1, sides))):
            columns = pl.ds(pl.multiple_of(side * wide, LANES), wide)
            for b in range(blocks):
                here = slice(b * block, (b + 1) * block)
                out[here, :] = jnp.where(row < lengths[b], total[here, columns], 0.0)


def base_halves(tokens, base_key, sides, lengths):
    rows, depth = tokens.shape
    features = base_key.shape[1]
    wide = features // sides
    step = 512
    half = pl.BlockSpec((rows, wide), lambda i, n: (0, 0))
    return pl.pallas_call(
        functools.partial(base_kernel, sides),
        grid_spec=pltpu.PrefetchScalarGridSpec(
            num_scalar_prefetch=1,
            grid=(depth // step,),
            in_specs=[
                pl.BlockSpec((rows, step), lambda i, n: (0, i)),
                pl.BlockSpec((step, features), lambda i, n: (i, 0)),
            ],
            out_specs=[half, half, pl.BlockSpec((8, LANES), lambda i, n: (0, 0))],
            scratch_shapes=[pltpu.VMEM((rows, features), jnp.float32)],
        ),
        out_shape=[jax.ShapeDtypeStruct((rows, wide), jnp.float32)] * 2
        + [jax.ShapeDtypeStruct((8, LANES), jnp.float32)],
        cost_estimate=pl.CostEstimate(flops=0, bytes_accessed=0, transcendentals=0),
        compiler_params=FULL,
        name="base",
    )(lengths, tokens, base_key)


def mate_at(k, sign, groups, pair):
    kg, ky = k // pair, k % pair
    g = lax.rem(lax.axis_index("groups") + sign * kg + groups, groups)
    y = lax.rem(lax.axis_index("pair") + sign * ky + pair, pair)
    return g * pair + y


def collect_kernel(*refs):
    sems, held, pieces = refs[-1], refs[-2], refs[:-2]
    copies, start = [], 0
    for j, piece in enumerate(pieces):
        copies.append(pltpu.make_async_copy(piece, held.at[pl.ds(start, piece.shape[0])], sems.at[j]))
        start += piece.shape[0]
    for copy in copies:
        copy.start()
    for copy in copies:
        copy.wait()


def collect(pieces):
    count = sum(piece.shape[0] for piece in pieces)
    return pl.pallas_call(
        collect_kernel,
        in_specs=[ANY] * len(pieces),
        out_specs=VMEM,
        out_shape=jax.ShapeDtypeStruct((count,) + pieces[0].shape[1:], pieces[0].dtype),
        scratch_shapes=[pltpu.SemaphoreType.DMA((len(pieces),))],
        compiler_params=ROOM,
        name="collect",
    )(*pieces)


def rank_kernel(groups, ring, pair, rows, owner, tok, held, *outs):
    shares = groups * pair
    per, rank = held.shape[0] // (ring * pair), held.shape[1]
    blocks, _, block = outs[0].shape
    feats = tok.shape[2]
    z, y = lax.axis_index("ring"), lax.axis_index("pair")
    lane = lax.broadcasted_iota(jnp.int32, (16, LANES), 1)
    row = lax.broadcasted_iota(jnp.int32, (16, LANES), 0)
    mates = [mate_at(k, 1, groups, pair) for k in range(shares)]
    ids = []
    for mate in mates:
        named = tok[mate, rows:, :LANES].astype(jnp.float32)
        ids += [jnp.sum(jnp.where((lane == b) & (row == 0), named, 0.0)).astype(jnp.int32) for b in range(blocks)]
    for k, mate in enumerate(mates):
        for b in range(blocks):
            slot = owner[ids[k * blocks + b]]
            chip = slot // per
            away = lax.rem(chip // pair - z + ring, ring)
            way = lax.rem(lax.rem(chip, pair) - y + pair, pair)
            at = (way * ring + away) * per + lax.rem(slot, per)
            part = lax.dot_general(
                held[at, :, :feats],
                tok[mate, b * block : (b + 1) * block, :],
                (((1,), (1,)), ((), ())),
                preferred_element_type=jnp.float32,
            )
            outs[k][b, :rank, :] = part.astype(outs[k].dtype)
            outs[k][b, rank:, :] = held[at, :, feats:]


def rank_parts(owner, tok, held, groups, ring, pair, rows, blocks):
    shares, rank = tok.shape[0], held.shape[1]
    return pl.pallas_call(
        functools.partial(rank_kernel, groups, ring, pair, rows),
        in_specs=[SMEM, VMEM, VMEM],
        out_specs=[VMEM] * shares,
        out_shape=[jax.ShapeDtypeStruct((blocks, 2 * rank, rows // blocks), tok.dtype)] * shares,
        cost_estimate=pl.CostEstimate(flops=2 * tok.size * rank, bytes_accessed=2 * tok.size, transcendentals=0),
        compiler_params=ROOM,
        name="rank",
    )(owner, tok, held)


def final_kernel(groups, pair, base_a, base_b, *refs):
    shares = groups * pair
    mine, theirs, out_ref, up = refs[:shares], refs[shares : 2 * shares], refs[-2], refs[-1]
    blocks, tall, block = mine[0].shape
    rank = tall // 2
    tiles = out_ref.shape[1] // LANES
    for b in range(blocks):
        here = slice(b * block, (b + 1) * block)
        total = mine[0][b, :rank, :].astype(jnp.float32)
        for part in mine[1:] + theirs:
            total += part[b, :rank, :].astype(jnp.float32)
        for k in range(shares):
            tile = lax.rem(mate_at(k, -1, groups, pair), tiles)
            up[b, :, pl.ds(pl.multiple_of(tile * LANES, LANES), LANES)] = mine[k][b, rank:, :]
        delta = lax.dot_general(
            total.astype(jnp.bfloat16), up[b], (((0,), (0,)), ((), ())), preferred_element_type=jnp.float32
        )
        out_ref[here, :] = (base_a[here, :] + base_b[here, :] + delta).astype(out_ref.dtype)


def final(mine, theirs, base, groups, pair, dtype):
    blocks, tall, _ = mine[0].shape
    return pl.pallas_call(
        functools.partial(final_kernel, groups, pair),
        in_specs=[VMEM] * (2 + 2 * len(mine)),
        out_specs=VMEM,
        out_shape=jax.ShapeDtypeStruct(base[0].shape, dtype),
        scratch_shapes=[pltpu.VMEM((blocks, tall // 2, base[0].shape[1]), mine[0].dtype)],
        compiler_params=ROOM,
        name="final",
    )(*base, *mine, *theirs)


def body(tokens, base_key, adapter_down, adapter_up, adapter_ids, owner_slot, lengths):
    groups, ring, pair = lax.axis_size("groups"), lax.axis_size("ring"), lax.axis_size("pair")
    sides = lax.axis_size("tensor")
    shares = groups * pair
    rows = tokens.shape[0]
    blocks = lengths.shape[0]

    def across(x):
        return lax.ppermute(x, "tensor", [(i, (i + 1) % sides) for i in range(sides)])

    def to_plane(x):
        return lax.all_to_all(x, PLANE, split_axis=0, concat_axis=0, tiled=True)

    def along(x, step):
        return lax.ppermute(x, "ring", [(a, (a + step) % ring) for a in range(ring)])

    def first_hops(x):
        return {0: x, ring - 1: along(x, 1), **({1: along(x, -1)} if ring > 2 else {})}

    def in_plane(x, kg, ky):
        pairs = []
        for a in range(groups):
            for b in range(pair):
                pairs.append((a * pair + b, (a + kg) % groups * pair + (b + ky) % pair))
        return lax.ppermute(x, PLANE, pairs)

    def more_hops(held, way, *after):
        for k in range(2, ring // 2 + 1):
            if 2 * k < ring or way % 2 == 0:
                if k == 2:
                    held[ring - 1] = hand_on(held[ring - 1], held[1], *after)
                held[ring - k] = along(held[ring - k + 1], 1)
            if 2 * k < ring or way % 2 == 1:
                if k == 2:
                    held[1] = hand_on(held[1], held[ring - 1], *after)
                held[k] = along(held[k - 1], -1)
        return [held[k] for k in range(ring)]

    packed = pack(jnp.swapaxes(adapter_down, 1, 2), adapter_up, shares, pair)
    slabs = spread(tokens, lengths, adapter_ids.reshape(-1), shares)
    swapped = [
        lax.ppermute(packed[pair - w], "pair", [(a, (a - w) % pair) for a in range(pair)]) for w in range(1, pair)
    ]
    firsts = [first_hops(piece) for piece in [packed[0]] + swapped]
    tok = to_plane(hand_on(slabs, *swapped, firsts[0][ring - 1]))

    base_mine, base_out, flag = base_halves(tokens, base_key, sides, lengths)
    pieces = [
        more_hops(held, way, flag)
        for way, held in enumerate(firsts)
    ]

    flat = [piece for way in pieces for piece in way]
    parts = rank_parts(owner_slot, tok, collect(flat), groups, ring, pair, rows, blocks)
    mine = [parts[0]] + [in_plane(parts[k], k // pair, k % pair) for k in range(1, shares)]
    theirs = [across(part) for part in mine]
    base_in = across(hand_on(base_out, parts[0]))
    return final(mine, theirs, [base_mine, base_in], groups, pair, tokens.dtype)


def solution(mesh):
    groups, dp, sides = (mesh.shape[name] for name in ("groups", "dp", "tensor"))
    pair = 2 if dp % 2 == 0 else 1
    cut = Mesh(mesh.devices.reshape(groups, dp // pair, pair, sides), ("groups", "ring", "pair", "tensor"))
    stored = ("ring", "pair")
    placed = (
        P(WHOLE, "tensor"),
        P("tensor", None),
        P(stored, "tensor", None),
        P(stored, None, "tensor"),
        P(WHOLE, None),
        P(),
        P(WHOLE),
    )
    return jax.shard_map(body, mesh=cut, in_specs=placed, out_specs=P(WHOLE, "tensor"), check_vma=False)
```

```python
import functools

import jax
import jax.numpy as jnp
from jax import lax
from jax.experimental import pallas as pl
from jax.experimental.pallas import tpu as pltpu
from jax.sharding import Mesh
from jax.sharding import PartitionSpec as P

LANES = 128
ANY = pl.BlockSpec(memory_space=pl.ANY)
SMEM = pl.BlockSpec(memory_space=pltpu.SMEM)
VMEM = pl.BlockSpec(memory_space=pltpu.VMEM)
HBM = pl.BlockSpec(memory_space=pltpu.HBM)
ROOM = pltpu.CompilerParams(vmem_limit_bytes=32 * 1024 * 1024)
TOKENS_ROOM = pltpu.CompilerParams(vmem_limit_bytes=60 * 1000 * 1000)
FULL = pltpu.CompilerParams(vmem_limit_bytes=60 * 1024 * 1024)
PLANE = ("groups", "pair")
WHOLE = ("groups", "ring", "pair")


def hand_kernel(*refs):
    pass


def hand_on(x, *after):
    return pl.pallas_call(
        hand_kernel,
        in_specs=[ANY] * (1 + len(after)),
        out_specs=ANY,
        out_shape=jax.ShapeDtypeStruct(x.shape, x.dtype),
        input_output_aliases={0: 0},
        compiler_params=FULL,
        name="hand",
    )(x, *after)


def pack_kernel(down, up, *refs):
    outs, sems = refs[:-1], refs[-1]
    feats = outs[0].shape[2] - LANES
    copies = []
    for way, out in enumerate(outs):
        share = lax.axis_index("groups") * len(outs) + lax.rem(lax.axis_index("pair") + way, len(outs))
        start = pl.multiple_of(share * feats, LANES)
        tile = pl.multiple_of(lax.rem(share, up.shape[2] // LANES) * LANES, LANES)
        copies.append(pltpu.make_async_copy(down.at[:, :, pl.ds(start, feats)], out.at[:, :, :feats], sems.at[way, 0]))
        copies.append(pltpu.make_async_copy(up.at[:, :, pl.ds(tile, LANES)], out.at[:, :, feats:], sems.at[way, 1]))
    for copy in copies:
        copy.start()
    for copy in copies:
        copy.wait()


def pack(down, up, shares, ways):
    adapters, rank, feats = down.shape
    shape = jax.ShapeDtypeStruct((adapters, rank, feats // shares + LANES), down.dtype)
    return pl.pallas_call(
        pack_kernel,
        in_specs=[HBM, HBM],
        out_specs=[VMEM] * ways,
        out_shape=[shape] * ways,
        scratch_shapes=[pltpu.SemaphoreType.DMA((ways, 2))],
        compiler_params=FULL,
        name="pack",
    )(down, up)


def spread_kernel(lengths, ids, tok, out, held, in_sems, out_sems):
    blocks = lengths.shape[0]
    shares, tall, step = held.shape
    rows = tok.shape[0]
    block = rows // blocks

    def read(k, b):
        here = pl.ds(b * block, block)
        return pltpu.make_async_copy(tok.at[here, pl.ds(k * step, step)], held.at[k, here, :], in_sems.at[k, b])

    for k in range(shares):
        for b in range(blocks):
            read(k, b).start()
    lane = lax.broadcasted_iota(jnp.int32, (tall - rows, step), 1)
    named = jnp.zeros((tall - rows, step), jnp.float32)
    for b in range(blocks):
        named = jnp.where(lane == b, ids[b].astype(jnp.float32), named)
    named = named.astype(held.dtype)
    writes = [pltpu.make_async_copy(held.at[k], out.at[k], out_sems.at[k]) for k in range(shares)]
    for k in range(shares):
        held[k, rows:, :] = named
        for b in range(blocks):
            read(k, b).wait()

            @pl.when(lengths[b] < block)
            def _():
                here = slice(b * block, (b + 1) * block)
                row = lax.broadcasted_iota(jnp.int32, (block, step), 0)
                part = held[k, here, :]
                held[k, here, :] = jnp.where(row < lengths[b], part, jnp.zeros_like(part))

        writes[k].start()
    for write in writes:
        write.wait()


def spread(tokens, lengths, ids, shares):
    rows, feats = tokens.shape
    shape = (shares, rows + 16, feats // shares)
    return pl.pallas_call(
        spread_kernel,
        in_specs=[SMEM, SMEM, ANY],
        out_specs=ANY,
        out_shape=jax.ShapeDtypeStruct(shape, tokens.dtype),
        scratch_shapes=[
            pltpu.VMEM(shape, tokens.dtype),
            pltpu.SemaphoreType.DMA((shares, lengths.shape[0])),
            pltpu.SemaphoreType.DMA((shares,)),
        ],
        compiler_params=FULL,
        name="spread",
    )(lengths, ids, tokens)


def base_kernel(sides, lengths, tok_ref, key_ref, mine, other, flag_ref, total):
    step = pl.program_id(0)
    part = jnp.dot(tok_ref[...], key_ref[...], preferred_element_type=jnp.float32)

    @pl.when(step == 0)
    def _():
        total[...] = part

    @pl.when(step > 0)
    def _():
        total[...] += part

    @pl.when(step == pl.num_programs(0) - 1)
    def _():
        flag_ref[...] = jnp.zeros_like(flag_ref)
        blocks = lengths.shape[0]
        rows, wide = mine.shape
        block = rows // blocks
        row = lax.broadcasted_iota(jnp.int32, (block, wide), 0)
        t = lax.axis_index("tensor")
        for out, side in ((mine, t), (other, lax.rem(t + 1, sides))):
            columns = pl.ds(pl.multiple_of(side * wide, LANES), wide)
            for b in range(blocks):
                here = slice(b * block, (b + 1) * block)
                out[here, :] = jnp.where(row < lengths[b], total[here, columns], 0.0)


def base_halves(tokens, base_key, sides, lengths):
    rows, depth = tokens.shape
    features = base_key.shape[1]
    wide = features // sides
    step = 512
    half = pl.BlockSpec((rows, wide), lambda i, n: (0, 0))
    return pl.pallas_call(
        functools.partial(base_kernel, sides),
        grid_spec=pltpu.PrefetchScalarGridSpec(
            num_scalar_prefetch=1,
            grid=(depth // step,),
            in_specs=[
                pl.BlockSpec((rows, step), lambda i, n: (0, i)),
                pl.BlockSpec((step, features), lambda i, n: (i, 0)),
            ],
            out_specs=[half, half, pl.BlockSpec((8, LANES), lambda i, n: (0, 0))],
            scratch_shapes=[pltpu.VMEM((rows, features), jnp.float32)],
        ),
        out_shape=[jax.ShapeDtypeStruct((rows, wide), jnp.float32)] * 2
        + [jax.ShapeDtypeStruct((8, LANES), jnp.float32)],
        cost_estimate=pl.CostEstimate(flops=0, bytes_accessed=0, transcendentals=0),
        compiler_params=FULL,
        name="base",
    )(lengths, tokens, base_key)


def mate_at(k, sign, groups, pair):
    kg, ky = k // pair, k % pair
    g = lax.rem(lax.axis_index("groups") + sign * kg + groups, groups)
    y = lax.rem(lax.axis_index("pair") + sign * ky + pair, pair)
    return g * pair + y


def rank_kernel(groups, ring, pair, rows, owner, tok, *refs):
    shares = groups * pair
    held, sems = refs[-2:]
    pieces, outs = refs[: -2 - shares], refs[-2 - shares : -2]
    copies, start = [], 0
    for j, piece in enumerate(pieces):
        copies.append(pltpu.make_async_copy(piece, held.at[pl.ds(start, piece.shape[0])], sems.at[j]))
        start += piece.shape[0]
    for copy in copies:
        copy.start()
    per, rank = held.shape[0] // (ring * pair), held.shape[1]
    blocks, _, block = outs[0].shape
    feats = tok.shape[2]
    z, y = lax.axis_index("ring"), lax.axis_index("pair")
    lane = lax.broadcasted_iota(jnp.int32, (16, LANES), 1)
    row = lax.broadcasted_iota(jnp.int32, (16, LANES), 0)
    mates = [mate_at(k, 1, groups, pair) for k in range(shares)]
    ids = []
    for mate in mates:
        named = tok[mate, rows:, :LANES].astype(jnp.float32)
        ids += [jnp.sum(jnp.where((lane == b) & (row == 0), named, 0.0)).astype(jnp.int32) for b in range(blocks)]
    for copy in copies:
        copy.wait()
    for k, mate in enumerate(mates):
        for b in range(blocks):
            slot = owner[ids[k * blocks + b]]
            chip = slot // per
            away = lax.rem(chip // pair - z + ring, ring)
            way = lax.rem(lax.rem(chip, pair) - y + pair, pair)
            at = (way * ring + away) * per + lax.rem(slot, per)
            part = lax.dot_general(
                held[at, :, :feats],
                tok[mate, b * block : (b + 1) * block, :],
                (((1,), (1,)), ((), ())),
                preferred_element_type=jnp.float32,
            )
            outs[k][b, :rank, :] = part.astype(outs[k].dtype)
            outs[k][b, rank:, :] = held[at, :, feats:]


def rank_parts(owner, tok, pieces, groups, ring, pair, rows, blocks):
    shares, rank = tok.shape[0], pieces[0].shape[1]
    held = (sum(piece.shape[0] for piece in pieces),) + pieces[0].shape[1:]
    return pl.pallas_call(
        functools.partial(rank_kernel, groups, ring, pair, rows),
        in_specs=[SMEM, VMEM] + [ANY] * len(pieces),
        out_specs=[VMEM] * shares,
        out_shape=[jax.ShapeDtypeStruct((blocks, 2 * rank, rows // blocks), tok.dtype)] * shares,
        scratch_shapes=[pltpu.VMEM(held, tok.dtype), pltpu.SemaphoreType.DMA((len(pieces),))],
        cost_estimate=pl.CostEstimate(flops=2 * tok.size * rank, bytes_accessed=2 * tok.size, transcendentals=0),
        compiler_params=TOKENS_ROOM,
        name="rank",
    )(owner, tok, *pieces)


def final_kernel(groups, pair, base, *refs):
    shares = groups * pair
    mine, theirs, out_ref, up = refs[:shares], refs[shares : 2 * shares], refs[-2], refs[-1]
    blocks, tall, block = mine[0].shape
    rank = tall // 2
    tiles = out_ref.shape[1] // LANES
    for b in range(blocks):
        here = slice(b * block, (b + 1) * block)
        total = mine[0][b, :rank, :].astype(jnp.float32)
        for part in mine[1:] + theirs:
            total += part[b, :rank, :].astype(jnp.float32)
        for k in range(shares):
            tile = lax.rem(mate_at(k, -1, groups, pair), tiles)
            up[b, :, pl.ds(pl.multiple_of(tile * LANES, LANES), LANES)] = mine[k][b, rank:, :].astype(up.dtype)
        delta = lax.dot_general(
            total.astype(jnp.bfloat16), up[b], (((0,), (0,)), ((), ())), preferred_element_type=jnp.float32
        )
        out_ref[here, :] = (base[here, :] + delta).astype(out_ref.dtype)


def final(mine, theirs, base, groups, pair, dtype):
    blocks, tall, _ = mine[0].shape
    return pl.pallas_call(
        functools.partial(final_kernel, groups, pair),
        in_specs=[VMEM] * (1 + 2 * len(mine)),
        out_specs=VMEM,
        out_shape=jax.ShapeDtypeStruct(base.shape, dtype),
        scratch_shapes=[pltpu.VMEM((blocks, tall // 2, base.shape[1]), theirs[0].dtype)],
        compiler_params=ROOM,
        name="final",
    )(base, *mine, *theirs)


def body(tokens, base_key, adapter_down, adapter_up, adapter_ids, owner_slot, lengths):
    groups, ring, pair = lax.axis_size("groups"), lax.axis_size("ring"), lax.axis_size("pair")
    sides = lax.axis_size("tensor")
    shares = groups * pair
    rows = tokens.shape[0]
    blocks = lengths.shape[0]

    def across(x):
        return lax.ppermute(x, "tensor", [(i, (i + 1) % sides) for i in range(sides)])

    def to_plane(x):
        return lax.all_to_all(x, PLANE, split_axis=0, concat_axis=0, tiled=True)

    def along(x, step):
        return lax.ppermute(x, "ring", [(a, (a + step) % ring) for a in range(ring)])

    def first_hops(x):
        return {0: x, ring - 1: along(x, 1), **({1: along(x, -1)} if ring > 2 else {})}

    def in_plane(x, kg, ky):
        pairs = []
        for a in range(groups):
            for b in range(pair):
                pairs.append((a * pair + b, (a + kg) % groups * pair + (b + ky) % pair))
        return lax.ppermute(x, PLANE, pairs)

    def more_hops(held, way, *after):
        for k in range(2, ring // 2 + 1):
            if 2 * k < ring or way % 2 == 0:
                if k == 2:
                    held[ring - 1] = hand_on(held[ring - 1], held[1], *after)
                held[ring - k] = along(held[ring - k + 1], 1)
            if 2 * k < ring or way % 2 == 1:
                if k == 2:
                    held[1] = hand_on(held[1], held[ring - 1], *after)
                held[k] = along(held[k - 1], -1)
        return [held[k] for k in range(ring)]

    packed = pack(jnp.swapaxes(adapter_down, 1, 2), adapter_up, shares, pair)
    slabs = spread(tokens, lengths, adapter_ids.reshape(-1), shares)
    swapped = [
        lax.ppermute(packed[pair - w], "pair", [(a, (a - w) % pair) for a in range(pair)]) for w in range(1, pair)
    ]
    firsts = [first_hops(piece) for piece in [packed[0]] + swapped]
    tok = to_plane(hand_on(slabs, *swapped))

    base_mine, base_out, flag = base_halves(tokens, base_key, sides, lengths)
    pieces = [
        more_hops(held, way, flag)
        for way, held in enumerate(firsts)
    ]

    flat = [piece for way in pieces for piece in way]
    parts = rank_parts(owner_slot, tok, flat, groups, ring, pair, rows, blocks)
    mine = [parts[0]] + [in_plane(parts[k], k // pair, k % pair) for k in range(1, shares)]
    theirs = [across(part) for part in mine]
    base_in = across(hand_on(base_out, parts[0]))
    mine[0] = mine[0].astype(jnp.float32)
    return final(mine, theirs, base_mine + base_in, groups, pair, tokens.dtype)


def solution(mesh):
    groups, dp, sides = (mesh.shape[name] for name in ("groups", "dp", "tensor"))
    pair = 2 if dp % 2 == 0 else 1
    cut = Mesh(mesh.devices.reshape(groups, dp // pair, pair, sides), ("groups", "ring", "pair", "tensor"))
    stored = ("ring", "pair")
    placed = (
        P(WHOLE, "tensor"),
        P("tensor", None),
        P(stored, "tensor", None),
        P(stored, None, "tensor"),
        P(WHOLE, None),
        P(),
        P(WHOLE),
    )
    return jax.shard_map(body, mesh=cut, in_specs=placed, out_specs=P(WHOLE, "tensor"), check_vma=False)
```

```python
import functools

import jax
import jax.numpy as jnp
from jax import lax
from jax.experimental import pallas as pl
from jax.experimental.pallas import tpu as pltpu
from jax.sharding import Mesh
from jax.sharding import PartitionSpec as P

LANES = 128
ANY = pl.BlockSpec(memory_space=pl.ANY)
SMEM = pl.BlockSpec(memory_space=pltpu.SMEM)
VMEM = pl.BlockSpec(memory_space=pltpu.VMEM)
HBM = pl.BlockSpec(memory_space=pltpu.HBM)
ROOM = pltpu.CompilerParams(vmem_limit_bytes=32 * 1024 * 1024)
TOKENS_ROOM = pltpu.CompilerParams(vmem_limit_bytes=58_200_000)
FULL = pltpu.CompilerParams(vmem_limit_bytes=60 * 1024 * 1024)
PLANE = ("groups", "pair")
WHOLE = ("groups", "ring", "pair")


def hand_kernel(*refs):
    pass


def hand_on(x, *after):
    return pl.pallas_call(
        hand_kernel,
        in_specs=[ANY] * (1 + len(after)),
        out_specs=ANY,
        out_shape=jax.ShapeDtypeStruct(x.shape, x.dtype),
        input_output_aliases={0: 0},
        compiler_params=FULL,
        name="hand",
    )(x, *after)


def pack_kernel(down, up, *refs):
    outs, sems = refs[:-1], refs[-1]
    feats = outs[0].shape[2] - LANES
    copies = []
    for way, out in enumerate(outs):
        share = lax.axis_index("groups") * len(outs) + lax.rem(lax.axis_index("pair") + way, len(outs))
        start = pl.multiple_of(share * feats, LANES)
        tile = pl.multiple_of(lax.rem(share, up.shape[2] // LANES) * LANES, LANES)
        copies.append(pltpu.make_async_copy(down.at[:, :, pl.ds(start, feats)], out.at[:, :, :feats], sems.at[way, 0]))
        copies.append(pltpu.make_async_copy(up.at[:, :, pl.ds(tile, LANES)], out.at[:, :, feats:], sems.at[way, 1]))
    for copy in copies:
        copy.start()
    for copy in copies:
        copy.wait()


def pack(down, up, shares, ways):
    adapters, rank, feats = down.shape
    shape = jax.ShapeDtypeStruct((adapters, rank, feats // shares + LANES), down.dtype)
    return pl.pallas_call(
        pack_kernel,
        in_specs=[HBM, HBM],
        out_specs=[VMEM] * ways,
        out_shape=[shape] * ways,
        scratch_shapes=[pltpu.SemaphoreType.DMA((ways, 2))],
        compiler_params=FULL,
        name="pack",
    )(down, up)


def spread_kernel(lengths, ids, tok, out, held, in_sems, out_sems):
    blocks = lengths.shape[0]
    shares, tall, step = held.shape
    rows = tok.shape[0]
    block = rows // blocks

    def read(k, b):
        here = pl.ds(b * block, block)
        return pltpu.make_async_copy(tok.at[here, pl.ds(k * step, step)], held.at[k, here, :], in_sems.at[k, b])

    for k in range(shares):
        for b in range(blocks):
            read(k, b).start()
    lane = lax.broadcasted_iota(jnp.int32, (tall - rows, step), 1)
    named = jnp.zeros((tall - rows, step), jnp.float32)
    for b in range(blocks):
        named = jnp.where(lane == b, ids[b].astype(jnp.float32), named)
    named = named.astype(held.dtype)
    writes = [pltpu.make_async_copy(held.at[k], out.at[k], out_sems.at[k]) for k in range(shares)]
    for k in range(shares):
        held[k, rows:, :] = named
        for b in range(blocks):
            read(k, b).wait()

            @pl.when(lengths[b] < block)
            def _():
                here = slice(b * block, (b + 1) * block)
                row = lax.broadcasted_iota(jnp.int32, (block, step), 0)
                part = held[k, here, :]
                held[k, here, :] = jnp.where(row < lengths[b], part, jnp.zeros_like(part))

        writes[k].start()
    for write in writes:
        write.wait()


def spread(tokens, lengths, ids, shares):
    rows, feats = tokens.shape
    shape = (shares, rows + 16, feats // shares)
    return pl.pallas_call(
        spread_kernel,
        in_specs=[SMEM, SMEM, ANY],
        out_specs=ANY,
        out_shape=jax.ShapeDtypeStruct(shape, tokens.dtype),
        scratch_shapes=[
            pltpu.VMEM(shape, tokens.dtype),
            pltpu.SemaphoreType.DMA((shares, lengths.shape[0])),
            pltpu.SemaphoreType.DMA((shares,)),
        ],
        compiler_params=FULL,
        name="spread",
    )(lengths, ids, tokens)


def base_kernel(sides, lengths, tok_ref, key_ref, mine, other, flag_ref, total):
    step = pl.program_id(0)
    part = jnp.dot(tok_ref[...], key_ref[...], preferred_element_type=jnp.float32)

    @pl.when(step == 0)
    def _():
        total[...] = part

    @pl.when(step > 0)
    def _():
        total[...] += part

    @pl.when(step == pl.num_programs(0) - 1)
    def _():
        flag_ref[...] = jnp.zeros_like(flag_ref)
        blocks = lengths.shape[0]
        rows, wide = mine.shape
        block = rows // blocks
        row = lax.broadcasted_iota(jnp.int32, (block, wide), 0)
        t = lax.axis_index("tensor")
        for out, side in ((mine, t), (other, lax.rem(t + 1, sides))):
            columns = pl.ds(pl.multiple_of(side * wide, LANES), wide)
            for b in range(blocks):
                here = slice(b * block, (b + 1) * block)
                out[here, :] = jnp.where(row < lengths[b], total[here, columns], 0.0)


def base_halves(tokens, base_key, sides, lengths):
    rows, depth = tokens.shape
    features = base_key.shape[1]
    wide = features // sides
    step = 512
    half = pl.BlockSpec((rows, wide), lambda i, n: (0, 0))
    return pl.pallas_call(
        functools.partial(base_kernel, sides),
        grid_spec=pltpu.PrefetchScalarGridSpec(
            num_scalar_prefetch=1,
            grid=(depth // step,),
            in_specs=[
                pl.BlockSpec((rows, step), lambda i, n: (0, i)),
                pl.BlockSpec((step, features), lambda i, n: (i, 0)),
            ],
            out_specs=[half, half, pl.BlockSpec((8, LANES), lambda i, n: (0, 0))],
            scratch_shapes=[pltpu.VMEM((rows, features), jnp.float32)],
        ),
        out_shape=[jax.ShapeDtypeStruct((rows, wide), jnp.float32)] * 2
        + [jax.ShapeDtypeStruct((8, LANES), jnp.float32)],
        cost_estimate=pl.CostEstimate(flops=0, bytes_accessed=0, transcendentals=0),
        compiler_params=FULL,
        name="base",
    )(lengths, tokens, base_key)


def mate_at(k, sign, groups, pair):
    kg, ky = k // pair, k % pair
    g = lax.rem(lax.axis_index("groups") + sign * kg + groups, groups)
    y = lax.rem(lax.axis_index("pair") + sign * ky + pair, pair)
    return g * pair + y


def collect_kernel(*refs):
    sems, held, pieces = refs[-1], refs[-2], refs[:-2]
    copies, start = [], 0
    for j, piece in enumerate(pieces):
        copies.append(pltpu.make_async_copy(piece, held.at[pl.ds(start, piece.shape[0])], sems.at[j]))
        start += piece.shape[0]
    for copy in copies:
        copy.start()
    for copy in copies:
        copy.wait()


def collect(pieces):
    count = sum(piece.shape[0] for piece in pieces)
    return pl.pallas_call(
        collect_kernel,
        in_specs=[ANY] * len(pieces),
        out_specs=VMEM,
        out_shape=jax.ShapeDtypeStruct((count,) + pieces[0].shape[1:], pieces[0].dtype),
        scratch_shapes=[pltpu.SemaphoreType.DMA((len(pieces),))],
        compiler_params=FULL,
        name="collect",
    )(*pieces)


def rank_kernel(groups, ring, pair, rows, owner, tok, pieces, *refs):
    shares = groups * pair
    outs, held, sem = refs[:-2], refs[-2], refs[-1]
    copy = pltpu.make_async_copy(pieces, held, sem)
    copy.start()
    per, rank = held.shape[0] // (ring * pair), held.shape[1]
    blocks, _, block = outs[0].shape
    feats = tok.shape[2]
    z, y = lax.axis_index("ring"), lax.axis_index("pair")
    lane = lax.broadcasted_iota(jnp.int32, (16, LANES), 1)
    row = lax.broadcasted_iota(jnp.int32, (16, LANES), 0)
    mates = [mate_at(k, 1, groups, pair) for k in range(shares)]
    ids = []
    for mate in mates:
        named = tok[mate, rows:, :LANES].astype(jnp.float32)
        ids += [jnp.sum(jnp.where((lane == b) & (row == 0), named, 0.0)).astype(jnp.int32) for b in range(blocks)]
    copy.wait()
    for k, mate in enumerate(mates):
        for b in range(blocks):
            slot = owner[ids[k * blocks + b]]
            chip = slot // per
            away = lax.rem(chip // pair - z + ring, ring)
            way = lax.rem(lax.rem(chip, pair) - y + pair, pair)
            at = (way * ring + away) * per + lax.rem(slot, per)
            part = lax.dot_general(
                held[at, :, :feats],
                tok[mate, b * block : (b + 1) * block, :],
                (((1,), (1,)), ((), ())),
                preferred_element_type=jnp.float32,
            )
            outs[k][b, :rank, :] = part.astype(outs[k].dtype)
            outs[k][b, rank:, :] = held[at, :, feats:]


def rank_parts(owner, tok, held, groups, ring, pair, rows, blocks):
    shares, rank = tok.shape[0], held.shape[1]
    return pl.pallas_call(
        functools.partial(rank_kernel, groups, ring, pair, rows),
        in_specs=[SMEM, VMEM, ANY],
        out_specs=[VMEM] * shares,
        out_shape=[jax.ShapeDtypeStruct((blocks, 2 * rank, rows // blocks), tok.dtype)] * shares,
        scratch_shapes=[pltpu.VMEM(held.shape, held.dtype), pltpu.SemaphoreType.DMA],
        cost_estimate=pl.CostEstimate(flops=2 * tok.size * rank, bytes_accessed=2 * tok.size, transcendentals=0),
        compiler_params=TOKENS_ROOM,
        name="rank",
    )(owner, tok, held)


def final_kernel(groups, pair, base_a, base_b, *refs):
    shares = groups * pair
    mine, theirs, out_ref, up = refs[:shares], refs[shares : 2 * shares], refs[-2], refs[-1]
    blocks, tall, block = mine[0].shape
    rank = tall // 2
    tiles = out_ref.shape[1] // LANES
    for b in range(blocks):
        here = slice(b * block, (b + 1) * block)
        total = mine[0][b, :rank, :].astype(jnp.float32)
        for part in mine[1:] + theirs:
            total += part[b, :rank, :].astype(jnp.float32)
        for k in range(shares):
            tile = lax.rem(mate_at(k, -1, groups, pair), tiles)
            up[b, :, pl.ds(pl.multiple_of(tile * LANES, LANES), LANES)] = mine[k][b, rank:, :]
        delta = lax.dot_general(
            total.astype(jnp.bfloat16), up[b], (((0,), (0,)), ((), ())), preferred_element_type=jnp.float32
        )
        out_ref[here, :] = (base_a[here, :] + base_b[here, :] + delta).astype(out_ref.dtype)


def final(mine, theirs, base, groups, pair, dtype):
    blocks, tall, _ = mine[0].shape
    return pl.pallas_call(
        functools.partial(final_kernel, groups, pair),
        in_specs=[VMEM] * (2 + 2 * len(mine)),
        out_specs=VMEM,
        out_shape=jax.ShapeDtypeStruct(base[0].shape, dtype),
        scratch_shapes=[pltpu.VMEM((blocks, tall // 2, base[0].shape[1]), mine[0].dtype)],
        compiler_params=ROOM,
        name="final",
    )(*base, *mine, *theirs)


def body(tokens, base_key, adapter_down, adapter_up, adapter_ids, owner_slot, lengths):
    groups, ring, pair = lax.axis_size("groups"), lax.axis_size("ring"), lax.axis_size("pair")
    sides = lax.axis_size("tensor")
    shares = groups * pair
    rows = tokens.shape[0]
    blocks = lengths.shape[0]

    def across(x):
        return lax.ppermute(x, "tensor", [(i, (i + 1) % sides) for i in range(sides)])

    def to_plane(x):
        return lax.all_to_all(x, PLANE, split_axis=0, concat_axis=0, tiled=True)

    def along(x, step):
        return lax.ppermute(x, "ring", [(a, (a + step) % ring) for a in range(ring)])

    def first_hops(x):
        return {0: x, ring - 1: along(x, 1), **({1: along(x, -1)} if ring > 2 else {})}

    def in_plane(x, kg, ky):
        pairs = []
        for a in range(groups):
            for b in range(pair):
                pairs.append((a * pair + b, (a + kg) % groups * pair + (b + ky) % pair))
        return lax.ppermute(x, PLANE, pairs)

    def more_hops(held, way, *after):
        for k in range(2, ring // 2 + 1):
            if 2 * k < ring or way % 2 == 0:
                if k == 2:
                    held[ring - 1] = hand_on(held[ring - 1], held[1], *after)
                held[ring - k] = along(held[ring - k + 1], 1)
            if 2 * k < ring or way % 2 == 1:
                if k == 2:
                    held[1] = hand_on(held[1], held[ring - 1], *after)
                held[k] = along(held[k - 1], -1)
        return [held[k] for k in range(ring)]

    packed = pack(jnp.swapaxes(adapter_down, 1, 2), adapter_up, shares, pair)
    slabs = spread(tokens, lengths, adapter_ids.reshape(-1), shares)
    swapped = [
        lax.ppermute(packed[pair - w], "pair", [(a, (a - w) % pair) for a in range(pair)]) for w in range(1, pair)
    ]
    firsts = [first_hops(piece) for piece in [packed[0]] + swapped]
    tok = to_plane(hand_on(slabs, *swapped, firsts[0][ring - 1]))

    base_mine, base_out, flag = base_halves(tokens, base_key, sides, lengths)
    pieces = [
        more_hops(held, way, flag)
        for way, held in enumerate(firsts)
    ]

    flat = [piece for way in pieces for piece in way]
    parts = rank_parts(owner_slot, tok, collect(flat), groups, ring, pair, rows, blocks)
    mine = [parts[0]] + [in_plane(parts[k], k // pair, k % pair) for k in range(1, shares)]
    theirs = [across(part) for part in mine]
    base_in = across(hand_on(base_out, pieces[-1][ring // 2]))
    return final(mine, theirs, [base_mine, base_in], groups, pair, tokens.dtype)


def solution(mesh):
    groups, dp, sides = (mesh.shape[name] for name in ("groups", "dp", "tensor"))
    pair = 2 if dp % 2 == 0 else 1
    cut = Mesh(mesh.devices.reshape(groups, dp // pair, pair, sides), ("groups", "ring", "pair", "tensor"))
    stored = ("ring", "pair")
    placed = (
        P(WHOLE, "tensor"),
        P("tensor", None),
        P(stored, "tensor", None),
        P(stored, None, "tensor"),
        P(WHOLE, None),
        P(),
        P(WHOLE),
    )
    return jax.shard_map(body, mesh=cut, in_specs=placed, out_specs=P(WHOLE, "tensor"), check_vma=False)
```

```python
import functools

import jax
import jax.numpy as jnp
from jax import lax
from jax.experimental import pallas as pl
from jax.experimental.pallas import tpu as pltpu
from jax.sharding import Mesh
from jax.sharding import PartitionSpec as P

LANES = 128
ANY = pl.BlockSpec(memory_space=pl.ANY)
SMEM = pl.BlockSpec(memory_space=pltpu.SMEM)
VMEM = pl.BlockSpec(memory_space=pltpu.VMEM)
HBM = pl.BlockSpec(memory_space=pltpu.HBM)
ROOM = pltpu.CompilerParams(vmem_limit_bytes=32 * 1024 * 1024)
FULL = pltpu.CompilerParams(vmem_limit_bytes=60 * 1024 * 1024)
PLANE = ("groups", "pair")
WHOLE = ("groups", "ring", "pair")


def hand_kernel(*refs):
    pass


def hand_on(x, *after):
    return pl.pallas_call(
        hand_kernel,
        in_specs=[ANY] * (1 + len(after)),
        out_specs=ANY,
        out_shape=jax.ShapeDtypeStruct(x.shape, x.dtype),
        input_output_aliases={0: 0},
        compiler_params=FULL,
        name="hand",
    )(x, *after)


def pack_kernel(down, up, *refs):
    outs, sems = refs[:-1], refs[-1]
    feats = outs[0].shape[2] - LANES
    copies = []
    for way, out in enumerate(outs):
        share = lax.axis_index("groups") * len(outs) + lax.rem(lax.axis_index("pair") + way, len(outs))
        start = pl.multiple_of(share * feats, LANES)
        tile = pl.multiple_of(lax.rem(share, up.shape[2] // LANES) * LANES, LANES)
        copies.append(pltpu.make_async_copy(down.at[:, :, pl.ds(start, feats)], out.at[:, :, :feats], sems.at[way, 0]))
        copies.append(pltpu.make_async_copy(up.at[:, :, pl.ds(tile, LANES)], out.at[:, :, feats:], sems.at[way, 1]))
    for copy in copies:
        copy.start()
    for copy in copies:
        copy.wait()


def pack(down, up, shares, ways):
    adapters, rank, feats = down.shape
    shape = jax.ShapeDtypeStruct((adapters, rank, feats // shares + LANES), down.dtype)
    return pl.pallas_call(
        pack_kernel,
        in_specs=[HBM, HBM],
        out_specs=[VMEM] * ways,
        out_shape=[shape] * ways,
        scratch_shapes=[pltpu.SemaphoreType.DMA((ways, 2))],
        compiler_params=FULL,
        name="pack",
    )(down, up)


def spread_kernel(lengths, ids, tok, out, held, in_sems, out_sems):
    blocks = lengths.shape[0]
    shares, tall, step = held.shape
    rows = tok.shape[0]
    block = rows // blocks

    def read(k, b):
        here = pl.ds(b * block, block)
        return pltpu.make_async_copy(tok.at[here, pl.ds(k * step, step)], held.at[k, here, :], in_sems.at[k, b])

    for k in range(shares):
        for b in range(blocks):
            read(k, b).start()
    lane = lax.broadcasted_iota(jnp.int32, (tall - rows, step), 1)
    named = jnp.zeros((tall - rows, step), jnp.float32)
    for b in range(blocks):
        named = jnp.where(lane == b, ids[b].astype(jnp.float32), named)
    named = named.astype(held.dtype)
    writes = [pltpu.make_async_copy(held.at[k], out.at[k], out_sems.at[k]) for k in range(shares)]
    for k in range(shares):
        held[k, rows:, :] = named
        for b in range(blocks):
            read(k, b).wait()

            @pl.when(lengths[b] < block)
            def _():
                here = slice(b * block, (b + 1) * block)
                row = lax.broadcasted_iota(jnp.int32, (block, step), 0)
                part = held[k, here, :]
                held[k, here, :] = jnp.where(row < lengths[b], part, jnp.zeros_like(part))

        writes[k].start()
    for write in writes:
        write.wait()


def spread(tokens, lengths, ids, shares):
    rows, feats = tokens.shape
    shape = (shares, rows + 16, feats // shares)
    return pl.pallas_call(
        spread_kernel,
        in_specs=[SMEM, SMEM, ANY],
        out_specs=ANY,
        out_shape=jax.ShapeDtypeStruct(shape, tokens.dtype),
        scratch_shapes=[
            pltpu.VMEM(shape, tokens.dtype),
            pltpu.SemaphoreType.DMA((shares, lengths.shape[0])),
            pltpu.SemaphoreType.DMA((shares,)),
        ],
        compiler_params=FULL,
        name="spread",
    )(lengths, ids, tokens)


def base_kernel(sides, lengths, tok_ref, key_ref, mine, other, flag_ref, total):
    step = pl.program_id(0)
    part = jnp.dot(tok_ref[...], key_ref[...], preferred_element_type=jnp.float32)

    @pl.when(step == 0)
    def _():
        total[...] = part

    @pl.when(step > 0)
    def _():
        total[...] += part

    @pl.when(step == pl.num_programs(0) - 1)
    def _():
        flag_ref[...] = jnp.zeros_like(flag_ref)
        blocks = lengths.shape[0]
        rows, wide = mine.shape
        block = rows // blocks
        row = lax.broadcasted_iota(jnp.int32, (block, wide), 0)
        t = lax.axis_index("tensor")
        for out, side in ((mine, t), (other, lax.rem(t + 1, sides))):
            columns = pl.ds(pl.multiple_of(side * wide, LANES), wide)
            for b in range(blocks):
                here = slice(b * block, (b + 1) * block)
                out[here, :] = jnp.where(row < lengths[b], total[here, columns], 0.0)


def base_halves(tokens, base_key, sides, lengths):
    rows, depth = tokens.shape
    features = base_key.shape[1]
    wide = features // sides
    step = 512
    half = pl.BlockSpec((rows, wide), lambda i, n: (0, 0))
    return pl.pallas_call(
        functools.partial(base_kernel, sides),
        grid_spec=pltpu.PrefetchScalarGridSpec(
            num_scalar_prefetch=1,
            grid=(depth // step,),
            in_specs=[
                pl.BlockSpec((rows, step), lambda i, n: (0, i)),
                pl.BlockSpec((step, features), lambda i, n: (i, 0)),
            ],
            out_specs=[half, half, pl.BlockSpec((8, LANES), lambda i, n: (0, 0))],
            scratch_shapes=[pltpu.VMEM((rows, features), jnp.float32)],
        ),
        out_shape=[jax.ShapeDtypeStruct((rows, wide), jnp.float32)] * 2
        + [jax.ShapeDtypeStruct((8, LANES), jnp.float32)],
        cost_estimate=pl.CostEstimate(flops=0, bytes_accessed=0, transcendentals=0),
        compiler_params=FULL,
        name="base",
    )(lengths, tokens, base_key)


def mate_at(k, sign, groups, pair):
    kg, ky = k // pair, k % pair
    g = lax.rem(lax.axis_index("groups") + sign * kg + groups, groups)
    y = lax.rem(lax.axis_index("pair") + sign * ky + pair, pair)
    return g * pair + y


def collect_kernel(*refs):
    sems, held, pieces = refs[-1], refs[-2], refs[:-2]
    copies, start = [], 0
    for j, piece in enumerate(pieces):
        copies.append(pltpu.make_async_copy(piece, held.at[pl.ds(start, piece.shape[0])], sems.at[j]))
        start += piece.shape[0]
    for copy in copies:
        copy.start()
    for copy in copies:
        copy.wait()


def collect(pieces):
    count = sum(piece.shape[0] for piece in pieces)
    return pl.pallas_call(
        collect_kernel,
        in_specs=[ANY] * len(pieces),
        out_specs=VMEM,
        out_shape=jax.ShapeDtypeStruct((count,) + pieces[0].shape[1:], pieces[0].dtype),
        scratch_shapes=[pltpu.SemaphoreType.DMA((len(pieces),))],
        compiler_params=ROOM,
        name="collect",
    )(*pieces)


def rank_kernel(groups, ring, pair, rows, owner, tok, held, *refs):
    shares = groups * pair
    outs, flag = refs[:-1], refs[-1]
    flag[...] = jnp.zeros_like(flag)
    per, rank = held.shape[0] // (ring * pair), held.shape[1]
    blocks, _, block = outs[0].shape
    feats = tok.shape[2]
    z, y = lax.axis_index("ring"), lax.axis_index("pair")
    lane = lax.broadcasted_iota(jnp.int32, (16, LANES), 1)
    row = lax.broadcasted_iota(jnp.int32, (16, LANES), 0)
    mates = [mate_at(k, 1, groups, pair) for k in range(shares)]
    ids = []
    for mate in mates:
        named = tok[mate, rows:, :LANES].astype(jnp.float32)
        ids += [jnp.sum(jnp.where((lane == b) & (row == 0), named, 0.0)).astype(jnp.int32) for b in range(blocks)]
    for k, mate in enumerate(mates):
        for b in range(blocks):
            slot = owner[ids[k * blocks + b]]
            chip = slot // per
            away = lax.rem(chip // pair - z + ring, ring)
            way = lax.rem(lax.rem(chip, pair) - y + pair, pair)
            at = (way * ring + away) * per + lax.rem(slot, per)
            part = lax.dot_general(
                held[at, :, :feats],
                tok[mate, b * block : (b + 1) * block, :],
                (((1,), (1,)), ((), ())),
                preferred_element_type=jnp.float32,
            )
            outs[k][b, :rank, :] = part.astype(outs[k].dtype)
            outs[k][b, rank:, :] = held[at, :, feats:]


def rank_parts(owner, tok, held, groups, ring, pair, rows, blocks):
    shares, rank = tok.shape[0], held.shape[1]
    return pl.pallas_call(
        functools.partial(rank_kernel, groups, ring, pair, rows),
        in_specs=[SMEM, VMEM, VMEM],
        out_specs=[VMEM] * (shares + 1),
        out_shape=[jax.ShapeDtypeStruct((blocks, 2 * rank, rows // blocks), tok.dtype)] * shares
        + [jax.ShapeDtypeStruct((8, LANES), jnp.float32)],
        cost_estimate=pl.CostEstimate(flops=2 * tok.size * rank, bytes_accessed=2 * tok.size, transcendentals=0),
        compiler_params=ROOM,
        name="rank",
    )(owner, tok, held)


def sums_kernel(base_a, base_b, one, two, base, total):
    rank = total.shape[1]
    base[...] = base_a[...] + base_b[...]
    for b in range(one.shape[0]):
        total[b] = one[b, :rank, :].astype(jnp.float32) + two[b, :rank, :].astype(jnp.float32)


def first_sums(base_a, base_b, one, two):
    blocks, tall, block = one.shape
    return pl.pallas_call(
        sums_kernel,
        in_specs=[VMEM] * 4,
        out_specs=[VMEM] * 2,
        out_shape=[
            jax.ShapeDtypeStruct(base_a.shape, base_a.dtype),
            jax.ShapeDtypeStruct((blocks, tall // 2, block), jnp.float32),
        ],
        compiler_params=ROOM,
        name="sums",
    )(base_a, base_b, one, two)


def final_kernel(groups, pair, base, mine_sum, their_sum, *refs):
    shares = groups * pair
    mine, theirs, out_ref, up = refs[:shares], refs[shares:-2], refs[-2], refs[-1]
    blocks, tall, block = mine[0].shape
    rank = tall // 2
    tiles = out_ref.shape[1] // LANES
    for b in range(blocks):
        here = slice(b * block, (b + 1) * block)
        total = mine_sum[b] + their_sum[b]
        for part in mine[2:] + theirs:
            total += part[b, :rank, :].astype(jnp.float32)
        for k in range(shares):
            tile = lax.rem(mate_at(k, -1, groups, pair), tiles)
            up[b, :, pl.ds(pl.multiple_of(tile * LANES, LANES), LANES)] = mine[k][b, rank:, :]
        delta = lax.dot_general(
            total.astype(jnp.bfloat16), up[b], (((0,), (0,)), ((), ())), preferred_element_type=jnp.float32
        )
        out_ref[here, :] = (base[here, :] + delta).astype(out_ref.dtype)


def final(mine, theirs, sums, base, groups, pair, dtype):
    blocks, tall, _ = mine[0].shape
    return pl.pallas_call(
        functools.partial(final_kernel, groups, pair),
        in_specs=[VMEM] * (3 + len(mine) + len(theirs)),
        out_specs=VMEM,
        out_shape=jax.ShapeDtypeStruct(base.shape, dtype),
        scratch_shapes=[pltpu.VMEM((blocks, tall // 2, base.shape[1]), mine[0].dtype)],
        compiler_params=ROOM,
        name="final",
    )(base, *sums, *mine, *theirs)


def body(tokens, base_key, adapter_down, adapter_up, adapter_ids, owner_slot, lengths):
    groups, ring, pair = lax.axis_size("groups"), lax.axis_size("ring"), lax.axis_size("pair")
    sides = lax.axis_size("tensor")
    shares = groups * pair
    rows = tokens.shape[0]
    blocks = lengths.shape[0]

    def across(x):
        return lax.ppermute(x, "tensor", [(i, (i + 1) % sides) for i in range(sides)])

    def to_plane(x):
        return lax.all_to_all(x, PLANE, split_axis=0, concat_axis=0, tiled=True)

    def along(x, step):
        return lax.ppermute(x, "ring", [(a, (a + step) % ring) for a in range(ring)])

    def first_hops(x):
        return {0: x, ring - 1: along(x, 1), **({1: along(x, -1)} if ring > 2 else {})}

    def in_plane(x, kg, ky):
        pairs = []
        for a in range(groups):
            for b in range(pair):
                pairs.append((a * pair + b, (a + kg) % groups * pair + (b + ky) % pair))
        return lax.ppermute(x, PLANE, pairs)

    def more_hops(held, way, *after):
        for k in range(2, ring // 2 + 1):
            if 2 * k < ring or way % 2 == 0:
                if k == 2:
                    held[ring - 1] = hand_on(held[ring - 1], held[1], *after)
                held[ring - k] = along(held[ring - k + 1], 1)
            if 2 * k < ring or way % 2 == 1:
                if k == 2:
                    held[1] = hand_on(held[1], held[ring - 1], *after)
                held[k] = along(held[k - 1], -1)
        return [held[k] for k in range(ring)]

    packed = pack(jnp.swapaxes(adapter_down, 1, 2), adapter_up, shares, pair)
    slabs = spread(tokens, lengths, adapter_ids.reshape(-1), shares)
    swapped = [
        lax.ppermute(packed[pair - w], "pair", [(a, (a - w) % pair) for a in range(pair)]) for w in range(1, pair)
    ]
    firsts = [first_hops(piece) for piece in [packed[0]] + swapped]
    tok = to_plane(hand_on(slabs, *swapped, firsts[0][ring - 1]))

    base_mine, base_out, flag = base_halves(tokens, base_key, sides, lengths)
    pieces = [
        more_hops(held, way, flag)
        for way, held in enumerate(firsts)
    ]

    flat = [piece for way in pieces for piece in way]
    *parts, flag = rank_parts(owner_slot, tok, collect(flat), groups, ring, pair, rows, blocks)
    base_in = across(hand_on(base_out, flag))
    mine = [parts[0]] + [in_plane(parts[k], k // pair, k % pair) for k in range(1, shares)]
    base, first = first_sums(base_mine, base_in, mine[0], mine[1])
    theirs = [across(part) for part in mine[2:]]
    return final(mine, theirs, [first, across(first)], base, groups, pair, tokens.dtype)


def solution(mesh):
    groups, dp, sides = (mesh.shape[name] for name in ("groups", "dp", "tensor"))
    pair = 2 if dp % 2 == 0 else 1
    cut = Mesh(mesh.devices.reshape(groups, dp // pair, pair, sides), ("groups", "ring", "pair", "tensor"))
    stored = ("ring", "pair")
    placed = (
        P(WHOLE, "tensor"),
        P("tensor", None),
        P(stored, "tensor", None),
        P(stored, None, "tensor"),
        P(WHOLE, None),
        P(),
        P(WHOLE),
    )
    return jax.shard_map(body, mesh=cut, in_specs=placed, out_specs=P(WHOLE, "tensor"), check_vma=False)
```

```python
import functools

import jax
import jax.numpy as jnp
from jax import lax
from jax.experimental import pallas as pl
from jax.experimental.pallas import tpu as pltpu
from jax.sharding import Mesh
from jax.sharding import PartitionSpec as P

LANES = 128
ANY = pl.BlockSpec(memory_space=pl.ANY)
SMEM = pl.BlockSpec(memory_space=pltpu.SMEM)
VMEM = pl.BlockSpec(memory_space=pltpu.VMEM)
HBM = pl.BlockSpec(memory_space=pltpu.HBM)
ROOM = pltpu.CompilerParams(vmem_limit_bytes=32 * 1024 * 1024)
TOKENS_ROOM = pltpu.CompilerParams(vmem_limit_bytes=59_550_000)
FULL = pltpu.CompilerParams(vmem_limit_bytes=60 * 1024 * 1024)
PLANE = ("groups", "pair")
WHOLE = ("groups", "ring", "pair")


def hand_kernel(*refs):
    pass


def hand_on(x, *after):
    return pl.pallas_call(
        hand_kernel,
        in_specs=[ANY] * (1 + len(after)),
        out_specs=ANY,
        out_shape=jax.ShapeDtypeStruct(x.shape, x.dtype),
        input_output_aliases={0: 0},
        compiler_params=FULL,
        name="hand",
    )(x, *after)


def pack_kernel(ways, down, up, *refs):
    outs, sems = refs[:-1], refs[-1]
    feats = outs[0].shape[2] - LANES
    adapters = down.shape[0]
    copies = []
    for j, out in enumerate(outs):
        way = j if j < ways else 0
        share = lax.axis_index("groups") * ways + lax.rem(lax.axis_index("pair") + way, ways)
        start = pl.multiple_of(share * feats, LANES)
        tile = pl.multiple_of(lax.rem(share, up.shape[2] // LANES) * LANES, LANES)
        own = pl.ds(0, adapters) if j < ways else pl.ds(j - ways, 1)
        copies.append(pltpu.make_async_copy(down.at[own, :, pl.ds(start, feats)], out.at[:, :, :feats], sems.at[j, 0]))
        copies.append(pltpu.make_async_copy(up.at[own, :, pl.ds(tile, LANES)], out.at[:, :, feats:], sems.at[j, 1]))
    for copy in copies:
        copy.start()
    for copy in copies:
        copy.wait()


def pack(down, up, shares, ways, apart):
    adapters, rank, feats = down.shape
    wide = feats // shares + LANES
    shapes = [(adapters, rank, wide)] * ways + [(1, rank, wide)] * (adapters if apart else 0)
    outs = pl.pallas_call(
        functools.partial(pack_kernel, ways),
        in_specs=[HBM, HBM],
        out_specs=[VMEM] * len(shapes),
        out_shape=[jax.ShapeDtypeStruct(shape, down.dtype) for shape in shapes],
        scratch_shapes=[pltpu.SemaphoreType.DMA((len(shapes), 2))],
        compiler_params=FULL,
        name="pack",
    )(down, up)
    return outs[:ways], outs[ways:]


def spread_kernel(lengths, ids, tok, out, held, in_sems, out_sems):
    blocks = lengths.shape[0]
    shares, tall, step = held.shape
    rows = tok.shape[0]
    block = rows // blocks

    def read(k, b):
        here = pl.ds(b * block, block)
        return pltpu.make_async_copy(tok.at[here, pl.ds(k * step, step)], held.at[k, here, :], in_sems.at[k, b])

    for k in range(shares):
        for b in range(blocks):
            read(k, b).start()
    lane = lax.broadcasted_iota(jnp.int32, (tall - rows, step), 1)
    named = jnp.zeros((tall - rows, step), jnp.float32)
    for b in range(blocks):
        named = jnp.where(lane == b, ids[b].astype(jnp.float32), named)
    named = named.astype(held.dtype)
    writes = [pltpu.make_async_copy(held.at[k], out.at[k], out_sems.at[k]) for k in range(shares)]
    for k in range(shares):
        held[k, rows:, :] = named
        for b in range(blocks):
            read(k, b).wait()

            @pl.when(lengths[b] < block)
            def _():
                here = slice(b * block, (b + 1) * block)
                row = lax.broadcasted_iota(jnp.int32, (block, step), 0)
                part = held[k, here, :]
                held[k, here, :] = jnp.where(row < lengths[b], part, jnp.zeros_like(part))

        writes[k].start()
    for write in writes:
        write.wait()


def spread(tokens, lengths, ids, shares):
    rows, feats = tokens.shape
    shape = (shares, rows + 16, feats // shares)
    return pl.pallas_call(
        spread_kernel,
        in_specs=[SMEM, SMEM, ANY],
        out_specs=ANY,
        out_shape=jax.ShapeDtypeStruct(shape, tokens.dtype),
        scratch_shapes=[
            pltpu.VMEM(shape, tokens.dtype),
            pltpu.SemaphoreType.DMA((shares, lengths.shape[0])),
            pltpu.SemaphoreType.DMA((shares,)),
        ],
        compiler_params=FULL,
        name="spread",
    )(lengths, ids, tokens)


def base_kernel(sides, lengths, tok_ref, key_ref, mine, other, flag_ref, total):
    step = pl.program_id(0)
    part = jnp.dot(tok_ref[...], key_ref[...], preferred_element_type=jnp.float32)

    @pl.when(step == 0)
    def _():
        total[...] = part

    @pl.when(step > 0)
    def _():
        total[...] += part

    @pl.when(step == pl.num_programs(0) - 1)
    def _():
        flag_ref[...] = jnp.zeros_like(flag_ref)
        blocks = lengths.shape[0]
        rows, wide = mine.shape
        block = rows // blocks
        row = lax.broadcasted_iota(jnp.int32, (block, wide), 0)
        t = lax.axis_index("tensor")
        for out, side in ((mine, t), (other, lax.rem(t + 1, sides))):
            columns = pl.ds(pl.multiple_of(side * wide, LANES), wide)
            for b in range(blocks):
                here = slice(b * block, (b + 1) * block)
                out[here, :] = jnp.where(row < lengths[b], total[here, columns], 0.0)


def base_halves(tokens, base_key, sides, lengths):
    rows, depth = tokens.shape
    features = base_key.shape[1]
    wide = features // sides
    step = 512
    half = pl.BlockSpec((rows, wide), lambda i, n: (0, 0))
    return pl.pallas_call(
        functools.partial(base_kernel, sides),
        grid_spec=pltpu.PrefetchScalarGridSpec(
            num_scalar_prefetch=1,
            grid=(depth // step,),
            in_specs=[
                pl.BlockSpec((rows, step), lambda i, n: (0, i)),
                pl.BlockSpec((step, features), lambda i, n: (i, 0)),
            ],
            out_specs=[half, half, pl.BlockSpec((8, LANES), lambda i, n: (0, 0))],
            scratch_shapes=[pltpu.VMEM((rows, features), jnp.float32)],
        ),
        out_shape=[jax.ShapeDtypeStruct((rows, wide), jnp.float32)] * 2
        + [jax.ShapeDtypeStruct((8, LANES), jnp.float32)],
        cost_estimate=pl.CostEstimate(flops=0, bytes_accessed=0, transcendentals=0),
        compiler_params=FULL,
        name="base",
    )(lengths, tokens, base_key)


def mate_at(k, sign, groups, pair):
    kg, ky = k // pair, k % pair
    g = lax.rem(lax.axis_index("groups") + sign * kg + groups, groups)
    y = lax.rem(lax.axis_index("pair") + sign * ky + pair, pair)
    return g * pair + y


def rank_kernel(groups, ring, pair, rows, owner, tok, *refs):
    shares = groups * pair
    held, sems = refs[-2:]
    pieces, outs, flag = refs[: -3 - shares], refs[-3 - shares : -3], refs[-3]
    flag[...] = jnp.zeros_like(flag)
    half = held.shape[1] // 2
    copies = []
    for piece in pieces:
        for a in range(piece.shape[0]):
            at = len(copies) // 2
            for rank_rows in (pl.ds(0, half), pl.ds(half, half)):
                sem = sems.at[len(copies)]
                copies.append(pltpu.make_async_copy(piece.at[a, rank_rows, :], held.at[at, rank_rows, :], sem))
    for copy in copies:
        copy.start()
    per, rank = held.shape[0] // (ring * pair), held.shape[1]
    blocks, _, block = outs[0].shape
    feats = tok.shape[2]
    z, y = lax.axis_index("ring"), lax.axis_index("pair")
    lane = lax.broadcasted_iota(jnp.int32, (16, LANES), 1)
    row = lax.broadcasted_iota(jnp.int32, (16, LANES), 0)
    mates = [mate_at(k, 1, groups, pair) for k in range(shares)]
    ids = []
    for mate in mates:
        named = tok[mate, rows:, :LANES].astype(jnp.float32)
        ids += [jnp.sum(jnp.where((lane == b) & (row == 0), named, 0.0)).astype(jnp.int32) for b in range(blocks)]
    for copy in copies:
        copy.wait()
    for k, mate in enumerate(mates):
        for b in range(blocks):
            slot = owner[ids[k * blocks + b]]
            chip = slot // per
            away = lax.rem(chip // pair - z + ring, ring)
            way = lax.rem(lax.rem(chip, pair) - y + pair, pair)
            at = (way * ring + away) * per + lax.rem(slot, per)
            part = lax.dot_general(
                held[at, :, :feats],
                tok[mate, b * block : (b + 1) * block, :],
                (((1,), (1,)), ((), ())),
                preferred_element_type=jnp.float32,
            )
            outs[k][b, :rank, :] = part.astype(outs[k].dtype)
            outs[k][b, rank:, :] = held[at, :, feats:]


def rank_parts(owner, tok, pieces, groups, ring, pair, rows, blocks):
    shares, rank = tok.shape[0], pieces[0].shape[1]
    count = sum(piece.shape[0] for piece in pieces)
    return pl.pallas_call(
        functools.partial(rank_kernel, groups, ring, pair, rows),
        in_specs=[SMEM, VMEM] + [ANY] * len(pieces),
        out_specs=[VMEM] * (shares + 1),
        out_shape=[jax.ShapeDtypeStruct((blocks, 2 * rank, rows // blocks), tok.dtype)] * shares
        + [jax.ShapeDtypeStruct((8, LANES), jnp.float32)],
        scratch_shapes=[pltpu.VMEM((count,) + pieces[0].shape[1:], tok.dtype), pltpu.SemaphoreType.DMA((2 * count,))],
        cost_estimate=pl.CostEstimate(flops=2 * tok.size * rank, bytes_accessed=2 * tok.size, transcendentals=0),
        compiler_params=TOKENS_ROOM,
        name="rank",
    )(owner, tok, *pieces)


def final_kernel(groups, pair, base_a, base_b, *refs):
    shares = groups * pair
    mine, theirs, out_ref, up = refs[:shares], refs[shares : 2 * shares], refs[-2], refs[-1]
    blocks, tall, block = mine[0].shape
    rank = tall // 2
    tiles = out_ref.shape[1] // LANES
    for b in range(blocks):
        here = slice(b * block, (b + 1) * block)
        total = mine[0][b, :rank, :].astype(jnp.float32)
        for part in mine[1:] + theirs:
            total += part[b, :rank, :].astype(jnp.float32)
        for k in range(shares):
            tile = lax.rem(mate_at(k, -1, groups, pair), tiles)
            up[b, :, pl.ds(pl.multiple_of(tile * LANES, LANES), LANES)] = mine[k][b, rank:, :]
        delta = lax.dot_general(
            total.astype(jnp.bfloat16), up[b], (((0,), (0,)), ((), ())), preferred_element_type=jnp.float32
        )
        out_ref[here, :] = (base_a[here, :] + base_b[here, :] + delta).astype(out_ref.dtype)


def final(mine, theirs, base, groups, pair, dtype):
    blocks, tall, _ = mine[0].shape
    return pl.pallas_call(
        functools.partial(final_kernel, groups, pair),
        in_specs=[VMEM] * (2 + 2 * len(mine)),
        out_specs=VMEM,
        out_shape=jax.ShapeDtypeStruct(base[0].shape, dtype),
        scratch_shapes=[pltpu.VMEM((blocks, tall // 2, base[0].shape[1]), mine[0].dtype)],
        compiler_params=ROOM,
        name="final",
    )(*base, *mine, *theirs)


def body(tokens, base_key, adapter_down, adapter_up, adapter_ids, owner_slot, lengths):
    groups, ring, pair = lax.axis_size("groups"), lax.axis_size("ring"), lax.axis_size("pair")
    sides = lax.axis_size("tensor")
    shares = groups * pair
    rows = tokens.shape[0]
    blocks = lengths.shape[0]

    def across(x):
        return lax.ppermute(x, "tensor", [(i, (i + 1) % sides) for i in range(sides)])

    def to_plane(x):
        return lax.all_to_all(x, PLANE, split_axis=0, concat_axis=0, tiled=True)

    def along(x, step):
        return lax.ppermute(x, "ring", [(a, (a + step) % ring) for a in range(ring)])

    def first_hops(x, apart=()):
        held = {0: x, ring - 1: along(x, 1)}
        if ring > 2:
            held[1] = [along(one, -1) for one in apart] if apart else along(x, -1)
        return held

    def in_plane(x, kg, ky):
        pairs = []
        for a in range(groups):
            for b in range(pair):
                pairs.append((a * pair + b, (a + kg) % groups * pair + (b + ky) % pair))
        return lax.ppermute(x, PLANE, pairs)

    def more_hops(held, way, *after):
        for k in range(2, ring // 2 + 1):
            if 2 * k < ring or way % 2 == 0:
                if k == 2:
                    held[ring - 1] = hand_on(held[ring - 1], held[1][-1] if way == 0 and apart else held[1], *after)
                held[ring - k] = along(held[ring - k + 1], 1)
            if 2 * k < ring or way % 2 == 1:
                if k == 2:
                    held[1] = hand_on(held[1], held[ring - 1], *after)
                held[k] = along(held[k - 1], -1)
        return [held[k] for k in range(ring)]

    packed, apart = pack(jnp.swapaxes(adapter_down, 1, 2), adapter_up, shares, pair, ring == 4)
    slabs = spread(tokens, lengths, adapter_ids.reshape(-1), shares)
    swapped = [
        lax.ppermute(packed[pair - w], "pair", [(a, (a - w) % pair) for a in range(pair)]) for w in range(1, pair)
    ]
    firsts = [first_hops(packed[0], apart)] + [first_hops(piece) for piece in swapped]
    tok = to_plane(hand_on(slabs, *swapped, *(firsts[0][1][:1] if apart else [])))

    base_mine, base_out, flag = base_halves(tokens, base_key, sides, lengths)
    pieces = [
        more_hops(held, way, flag)
        for way, held in enumerate(firsts)
    ]

    flat = []
    for piece in [piece for way in pieces for piece in way]:
        flat += piece if isinstance(piece, list) else [piece]
    *parts, ready = rank_parts(owner_slot, tok, flat, groups, ring, pair, rows, blocks)
    mine = [parts[0]] + [in_plane(parts[k], k // pair, k % pair) for k in range(1, shares)]
    theirs = [across(part) for part in mine]
    base_in = across(hand_on(base_out, ready))
    return final(mine, theirs, [base_mine, base_in], groups, pair, tokens.dtype)


def solution(mesh):
    groups, dp, sides = (mesh.shape[name] for name in ("groups", "dp", "tensor"))
    pair = 2 if dp % 2 == 0 else 1
    cut = Mesh(mesh.devices.reshape(groups, dp // pair, pair, sides), ("groups", "ring", "pair", "tensor"))
    stored = ("ring", "pair")
    placed = (
        P(WHOLE, "tensor"),
        P("tensor", None),
        P(stored, "tensor", None),
        P(stored, None, "tensor"),
        P(WHOLE, None),
        P(),
        P(WHOLE),
    )
    return jax.shard_map(body, mesh=cut, in_specs=placed, out_specs=P(WHOLE, "tensor"), check_vma=False)
```

```python
import functools

import jax
import jax.numpy as jnp
from jax import lax
from jax.experimental import pallas as pl
from jax.experimental.pallas import tpu as pltpu
from jax.sharding import Mesh
from jax.sharding import PartitionSpec as P

LANES = 128
ANY = pl.BlockSpec(memory_space=pl.ANY)
SMEM = pl.BlockSpec(memory_space=pltpu.SMEM)
VMEM = pl.BlockSpec(memory_space=pltpu.VMEM)
HBM = pl.BlockSpec(memory_space=pltpu.HBM)
ROOM = pltpu.CompilerParams(vmem_limit_bytes=32 * 1024 * 1024)
FULL = pltpu.CompilerParams(vmem_limit_bytes=60 * 1024 * 1024)
PLANE = ("groups", "pair")
WHOLE = ("groups", "ring", "pair")


def hand_kernel(*refs):
    pass


def hand_on(x, *after):
    return pl.pallas_call(
        hand_kernel,
        in_specs=[ANY] * (1 + len(after)),
        out_specs=ANY,
        out_shape=jax.ShapeDtypeStruct(x.shape, x.dtype),
        input_output_aliases={0: 0},
        compiler_params=FULL,
        name="hand",
    )(x, *after)


def pack_kernel(down, up, *refs):
    outs, sems = refs[:-1], refs[-1]
    feats = outs[0].shape[2] - LANES
    copies = []
    for way, out in enumerate(outs):
        share = lax.axis_index("groups") * len(outs) + lax.rem(lax.axis_index("pair") + way, len(outs))
        start = pl.multiple_of(share * feats, LANES)
        tile = pl.multiple_of(lax.rem(share, up.shape[2] // LANES) * LANES, LANES)
        copies.append(pltpu.make_async_copy(down.at[:, :, pl.ds(start, feats)], out.at[:, :, :feats], sems.at[way, 0]))
        copies.append(pltpu.make_async_copy(up.at[:, :, pl.ds(tile, LANES)], out.at[:, :, feats:], sems.at[way, 1]))
    for copy in copies:
        copy.start()
    for copy in copies:
        copy.wait()


def pack(down, up, shares, ways):
    adapters, rank, feats = down.shape
    shape = jax.ShapeDtypeStruct((adapters, rank, feats // shares + LANES), down.dtype)
    return pl.pallas_call(
        pack_kernel,
        in_specs=[HBM, HBM],
        out_specs=[VMEM] * ways,
        out_shape=[shape] * ways,
        scratch_shapes=[pltpu.SemaphoreType.DMA((ways, 2))],
        compiler_params=FULL,
        name="pack",
    )(down, up)


def mate_at(k, sign, groups, pair):
    kg, ky = k // pair, k % pair
    g = lax.rem(lax.axis_index("groups") + sign * kg + groups, groups)
    y = lax.rem(lax.axis_index("pair") + sign * ky + pair, pair)
    return g * pair + y


def spread_kernel(groups, pair, lengths, ids, tok, *refs):
    held, in_sems, out_sems = refs[-3:]
    outs = refs[:-3]
    blocks = lengths.shape[0]
    shares, tall, step = held.shape
    rows = tok.shape[0]
    block = rows // blocks
    mates = [pl.multiple_of(mate_at(k, 1, groups, pair) * step, LANES) for k in range(shares)]
    order = list(range(1, shares)) + [0]

    def read(k, b):
        here = pl.ds(b * block, block)
        return pltpu.make_async_copy(tok.at[here, pl.ds(mates[k], step)], held.at[k, here, :], in_sems.at[k, b])

    for k in order:
        for b in range(blocks):
            read(k, b).start()
    lane = lax.broadcasted_iota(jnp.int32, (tall - rows, step), 1)
    named = jnp.zeros((tall - rows, step), jnp.float32)
    for b in range(blocks):
        named = jnp.where(lane == b, ids[b].astype(jnp.float32), named)
    named = named.astype(held.dtype)
    writes = [pltpu.make_async_copy(held.at[k], outs[k], out_sems.at[k]) for k in range(shares)]
    for k in order:
        held[k, rows:, :] = named
        for b in range(blocks):
            read(k, b).wait()

            @pl.when(lengths[b] < block)
            def _():
                here = slice(b * block, (b + 1) * block)
                row = lax.broadcasted_iota(jnp.int32, (block, step), 0)
                part = held[k, here, :]
                held[k, here, :] = jnp.where(row < lengths[b], part, jnp.zeros_like(part))

        writes[k].start()
    for write in writes:
        write.wait()


def spread(tokens, lengths, ids, groups, pair):
    rows, feats = tokens.shape
    shares = groups * pair
    shape = (rows + 16, feats // shares)
    return pl.pallas_call(
        functools.partial(spread_kernel, groups, pair),
        in_specs=[SMEM, SMEM, ANY],
        out_specs=[ANY] * shares,
        out_shape=[jax.ShapeDtypeStruct(shape, tokens.dtype)] * shares,
        scratch_shapes=[
            pltpu.VMEM((shares,) + shape, tokens.dtype),
            pltpu.SemaphoreType.DMA((shares, lengths.shape[0])),
            pltpu.SemaphoreType.DMA((shares,)),
        ],
        compiler_params=FULL,
        name="spread",
    )(lengths, ids, tokens)


def base_kernel(sides, lengths, tok_ref, key_ref, mine, other, flag_ref, total):
    step = pl.program_id(0)
    part = jnp.dot(tok_ref[...], key_ref[...], preferred_element_type=jnp.float32)

    @pl.when(step == 0)
    def _():
        total[...] = part

    @pl.when(step > 0)
    def _():
        total[...] += part

    @pl.when(step == pl.num_programs(0) - 1)
    def _():
        flag_ref[...] = jnp.zeros_like(flag_ref)
        blocks = lengths.shape[0]
        rows, wide = mine.shape
        block = rows // blocks
        row = lax.broadcasted_iota(jnp.int32, (block, wide), 0)
        t = lax.axis_index("tensor")
        for out, side in ((mine, t), (other, lax.rem(t + 1, sides))):
            columns = pl.ds(pl.multiple_of(side * wide, LANES), wide)
            for b in range(blocks):
                here = slice(b * block, (b + 1) * block)
                out[here, :] = jnp.where(row < lengths[b], total[here, columns], 0.0)


def base_halves(tokens, base_key, sides, lengths):
    rows, depth = tokens.shape
    features = base_key.shape[1]
    wide = features // sides
    step = 512
    half = pl.BlockSpec((rows, wide), lambda i, n: (0, 0))
    return pl.pallas_call(
        functools.partial(base_kernel, sides),
        grid_spec=pltpu.PrefetchScalarGridSpec(
            num_scalar_prefetch=1,
            grid=(depth // step,),
            in_specs=[
                pl.BlockSpec((rows, step), lambda i, n: (0, i)),
                pl.BlockSpec((step, features), lambda i, n: (i, 0)),
            ],
            out_specs=[half, half, pl.BlockSpec((8, LANES), lambda i, n: (0, 0))],
            scratch_shapes=[pltpu.VMEM((rows, features), jnp.float32)],
        ),
        out_shape=[jax.ShapeDtypeStruct((rows, wide), jnp.float32)] * 2
        + [jax.ShapeDtypeStruct((8, LANES), jnp.float32)],
        cost_estimate=pl.CostEstimate(flops=0, bytes_accessed=0, transcendentals=0),
        compiler_params=FULL,
        name="base",
    )(lengths, tokens, base_key)


def collect_kernel(*refs):
    sems, held, pieces = refs[-1], refs[-2], refs[:-2]
    copies, start = [], 0
    for j, piece in enumerate(pieces):
        copies.append(pltpu.make_async_copy(piece, held.at[pl.ds(start, piece.shape[0])], sems.at[j]))
        start += piece.shape[0]
    for copy in copies:
        copy.start()
    for copy in copies:
        copy.wait()


def collect(pieces):
    count = sum(piece.shape[0] for piece in pieces)
    return pl.pallas_call(
        collect_kernel,
        in_specs=[ANY] * len(pieces),
        out_specs=VMEM,
        out_shape=jax.ShapeDtypeStruct((count,) + pieces[0].shape[1:], pieces[0].dtype),
        scratch_shapes=[pltpu.SemaphoreType.DMA((len(pieces),))],
        compiler_params=ROOM,
        name="collect",
    )(*pieces)


def rank_kernel(ring, pair, rows, owner, held, *refs):
    shares = (len(refs) - 1) // 2
    toks, outs, flag = refs[:shares], refs[shares:-1], refs[-1]
    flag[...] = jnp.zeros_like(flag)
    per, rank = held.shape[0] // (ring * pair), held.shape[1]
    blocks, _, block = outs[0].shape
    feats = toks[0].shape[1]
    z, y = lax.axis_index("ring"), lax.axis_index("pair")
    lane = lax.broadcasted_iota(jnp.int32, (16, LANES), 1)
    row = lax.broadcasted_iota(jnp.int32, (16, LANES), 0)
    ids = []
    for tok in toks:
        named = tok[rows:, :LANES].astype(jnp.float32)
        ids += [jnp.sum(jnp.where((lane == b) & (row == 0), named, 0.0)).astype(jnp.int32) for b in range(blocks)]
    for k, tok in enumerate(toks):
        for b in range(blocks):
            slot = owner[ids[k * blocks + b]]
            chip = slot // per
            away = lax.rem(chip // pair - z + ring, ring)
            way = lax.rem(lax.rem(chip, pair) - y + pair, pair)
            at = (way * ring + away) * per + lax.rem(slot, per)
            part = lax.dot_general(
                held[at, :, :feats],
                tok[b * block : (b + 1) * block, :],
                (((1,), (1,)), ((), ())),
                preferred_element_type=jnp.float32,
            )
            outs[k][b, :rank, :] = part.astype(outs[k].dtype)
            outs[k][b, rank:, :] = held[at, :, feats:]


def rank_parts(owner, toks, held, ring, pair, rows, blocks):
    shares, rank = len(toks), held.shape[1]
    return pl.pallas_call(
        functools.partial(rank_kernel, ring, pair, rows),
        in_specs=[SMEM, VMEM] + [VMEM] * shares,
        out_specs=[VMEM] * (shares + 1),
        out_shape=[jax.ShapeDtypeStruct((blocks, 2 * rank, rows // blocks), held.dtype)] * shares
        + [jax.ShapeDtypeStruct((8, LANES), jnp.float32)],
        cost_estimate=pl.CostEstimate(flops=0, bytes_accessed=0, transcendentals=0),
        compiler_params=ROOM,
        name="rank",
    )(owner, held, *toks)


def final_kernel(groups, pair, base_a, base_b, *refs):
    shares = groups * pair
    mine, theirs, out_ref, up = refs[:shares], refs[shares : 2 * shares], refs[-2], refs[-1]
    blocks, tall, block = mine[0].shape
    rank = tall // 2
    tiles = out_ref.shape[1] // LANES
    for b in range(blocks):
        here = slice(b * block, (b + 1) * block)
        total = mine[0][b, :rank, :].astype(jnp.float32)
        for part in mine[1:] + theirs:
            total += part[b, :rank, :].astype(jnp.float32)
        for k in range(shares):
            tile = lax.rem(mate_at(k, 1, groups, pair), tiles)
            up[b, :, pl.ds(pl.multiple_of(tile * LANES, LANES), LANES)] = mine[k][b, rank:, :]
        delta = lax.dot_general(
            total.astype(jnp.bfloat16), up[b], (((0,), (0,)), ((), ())), preferred_element_type=jnp.float32
        )
        out_ref[here, :] = (base_a[here, :] + base_b[here, :] + delta).astype(out_ref.dtype)


def final(mine, theirs, base, groups, pair, dtype):
    blocks, tall, _ = mine[0].shape
    return pl.pallas_call(
        functools.partial(final_kernel, groups, pair),
        in_specs=[VMEM] * (2 + 2 * len(mine)),
        out_specs=VMEM,
        out_shape=jax.ShapeDtypeStruct(base[0].shape, dtype),
        scratch_shapes=[pltpu.VMEM((blocks, tall // 2, base[0].shape[1]), mine[0].dtype)],
        compiler_params=ROOM,
        name="final",
    )(*base, *mine, *theirs)


def body(tokens, base_key, adapter_down, adapter_up, adapter_ids, owner_slot, lengths):
    groups, ring, pair = lax.axis_size("groups"), lax.axis_size("ring"), lax.axis_size("pair")
    sides = lax.axis_size("tensor")
    shares = groups * pair
    rows = tokens.shape[0]
    blocks = lengths.shape[0]

    def across(x):
        return lax.ppermute(x, "tensor", [(i, (i + 1) % sides) for i in range(sides)])

    def along(x, step):
        return lax.ppermute(x, "ring", [(a, (a + step) % ring) for a in range(ring)])

    def first_hops(x):
        return {0: x, ring - 1: along(x, 1), **({1: along(x, -1)} if ring > 2 else {})}

    def in_plane(x, kg, ky):
        pairs = []
        for a in range(groups):
            for b in range(pair):
                pairs.append((a * pair + b, (a + kg) % groups * pair + (b + ky) % pair))
        return lax.ppermute(x, PLANE, pairs)

    def more_hops(held, way, *after):
        for k in range(2, ring // 2 + 1):
            if 2 * k < ring or way % 2 == 0:
                if k == 2:
                    held[ring - 1] = hand_on(held[ring - 1], held[1], *after)
                held[ring - k] = along(held[ring - k + 1], 1)
            if 2 * k < ring or way % 2 == 1:
                if k == 2:
                    held[1] = hand_on(held[1], held[ring - 1], *after)
                held[k] = along(held[k - 1], -1)
        return [held[k] for k in range(ring)]

    packed = pack(jnp.swapaxes(adapter_down, 1, 2), adapter_up, shares, pair)
    slabs = spread(tokens, lengths, adapter_ids.reshape(-1), groups, pair)
    swapped = [
        lax.ppermute(packed[pair - w], "pair", [(a, (a - w) % pair) for a in range(pair)]) for w in range(1, pair)
    ]
    firsts = [first_hops(piece) for piece in [packed[0]] + swapped]
    toks = [slabs[0]] + [in_plane(slabs[k], k // pair, k % pair) for k in range(1, shares)]

    base_mine, base_out, flag = base_halves(tokens, base_key, sides, lengths)
    pieces = [
        more_hops(held, way, flag)
        for way, held in enumerate(firsts)
    ]

    flat = [piece for way in pieces for piece in way]
    *parts, ready = rank_parts(owner_slot, toks, collect(flat), ring, pair, rows, blocks)
    mine = [parts[0]] + [in_plane(parts[k], -(k // pair), -(k % pair)) for k in range(1, shares)]
    theirs = [across(part) for part in mine]
    base_in = across(hand_on(base_out, ready))
    return final(mine, theirs, [base_mine, base_in], groups, pair, tokens.dtype)


def solution(mesh):
    groups, dp, sides = (mesh.shape[name] for name in ("groups", "dp", "tensor"))
    pair = 2 if dp % 2 == 0 else 1
    cut = Mesh(mesh.devices.reshape(groups, dp // pair, pair, sides), ("groups", "ring", "pair", "tensor"))
    stored = ("ring", "pair")
    placed = (
        P(WHOLE, "tensor"),
        P("tensor", None),
        P(stored, "tensor", None),
        P(stored, None, "tensor"),
        P(WHOLE, None),
        P(),
        P(WHOLE),
    )
    return jax.shard_map(body, mesh=cut, in_specs=placed, out_specs=P(WHOLE, "tensor"), check_vma=False)
```

```python
import functools

import jax
import jax.numpy as jnp
from jax import lax
from jax.experimental import pallas as pl
from jax.experimental.pallas import tpu as pltpu
from jax.sharding import Mesh
from jax.sharding import PartitionSpec as P

LANES = 128
ANY = pl.BlockSpec(memory_space=pl.ANY)
SMEM = pl.BlockSpec(memory_space=pltpu.SMEM)
VMEM = pl.BlockSpec(memory_space=pltpu.VMEM)
HBM = pl.BlockSpec(memory_space=pltpu.HBM)
ROOM = pltpu.CompilerParams(vmem_limit_bytes=32 * 1024 * 1024)
FULL = pltpu.CompilerParams(vmem_limit_bytes=60 * 1024 * 1024)
PLANE = ("groups", "pair")
WHOLE = ("groups", "ring", "pair")


def hand_kernel(*refs):
    pass


def hand_on(x, *after):
    return pl.pallas_call(
        hand_kernel,
        in_specs=[ANY] * (1 + len(after)),
        out_specs=ANY,
        out_shape=jax.ShapeDtypeStruct(x.shape, x.dtype),
        input_output_aliases={0: 0},
        compiler_params=FULL,
        name="hand",
    )(x, *after)


def pack_kernel(down, up, *refs):
    outs, sems = refs[:-1], refs[-1]
    feats = outs[0].shape[2] - LANES
    copies = []
    for way, out in enumerate(outs):
        share = lax.axis_index("groups") * len(outs) + lax.rem(lax.axis_index("pair") + way, len(outs))
        start = pl.multiple_of(share * feats, LANES)
        tile = pl.multiple_of(lax.rem(share, up.shape[2] // LANES) * LANES, LANES)
        copies.append(pltpu.make_async_copy(down.at[:, :, pl.ds(start, feats)], out.at[:, :, :feats], sems.at[way, 0]))
        copies.append(pltpu.make_async_copy(up.at[:, :, pl.ds(tile, LANES)], out.at[:, :, feats:], sems.at[way, 1]))
    for copy in copies:
        copy.start()
    for copy in copies:
        copy.wait()


def pack(down, up, shares, ways):
    adapters, rank, feats = down.shape
    shape = jax.ShapeDtypeStruct((adapters, rank, feats // shares + LANES), down.dtype)
    return pl.pallas_call(
        pack_kernel,
        in_specs=[HBM, HBM],
        out_specs=[VMEM] * ways,
        out_shape=[shape] * ways,
        scratch_shapes=[pltpu.SemaphoreType.DMA((ways, 2))],
        compiler_params=FULL,
        name="pack",
    )(down, up)


def mate_at(k, sign, groups, pair):
    kg, ky = k // pair, k % pair
    g = lax.rem(lax.axis_index("groups") + sign * kg + groups, groups)
    y = lax.rem(lax.axis_index("pair") + sign * ky + pair, pair)
    return g * pair + y


def spread_kernel(groups, pair, lengths, ids, tok, *refs):
    held, in_sems, out_sems = refs[-3:]
    outs = refs[:-3]
    blocks = lengths.shape[0]
    shares, tall, step = held.shape
    rows = tok.shape[0]
    block = rows // blocks
    mates = [pl.multiple_of(mate_at(k, 1, groups, pair) * step, LANES) for k in range(shares)]
    order = list(range(1, shares)) + [0]

    def read(k, b):
        here = pl.ds(b * block, block)
        return pltpu.make_async_copy(tok.at[here, pl.ds(mates[k], step)], held.at[k, here, :], in_sems.at[k, b])

    for k in order:
        for b in range(blocks):
            read(k, b).start()
    lane = lax.broadcasted_iota(jnp.int32, (tall - rows, step), 1)
    named = jnp.zeros((tall - rows, step), jnp.float32)
    for b in range(blocks):
        named = jnp.where(lane == b, ids[b].astype(jnp.float32), named)
    named = named.astype(held.dtype)
    writes = [pltpu.make_async_copy(held.at[k], outs[k], out_sems.at[k]) for k in range(shares)]
    for k in order:
        held[k, rows:, :] = named
        for b in range(blocks):
            read(k, b).wait()

            @pl.when(lengths[b] < block)
            def _():
                here = slice(b * block, (b + 1) * block)
                row = lax.broadcasted_iota(jnp.int32, (block, step), 0)
                part = held[k, here, :]
                held[k, here, :] = jnp.where(row < lengths[b], part, jnp.zeros_like(part))

        writes[k].start()
    for write in writes:
        write.wait()


def spread(tokens, lengths, ids, groups, pair):
    rows, feats = tokens.shape
    shares = groups * pair
    shape = (rows + 16, feats // shares)
    return pl.pallas_call(
        functools.partial(spread_kernel, groups, pair),
        in_specs=[SMEM, SMEM, ANY],
        out_specs=[ANY] * shares,
        out_shape=[jax.ShapeDtypeStruct(shape, tokens.dtype)] * shares,
        scratch_shapes=[
            pltpu.VMEM((shares,) + shape, tokens.dtype),
            pltpu.SemaphoreType.DMA((shares, lengths.shape[0])),
            pltpu.SemaphoreType.DMA((shares,)),
        ],
        compiler_params=FULL,
        name="spread",
    )(lengths, ids, tokens)


def base_kernel(sides, lengths, tok_ref, key_ref, mine, other, flag_ref, total):
    step = pl.program_id(0)
    part = jnp.dot(tok_ref[...], key_ref[...], preferred_element_type=jnp.float32)

    @pl.when(step == 0)
    def _():
        total[...] = part

    @pl.when(step > 0)
    def _():
        total[...] += part

    @pl.when(step == pl.num_programs(0) - 1)
    def _():
        flag_ref[...] = jnp.zeros_like(flag_ref)
        blocks = lengths.shape[0]
        rows, wide = mine.shape
        block = rows // blocks
        row = lax.broadcasted_iota(jnp.int32, (block, wide), 0)
        t = lax.axis_index("tensor")
        for out, side in ((mine, t), (other, lax.rem(t + 1, sides))):
            columns = pl.ds(pl.multiple_of(side * wide, LANES), wide)
            for b in range(blocks):
                here = slice(b * block, (b + 1) * block)
                out[here, :] = jnp.where(row < lengths[b], total[here, columns], 0.0)


def base_halves(tokens, base_key, sides, lengths):
    rows, depth = tokens.shape
    features = base_key.shape[1]
    wide = features // sides
    step = 512
    half = pl.BlockSpec((rows, wide), lambda i, n: (0, 0))
    return pl.pallas_call(
        functools.partial(base_kernel, sides),
        grid_spec=pltpu.PrefetchScalarGridSpec(
            num_scalar_prefetch=1,
            grid=(depth // step,),
            in_specs=[
                pl.BlockSpec((rows, step), lambda i, n: (0, i)),
                pl.BlockSpec((step, features), lambda i, n: (i, 0)),
            ],
            out_specs=[half, half, pl.BlockSpec((8, LANES), lambda i, n: (0, 0))],
            scratch_shapes=[pltpu.VMEM((rows, features), jnp.float32)],
        ),
        out_shape=[jax.ShapeDtypeStruct((rows, wide), jnp.float32)] * 2
        + [jax.ShapeDtypeStruct((8, LANES), jnp.float32)],
        cost_estimate=pl.CostEstimate(flops=0, bytes_accessed=0, transcendentals=0),
        compiler_params=FULL,
        name="base",
    )(lengths, tokens, base_key)


def collect_kernel(*refs):
    sems, held, pieces = refs[-1], refs[-2], refs[:-2]
    copies, start = [], 0
    for j, piece in enumerate(pieces):
        copies.append(pltpu.make_async_copy(piece, held.at[pl.ds(start, piece.shape[0])], sems.at[j]))
        start += piece.shape[0]
    for copy in copies:
        copy.start()
    for copy in copies:
        copy.wait()


def collect(pieces):
    count = sum(piece.shape[0] for piece in pieces)
    return pl.pallas_call(
        collect_kernel,
        in_specs=[ANY] * len(pieces),
        out_specs=VMEM,
        out_shape=jax.ShapeDtypeStruct((count,) + pieces[0].shape[1:], pieces[0].dtype),
        scratch_shapes=[pltpu.SemaphoreType.DMA((len(pieces),))],
        cost_estimate=pl.CostEstimate(flops=0, bytes_accessed=0, transcendentals=0),
        compiler_params=ROOM,
        name="collect",
    )(*pieces)


def rank_kernel(ring, pair, rows, owner, held, *refs):
    shares = len(refs) // 2
    toks, outs = refs[:shares], refs[shares:]
    per, rank = held.shape[0] // (ring * pair), held.shape[1]
    blocks, _, block = outs[0].shape
    feats = toks[0].shape[1]
    z, y = lax.axis_index("ring"), lax.axis_index("pair")
    lane = lax.broadcasted_iota(jnp.int32, (16, LANES), 1)
    row = lax.broadcasted_iota(jnp.int32, (16, LANES), 0)
    ids = []
    for tok in toks:
        named = tok[rows:, :LANES].astype(jnp.float32)
        ids += [jnp.sum(jnp.where((lane == b) & (row == 0), named, 0.0)).astype(jnp.int32) for b in range(blocks)]
    for k, tok in enumerate(toks):
        for b in range(blocks):
            slot = owner[ids[k * blocks + b]]
            chip = slot // per
            away = lax.rem(chip // pair - z + ring, ring)
            way = lax.rem(lax.rem(chip, pair) - y + pair, pair)
            at = (way * ring + away) * per + lax.rem(slot, per)
            part = lax.dot_general(
                held[at, :, :feats],
                tok[b * block : (b + 1) * block, :],
                (((1,), (1,)), ((), ())),
                preferred_element_type=jnp.float32,
            )
            outs[k][b, :rank, :] = part.astype(outs[k].dtype)
            outs[k][b, rank:, :] = held[at, :, feats:]


def rank_parts(owner, toks, held, ring, pair, rows, blocks):
    shares, rank = len(toks), held.shape[1]
    return pl.pallas_call(
        functools.partial(rank_kernel, ring, pair, rows),
        in_specs=[SMEM, VMEM] + [VMEM] * shares,
        out_specs=[VMEM] * shares,
        out_shape=[jax.ShapeDtypeStruct((blocks, 2 * rank, rows // blocks), held.dtype)] * shares,
        cost_estimate=pl.CostEstimate(flops=0, bytes_accessed=0, transcendentals=0),
        compiler_params=ROOM,
        name="rank",
    )(owner, held, *toks)


def final_kernel(groups, pair, base_a, base_b, *refs):
    shares = groups * pair
    mine, theirs, out_ref, up = refs[:shares], refs[shares : 2 * shares], refs[-2], refs[-1]
    blocks, tall, block = mine[0].shape
    rank = tall // 2
    tiles = out_ref.shape[1] // LANES
    for b in range(blocks):
        here = slice(b * block, (b + 1) * block)
        total = mine[0][b, :rank, :].astype(jnp.float32)
        for part in mine[1:] + theirs:
            total += part[b, :rank, :].astype(jnp.float32)
        for k in range(shares):
            tile = lax.rem(mate_at(k, 1, groups, pair), tiles)
            up[b, :, pl.ds(pl.multiple_of(tile * LANES, LANES), LANES)] = mine[k][b, rank:, :]
        delta = lax.dot_general(
            total.astype(jnp.bfloat16), up[b], (((0,), (0,)), ((), ())), preferred_element_type=jnp.float32
        )
        out_ref[here, :] = (base_a[here, :] + base_b[here, :] + delta).astype(out_ref.dtype)


def final(mine, theirs, base, groups, pair, dtype):
    blocks, tall, _ = mine[0].shape
    return pl.pallas_call(
        functools.partial(final_kernel, groups, pair),
        in_specs=[VMEM] * (2 + 2 * len(mine)),
        out_specs=VMEM,
        out_shape=jax.ShapeDtypeStruct(base[0].shape, dtype),
        scratch_shapes=[pltpu.VMEM((blocks, tall // 2, base[0].shape[1]), mine[0].dtype)],
        compiler_params=ROOM,
        name="final",
    )(*base, *mine, *theirs)


def body(tokens, base_key, adapter_down, adapter_up, adapter_ids, owner_slot, lengths):
    groups, ring, pair = lax.axis_size("groups"), lax.axis_size("ring"), lax.axis_size("pair")
    sides = lax.axis_size("tensor")
    shares = groups * pair
    rows = tokens.shape[0]
    blocks = lengths.shape[0]

    def across(x):
        return lax.ppermute(x, "tensor", [(i, (i + 1) % sides) for i in range(sides)])

    def along(x, step):
        return lax.ppermute(x, "ring", [(a, (a + step) % ring) for a in range(ring)])

    def first_hops(x):
        return {0: x, ring - 1: along(x, 1), **({1: along(x, -1)} if ring > 2 else {})}

    def in_plane(x, kg, ky):
        pairs = []
        for a in range(groups):
            for b in range(pair):
                pairs.append((a * pair + b, (a + kg) % groups * pair + (b + ky) % pair))
        return lax.ppermute(x, PLANE, pairs)

    def more_hops(held, way, *after):
        for k in range(2, ring // 2 + 1):
            if 2 * k < ring or way % 2 == 0:
                if k == 2:
                    held[ring - 1] = hand_on(held[ring - 1], held[1], *after)
                held[ring - k] = along(held[ring - k + 1], 1)
            if 2 * k < ring or way % 2 == 1:
                if k == 2:
                    held[1] = hand_on(held[1], held[ring - 1], *after)
                held[k] = along(held[k - 1], -1)
        return [held[k] for k in range(ring)]

    packed = pack(jnp.swapaxes(adapter_down, 1, 2), adapter_up, shares, pair)
    slabs = spread(tokens, lengths, adapter_ids.reshape(-1), groups, pair)
    swapped = [
        lax.ppermute(packed[pair - w], "pair", [(a, (a - w) % pair) for a in range(pair)]) for w in range(1, pair)
    ]
    firsts = [first_hops(piece) for piece in [packed[0]] + swapped]
    toks = [slabs[0]] + [in_plane(slabs[k], k // pair, k % pair) for k in range(1, shares)]

    base_mine, base_out, flag = base_halves(tokens, base_key, sides, lengths)
    pieces = [
        more_hops(held, way, flag)
        for way, held in enumerate(firsts)
    ]

    flat = [piece for way in pieces for piece in way]
    parts = rank_parts(owner_slot, toks, collect(flat), ring, pair, rows, blocks)
    mine, theirs = [parts[0]] * shares, [None] * shares
    for k in reversed(range(1, shares)):
        mine[k] = in_plane(parts[k], -(k // pair), -(k % pair))
    for k in reversed(range(shares)):
        theirs[k] = across(mine[k])
    base_in = across(hand_on(base_out, pieces[-1][1]))
    return final(mine, theirs, [base_mine, base_in], groups, pair, tokens.dtype)


def solution(mesh):
    groups, dp, sides = (mesh.shape[name] for name in ("groups", "dp", "tensor"))
    pair = 2 if dp % 2 == 0 else 1
    cut = Mesh(mesh.devices.reshape(groups, dp // pair, pair, sides), ("groups", "ring", "pair", "tensor"))
    stored = ("ring", "pair")
    placed = (
        P(WHOLE, "tensor"),
        P("tensor", None),
        P(stored, "tensor", None),
        P(stored, None, "tensor"),
        P(WHOLE, None),
        P(),
        P(WHOLE),
    )
    return jax.shard_map(body, mesh=cut, in_specs=placed, out_specs=P(WHOLE, "tensor"), check_vma=False)
```

```python
import functools

import jax
import jax.numpy as jnp
from jax import lax
from jax.experimental import pallas as pl
from jax.experimental.pallas import tpu as pltpu
from jax.sharding import Mesh
from jax.sharding import PartitionSpec as P

LANES = 128
ANY = pl.BlockSpec(memory_space=pl.ANY)
SMEM = pl.BlockSpec(memory_space=pltpu.SMEM)
VMEM = pl.BlockSpec(memory_space=pltpu.VMEM)
HBM = pl.BlockSpec(memory_space=pltpu.HBM)
ROOM = pltpu.CompilerParams(vmem_limit_bytes=32 * 1024 * 1024)
FULL = pltpu.CompilerParams(vmem_limit_bytes=60 * 1024 * 1024)
PLANE = ("groups", "pair")
WHOLE = ("groups", "ring", "pair")


def hand_kernel(*refs):
    pass


def hand_on(x, *after):
    return pl.pallas_call(
        hand_kernel,
        in_specs=[ANY] * (1 + len(after)),
        out_specs=ANY,
        out_shape=jax.ShapeDtypeStruct(x.shape, x.dtype),
        input_output_aliases={0: 0},
        compiler_params=FULL,
        name="hand",
    )(x, *after)


def pack_kernel(down, up, *refs):
    outs, sems = refs[:-1], refs[-1]
    feats = outs[0].shape[2] - LANES
    copies = []
    for way, out in enumerate(outs):
        share = lax.axis_index("groups") * len(outs) + lax.rem(lax.axis_index("pair") + way, len(outs))
        start = pl.multiple_of(share * feats, LANES)
        tile = pl.multiple_of(lax.rem(share, up.shape[2] // LANES) * LANES, LANES)
        copies.append(pltpu.make_async_copy(down.at[:, :, pl.ds(start, feats)], out.at[:, :, :feats], sems.at[way, 0]))
        copies.append(pltpu.make_async_copy(up.at[:, :, pl.ds(tile, LANES)], out.at[:, :, feats:], sems.at[way, 1]))
    for copy in copies:
        copy.start()
    for copy in copies:
        copy.wait()


def pack(down, up, shares, ways):
    adapters, rank, feats = down.shape
    shape = jax.ShapeDtypeStruct((adapters, rank, feats // shares + LANES), down.dtype)
    return pl.pallas_call(
        pack_kernel,
        in_specs=[HBM, HBM],
        out_specs=[VMEM] * ways,
        out_shape=[shape] * ways,
        scratch_shapes=[pltpu.SemaphoreType.DMA((ways, 2))],
        compiler_params=FULL,
        name="pack",
    )(down, up)


def mate_at(k, sign, groups, pair):
    kg, ky = k // pair, k % pair
    g = lax.rem(lax.axis_index("groups") + sign * kg + groups, groups)
    y = lax.rem(lax.axis_index("pair") + sign * ky + pair, pair)
    return g * pair + y


def spread_kernel(groups, pair, lengths, ids, tok, *refs):
    held, in_sems, out_sems = refs[-3:]
    outs = refs[:-3]
    blocks = lengths.shape[0]
    shares, tall, step = held.shape
    rows = tok.shape[0]
    block = rows // blocks
    mates = [pl.multiple_of(mate_at(k, 1, groups, pair) * step, LANES) for k in range(shares)]
    order = list(range(1, shares)) + [0]

    def read(k, b):
        here = pl.ds(b * block, block)
        return pltpu.make_async_copy(tok.at[here, pl.ds(mates[k], step)], held.at[k, here, :], in_sems.at[k, b])

    for k in order:
        for b in range(blocks):
            read(k, b).start()
    lane = lax.broadcasted_iota(jnp.int32, (tall - rows, step), 1)
    named = jnp.zeros((tall - rows, step), jnp.float32)
    for b in range(blocks):
        named = jnp.where(lane == b, ids[b].astype(jnp.float32), named)
    named = named.astype(held.dtype)
    writes = [pltpu.make_async_copy(held.at[k], outs[k], out_sems.at[k]) for k in range(shares)]
    for k in order:
        held[k, rows:, :] = named
        for b in range(blocks):
            read(k, b).wait()

            @pl.when(lengths[b] < block)
            def _():
                here = slice(b * block, (b + 1) * block)
                row = lax.broadcasted_iota(jnp.int32, (block, step), 0)
                part = held[k, here, :]
                held[k, here, :] = jnp.where(row < lengths[b], part, jnp.zeros_like(part))

        writes[k].start()
    for write in writes:
        write.wait()


def spread(tokens, lengths, ids, groups, pair):
    rows, feats = tokens.shape
    shares = groups * pair
    shape = (rows + 16, feats // shares)
    return pl.pallas_call(
        functools.partial(spread_kernel, groups, pair),
        in_specs=[SMEM, SMEM, ANY],
        out_specs=[ANY] * shares,
        out_shape=[jax.ShapeDtypeStruct(shape, tokens.dtype)] * shares,
        scratch_shapes=[
            pltpu.VMEM((shares,) + shape, tokens.dtype),
            pltpu.SemaphoreType.DMA((shares, lengths.shape[0])),
            pltpu.SemaphoreType.DMA((shares,)),
        ],
        compiler_params=FULL,
        name="spread",
    )(lengths, ids, tokens)


def base_kernel(sides, lengths, tok_ref, key_ref, mine, other, flag_ref, total):
    step = pl.program_id(0)
    part = jnp.dot(tok_ref[...], key_ref[...], preferred_element_type=jnp.float32)

    @pl.when(step == 0)
    def _():
        total[...] = part

    @pl.when(step > 0)
    def _():
        total[...] += part

    @pl.when(step == pl.num_programs(0) - 1)
    def _():
        flag_ref[...] = jnp.zeros_like(flag_ref)
        blocks = lengths.shape[0]
        rows, wide = mine.shape
        block = rows // blocks
        row = lax.broadcasted_iota(jnp.int32, (block, wide), 0)
        t = lax.axis_index("tensor")
        for out, side in ((mine, t), (other, lax.rem(t + 1, sides))):
            columns = pl.ds(pl.multiple_of(side * wide, LANES), wide)
            for b in range(blocks):
                here = slice(b * block, (b + 1) * block)
                out[here, :] = jnp.where(row < lengths[b], total[here, columns], 0.0)


def base_halves(tokens, base_key, sides, lengths):
    rows, depth = tokens.shape
    features = base_key.shape[1]
    wide = features // sides
    step = 512
    half = pl.BlockSpec((rows, wide), lambda i, n: (0, 0))
    return pl.pallas_call(
        functools.partial(base_kernel, sides),
        grid_spec=pltpu.PrefetchScalarGridSpec(
            num_scalar_prefetch=1,
            grid=(depth // step,),
            in_specs=[
                pl.BlockSpec((rows, step), lambda i, n: (0, i)),
                pl.BlockSpec((step, features), lambda i, n: (i, 0)),
            ],
            out_specs=[half, half, pl.BlockSpec((8, LANES), lambda i, n: (0, 0))],
            scratch_shapes=[pltpu.VMEM((rows, features), jnp.float32)],
        ),
        out_shape=[jax.ShapeDtypeStruct((rows, wide), jnp.float32)] * 2
        + [jax.ShapeDtypeStruct((8, LANES), jnp.float32)],
        cost_estimate=pl.CostEstimate(flops=0, bytes_accessed=0, transcendentals=0),
        compiler_params=FULL,
        name="base",
    )(lengths, tokens, base_key)


def collect_kernel(*refs):
    sems, flag, held, pieces = refs[-1], refs[-2], refs[-3], refs[:-3]
    flag[...] = jnp.zeros_like(flag)
    copies, start = [], 0
    for j, piece in enumerate(pieces):
        copies.append(pltpu.make_async_copy(piece, held.at[pl.ds(start, piece.shape[0])], sems.at[j]))
        start += piece.shape[0]
    for copy in copies:
        copy.start()
    for copy in copies:
        copy.wait()


def collect(pieces):
    count = sum(piece.shape[0] for piece in pieces)
    return pl.pallas_call(
        collect_kernel,
        in_specs=[ANY] * len(pieces),
        out_specs=[VMEM] * 2,
        out_shape=[
            jax.ShapeDtypeStruct((count,) + pieces[0].shape[1:], pieces[0].dtype),
            jax.ShapeDtypeStruct((8, LANES), jnp.float32),
        ],
        scratch_shapes=[pltpu.SemaphoreType.DMA((len(pieces),))],
        compiler_params=ROOM,
        name="collect",
    )(*pieces)


def rank_kernel(ring, pair, rows, shares, owner, held, *refs):
    late, toks, outs, picked = refs[: -1 - 2 * shares], refs[-1 - 2 * shares : -1 - shares], refs[-1 - shares : -1], refs[-1]
    rank = held.shape[1]
    per = owner.shape[0] // (ring * pair)
    blocks, _, block = outs[0].shape
    feats = toks[0].shape[1]
    z, y = lax.axis_index("ring"), lax.axis_index("pair")
    lane = lax.broadcasted_iota(jnp.int32, (16, LANES), 1)
    row = lax.broadcasted_iota(jnp.int32, (16, LANES), 0)
    ids = []
    for tok in toks:
        named = tok[rows:, :LANES].astype(jnp.float32)
        ids += [jnp.sum(jnp.where((lane == b) & (row == 0), named, 0.0)).astype(jnp.int32) for b in range(blocks)]
    for i, one in enumerate(ids):
        slot = owner[one]
        chip = slot // per
        local = lax.rem(slot, per)
        away = lax.rem(chip // pair - z + ring, ring)
        way = lax.rem(lax.rem(chip, pair) - y + pair, pair)
        if late:
            half = ring // 2
            near = away - jnp.where(away > half, 1, 0)

            @pl.when(away != half)
            def _():
                picked[i] = held[(way * (ring - 1) + near) * per + local]

            for w in range(pair):

                @pl.when((away == half) & (way == w))
                def _():
                    picked[i] = late[w][local]

        else:
            picked[i] = held[(way * ring + away) * per + local]
    for k, tok in enumerate(toks):
        for b in range(blocks):
            i = k * blocks + b
            part = lax.dot_general(
                picked[i, :, :feats],
                tok[b * block : (b + 1) * block, :],
                (((1,), (1,)), ((), ())),
                preferred_element_type=jnp.float32,
            )
            outs[k][b, :rank, :] = part.astype(outs[k].dtype)
            outs[k][b, rank:, :] = picked[i, :, feats:]


def rank_parts(owner, toks, held, late, ring, pair, rows, blocks):
    shares, rank = len(toks), held.shape[1]
    return pl.pallas_call(
        functools.partial(rank_kernel, ring, pair, rows, shares),
        in_specs=[SMEM, VMEM] + [VMEM] * (len(late) + shares),
        out_specs=[VMEM] * shares,
        out_shape=[jax.ShapeDtypeStruct((blocks, 2 * rank, rows // blocks), held.dtype)] * shares,
        scratch_shapes=[pltpu.VMEM((shares * blocks,) + held.shape[1:], held.dtype)],
        cost_estimate=pl.CostEstimate(flops=0, bytes_accessed=0, transcendentals=0),
        compiler_params=ROOM,
        name="rank",
    )(owner, held, *late, *toks)


def final_kernel(groups, pair, base_a, base_b, *refs):
    shares = groups * pair
    mine, theirs, out_ref, up = refs[:shares], refs[shares : 2 * shares], refs[-2], refs[-1]
    blocks, tall, block = mine[0].shape
    rank = tall // 2
    tiles = out_ref.shape[1] // LANES
    for b in range(blocks):
        here = slice(b * block, (b + 1) * block)
        total = mine[0][b, :rank, :].astype(jnp.float32)
        for part in mine[1:] + theirs:
            total += part[b, :rank, :].astype(jnp.float32)
        for k in range(shares):
            tile = lax.rem(mate_at(k, 1, groups, pair), tiles)
            up[b, :, pl.ds(pl.multiple_of(tile * LANES, LANES), LANES)] = mine[k][b, rank:, :]
        delta = lax.dot_general(
            total.astype(jnp.bfloat16), up[b], (((0,), (0,)), ((), ())), preferred_element_type=jnp.float32
        )
        out_ref[here, :] = (base_a[here, :] + base_b[here, :] + delta).astype(out_ref.dtype)


def final(mine, theirs, base, groups, pair, dtype):
    blocks, tall, _ = mine[0].shape
    return pl.pallas_call(
        functools.partial(final_kernel, groups, pair),
        in_specs=[VMEM] * (2 + 2 * len(mine)),
        out_specs=VMEM,
        out_shape=jax.ShapeDtypeStruct(base[0].shape, dtype),
        scratch_shapes=[pltpu.VMEM((blocks, tall // 2, base[0].shape[1]), mine[0].dtype)],
        compiler_params=ROOM,
        name="final",
    )(*base, *mine, *theirs)


def body(tokens, base_key, adapter_down, adapter_up, adapter_ids, owner_slot, lengths):
    groups, ring, pair = lax.axis_size("groups"), lax.axis_size("ring"), lax.axis_size("pair")
    sides = lax.axis_size("tensor")
    shares = groups * pair
    rows = tokens.shape[0]
    blocks = lengths.shape[0]

    def across(x):
        return lax.ppermute(x, "tensor", [(i, (i + 1) % sides) for i in range(sides)])

    def along(x, step):
        return lax.ppermute(x, "ring", [(a, (a + step) % ring) for a in range(ring)])

    def first_hops(x):
        return {0: x, ring - 1: along(x, 1), **({1: along(x, -1)} if ring > 2 else {})}

    def in_plane(x, kg, ky):
        pairs = []
        for a in range(groups):
            for b in range(pair):
                pairs.append((a * pair + b, (a + kg) % groups * pair + (b + ky) % pair))
        return lax.ppermute(x, PLANE, pairs)

    def more_hops(held, way, *after):
        for k in range(2, ring // 2 + 1):
            if 2 * k < ring or way % 2 == 0:
                if k == 2:
                    held[ring - 1] = hand_on(held[ring - 1], held[1], *after)
                held[ring - k] = along(held[ring - k + 1], 1)
            if 2 * k < ring or way % 2 == 1:
                if k == 2:
                    held[1] = hand_on(held[1], held[ring - 1], *after)
                held[k] = along(held[k - 1], -1)
        return [held[k] for k in range(ring)]

    packed = pack(jnp.swapaxes(adapter_down, 1, 2), adapter_up, shares, pair)
    slabs = spread(tokens, lengths, adapter_ids.reshape(-1), groups, pair)
    swapped = [
        lax.ppermute(packed[pair - w], "pair", [(a, (a - w) % pair) for a in range(pair)]) for w in range(1, pair)
    ]
    firsts = [first_hops(piece) for piece in [packed[0]] + swapped]
    toks = [slabs[0]] + [in_plane(slabs[k], k // pair, k % pair) for k in range(1, shares)]

    base_mine, base_out, flag = base_halves(tokens, base_key, sides, lengths)
    pieces = [
        more_hops(held, way, flag)
        for way, held in enumerate(firsts)
    ]

    halfway = ring // 2 if ring % 2 == 0 else ring
    held, ready = collect([piece for way in pieces for away, piece in enumerate(way) if away != halfway])
    late = [way[halfway] for way in pieces] if halfway < ring else []
    parts = rank_parts(owner_slot, toks, held, late, ring, pair, rows, blocks)
    mine = [parts[0]] + [in_plane(parts[k], -(k // pair), -(k % pair)) for k in range(1, shares)]
    theirs = [across(part) for part in mine]
    base_in = across(hand_on(base_out, ready))
    return final(mine, theirs, [base_mine, base_in], groups, pair, tokens.dtype)


def solution(mesh):
    groups, dp, sides = (mesh.shape[name] for name in ("groups", "dp", "tensor"))
    pair = 2 if dp % 2 == 0 else 1
    cut = Mesh(mesh.devices.reshape(groups, dp // pair, pair, sides), ("groups", "ring", "pair", "tensor"))
    stored = ("ring", "pair")
    placed = (
        P(WHOLE, "tensor"),
        P("tensor", None),
        P(stored, "tensor", None),
        P(stored, None, "tensor"),
        P(WHOLE, None),
        P(),
        P(WHOLE),
    )
    return jax.shard_map(body, mesh=cut, in_specs=placed, out_specs=P(WHOLE, "tensor"), check_vma=False)
```

```python
import functools

import jax
import jax.numpy as jnp
from jax import lax
from jax.experimental import pallas as pl
from jax.experimental.pallas import tpu as pltpu
from jax.sharding import Mesh
from jax.sharding import PartitionSpec as P

LANES = 128
ANY = pl.BlockSpec(memory_space=pl.ANY)
SMEM = pl.BlockSpec(memory_space=pltpu.SMEM)
VMEM = pl.BlockSpec(memory_space=pltpu.VMEM)
HBM = pl.BlockSpec(memory_space=pltpu.HBM)
ROOM = pltpu.CompilerParams(vmem_limit_bytes=32 * 1024 * 1024)
FULL = pltpu.CompilerParams(vmem_limit_bytes=60 * 1024 * 1024)
PLANE = ("groups", "pair")
WHOLE = ("groups", "ring", "pair")


def hand_kernel(*refs):
    pass


def hand_on(x, *after):
    return pl.pallas_call(
        hand_kernel,
        in_specs=[ANY] * (1 + len(after)),
        out_specs=ANY,
        out_shape=jax.ShapeDtypeStruct(x.shape, x.dtype),
        input_output_aliases={0: 0},
        compiler_params=FULL,
        name="hand",
    )(x, *after)


def pack_kernel(down, up, *refs):
    outs, sems = refs[:-1], refs[-1]
    feats = outs[0].shape[2] - LANES
    copies = []
    for way, out in enumerate(outs):
        share = lax.axis_index("groups") * len(outs) + lax.rem(lax.axis_index("pair") + way, len(outs))
        start = pl.multiple_of(share * feats, LANES)
        tile = pl.multiple_of(lax.rem(share, up.shape[2] // LANES) * LANES, LANES)
        copies.append(pltpu.make_async_copy(down.at[:, :, pl.ds(start, feats)], out.at[:, :, :feats], sems.at[way, 0]))
        copies.append(pltpu.make_async_copy(up.at[:, :, pl.ds(tile, LANES)], out.at[:, :, feats:], sems.at[way, 1]))
    for copy in copies:
        copy.start()
    for copy in copies:
        copy.wait()


def pack(down, up, shares, ways):
    adapters, rank, feats = down.shape
    shape = jax.ShapeDtypeStruct((adapters, rank, feats // shares + LANES), down.dtype)
    return pl.pallas_call(
        pack_kernel,
        in_specs=[HBM, HBM],
        out_specs=[VMEM] * ways,
        out_shape=[shape] * ways,
        scratch_shapes=[pltpu.SemaphoreType.DMA((ways, 2))],
        compiler_params=FULL,
        name="pack",
    )(down, up)


def mate_at(k, sign, groups, pair):
    kg, ky = k // pair, k % pair
    g = lax.rem(lax.axis_index("groups") + sign * kg + groups, groups)
    y = lax.rem(lax.axis_index("pair") + sign * ky + pair, pair)
    return g * pair + y


def spread_kernel(groups, pair, lengths, ids, tok, *refs):
    held, in_sems, out_sems = refs[-3:]
    outs = refs[:-3]
    blocks = lengths.shape[0]
    shares, tall, step = held.shape
    rows = tok.shape[0]
    block = rows // blocks
    mates = [pl.multiple_of(mate_at(k, 1, groups, pair) * step, LANES) for k in range(shares)]
    order = list(range(1, shares)) + [0]

    def read(k, b):
        here = pl.ds(b * block, block)
        return pltpu.make_async_copy(tok.at[here, pl.ds(mates[k], step)], held.at[k, here, :], in_sems.at[k, b])

    for k in order:
        for b in range(blocks):
            read(k, b).start()
    lane = lax.broadcasted_iota(jnp.int32, (tall - rows, step), 1)
    named = jnp.zeros((tall - rows, step), jnp.float32)
    for b in range(blocks):
        named = jnp.where(lane == b, ids[b].astype(jnp.float32), named)
    named = named.astype(held.dtype)
    writes = [pltpu.make_async_copy(held.at[k], outs[k], out_sems.at[k]) for k in range(shares)]
    for k in order:
        held[k, rows:, :] = named
        for b in range(blocks):
            read(k, b).wait()

            @pl.when(lengths[b] < block)
            def _():
                here = slice(b * block, (b + 1) * block)
                row = lax.broadcasted_iota(jnp.int32, (block, step), 0)
                part = held[k, here, :]
                held[k, here, :] = jnp.where(row < lengths[b], part, jnp.zeros_like(part))

        writes[k].start()
    for write in writes:
        write.wait()


def spread(tokens, lengths, ids, groups, pair):
    rows, feats = tokens.shape
    shares = groups * pair
    shape = (rows + 16, feats // shares)
    return pl.pallas_call(
        functools.partial(spread_kernel, groups, pair),
        in_specs=[SMEM, SMEM, ANY],
        out_specs=[ANY] * shares,
        out_shape=[jax.ShapeDtypeStruct(shape, tokens.dtype)] * shares,
        scratch_shapes=[
            pltpu.VMEM((shares,) + shape, tokens.dtype),
            pltpu.SemaphoreType.DMA((shares, lengths.shape[0])),
            pltpu.SemaphoreType.DMA((shares,)),
        ],
        compiler_params=FULL,
        name="spread",
    )(lengths, ids, tokens)


def base_kernel(sides, lengths, tok_ref, key_ref, mine, other, flag_ref, total):
    step = pl.program_id(0)
    part = jnp.dot(tok_ref[...], key_ref[...], preferred_element_type=jnp.float32)

    @pl.when(step == 0)
    def _():
        total[...] = part

    @pl.when(step > 0)
    def _():
        total[...] += part

    @pl.when(step == pl.num_programs(0) - 1)
    def _():
        flag_ref[...] = jnp.zeros_like(flag_ref)
        blocks = lengths.shape[0]
        rows, wide = mine.shape
        block = rows // blocks
        row = lax.broadcasted_iota(jnp.int32, (block, wide), 0)
        t = lax.axis_index("tensor")
        for out, side in ((mine, t), (other, lax.rem(t + 1, sides))):
            columns = pl.ds(pl.multiple_of(side * wide, LANES), wide)
            for b in range(blocks):
                here = slice(b * block, (b + 1) * block)
                out[here, :] = jnp.where(row < lengths[b], total[here, columns], 0.0)


def base_halves(tokens, base_key, sides, lengths):
    rows, depth = tokens.shape
    features = base_key.shape[1]
    wide = features // sides
    step = 512
    half = pl.BlockSpec((rows, wide), lambda i, n: (0, 0))
    return pl.pallas_call(
        functools.partial(base_kernel, sides),
        grid_spec=pltpu.PrefetchScalarGridSpec(
            num_scalar_prefetch=1,
            grid=(depth // step,),
            in_specs=[
                pl.BlockSpec((rows, step), lambda i, n: (0, i)),
                pl.BlockSpec((step, features), lambda i, n: (i, 0)),
            ],
            out_specs=[half, half, pl.BlockSpec((8, LANES), lambda i, n: (0, 0))],
            scratch_shapes=[pltpu.VMEM((rows, features), jnp.float32)],
        ),
        out_shape=[jax.ShapeDtypeStruct((rows, wide), jnp.float32)] * 2
        + [jax.ShapeDtypeStruct((8, LANES), jnp.float32)],
        cost_estimate=pl.CostEstimate(flops=0, bytes_accessed=0, transcendentals=0),
        compiler_params=FULL,
        name="base",
    )(lengths, tokens, base_key)


def collect_kernel(*refs):
    sems, held, pieces = refs[-1], refs[-2], refs[:-2]
    copies, start = [], 0
    for j, piece in enumerate(pieces):
        copies.append(pltpu.make_async_copy(piece, held.at[pl.ds(start, piece.shape[0])], sems.at[j]))
        start += piece.shape[0]
    for copy in copies:
        copy.start()
    for copy in copies:
        copy.wait()


def collect(pieces):
    count = sum(piece.shape[0] for piece in pieces)
    return pl.pallas_call(
        collect_kernel,
        in_specs=[ANY] * len(pieces),
        out_specs=VMEM,
        out_shape=jax.ShapeDtypeStruct((count,) + pieces[0].shape[1:], pieces[0].dtype),
        scratch_shapes=[pltpu.SemaphoreType.DMA((len(pieces),))],
        compiler_params=ROOM,
        name="collect",
    )(*pieces)


def rank_kernel(ring, pair, rows, owner, flag, held, *refs):
    shares = len(refs) // 2
    toks, outs = refs[:shares], refs[shares:]
    per, rank = held.shape[0] // (ring * pair), held.shape[1]
    blocks, _, block = outs[0].shape
    feats = toks[0].shape[1]
    z, y = lax.axis_index("ring"), lax.axis_index("pair")
    lane = lax.broadcasted_iota(jnp.int32, (16, LANES), 1)
    row = lax.broadcasted_iota(jnp.int32, (16, LANES), 0)
    ids = []
    for tok in toks:
        named = tok[rows:, :LANES].astype(jnp.float32)
        ids += [jnp.sum(jnp.where((lane == b) & (row == 0), named, 0.0)).astype(jnp.int32) for b in range(blocks)]
    for k, tok in enumerate(toks):
        for b in range(blocks):
            slot = owner[ids[k * blocks + b]]
            chip = slot // per
            away = lax.rem(chip // pair - z + ring, ring)
            way = lax.rem(lax.rem(chip, pair) - y + pair, pair)
            at = (way * ring + away) * per + lax.rem(slot, per)
            part = lax.dot_general(
                held[at, :, :feats],
                tok[b * block : (b + 1) * block, :],
                (((1,), (1,)), ((), ())),
                preferred_element_type=jnp.float32,
            )
            outs[k][b, :rank, :] = part.astype(outs[k].dtype)
            outs[k][b, rank:, :] = held[at, :, feats:]


def rank_parts(owner, flag, toks, held, ring, pair, rows, blocks):
    shares, rank = len(toks), held.shape[1]
    return pl.pallas_call(
        functools.partial(rank_kernel, ring, pair, rows),
        in_specs=[SMEM, ANY, VMEM] + [VMEM] * shares,
        out_specs=[VMEM] * shares,
        out_shape=[jax.ShapeDtypeStruct((blocks, 2 * rank, rows // blocks), held.dtype)] * shares,
        cost_estimate=pl.CostEstimate(flops=0, bytes_accessed=0, transcendentals=0),
        compiler_params=ROOM,
        name="rank",
    )(owner, flag, held, *toks)


def final_kernel(groups, pair, base_a, base_b, *refs):
    shares = groups * pair
    mine, theirs, out_ref, up = refs[:shares], refs[shares : 2 * shares], refs[-2], refs[-1]
    blocks, tall, block = mine[0].shape
    rank = tall // 2
    tiles = out_ref.shape[1] // LANES
    for b in range(blocks):
        here = slice(b * block, (b + 1) * block)
        total = mine[0][b, :rank, :].astype(jnp.float32)
        for part in mine[1:] + theirs:
            total += part[b, :rank, :].astype(jnp.float32)
        for k in range(shares):
            tile = lax.rem(mate_at(k, 1, groups, pair), tiles)
            up[b, :, pl.ds(pl.multiple_of(tile * LANES, LANES), LANES)] = mine[k][b, rank:, :]
        delta = lax.dot_general(
            total.astype(jnp.bfloat16), up[b], (((0,), (0,)), ((), ())), preferred_element_type=jnp.float32
        )
        out_ref[here, :] = (base_a[here, :] + base_b[here, :] + delta).astype(out_ref.dtype)


def final(mine, theirs, base, groups, pair, dtype):
    blocks, tall, _ = mine[0].shape
    return pl.pallas_call(
        functools.partial(final_kernel, groups, pair),
        in_specs=[VMEM] * (2 + 2 * len(mine)),
        out_specs=VMEM,
        out_shape=jax.ShapeDtypeStruct(base[0].shape, dtype),
        scratch_shapes=[pltpu.VMEM((blocks, tall // 2, base[0].shape[1]), mine[0].dtype)],
        compiler_params=ROOM,
        name="final",
    )(*base, *mine, *theirs)


def body(tokens, base_key, adapter_down, adapter_up, adapter_ids, owner_slot, lengths):
    groups, ring, pair = lax.axis_size("groups"), lax.axis_size("ring"), lax.axis_size("pair")
    sides = lax.axis_size("tensor")
    shares = groups * pair
    rows = tokens.shape[0]
    blocks = lengths.shape[0]

    def across(x):
        return lax.ppermute(x, "tensor", [(i, (i + 1) % sides) for i in range(sides)])

    def along(x, step):
        return lax.ppermute(x, "ring", [(a, (a + step) % ring) for a in range(ring)])

    def first_hops(x):
        return {0: x, ring - 1: along(x, 1), **({1: along(x, -1)} if ring > 2 else {})}

    def in_plane(x, kg, ky):
        pairs = []
        for a in range(groups):
            for b in range(pair):
                pairs.append((a * pair + b, (a + kg) % groups * pair + (b + ky) % pair))
        return lax.ppermute(x, PLANE, pairs)

    def more_hops(held, way, *after):
        for k in range(2, ring // 2 + 1):
            if 2 * k < ring or way % 2 == 0:
                if k == 2:
                    held[ring - 1] = hand_on(held[ring - 1], held[1], *after)
                held[ring - k] = along(held[ring - k + 1], 1)
            if 2 * k < ring or way % 2 == 1:
                if k == 2:
                    held[1] = hand_on(held[1], held[ring - 1], *after)
                held[k] = along(held[k - 1], -1)
        return [held[k] for k in range(ring)]

    packed = pack(jnp.swapaxes(adapter_down, 1, 2), adapter_up, shares, pair)
    slabs = spread(tokens, lengths, adapter_ids.reshape(-1), groups, pair)
    swapped = [
        lax.ppermute(packed[pair - w], "pair", [(a, (a - w) % pair) for a in range(pair)]) for w in range(1, pair)
    ]
    firsts = [first_hops(piece) for piece in [packed[0]] + swapped]
    toks = [slabs[0]] + [in_plane(slabs[k], k // pair, k % pair) for k in range(1, shares)]

    base_mine, base_out, flag = base_halves(tokens, base_key, sides, lengths)
    pieces = [
        more_hops(held, way)
        for way, held in enumerate(firsts)
    ]

    flat = [piece for way in pieces for piece in way]
    parts = rank_parts(owner_slot, flag, toks, collect(flat), ring, pair, rows, blocks)
    mine = [parts[0]] + [in_plane(parts[k], -(k // pair), -(k % pair)) for k in range(1, shares)]
    theirs = [across(part) for part in mine]
    base_in = across(base_out)
    return final(mine, theirs, [base_mine, base_in], groups, pair, tokens.dtype)


def solution(mesh):
    groups, dp, sides = (mesh.shape[name] for name in ("groups", "dp", "tensor"))
    pair = 2 if dp % 2 == 0 else 1
    cut = Mesh(mesh.devices.reshape(groups, dp // pair, pair, sides), ("groups", "ring", "pair", "tensor"))
    stored = ("ring", "pair")
    placed = (
        P(WHOLE, "tensor"),
        P("tensor", None),
        P(stored, "tensor", None),
        P(stored, None, "tensor"),
        P(WHOLE, None),
        P(),
        P(WHOLE),
    )
    return jax.shard_map(body, mesh=cut, in_specs=placed, out_specs=P(WHOLE, "tensor"), check_vma=False)
```

```python
import functools

import jax
import jax.numpy as jnp
from jax import lax
from jax.experimental import pallas as pl
from jax.experimental.pallas import tpu as pltpu
from jax.sharding import Mesh
from jax.sharding import PartitionSpec as P

LANES = 128
ANY = pl.BlockSpec(memory_space=pl.ANY)
SMEM = pl.BlockSpec(memory_space=pltpu.SMEM)
VMEM = pl.BlockSpec(memory_space=pltpu.VMEM)
HBM = pl.BlockSpec(memory_space=pltpu.HBM)
ROOM = pltpu.CompilerParams(vmem_limit_bytes=32 * 1024 * 1024)
FULL = pltpu.CompilerParams(vmem_limit_bytes=60 * 1024 * 1024)
PLANE = ("groups", "pair")
WHOLE = ("groups", "ring", "pair")


def hand_kernel(*refs):
    pass


def hand_on(x, *after):
    return pl.pallas_call(
        hand_kernel,
        in_specs=[ANY] * (1 + len(after)),
        out_specs=ANY,
        out_shape=jax.ShapeDtypeStruct(x.shape, x.dtype),
        input_output_aliases={0: 0},
        compiler_params=FULL,
        name="hand",
    )(x, *after)


def pack_kernel(down, up, *refs):
    outs, sems = refs[:-1], refs[-1]
    feats = outs[0].shape[2] - LANES
    copies = []
    for way, out in enumerate(outs):
        share = lax.axis_index("groups") * len(outs) + lax.rem(lax.axis_index("pair") + way, len(outs))
        start = pl.multiple_of(share * feats, LANES)
        tile = pl.multiple_of(lax.rem(share, up.shape[2] // LANES) * LANES, LANES)
        copies.append(pltpu.make_async_copy(down.at[:, :, pl.ds(start, feats)], out.at[:, :, :feats], sems.at[way, 0]))
        copies.append(pltpu.make_async_copy(up.at[:, :, pl.ds(tile, LANES)], out.at[:, :, feats:], sems.at[way, 1]))
    for copy in copies:
        copy.start()
    for copy in copies:
        copy.wait()


def pack(down, up, shares, ways):
    adapters, rank, feats = down.shape
    shape = jax.ShapeDtypeStruct((adapters, rank, feats // shares + LANES), down.dtype)
    return pl.pallas_call(
        pack_kernel,
        in_specs=[HBM, HBM],
        out_specs=[VMEM] * ways,
        out_shape=[shape] * ways,
        scratch_shapes=[pltpu.SemaphoreType.DMA((ways, 2))],
        compiler_params=FULL,
        name="pack",
    )(down, up)


def mate_at(k, sign, groups, pair):
    kg, ky = k // pair, k % pair
    g = lax.rem(lax.axis_index("groups") + sign * kg + groups, groups)
    y = lax.rem(lax.axis_index("pair") + sign * ky + pair, pair)
    return g * pair + y


def spread_kernel(groups, pair, lengths, ids, tok, *refs):
    held, in_sems, out_sems = refs[-3:]
    outs = refs[:-3]
    blocks = lengths.shape[0]
    shares, tall, step = held.shape
    rows = tok.shape[0]
    block = rows // blocks
    mates = [pl.multiple_of(mate_at(k, 1, groups, pair) * step, LANES) for k in range(shares)]
    order = list(range(1, shares)) + [0]

    def read(k, b):
        here = pl.ds(b * block, block)
        return pltpu.make_async_copy(tok.at[here, pl.ds(mates[k], step)], held.at[k, here, :], in_sems.at[k, b])

    for k in order:
        for b in range(blocks):
            read(k, b).start()
    lane = lax.broadcasted_iota(jnp.int32, (tall - rows, step), 1)
    named = jnp.zeros((tall - rows, step), jnp.float32)
    for b in range(blocks):
        named = jnp.where(lane == b, ids[b].astype(jnp.float32), named)
    named = named.astype(held.dtype)
    writes = [pltpu.make_async_copy(held.at[k], outs[k], out_sems.at[k]) for k in range(shares)]
    for k in order:
        held[k, rows:, :] = named
        for b in range(blocks):
            read(k, b).wait()

            @pl.when(lengths[b] < block)
            def _():
                here = slice(b * block, (b + 1) * block)
                row = lax.broadcasted_iota(jnp.int32, (block, step), 0)
                part = held[k, here, :]
                held[k, here, :] = jnp.where(row < lengths[b], part, jnp.zeros_like(part))

        writes[k].start()
    for write in writes:
        write.wait()


def spread(tokens, lengths, ids, groups, pair):
    rows, feats = tokens.shape
    shares = groups * pair
    shape = (rows + 16, feats // shares)
    return pl.pallas_call(
        functools.partial(spread_kernel, groups, pair),
        in_specs=[SMEM, SMEM, ANY],
        out_specs=[ANY] * shares,
        out_shape=[jax.ShapeDtypeStruct(shape, tokens.dtype)] * shares,
        scratch_shapes=[
            pltpu.VMEM((shares,) + shape, tokens.dtype),
            pltpu.SemaphoreType.DMA((shares, lengths.shape[0])),
            pltpu.SemaphoreType.DMA((shares,)),
        ],
        compiler_params=FULL,
        name="spread",
    )(lengths, ids, tokens)


def base_kernel(sides, lengths, tok_ref, key_ref, *refs):
    mine, other, flag_ref, total = refs[-4:]
    step = pl.program_id(0)
    part = jnp.dot(tok_ref[...], key_ref[...], preferred_element_type=jnp.float32)

    @pl.when(step == 0)
    def _():
        total[...] = part

    @pl.when(step > 0)
    def _():
        total[...] += part

    @pl.when(step == pl.num_programs(0) - 1)
    def _():
        flag_ref[...] = jnp.zeros_like(flag_ref)
        blocks = lengths.shape[0]
        rows, wide = mine.shape
        block = rows // blocks
        row = lax.broadcasted_iota(jnp.int32, (block, wide), 0)
        t = lax.axis_index("tensor")
        for out, side in ((mine, t), (other, lax.rem(t + 1, sides))):
            columns = pl.ds(pl.multiple_of(side * wide, LANES), wide)
            for b in range(blocks):
                here = slice(b * block, (b + 1) * block)
                out[here, :] = jnp.where(row < lengths[b], total[here, columns], 0.0)


def base_halves(tokens, base_key, sides, lengths, *after):
    rows, depth = tokens.shape
    features = base_key.shape[1]
    wide = features // sides
    step = 512
    half = pl.BlockSpec((rows, wide), lambda i, n: (0, 0))
    return pl.pallas_call(
        functools.partial(base_kernel, sides),
        grid_spec=pltpu.PrefetchScalarGridSpec(
            num_scalar_prefetch=1,
            grid=(depth // step,),
            in_specs=[
                pl.BlockSpec((rows, step), lambda i, n: (0, i)),
                pl.BlockSpec((step, features), lambda i, n: (i, 0)),
            ]
            + [ANY] * len(after),
            out_specs=[half, half, pl.BlockSpec((8, LANES), lambda i, n: (0, 0))],
            scratch_shapes=[pltpu.VMEM((rows, features), jnp.float32)],
        ),
        out_shape=[jax.ShapeDtypeStruct((rows, wide), jnp.float32)] * 2
        + [jax.ShapeDtypeStruct((8, LANES), jnp.float32)],
        cost_estimate=pl.CostEstimate(flops=0, bytes_accessed=0, transcendentals=0),
        compiler_params=FULL,
        name="base",
    )(lengths, tokens, base_key, *after)


def collect_kernel(*refs):
    sems, held, pieces = refs[-1], refs[-2], refs[:-2]
    copies, start = [], 0
    for j, piece in enumerate(pieces):
        copies.append(pltpu.make_async_copy(piece, held.at[pl.ds(start, piece.shape[0])], sems.at[j]))
        start += piece.shape[0]
    for copy in copies:
        copy.start()
    for copy in copies:
        copy.wait()


def collect(pieces):
    count = sum(piece.shape[0] for piece in pieces)
    return pl.pallas_call(
        collect_kernel,
        in_specs=[ANY] * len(pieces),
        out_specs=VMEM,
        out_shape=jax.ShapeDtypeStruct((count,) + pieces[0].shape[1:], pieces[0].dtype),
        scratch_shapes=[pltpu.SemaphoreType.DMA((len(pieces),))],
        compiler_params=ROOM,
        name="collect",
    )(*pieces)


def rank_kernel(ring, pair, rows, owner, flag, held, *refs):
    shares = len(refs) // 2
    toks, outs = refs[:shares], refs[shares:]
    per, rank = held.shape[0] // (ring * pair), held.shape[1]
    blocks, _, block = outs[0].shape
    feats = toks[0].shape[1]
    z, y = lax.axis_index("ring"), lax.axis_index("pair")
    lane = lax.broadcasted_iota(jnp.int32, (16, LANES), 1)
    row = lax.broadcasted_iota(jnp.int32, (16, LANES), 0)
    ids = []
    for tok in toks:
        named = tok[rows:, :LANES].astype(jnp.float32)
        ids += [jnp.sum(jnp.where((lane == b) & (row == 0), named, 0.0)).astype(jnp.int32) for b in range(blocks)]
    for k, tok in enumerate(toks):
        for b in range(blocks):
            slot = owner[ids[k * blocks + b]]
            chip = slot // per
            away = lax.rem(chip // pair - z + ring, ring)
            way = lax.rem(lax.rem(chip, pair) - y + pair, pair)
            at = (way * ring + away) * per + lax.rem(slot, per)
            part = lax.dot_general(
                held[at, :, :feats],
                tok[b * block : (b + 1) * block, :],
                (((1,), (1,)), ((), ())),
                preferred_element_type=jnp.float32,
            )
            outs[k][b, :rank, :] = part.astype(outs[k].dtype)
            outs[k][b, rank:, :] = held[at, :, feats:]


def rank_parts(owner, flag, toks, held, ring, pair, rows, blocks):
    shares, rank = len(toks), held.shape[1]
    return pl.pallas_call(
        functools.partial(rank_kernel, ring, pair, rows),
        in_specs=[SMEM, ANY, VMEM] + [VMEM] * shares,
        out_specs=[VMEM] * shares,
        out_shape=[jax.ShapeDtypeStruct((blocks, 2 * rank, rows // blocks), held.dtype)] * shares,
        cost_estimate=pl.CostEstimate(flops=0, bytes_accessed=0, transcendentals=0),
        compiler_params=ROOM,
        name="rank",
    )(owner, flag, held, *toks)


def final_kernel(groups, pair, base_a, base_b, *refs):
    shares = groups * pair
    mine, theirs, out_ref, up = refs[:shares], refs[shares : 2 * shares], refs[-2], refs[-1]
    blocks, tall, block = mine[0].shape
    rank = tall // 2
    tiles = out_ref.shape[1] // LANES
    for b in range(blocks):
        here = slice(b * block, (b + 1) * block)
        total = mine[0][b, :rank, :].astype(jnp.float32)
        for part in mine[1:] + theirs:
            total += part[b, :rank, :].astype(jnp.float32)
        for k in range(shares):
            tile = lax.rem(mate_at(k, 1, groups, pair), tiles)
            up[b, :, pl.ds(pl.multiple_of(tile * LANES, LANES), LANES)] = mine[k][b, rank:, :]
        delta = lax.dot_general(
            total.astype(jnp.bfloat16), up[b], (((0,), (0,)), ((), ())), preferred_element_type=jnp.float32
        )
        out_ref[here, :] = (base_a[here, :] + base_b[here, :] + delta).astype(out_ref.dtype)


def final(mine, theirs, base, groups, pair, dtype):
    blocks, tall, _ = mine[0].shape
    return pl.pallas_call(
        functools.partial(final_kernel, groups, pair),
        in_specs=[VMEM] * (2 + 2 * len(mine)),
        out_specs=VMEM,
        out_shape=jax.ShapeDtypeStruct(base[0].shape, dtype),
        scratch_shapes=[pltpu.VMEM((blocks, tall // 2, base[0].shape[1]), mine[0].dtype)],
        compiler_params=ROOM,
        name="final",
    )(*base, *mine, *theirs)


def body(tokens, base_key, adapter_down, adapter_up, adapter_ids, owner_slot, lengths):
    groups, ring, pair = lax.axis_size("groups"), lax.axis_size("ring"), lax.axis_size("pair")
    sides = lax.axis_size("tensor")
    shares = groups * pair
    rows = tokens.shape[0]
    blocks = lengths.shape[0]

    def across(x):
        return lax.ppermute(x, "tensor", [(i, (i + 1) % sides) for i in range(sides)])

    def along(x, step):
        return lax.ppermute(x, "ring", [(a, (a + step) % ring) for a in range(ring)])

    def first_hops(x):
        return {0: x, ring - 1: along(x, 1), **({1: along(x, -1)} if ring > 2 else {})}

    def in_plane(x, kg, ky):
        pairs = []
        for a in range(groups):
            for b in range(pair):
                pairs.append((a * pair + b, (a + kg) % groups * pair + (b + ky) % pair))
        return lax.ppermute(x, PLANE, pairs)

    def more_hops(held, way, *after):
        for k in range(2, ring // 2 + 1):
            if 2 * k < ring or way % 2 == 0:
                if k == 2:
                    held[ring - 1] = hand_on(held[ring - 1], held[1], *after)
                held[ring - k] = along(held[ring - k + 1], 1)
            if 2 * k < ring or way % 2 == 1:
                if k == 2:
                    held[1] = hand_on(held[1], held[ring - 1], *after)
                held[k] = along(held[k - 1], -1)
        return [held[k] for k in range(ring)]

    packed = pack(jnp.swapaxes(adapter_down, 1, 2), adapter_up, shares, pair)
    slabs = spread(tokens, lengths, adapter_ids.reshape(-1), groups, pair)
    swapped = [
        lax.ppermute(packed[pair - w], "pair", [(a, (a - w) % pair) for a in range(pair)]) for w in range(1, pair)
    ]
    swapped = [hand_on(piece, slabs[0]) for piece in swapped]
    firsts = [first_hops(piece) for piece in [packed[0]] + swapped]
    toks = [slabs[0]] + [in_plane(slabs[k], k // pair, k % pair) for k in range(1, shares)]

    pieces = [
        more_hops(held, way)
        for way, held in enumerate(firsts)
    ]

    sent = [pieces[0][ring - 1], pieces[-1][1]]
    base_mine, base_out, flag = base_halves(tokens, base_key, sides, lengths, *sent)
    flat = [piece for way in pieces for piece in way]
    parts = rank_parts(owner_slot, flag, toks, collect(flat), ring, pair, rows, blocks)
    mine = [parts[0]] + [in_plane(parts[k], -(k // pair), -(k % pair)) for k in range(1, shares)]
    theirs = [across(part) for part in mine]
    base_in = across(base_out)
    return final(mine, theirs, [base_mine, base_in], groups, pair, tokens.dtype)


def solution(mesh):
    groups, dp, sides = (mesh.shape[name] for name in ("groups", "dp", "tensor"))
    pair = 2 if dp % 2 == 0 else 1
    cut = Mesh(mesh.devices.reshape(groups, dp // pair, pair, sides), ("groups", "ring", "pair", "tensor"))
    stored = ("ring", "pair")
    placed = (
        P(WHOLE, "tensor"),
        P("tensor", None),
        P(stored, "tensor", None),
        P(stored, None, "tensor"),
        P(WHOLE, None),
        P(),
        P(WHOLE),
    )
    return jax.shard_map(body, mesh=cut, in_specs=placed, out_specs=P(WHOLE, "tensor"), check_vma=False)
```

```python
import functools

import jax
import jax.numpy as jnp
from jax import lax
from jax.experimental import pallas as pl
from jax.experimental.pallas import tpu as pltpu
from jax.sharding import Mesh
from jax.sharding import PartitionSpec as P

LANES = 128
ANY = pl.BlockSpec(memory_space=pl.ANY)
SMEM = pl.BlockSpec(memory_space=pltpu.SMEM)
VMEM = pl.BlockSpec(memory_space=pltpu.VMEM)
HBM = pl.BlockSpec(memory_space=pltpu.HBM)
ROOM = pltpu.CompilerParams(vmem_limit_bytes=32 * 1024 * 1024)
FULL = pltpu.CompilerParams(vmem_limit_bytes=60 * 1024 * 1024)
PLANE = ("groups", "pair")
WHOLE = ("groups", "ring", "pair")


def hand_kernel(*refs):
    pass


def hand_on(x, *after):
    return pl.pallas_call(
        hand_kernel,
        in_specs=[ANY] * (1 + len(after)),
        out_specs=ANY,
        out_shape=jax.ShapeDtypeStruct(x.shape, x.dtype),
        input_output_aliases={0: 0},
        compiler_params=FULL,
        name="hand",
    )(x, *after)


def pack_kernel(down, up, *refs):
    outs, sems = refs[:-1], refs[-1]
    feats = outs[0].shape[2] - LANES
    copies = []
    for way, out in enumerate(outs):
        share = lax.axis_index("groups") * len(outs) + lax.rem(lax.axis_index("pair") + way, len(outs))
        start = pl.multiple_of(share * feats, LANES)
        tile = pl.multiple_of(lax.rem(share, up.shape[2] // LANES) * LANES, LANES)
        copies.append(pltpu.make_async_copy(down.at[:, :, pl.ds(start, feats)], out.at[:, :, :feats], sems.at[way, 0]))
        copies.append(pltpu.make_async_copy(up.at[:, :, pl.ds(tile, LANES)], out.at[:, :, feats:], sems.at[way, 1]))
    for copy in copies:
        copy.start()
    for copy in copies:
        copy.wait()


def pack(down, up, shares, ways):
    adapters, rank, feats = down.shape
    shape = jax.ShapeDtypeStruct((adapters, rank, feats // shares + LANES), down.dtype)
    return pl.pallas_call(
        pack_kernel,
        in_specs=[HBM, HBM],
        out_specs=[VMEM] * ways,
        out_shape=[shape] * ways,
        scratch_shapes=[pltpu.SemaphoreType.DMA((ways, 2))],
        compiler_params=FULL,
        name="pack",
    )(down, up)


def mate_at(k, sign, groups, pair):
    kg, ky = k // pair, k % pair
    g = lax.rem(lax.axis_index("groups") + sign * kg + groups, groups)
    y = lax.rem(lax.axis_index("pair") + sign * ky + pair, pair)
    return g * pair + y


def spread_kernel(groups, pair, lengths, ids, tok, *refs):
    held, in_sems, out_sems = refs[-3:]
    outs = refs[:-3]
    blocks = lengths.shape[0]
    shares, tall, step = held.shape
    rows = tok.shape[0]
    block = rows // blocks
    mates = [pl.multiple_of(mate_at(k, 1, groups, pair) * step, LANES) for k in range(shares)]
    order = list(range(1, shares)) + [0]

    def read(k, b):
        here = pl.ds(b * block, block)
        return pltpu.make_async_copy(tok.at[here, pl.ds(mates[k], step)], held.at[k, here, :], in_sems.at[k, b])

    for k in order:
        for b in range(blocks):
            read(k, b).start()
    lane = lax.broadcasted_iota(jnp.int32, (tall - rows, step), 1)
    named = jnp.zeros((tall - rows, step), jnp.float32)
    for b in range(blocks):
        named = jnp.where(lane == b, ids[b].astype(jnp.float32), named)
    named = named.astype(held.dtype)
    writes = [pltpu.make_async_copy(held.at[k], outs[k], out_sems.at[k]) for k in range(shares)]
    for k in order:
        held[k, rows:, :] = named
        for b in range(blocks):
            read(k, b).wait()

            @pl.when(lengths[b] < block)
            def _():
                here = slice(b * block, (b + 1) * block)
                row = lax.broadcasted_iota(jnp.int32, (block, step), 0)
                part = held[k, here, :]
                held[k, here, :] = jnp.where(row < lengths[b], part, jnp.zeros_like(part))

        writes[k].start()
    for write in writes:
        write.wait()


def spread(tokens, lengths, ids, groups, pair):
    rows, feats = tokens.shape
    shares = groups * pair
    shape = (rows + 16, feats // shares)
    return pl.pallas_call(
        functools.partial(spread_kernel, groups, pair),
        in_specs=[SMEM, SMEM, ANY],
        out_specs=[ANY] * shares,
        out_shape=[jax.ShapeDtypeStruct(shape, tokens.dtype)] * shares,
        scratch_shapes=[
            pltpu.VMEM((shares,) + shape, tokens.dtype),
            pltpu.SemaphoreType.DMA((shares, lengths.shape[0])),
            pltpu.SemaphoreType.DMA((shares,)),
        ],
        compiler_params=FULL,
        name="spread",
    )(lengths, ids, tokens)


def base_kernel(sides, lengths, tok, key, mine, other, flag_ref, tok_held, key_held, total, tok_sems, key_sems):
    depth, rows = key.shape[0], tok.shape[0]
    chunk = depth // key_sems.shape[0]
    steps = tok_sems.shape[0]
    step = depth // steps

    def key_copy(i):
        here = pl.ds(i * chunk, chunk)
        return pltpu.make_async_copy(key.at[here, :], key_held.at[here, :], key_sems.at[i])

    def tok_copy(i, b):
        here = pl.ds(i * step, step)
        some = pl.ds(b * (rows // tok_sems.shape[1]), rows // tok_sems.shape[1])
        return pltpu.make_async_copy(tok.at[some, here], tok_held.at[some, here], tok_sems.at[i, b])

    flag_ref[...] = jnp.zeros_like(flag_ref)
    for i in range(steps):
        for b in range(tok_sems.shape[1]):
            tok_copy(i, b).start()
        for j in range(step // chunk):
            key_copy(i * (step // chunk) + j).start()
    for i in range(steps):
        for b in range(tok_sems.shape[1]):
            tok_copy(i, b).wait()
        for j in range(step // chunk):
            key_copy(i * (step // chunk) + j).wait()
        here = slice(i * step, (i + 1) * step)
        part = jnp.dot(tok_held[:, here], key_held[here, :], preferred_element_type=jnp.float32)
        if i == 0:
            total[...] = part
        else:
            total[...] += part
    blocks = lengths.shape[0]
    wide = mine.shape[1]
    block = rows // blocks
    row = lax.broadcasted_iota(jnp.int32, (block, wide), 0)
    t = lax.axis_index("tensor")
    for out, side in ((mine, t), (other, lax.rem(t + 1, sides))):
        columns = pl.ds(pl.multiple_of(side * wide, LANES), wide)
        for b in range(blocks):
            here = slice(b * block, (b + 1) * block)
            out[here, :] = jnp.where(row < lengths[b], total[here, columns], 0.0)


def base_halves(tokens, base_key, sides, lengths):
    rows, depth = tokens.shape
    features = base_key.shape[1]
    half = jax.ShapeDtypeStruct((rows, features // sides), jnp.float32)
    steps, chunks = depth // 1024, depth // 256
    return pl.pallas_call(
        functools.partial(base_kernel, sides),
        in_specs=[SMEM, ANY, ANY],
        out_specs=[VMEM] * 3,
        out_shape=[half, half, jax.ShapeDtypeStruct((8, LANES), jnp.float32)],
        scratch_shapes=[
            pltpu.VMEM(tokens.shape, tokens.dtype),
            pltpu.VMEM(base_key.shape, base_key.dtype),
            pltpu.VMEM((rows, features), jnp.float32),
            pltpu.SemaphoreType.DMA((steps, lengths.shape[0])),
            pltpu.SemaphoreType.DMA((chunks,)),
        ],
        cost_estimate=pl.CostEstimate(flops=0, bytes_accessed=0, transcendentals=0),
        compiler_params=FULL,
        name="base",
    )(lengths, tokens, base_key)


def collect_kernel(*refs):
    sems, held, pieces = refs[-1], refs[-2], refs[:-2]
    copies, start = [], 0
    for j, piece in enumerate(pieces):
        copies.append(pltpu.make_async_copy(piece, held.at[pl.ds(start, piece.shape[0])], sems.at[j]))
        start += piece.shape[0]
    for copy in copies:
        copy.start()
    for copy in copies:
        copy.wait()


def collect(pieces):
    count = sum(piece.shape[0] for piece in pieces)
    return pl.pallas_call(
        collect_kernel,
        in_specs=[ANY] * len(pieces),
        out_specs=VMEM,
        out_shape=jax.ShapeDtypeStruct((count,) + pieces[0].shape[1:], pieces[0].dtype),
        scratch_shapes=[pltpu.SemaphoreType.DMA((len(pieces),))],
        compiler_params=ROOM,
        name="collect",
    )(*pieces)


def rank_kernel(ring, pair, rows, owner, held, *refs):
    shares = (len(refs) - 1) // 2
    toks, outs, flag = refs[:shares], refs[shares:-1], refs[-1]
    flag[...] = jnp.zeros_like(flag)
    per, rank = held.shape[0] // (ring * pair), held.shape[1]
    blocks, _, block = outs[0].shape
    feats = toks[0].shape[1]
    z, y = lax.axis_index("ring"), lax.axis_index("pair")
    lane = lax.broadcasted_iota(jnp.int32, (16, LANES), 1)
    row = lax.broadcasted_iota(jnp.int32, (16, LANES), 0)
    ids = []
    for tok in toks:
        named = tok[rows:, :LANES].astype(jnp.float32)
        ids += [jnp.sum(jnp.where((lane == b) & (row == 0), named, 0.0)).astype(jnp.int32) for b in range(blocks)]
    for k, tok in enumerate(toks):
        for b in range(blocks):
            slot = owner[ids[k * blocks + b]]
            chip = slot // per
            away = lax.rem(chip // pair - z + ring, ring)
            way = lax.rem(lax.rem(chip, pair) - y + pair, pair)
            at = (way * ring + away) * per + lax.rem(slot, per)
            part = lax.dot_general(
                held[at, :, :feats],
                tok[b * block : (b + 1) * block, :],
                (((1,), (1,)), ((), ())),
                preferred_element_type=jnp.float32,
            )
            outs[k][b, :rank, :] = part.astype(outs[k].dtype)
            outs[k][b, rank:, :] = held[at, :, feats:]


def rank_parts(owner, toks, held, ring, pair, rows, blocks):
    shares, rank = len(toks), held.shape[1]
    return pl.pallas_call(
        functools.partial(rank_kernel, ring, pair, rows),
        in_specs=[SMEM, VMEM] + [VMEM] * shares,
        out_specs=[VMEM] * (shares + 1),
        out_shape=[jax.ShapeDtypeStruct((blocks, 2 * rank, rows // blocks), held.dtype)] * shares
        + [jax.ShapeDtypeStruct((8, LANES), jnp.float32)],
        cost_estimate=pl.CostEstimate(flops=0, bytes_accessed=0, transcendentals=0),
        compiler_params=ROOM,
        name="rank",
    )(owner, held, *toks)


def final_kernel(groups, pair, base_a, base_b, *refs):
    shares = groups * pair
    mine, theirs, out_ref, up = refs[:shares], refs[shares : 2 * shares], refs[-2], refs[-1]
    blocks, tall, block = mine[0].shape
    rank = tall // 2
    tiles = out_ref.shape[1] // LANES
    for b in range(blocks):
        here = slice(b * block, (b + 1) * block)
        total = mine[0][b, :rank, :].astype(jnp.float32)
        for part in mine[1:] + theirs:
            total += part[b, :rank, :].astype(jnp.float32)
        for k in range(shares):
            tile = lax.rem(mate_at(k, 1, groups, pair), tiles)
            up[b, :, pl.ds(pl.multiple_of(tile * LANES, LANES), LANES)] = mine[k][b, rank:, :]
        delta = lax.dot_general(
            total.astype(jnp.bfloat16), up[b], (((0,), (0,)), ((), ())), preferred_element_type=jnp.float32
        )
        out_ref[here, :] = (base_a[here, :] + base_b[here, :] + delta).astype(out_ref.dtype)


def final(mine, theirs, base, groups, pair, dtype):
    blocks, tall, _ = mine[0].shape
    return pl.pallas_call(
        functools.partial(final_kernel, groups, pair),
        in_specs=[VMEM] * (2 + 2 * len(mine)),
        out_specs=VMEM,
        out_shape=jax.ShapeDtypeStruct(base[0].shape, dtype),
        scratch_shapes=[pltpu.VMEM((blocks, tall // 2, base[0].shape[1]), mine[0].dtype)],
        compiler_params=ROOM,
        name="final",
    )(*base, *mine, *theirs)


def body(tokens, base_key, adapter_down, adapter_up, adapter_ids, owner_slot, lengths):
    groups, ring, pair = lax.axis_size("groups"), lax.axis_size("ring"), lax.axis_size("pair")
    sides = lax.axis_size("tensor")
    shares = groups * pair
    rows = tokens.shape[0]
    blocks = lengths.shape[0]

    def across(x):
        return lax.ppermute(x, "tensor", [(i, (i + 1) % sides) for i in range(sides)])

    def along(x, step):
        return lax.ppermute(x, "ring", [(a, (a + step) % ring) for a in range(ring)])

    def first_hops(x):
        return {0: x, ring - 1: along(x, 1), **({1: along(x, -1)} if ring > 2 else {})}

    def in_plane(x, kg, ky):
        pairs = []
        for a in range(groups):
            for b in range(pair):
                pairs.append((a * pair + b, (a + kg) % groups * pair + (b + ky) % pair))
        return lax.ppermute(x, PLANE, pairs)

    def more_hops(held, way, *after):
        for k in range(2, ring // 2 + 1):
            if 2 * k < ring or way % 2 == 0:
                if k == 2:
                    held[ring - 1] = hand_on(held[ring - 1], held[1], *after)
                held[ring - k] = along(held[ring - k + 1], 1)
            if 2 * k < ring or way % 2 == 1:
                if k == 2:
                    held[1] = hand_on(held[1], held[ring - 1], *after)
                held[k] = along(held[k - 1], -1)
        return [held[k] for k in range(ring)]

    packed = pack(jnp.swapaxes(adapter_down, 1, 2), adapter_up, shares, pair)
    slabs = spread(tokens, lengths, adapter_ids.reshape(-1), groups, pair)
    swapped = [
        lax.ppermute(packed[pair - w], "pair", [(a, (a - w) % pair) for a in range(pair)]) for w in range(1, pair)
    ]
    firsts = [first_hops(piece) for piece in [packed[0]] + swapped]
    toks = [slabs[0]] + [in_plane(slabs[k], k // pair, k % pair) for k in range(1, shares)]

    base_mine, base_out, flag = base_halves(tokens, base_key, sides, lengths)
    pieces = [
        more_hops(held, way, flag)
        for way, held in enumerate(firsts)
    ]

    flat = [piece for way in pieces for piece in way]
    *parts, ready = rank_parts(owner_slot, toks, collect(flat), ring, pair, rows, blocks)
    mine = [parts[0]] + [in_plane(parts[k], -(k // pair), -(k % pair)) for k in range(1, shares)]
    theirs = [across(part) for part in mine]
    base_in = across(hand_on(base_out, ready))
    return final(mine, theirs, [base_mine, base_in], groups, pair, tokens.dtype)


def solution(mesh):
    groups, dp, sides = (mesh.shape[name] for name in ("groups", "dp", "tensor"))
    pair = 2 if dp % 2 == 0 else 1
    cut = Mesh(mesh.devices.reshape(groups, dp // pair, pair, sides), ("groups", "ring", "pair", "tensor"))
    stored = ("ring", "pair")
    placed = (
        P(WHOLE, "tensor"),
        P("tensor", None),
        P(stored, "tensor", None),
        P(stored, None, "tensor"),
        P(WHOLE, None),
        P(),
        P(WHOLE),
    )
    return jax.shard_map(body, mesh=cut, in_specs=placed, out_specs=P(WHOLE, "tensor"), check_vma=False)
```

```python
import functools

import jax
import jax.numpy as jnp
from jax import lax
from jax.experimental import pallas as pl
from jax.experimental.pallas import tpu as pltpu
from jax.sharding import Mesh
from jax.sharding import PartitionSpec as P

LANES = 128
ANY = pl.BlockSpec(memory_space=pl.ANY)
SMEM = pl.BlockSpec(memory_space=pltpu.SMEM)
VMEM = pl.BlockSpec(memory_space=pltpu.VMEM)
HBM = pl.BlockSpec(memory_space=pltpu.HBM)
ROOM = pltpu.CompilerParams(vmem_limit_bytes=32 * 1024 * 1024)
FULL = pltpu.CompilerParams(vmem_limit_bytes=60 * 1024 * 1024)
PLANE = ("groups", "pair")
WHOLE = ("groups", "ring", "pair")


def hand_kernel(*refs):
    pass


def hand_on(x, *after):
    return pl.pallas_call(
        hand_kernel,
        in_specs=[ANY] * (1 + len(after)),
        out_specs=ANY,
        out_shape=jax.ShapeDtypeStruct(x.shape, x.dtype),
        input_output_aliases={0: 0},
        compiler_params=FULL,
        name="hand",
    )(x, *after)


def pack_kernel(down, up, *refs):
    outs, sems = refs[:-1], refs[-1]
    feats = outs[0].shape[2] - LANES
    copies = []
    for way, out in enumerate(outs):
        share = lax.axis_index("groups") * len(outs) + lax.rem(lax.axis_index("pair") + way, len(outs))
        start = pl.multiple_of(share * feats, LANES)
        tile = pl.multiple_of(lax.rem(share, up.shape[2] // LANES) * LANES, LANES)
        copies.append(pltpu.make_async_copy(down.at[:, :, pl.ds(start, feats)], out.at[:, :, :feats], sems.at[way, 0]))
        copies.append(pltpu.make_async_copy(up.at[:, :, pl.ds(tile, LANES)], out.at[:, :, feats:], sems.at[way, 1]))
    for copy in copies:
        copy.start()
    for copy in copies:
        copy.wait()


def pack(down, up, shares, ways):
    adapters, rank, feats = down.shape
    shape = jax.ShapeDtypeStruct((adapters, rank, feats // shares + LANES), down.dtype)
    return pl.pallas_call(
        pack_kernel,
        in_specs=[HBM, HBM],
        out_specs=[VMEM] * ways,
        out_shape=[shape] * ways,
        scratch_shapes=[pltpu.SemaphoreType.DMA((ways, 2))],
        compiler_params=FULL,
        name="pack",
    )(down, up)


def mate_at(k, sign, groups, pair):
    kg, ky = k // pair, k % pair
    g = lax.rem(lax.axis_index("groups") + sign * kg + groups, groups)
    y = lax.rem(lax.axis_index("pair") + sign * ky + pair, pair)
    return g * pair + y


def spread_kernel(groups, pair, lengths, ids, tok, *refs):
    held, in_sems, out_sems = refs[-3:]
    outs = refs[:-3]
    blocks = lengths.shape[0]
    shares, tall, step = held.shape
    rows = tok.shape[0]
    block = rows // blocks
    mates = [pl.multiple_of(mate_at(k, 1, groups, pair) * step, LANES) for k in range(shares)]
    order = list(range(1, shares)) + [0]

    def read(k, b):
        here = pl.ds(b * block, block)
        return pltpu.make_async_copy(tok.at[here, pl.ds(mates[k], step)], held.at[k, here, :], in_sems.at[k, b])

    for k in order:
        for b in range(blocks):
            read(k, b).start()
    lane = lax.broadcasted_iota(jnp.int32, (tall - rows, step), 1)
    named = jnp.zeros((tall - rows, step), jnp.float32)
    for b in range(blocks):
        named = jnp.where(lane == b, ids[b].astype(jnp.float32), named)
    named = named.astype(held.dtype)
    writes = [pltpu.make_async_copy(held.at[k], outs[k], out_sems.at[k]) for k in range(shares)]
    for k in order:
        held[k, rows:, :] = named
        for b in range(blocks):
            read(k, b).wait()

            @pl.when(lengths[b] < block)
            def _():
                here = slice(b * block, (b + 1) * block)
                row = lax.broadcasted_iota(jnp.int32, (block, step), 0)
                part = held[k, here, :]
                held[k, here, :] = jnp.where(row < lengths[b], part, jnp.zeros_like(part))

        writes[k].start()
    for write in writes:
        write.wait()


def spread(tokens, lengths, ids, groups, pair):
    rows, feats = tokens.shape
    shares = groups * pair
    shape = (rows + 16, feats // shares)
    return pl.pallas_call(
        functools.partial(spread_kernel, groups, pair),
        in_specs=[SMEM, SMEM, ANY],
        out_specs=[ANY] * shares,
        out_shape=[jax.ShapeDtypeStruct(shape, tokens.dtype)] * shares,
        scratch_shapes=[
            pltpu.VMEM((shares,) + shape, tokens.dtype),
            pltpu.SemaphoreType.DMA((shares, lengths.shape[0])),
            pltpu.SemaphoreType.DMA((shares,)),
        ],
        compiler_params=FULL,
        name="spread",
    )(lengths, ids, tokens)


def base_kernel(sides, lengths, tok, key, mine, other, flag_ref, tok_held, key_held, total, tok_sems, key_sems):
    depth, rows = key.shape[0], tok.shape[0]
    chunk = depth // key_sems.shape[0]
    steps = tok_sems.shape[0]
    step = depth // steps

    def key_copy(i):
        here = pl.ds(i * chunk, chunk)
        return pltpu.make_async_copy(key.at[here, :], key_held.at[here, :], key_sems.at[i])

    def tok_copy(i, b):
        here = pl.ds(i * step, step)
        some = pl.ds(b * (rows // tok_sems.shape[1]), rows // tok_sems.shape[1])
        return pltpu.make_async_copy(tok.at[some, here], tok_held.at[some, here], tok_sems.at[i, b])

    flag_ref[...] = jnp.zeros_like(flag_ref)
    for i in range(steps):
        for b in range(tok_sems.shape[1]):
            tok_copy(i, b).start()
        for j in range(step // chunk):
            key_copy(i * (step // chunk) + j).start()
    for i in range(steps):
        for b in range(tok_sems.shape[1]):
            tok_copy(i, b).wait()
        for j in range(step // chunk):
            key_copy(i * (step // chunk) + j).wait()
        here = slice(i * step, (i + 1) * step)
        part = jnp.dot(tok_held[:, here], key_held[here, :], preferred_element_type=jnp.float32)
        if i == 0:
            total[...] = part
        else:
            total[...] += part
    blocks = lengths.shape[0]
    wide = mine.shape[1]
    block = rows // blocks
    row = lax.broadcasted_iota(jnp.int32, (block, wide), 0)
    t = lax.axis_index("tensor")
    for out, side in ((mine, t), (other, lax.rem(t + 1, sides))):
        columns = pl.ds(pl.multiple_of(side * wide, LANES), wide)
        for b in range(blocks):
            here = slice(b * block, (b + 1) * block)
            out[here, :] = jnp.where(row < lengths[b], total[here, columns], 0.0)


def base_halves(tokens, base_key, sides, lengths):
    rows, depth = tokens.shape
    features = base_key.shape[1]
    half = jax.ShapeDtypeStruct((rows, features // sides), jnp.float32)
    steps, chunks = depth // 1024, depth // 256
    return pl.pallas_call(
        functools.partial(base_kernel, sides),
        in_specs=[SMEM, ANY, ANY],
        out_specs=[VMEM] * 3,
        out_shape=[half, half, jax.ShapeDtypeStruct((8, LANES), jnp.float32)],
        scratch_shapes=[
            pltpu.VMEM(tokens.shape, tokens.dtype),
            pltpu.VMEM(base_key.shape, base_key.dtype),
            pltpu.VMEM((rows, features), jnp.float32),
            pltpu.SemaphoreType.DMA((steps, lengths.shape[0])),
            pltpu.SemaphoreType.DMA((chunks,)),
        ],
        cost_estimate=pl.CostEstimate(flops=0, bytes_accessed=0, transcendentals=0),
        compiler_params=FULL,
        name="base",
    )(lengths, tokens, base_key)


def collect_kernel(*refs):
    sems, held, pieces = refs[-1], refs[-2], refs[:-2]
    copies, start = [], 0
    for j, piece in enumerate(pieces):
        copies.append(pltpu.make_async_copy(piece, held.at[pl.ds(start, piece.shape[0])], sems.at[j]))
        start += piece.shape[0]
    for copy in copies:
        copy.start()
    for copy in copies:
        copy.wait()


def collect(pieces):
    count = sum(piece.shape[0] for piece in pieces)
    return pl.pallas_call(
        collect_kernel,
        in_specs=[ANY] * len(pieces),
        out_specs=VMEM,
        out_shape=jax.ShapeDtypeStruct((count,) + pieces[0].shape[1:], pieces[0].dtype),
        scratch_shapes=[pltpu.SemaphoreType.DMA((len(pieces),))],
        compiler_params=ROOM,
        name="collect",
    )(*pieces)


def rank_kernel(ring, pair, rows, shares, owner, held, *refs):
    late, toks, outs = refs[: -2 - 2 * shares], refs[-2 - 2 * shares : -2 - shares], refs[-2 - shares : -2]
    flag, picked = refs[-2:]
    flag[...] = jnp.zeros_like(flag)
    rank = held.shape[1]
    per = owner.shape[0] // (ring * pair)
    blocks, _, block = outs[0].shape
    feats = toks[0].shape[1]
    z, y = lax.axis_index("ring"), lax.axis_index("pair")
    lane = lax.broadcasted_iota(jnp.int32, (16, LANES), 1)
    row = lax.broadcasted_iota(jnp.int32, (16, LANES), 0)
    ids = []
    for tok in toks:
        named = tok[rows:, :LANES].astype(jnp.float32)
        ids += [jnp.sum(jnp.where((lane == b) & (row == 0), named, 0.0)).astype(jnp.int32) for b in range(blocks)]
    for i, one in enumerate(ids):
        slot = owner[one]
        chip = slot // per
        local = lax.rem(slot, per)
        away = lax.rem(chip // pair - z + ring, ring)
        way = lax.rem(lax.rem(chip, pair) - y + pair, pair)
        if late:
            half = ring // 2
            near = away - jnp.where(away > half, 1, 0)

            @pl.when(away != half)
            def _():
                picked[i] = held[(way * (ring - 1) + near) * per + local]

            for w in range(pair):

                @pl.when((away == half) & (way == w))
                def _():
                    picked[i] = late[w][local]

        else:
            picked[i] = held[(way * ring + away) * per + local]
    for k, tok in enumerate(toks):
        for b in range(blocks):
            i = k * blocks + b
            part = lax.dot_general(
                picked[i, :, :feats],
                tok[b * block : (b + 1) * block, :],
                (((1,), (1,)), ((), ())),
                preferred_element_type=jnp.float32,
            )
            outs[k][b, :rank, :] = part.astype(outs[k].dtype)
            outs[k][b, rank:, :] = picked[i, :, feats:]


def rank_parts(owner, toks, held, late, ring, pair, rows, blocks):
    shares, rank = len(toks), held.shape[1]
    return pl.pallas_call(
        functools.partial(rank_kernel, ring, pair, rows, shares),
        in_specs=[SMEM, VMEM] + [VMEM] * (len(late) + shares),
        out_specs=[VMEM] * (shares + 1),
        out_shape=[jax.ShapeDtypeStruct((blocks, 2 * rank, rows // blocks), held.dtype)] * shares
        + [jax.ShapeDtypeStruct((8, LANES), jnp.float32)],
        scratch_shapes=[pltpu.VMEM((shares * blocks,) + held.shape[1:], held.dtype)],
        cost_estimate=pl.CostEstimate(flops=0, bytes_accessed=0, transcendentals=0),
        compiler_params=ROOM,
        name="rank",
    )(owner, held, *late, *toks)


def final_kernel(groups, pair, base_a, base_b, *refs):
    shares = groups * pair
    mine, theirs, out_ref, up = refs[:shares], refs[shares : 2 * shares], refs[-2], refs[-1]
    blocks, tall, block = mine[0].shape
    rank = tall // 2
    tiles = out_ref.shape[1] // LANES
    for b in range(blocks):
        here = slice(b * block, (b + 1) * block)
        total = mine[0][b, :rank, :].astype(jnp.float32)
        for part in mine[1:] + theirs:
            total += part[b, :rank, :].astype(jnp.float32)
        for k in range(shares):
            tile = lax.rem(mate_at(k, 1, groups, pair), tiles)
            up[b, :, pl.ds(pl.multiple_of(tile * LANES, LANES), LANES)] = mine[k][b, rank:, :]
        delta = lax.dot_general(
            total.astype(jnp.bfloat16), up[b], (((0,), (0,)), ((), ())), preferred_element_type=jnp.float32
        )
        out_ref[here, :] = (base_a[here, :] + base_b[here, :] + delta).astype(out_ref.dtype)


def final(mine, theirs, base, groups, pair, dtype):
    blocks, tall, _ = mine[0].shape
    return pl.pallas_call(
        functools.partial(final_kernel, groups, pair),
        in_specs=[VMEM] * (2 + 2 * len(mine)),
        out_specs=VMEM,
        out_shape=jax.ShapeDtypeStruct(base[0].shape, dtype),
        scratch_shapes=[pltpu.VMEM((blocks, tall // 2, base[0].shape[1]), mine[0].dtype)],
        compiler_params=ROOM,
        name="final",
    )(*base, *mine, *theirs)


def body(tokens, base_key, adapter_down, adapter_up, adapter_ids, owner_slot, lengths):
    groups, ring, pair = lax.axis_size("groups"), lax.axis_size("ring"), lax.axis_size("pair")
    sides = lax.axis_size("tensor")
    shares = groups * pair
    rows = tokens.shape[0]
    blocks = lengths.shape[0]

    def across(x):
        return lax.ppermute(x, "tensor", [(i, (i + 1) % sides) for i in range(sides)])

    def along(x, step):
        return lax.ppermute(x, "ring", [(a, (a + step) % ring) for a in range(ring)])

    def first_hops(x):
        return {0: x, ring - 1: along(x, 1), **({1: along(x, -1)} if ring > 2 else {})}

    def in_plane(x, kg, ky):
        pairs = []
        for a in range(groups):
            for b in range(pair):
                pairs.append((a * pair + b, (a + kg) % groups * pair + (b + ky) % pair))
        return lax.ppermute(x, PLANE, pairs)

    def more_hops(held, way, *after):
        for k in range(2, ring // 2 + 1):
            if 2 * k < ring or way % 2 == 0:
                if k == 2:
                    held[ring - 1] = hand_on(held[ring - 1], held[1], *after)
                held[ring - k] = along(held[ring - k + 1], 1)
            if 2 * k < ring or way % 2 == 1:
                if k == 2:
                    held[1] = hand_on(held[1], held[ring - 1], *after)
                held[k] = along(held[k - 1], -1)
        return [held[k] for k in range(ring)]

    packed = pack(jnp.swapaxes(adapter_down, 1, 2), adapter_up, shares, pair)
    slabs = spread(tokens, lengths, adapter_ids.reshape(-1), groups, pair)
    swapped = [
        lax.ppermute(packed[pair - w], "pair", [(a, (a - w) % pair) for a in range(pair)]) for w in range(1, pair)
    ]
    firsts = [first_hops(piece) for piece in [packed[0]] + swapped]
    toks = [slabs[0]] + [in_plane(slabs[k], k // pair, k % pair) for k in range(1, shares)]

    base_mine, base_out, flag = base_halves(tokens, base_key, sides, lengths)
    pieces = [
        more_hops(held, way, flag)
        for way, held in enumerate(firsts)
    ]

    halfway = ring // 2 if ring % 2 == 0 else ring
    held = collect([piece for way in pieces for away, piece in enumerate(way) if away != halfway])
    late = [way[halfway] for way in pieces] if halfway < ring else []
    *parts, ready = rank_parts(owner_slot, toks, held, late, ring, pair, rows, blocks)
    mine = [parts[0]] + [in_plane(parts[k], -(k // pair), -(k % pair)) for k in range(1, shares)]
    theirs = [across(part) for part in mine]
    base_in = across(hand_on(base_out, ready))
    return final(mine, theirs, [base_mine, base_in], groups, pair, tokens.dtype)


def solution(mesh):
    groups, dp, sides = (mesh.shape[name] for name in ("groups", "dp", "tensor"))
    pair = 2 if dp % 2 == 0 else 1
    cut = Mesh(mesh.devices.reshape(groups, dp // pair, pair, sides), ("groups", "ring", "pair", "tensor"))
    stored = ("ring", "pair")
    placed = (
        P(WHOLE, "tensor"),
        P("tensor", None),
        P(stored, "tensor", None),
        P(stored, None, "tensor"),
        P(WHOLE, None),
        P(),
        P(WHOLE),
    )
    return jax.shard_map(body, mesh=cut, in_specs=placed, out_specs=P(WHOLE, "tensor"), check_vma=False)
```

```python
import functools

import jax
import jax.numpy as jnp
from jax import lax
from jax.experimental import pallas as pl
from jax.experimental.pallas import tpu as pltpu
from jax.sharding import Mesh
from jax.sharding import PartitionSpec as P

LANES = 128
ANY = pl.BlockSpec(memory_space=pl.ANY)
SMEM = pl.BlockSpec(memory_space=pltpu.SMEM)
VMEM = pl.BlockSpec(memory_space=pltpu.VMEM)
HBM = pl.BlockSpec(memory_space=pltpu.HBM)
ROOM = pltpu.CompilerParams(vmem_limit_bytes=32 * 1024 * 1024)
FULL = pltpu.CompilerParams(vmem_limit_bytes=60 * 1024 * 1024)
PLANE = ("groups", "pair")
WHOLE = ("groups", "ring", "pair")


def hand_kernel(*refs):
    pass


def hand_on(x, *after):
    return pl.pallas_call(
        hand_kernel,
        in_specs=[ANY] * (1 + len(after)),
        out_specs=ANY,
        out_shape=jax.ShapeDtypeStruct(x.shape, x.dtype),
        input_output_aliases={0: 0},
        compiler_params=FULL,
        name="hand",
    )(x, *after)


def pack_kernel(down, up, *refs):
    outs, sems = refs[:-1], refs[-1]
    feats = outs[0].shape[2] - LANES
    copies = []
    for way, out in enumerate(outs):
        share = lax.axis_index("groups") * len(outs) + lax.rem(lax.axis_index("pair") + way, len(outs))
        start = pl.multiple_of(share * feats, LANES)
        tile = pl.multiple_of(lax.rem(share, up.shape[2] // LANES) * LANES, LANES)
        copies.append(pltpu.make_async_copy(down.at[:, :, pl.ds(start, feats)], out.at[:, :, :feats], sems.at[way, 0]))
        copies.append(pltpu.make_async_copy(up.at[:, :, pl.ds(tile, LANES)], out.at[:, :, feats:], sems.at[way, 1]))
    for copy in copies:
        copy.start()
    for copy in copies:
        copy.wait()


def pack(down, up, shares, ways):
    adapters, rank, feats = down.shape
    shape = jax.ShapeDtypeStruct((adapters, rank, feats // shares + LANES), down.dtype)
    return pl.pallas_call(
        pack_kernel,
        in_specs=[HBM, HBM],
        out_specs=[VMEM] * ways,
        out_shape=[shape] * ways,
        scratch_shapes=[pltpu.SemaphoreType.DMA((ways, 2))],
        compiler_params=FULL,
        name="pack",
    )(down, up)


def mate_at(k, sign, groups, pair):
    kg, ky = k // pair, k % pair
    g = lax.rem(lax.axis_index("groups") + sign * kg + groups, groups)
    y = lax.rem(lax.axis_index("pair") + sign * ky + pair, pair)
    return g * pair + y


def spread_kernel(groups, pair, lengths, ids, tok, *refs):
    held, in_sems, out_sems = refs[-3:]
    outs = refs[:-3]
    blocks = lengths.shape[0]
    shares, tall, step = held.shape
    rows = tok.shape[0]
    block = rows // blocks
    mates = [pl.multiple_of(mate_at(k, 1, groups, pair) * step, LANES) for k in range(shares)]
    order = list(range(1, shares)) + [0]

    def read(k, b):
        here = pl.ds(b * block, block)
        return pltpu.make_async_copy(tok.at[here, pl.ds(mates[k], step)], held.at[k, here, :], in_sems.at[k, b])

    for k in order:
        for b in range(blocks):
            read(k, b).start()
    lane = lax.broadcasted_iota(jnp.int32, (tall - rows, step), 1)
    named = jnp.zeros((tall - rows, step), jnp.float32)
    for b in range(blocks):
        named = jnp.where(lane == b, ids[b].astype(jnp.float32), named)
    named = named.astype(held.dtype)
    writes = []

    def write(k, b):
        here = pl.ds(b * block, block if b < blocks else tall - rows)
        writes.append(pltpu.make_async_copy(held.at[k, here, :], outs[k].at[here, :], out_sems.at[k, b]))
        writes[-1].start()

    for k in order:
        held[k, rows:, :] = named
        write(k, blocks)
        for b in range(blocks):
            read(k, b).wait()

            @pl.when(lengths[b] < block)
            def _():
                here = slice(b * block, (b + 1) * block)
                row = lax.broadcasted_iota(jnp.int32, (block, step), 0)
                part = held[k, here, :]
                held[k, here, :] = jnp.where(row < lengths[b], part, jnp.zeros_like(part))

            write(k, b)
    for one in writes:
        one.wait()


def spread(tokens, lengths, ids, groups, pair):
    rows, feats = tokens.shape
    shares = groups * pair
    shape = (rows + 16, feats // shares)
    return pl.pallas_call(
        functools.partial(spread_kernel, groups, pair),
        in_specs=[SMEM, SMEM, ANY],
        out_specs=[ANY] * shares,
        out_shape=[jax.ShapeDtypeStruct(shape, tokens.dtype)] * shares,
        scratch_shapes=[
            pltpu.VMEM((shares,) + shape, tokens.dtype),
            pltpu.SemaphoreType.DMA((shares, lengths.shape[0])),
            pltpu.SemaphoreType.DMA((shares, lengths.shape[0] + 1)),
        ],
        compiler_params=FULL,
        name="spread",
    )(lengths, ids, tokens)


def base_kernel(sides, lengths, tok, key, mine, other, flag_ref, tok_held, key_held, total, tok_sems, key_sems):
    depth, rows = key.shape[0], tok.shape[0]
    chunk = depth // key_sems.shape[0]
    steps = tok_sems.shape[0]
    step = depth // steps

    def key_copy(i):
        here = pl.ds(i * chunk, chunk)
        return pltpu.make_async_copy(key.at[here, :], key_held.at[here, :], key_sems.at[i])

    def tok_copy(i, b):
        here = pl.ds(i * step, step)
        some = pl.ds(b * (rows // tok_sems.shape[1]), rows // tok_sems.shape[1])
        return pltpu.make_async_copy(tok.at[some, here], tok_held.at[some, here], tok_sems.at[i, b])

    flag_ref[...] = jnp.zeros_like(flag_ref)
    for i in range(steps):
        for b in range(tok_sems.shape[1]):
            tok_copy(i, b).start()
        for j in range(step // chunk):
            key_copy(i * (step // chunk) + j).start()
    for i in range(steps):
        for b in range(tok_sems.shape[1]):
            tok_copy(i, b).wait()
        for j in range(step // chunk):
            key_copy(i * (step // chunk) + j).wait()
        here = slice(i * step, (i + 1) * step)
        part = jnp.dot(tok_held[:, here], key_held[here, :], preferred_element_type=jnp.float32)
        if i == 0:
            total[...] = part
        else:
            total[...] += part
    blocks = lengths.shape[0]
    wide = mine.shape[1]
    block = rows // blocks
    row = lax.broadcasted_iota(jnp.int32, (block, wide), 0)
    t = lax.axis_index("tensor")
    for out, side in ((mine, t), (other, lax.rem(t + 1, sides))):
        columns = pl.ds(pl.multiple_of(side * wide, LANES), wide)
        for b in range(blocks):
            here = slice(b * block, (b + 1) * block)
            out[here, :] = jnp.where(row < lengths[b], total[here, columns], 0.0)


def base_halves(tokens, base_key, sides, lengths):
    rows, depth = tokens.shape
    features = base_key.shape[1]
    half = jax.ShapeDtypeStruct((rows, features // sides), jnp.float32)
    steps, chunks = depth // 1024, depth // 256
    return pl.pallas_call(
        functools.partial(base_kernel, sides),
        in_specs=[SMEM, ANY, ANY],
        out_specs=[VMEM] * 3,
        out_shape=[half, half, jax.ShapeDtypeStruct((8, LANES), jnp.float32)],
        scratch_shapes=[
            pltpu.VMEM(tokens.shape, tokens.dtype),
            pltpu.VMEM(base_key.shape, base_key.dtype),
            pltpu.VMEM((rows, features), jnp.float32),
            pltpu.SemaphoreType.DMA((steps, lengths.shape[0])),
            pltpu.SemaphoreType.DMA((chunks,)),
        ],
        cost_estimate=pl.CostEstimate(flops=0, bytes_accessed=0, transcendentals=0),
        compiler_params=FULL,
        name="base",
    )(lengths, tokens, base_key)


def collect_kernel(*refs):
    sems, held, pieces = refs[-1], refs[-2], refs[:-2]
    copies, start = [], 0
    for j, piece in enumerate(pieces):
        copies.append(pltpu.make_async_copy(piece, held.at[pl.ds(start, piece.shape[0])], sems.at[j]))
        start += piece.shape[0]
    for copy in copies:
        copy.start()
    for copy in copies:
        copy.wait()


def collect(pieces):
    count = sum(piece.shape[0] for piece in pieces)
    return pl.pallas_call(
        collect_kernel,
        in_specs=[ANY] * len(pieces),
        out_specs=VMEM,
        out_shape=jax.ShapeDtypeStruct((count,) + pieces[0].shape[1:], pieces[0].dtype),
        scratch_shapes=[pltpu.SemaphoreType.DMA((len(pieces),))],
        compiler_params=ROOM,
        name="collect",
    )(*pieces)


def rank_kernel(ring, pair, rows, shares, owner, held, *refs):
    late, toks, outs = refs[: -1 - 2 * shares], refs[-1 - 2 * shares : -1 - shares], refs[-1 - shares : -1]
    flag = refs[-1]
    flag[...] = jnp.zeros_like(flag)
    rank = held.shape[1]
    per = owner.shape[0] // (ring * pair)
    blocks, _, block = outs[0].shape
    feats = toks[0].shape[1]
    z, y = lax.axis_index("ring"), lax.axis_index("pair")
    lane = lax.broadcasted_iota(jnp.int32, (16, LANES), 1)
    row = lax.broadcasted_iota(jnp.int32, (16, LANES), 0)
    ids = []
    for tok in toks:
        named = tok[rows:, :LANES].astype(jnp.float32)
        ids += [jnp.sum(jnp.where((lane == b) & (row == 0), named, 0.0)).astype(jnp.int32) for b in range(blocks)]
    for i, one in enumerate(ids):
        slot = owner[one]
        chip = slot // per
        local = lax.rem(slot, per)
        away = lax.rem(chip // pair - z + ring, ring)
        way = lax.rem(lax.rem(chip, pair) - y + pair, pair)
        if late:
            half = ring // 2
            near = jnp.where(away == half, 0, away - jnp.where(away > half, 1, 0))
            piece = held[(way * (ring - 1) + near) * per + local]
            for w in range(pair):
                piece = jnp.where((away == half) & (way == w), late[w][local], piece)
        else:
            piece = held[(way * ring + away) * per + local]
        k, b = i // blocks, i % blocks
        part = lax.dot_general(
            piece[:, :feats],
            toks[k][b * block : (b + 1) * block, :],
            (((1,), (1,)), ((), ())),
            preferred_element_type=jnp.float32,
        )
        outs[k][b, :rank, :] = part.astype(outs[k].dtype)
        outs[k][b, rank:, :] = piece[:, feats:]


def rank_parts(owner, toks, held, late, ring, pair, rows, blocks):
    shares, rank = len(toks), held.shape[1]
    return pl.pallas_call(
        functools.partial(rank_kernel, ring, pair, rows, shares),
        in_specs=[SMEM, VMEM] + [VMEM] * (len(late) + shares),
        out_specs=[VMEM] * (shares + 1),
        out_shape=[jax.ShapeDtypeStruct((blocks, 2 * rank, rows // blocks), held.dtype)] * shares
        + [jax.ShapeDtypeStruct((8, LANES), jnp.float32)],
        cost_estimate=pl.CostEstimate(flops=0, bytes_accessed=0, transcendentals=0),
        compiler_params=ROOM,
        name="rank",
    )(owner, held, *late, *toks)


def final_kernel(groups, pair, base_a, base_b, *refs):
    shares = groups * pair
    mine, theirs, out_ref, up = refs[:shares], refs[shares : 2 * shares], refs[-2], refs[-1]
    blocks, tall, block = mine[0].shape
    rank = tall // 2
    tiles = out_ref.shape[1] // LANES
    for b in range(blocks):
        here = slice(b * block, (b + 1) * block)
        total = mine[0][b, :rank, :].astype(jnp.float32)
        for part in mine[1:] + theirs:
            total += part[b, :rank, :].astype(jnp.float32)
        for k in range(shares):
            tile = lax.rem(mate_at(k, 1, groups, pair), tiles)
            up[b, :, pl.ds(pl.multiple_of(tile * LANES, LANES), LANES)] = mine[k][b, rank:, :]
        delta = lax.dot_general(
            total.astype(jnp.bfloat16), up[b], (((0,), (0,)), ((), ())), preferred_element_type=jnp.float32
        )
        out_ref[here, :] = (base_a[here, :] + base_b[here, :] + delta).astype(out_ref.dtype)


def final(mine, theirs, base, groups, pair, dtype):
    blocks, tall, _ = mine[0].shape
    return pl.pallas_call(
        functools.partial(final_kernel, groups, pair),
        in_specs=[VMEM] * (2 + 2 * len(mine)),
        out_specs=VMEM,
        out_shape=jax.ShapeDtypeStruct(base[0].shape, dtype),
        scratch_shapes=[pltpu.VMEM((blocks, tall // 2, base[0].shape[1]), mine[0].dtype)],
        compiler_params=ROOM,
        name="final",
    )(*base, *mine, *theirs)


def body(tokens, base_key, adapter_down, adapter_up, adapter_ids, owner_slot, lengths):
    groups, ring, pair = lax.axis_size("groups"), lax.axis_size("ring"), lax.axis_size("pair")
    sides = lax.axis_size("tensor")
    shares = groups * pair
    rows = tokens.shape[0]
    blocks = lengths.shape[0]

    def across(x):
        return lax.ppermute(x, "tensor", [(i, (i + 1) % sides) for i in range(sides)])

    def along(x, step):
        return lax.ppermute(x, "ring", [(a, (a + step) % ring) for a in range(ring)])

    def first_hops(x):
        return {0: x, ring - 1: along(x, 1), **({1: along(x, -1)} if ring > 2 else {})}

    def in_plane(x, kg, ky):
        pairs = []
        for a in range(groups):
            for b in range(pair):
                pairs.append((a * pair + b, (a + kg) % groups * pair + (b + ky) % pair))
        return lax.ppermute(x, PLANE, pairs)

    def more_hops(held, way, *after):
        for k in range(2, ring // 2 + 1):
            if 2 * k < ring or way % 2 == 0:
                if k == 2:
                    held[ring - 1] = hand_on(held[ring - 1], held[1], *after)
                held[ring - k] = along(held[ring - k + 1], 1)
            if 2 * k < ring or way % 2 == 1:
                if k == 2:
                    held[1] = hand_on(held[1], held[ring - 1], *after)
                held[k] = along(held[k - 1], -1)
        return [held[k] for k in range(ring)]

    packed = pack(jnp.swapaxes(adapter_down, 1, 2), adapter_up, shares, pair)
    slabs = spread(tokens, lengths, adapter_ids.reshape(-1), groups, pair)
    swapped = [
        lax.ppermute(packed[pair - w], "pair", [(a, (a - w) % pair) for a in range(pair)]) for w in range(1, pair)
    ]
    firsts = [first_hops(piece) for piece in [packed[0]] + swapped]
    toks = [slabs[0]] + [in_plane(slabs[k], k // pair, k % pair) for k in range(1, shares)]

    base_mine, base_out, flag = base_halves(tokens, base_key, sides, lengths)
    pieces = [
        more_hops(held, way, flag)
        for way, held in enumerate(firsts)
    ]

    halfway = ring // 2 if ring % 2 == 0 else ring
    held = collect([piece for way in pieces for away, piece in enumerate(way) if away != halfway])
    late = [way[halfway] for way in pieces] if halfway < ring else []
    *parts, ready = rank_parts(owner_slot, toks, held, late, ring, pair, rows, blocks)
    mine = [parts[0]] + [in_plane(parts[k], -(k // pair), -(k % pair)) for k in range(1, shares)]
    theirs = [across(part) for part in mine]
    base_in = across(hand_on(base_out, ready))
    return final(mine, theirs, [base_mine, base_in], groups, pair, tokens.dtype)


def solution(mesh):
    groups, dp, sides = (mesh.shape[name] for name in ("groups", "dp", "tensor"))
    pair = 2 if dp % 2 == 0 else 1
    cut = Mesh(mesh.devices.reshape(groups, dp // pair, pair, sides), ("groups", "ring", "pair", "tensor"))
    stored = ("ring", "pair")
    placed = (
        P(WHOLE, "tensor"),
        P("tensor", None),
        P(stored, "tensor", None),
        P(stored, None, "tensor"),
        P(WHOLE, None),
        P(),
        P(WHOLE),
    )
    return jax.shard_map(body, mesh=cut, in_specs=placed, out_specs=P(WHOLE, "tensor"), check_vma=False)
```

```python
import functools

import jax
import jax.numpy as jnp
from jax import lax
from jax.experimental import pallas as pl
from jax.experimental.pallas import tpu as pltpu
from jax.sharding import Mesh
from jax.sharding import PartitionSpec as P

LANES = 128
ANY = pl.BlockSpec(memory_space=pl.ANY)
SMEM = pl.BlockSpec(memory_space=pltpu.SMEM)
VMEM = pl.BlockSpec(memory_space=pltpu.VMEM)
HBM = pl.BlockSpec(memory_space=pltpu.HBM)
ROOM = pltpu.CompilerParams(vmem_limit_bytes=32 * 1024 * 1024)
FULL = pltpu.CompilerParams(vmem_limit_bytes=60 * 1024 * 1024)
PLANE = ("groups", "pair")
WHOLE = ("groups", "ring", "pair")


def hand_kernel(*refs):
    pass


def hand_on(x, *after):
    return pl.pallas_call(
        hand_kernel,
        in_specs=[ANY] * (1 + len(after)),
        out_specs=ANY,
        out_shape=jax.ShapeDtypeStruct(x.shape, x.dtype),
        input_output_aliases={0: 0},
        compiler_params=FULL,
        name="hand",
    )(x, *after)


def pack_kernel(down, up, *refs):
    outs, sems = refs[:-1], refs[-1]
    feats = outs[0].shape[2] - LANES
    copies = []
    for way, out in enumerate(outs):
        share = lax.axis_index("groups") * len(outs) + lax.rem(lax.axis_index("pair") + way, len(outs))
        start = pl.multiple_of(share * feats, LANES)
        tile = pl.multiple_of(lax.rem(share, up.shape[2] // LANES) * LANES, LANES)
        copies.append(pltpu.make_async_copy(down.at[:, :, pl.ds(start, feats)], out.at[:, :, :feats], sems.at[way, 0]))
        copies.append(pltpu.make_async_copy(up.at[:, :, pl.ds(tile, LANES)], out.at[:, :, feats:], sems.at[way, 1]))
    for copy in copies:
        copy.start()
    for copy in copies:
        copy.wait()


def pack(down, up, shares, ways):
    adapters, rank, feats = down.shape
    shape = jax.ShapeDtypeStruct((adapters, rank, feats // shares + LANES), down.dtype)
    return pl.pallas_call(
        pack_kernel,
        in_specs=[HBM, HBM],
        out_specs=[VMEM] * ways,
        out_shape=[shape] * ways,
        scratch_shapes=[pltpu.SemaphoreType.DMA((ways, 2))],
        compiler_params=FULL,
        name="pack",
    )(down, up)


def mate_at(k, sign, groups, pair):
    kg, ky = k // pair, k % pair
    g = lax.rem(lax.axis_index("groups") + sign * kg + groups, groups)
    y = lax.rem(lax.axis_index("pair") + sign * ky + pair, pair)
    return g * pair + y


def spread_kernel(groups, pair, lengths, ids, tok, *refs):
    held, in_sems, out_sems = refs[-3:]
    outs = refs[:-3]
    blocks = lengths.shape[0]
    shares, tall, step = held.shape
    rows = tok.shape[0]
    block = rows // blocks
    mates = [pl.multiple_of(mate_at(k, 1, groups, pair) * step, LANES) for k in range(shares)]
    order = list(range(1, shares)) + [0]

    def read(k, b):
        here = pl.ds(b * block, block)
        return pltpu.make_async_copy(tok.at[here, pl.ds(mates[k], step)], held.at[k, here, :], in_sems.at[k, b])

    for k in order:
        for b in range(blocks):
            read(k, b).start()
    lane = lax.broadcasted_iota(jnp.int32, (tall - rows, step), 1)
    named = jnp.zeros((tall - rows, step), jnp.float32)
    for b in range(blocks):
        named = jnp.where(lane == b, ids[b].astype(jnp.float32), named)
    named = named.astype(held.dtype)
    writes = []

    def write(k, b):
        here = pl.ds(b * block, block if b < blocks else tall - rows)
        writes.append(pltpu.make_async_copy(held.at[k, here, :], outs[k].at[here, :], out_sems.at[k, b]))
        writes[-1].start()

    for k in order:
        held[k, rows:, :] = named
        write(k, blocks)
        for b in range(blocks):
            read(k, b).wait()

            @pl.when(lengths[b] < block)
            def _():
                here = slice(b * block, (b + 1) * block)
                row = lax.broadcasted_iota(jnp.int32, (block, step), 0)
                part = held[k, here, :]
                held[k, here, :] = jnp.where(row < lengths[b], part, jnp.zeros_like(part))

            write(k, b)
    for one in writes:
        one.wait()


def spread(tokens, lengths, ids, groups, pair):
    rows, feats = tokens.shape
    shares = groups * pair
    shape = (rows + 16, feats // shares)
    return pl.pallas_call(
        functools.partial(spread_kernel, groups, pair),
        in_specs=[SMEM, SMEM, ANY],
        out_specs=[ANY] * shares,
        out_shape=[jax.ShapeDtypeStruct(shape, tokens.dtype)] * shares,
        scratch_shapes=[
            pltpu.VMEM((shares,) + shape, tokens.dtype),
            pltpu.SemaphoreType.DMA((shares, lengths.shape[0])),
            pltpu.SemaphoreType.DMA((shares, lengths.shape[0] + 1)),
        ],
        compiler_params=FULL,
        name="spread",
    )(lengths, ids, tokens)


def base_kernel(sides, lengths, tok, key, mine, other, flag_ref, tok_held, key_held, total, tok_sems, key_sems):
    depth, rows = key.shape[0], tok.shape[0]
    chunk = depth // key_sems.shape[0]
    steps = tok_sems.shape[0]
    step = depth // steps

    def key_copy(i):
        here = pl.ds(i * chunk, chunk)
        return pltpu.make_async_copy(key.at[here, :], key_held.at[here, :], key_sems.at[i])

    def tok_copy(i, b):
        here = pl.ds(i * step, step)
        some = pl.ds(b * (rows // tok_sems.shape[1]), rows // tok_sems.shape[1])
        return pltpu.make_async_copy(tok.at[some, here], tok_held.at[some, here], tok_sems.at[i, b])

    flag_ref[...] = jnp.zeros_like(flag_ref)
    for i in range(steps):
        for b in range(tok_sems.shape[1]):
            tok_copy(i, b).start()
        for j in range(step // chunk):
            key_copy(i * (step // chunk) + j).start()
    for i in range(steps):
        for b in range(tok_sems.shape[1]):
            tok_copy(i, b).wait()
        for j in range(step // chunk):
            key_copy(i * (step // chunk) + j).wait()
        here = slice(i * step, (i + 1) * step)
        part = jnp.dot(tok_held[:, here], key_held[here, :], preferred_element_type=jnp.float32)
        if i == 0:
            total[...] = part
        else:
            total[...] += part
    blocks = lengths.shape[0]
    wide = mine.shape[1]
    block = rows // blocks
    row = lax.broadcasted_iota(jnp.int32, (block, wide), 0)
    t = lax.axis_index("tensor")
    for out, side in ((mine, t), (other, lax.rem(t + 1, sides))):
        columns = pl.ds(pl.multiple_of(side * wide, LANES), wide)
        for b in range(blocks):
            here = slice(b * block, (b + 1) * block)
            out[here, :] = jnp.where(row < lengths[b], total[here, columns], 0.0)


def base_halves(tokens, base_key, sides, lengths):
    rows, depth = tokens.shape
    features = base_key.shape[1]
    half = jax.ShapeDtypeStruct((rows, features // sides), jnp.float32)
    steps, chunks = depth // 1024, depth // 256
    return pl.pallas_call(
        functools.partial(base_kernel, sides),
        in_specs=[SMEM, ANY, ANY],
        out_specs=[VMEM] * 3,
        out_shape=[half, half, jax.ShapeDtypeStruct((8, LANES), jnp.float32)],
        scratch_shapes=[
            pltpu.VMEM(tokens.shape, tokens.dtype),
            pltpu.VMEM(base_key.shape, base_key.dtype),
            pltpu.VMEM((rows, features), jnp.float32),
            pltpu.SemaphoreType.DMA((steps, lengths.shape[0])),
            pltpu.SemaphoreType.DMA((chunks,)),
        ],
        cost_estimate=pl.CostEstimate(flops=0, bytes_accessed=0, transcendentals=0),
        compiler_params=FULL,
        name="base",
    )(lengths, tokens, base_key)


def collect_kernel(*refs):
    sems, held, pieces = refs[-1], refs[-2], refs[:-2]
    copies, start = [], 0
    for j, piece in enumerate(pieces):
        copies.append(pltpu.make_async_copy(piece, held.at[pl.ds(start, piece.shape[0])], sems.at[j]))
        start += piece.shape[0]
    for copy in copies:
        copy.start()
    for copy in copies:
        copy.wait()


def collect(pieces):
    count = sum(piece.shape[0] for piece in pieces)
    return pl.pallas_call(
        collect_kernel,
        in_specs=[ANY] * len(pieces),
        out_specs=VMEM,
        out_shape=jax.ShapeDtypeStruct((count,) + pieces[0].shape[1:], pieces[0].dtype),
        scratch_shapes=[pltpu.SemaphoreType.DMA((len(pieces),))],
        compiler_params=ROOM,
        name="collect",
    )(*pieces)


def rank_kernel(ring, pair, rows, count, owner, held, *refs):
    late, toks, outs = refs[: -1 - 2 * count], refs[-1 - 2 * count : -1 - count], refs[-1 - count : -1]
    flag = refs[-1]
    flag[...] = jnp.zeros_like(flag)
    rank = held.shape[1]
    per = owner.shape[0] // (ring * pair)
    blocks, _, block = outs[0].shape
    feats = toks[0].shape[1]
    z, y = lax.axis_index("ring"), lax.axis_index("pair")
    lane = lax.broadcasted_iota(jnp.int32, (16, LANES), 1)
    row = lax.broadcasted_iota(jnp.int32, (16, LANES), 0)
    ids = []
    for tok in toks:
        named = tok[rows:, :LANES].astype(jnp.float32)
        ids += [jnp.sum(jnp.where((lane == b) & (row == 0), named, 0.0)).astype(jnp.int32) for b in range(blocks)]
    for i, one in enumerate(ids):
        slot = owner[one]
        chip = slot // per
        local = lax.rem(slot, per)
        away = lax.rem(chip // pair - z + ring, ring)
        way = lax.rem(lax.rem(chip, pair) - y + pair, pair)
        at = way * ring + away
        if late:
            missing = (pair - 1) * ring + ring // 2
            piece = held[jnp.where(at == missing, 0, at - jnp.where(at > missing, 1, 0)) * per + local]
            piece = jnp.where(at == missing, late[0][local], piece)
        else:
            piece = held[at * per + local]
        k, b = i // blocks, i % blocks
        part = lax.dot_general(
            piece[:, :feats],
            toks[k][b * block : (b + 1) * block, :],
            (((1,), (1,)), ((), ())),
            preferred_element_type=jnp.float32,
        )
        outs[k][b, :rank, :] = part.astype(outs[k].dtype)
        outs[k][b, rank:, :] = piece[:, feats:]


def rank_parts(owner, toks, held, late, ring, pair, rows, blocks):
    count, rank = len(toks), held.shape[1]
    return pl.pallas_call(
        functools.partial(rank_kernel, ring, pair, rows, count),
        in_specs=[SMEM, VMEM] + [VMEM] * (len(late) + count),
        out_specs=[VMEM] * (count + 1),
        out_shape=[jax.ShapeDtypeStruct((blocks, 2 * rank, rows // blocks), held.dtype)] * count
        + [jax.ShapeDtypeStruct((8, LANES), jnp.float32)],
        cost_estimate=pl.CostEstimate(flops=0, bytes_accessed=0, transcendentals=0),
        compiler_params=ROOM,
        name="rank",
    )(owner, held, *late, *toks)


def final_kernel(groups, pair, base_a, base_b, *refs):
    shares = groups * pair
    mine, theirs, out_ref, up = refs[:shares], refs[shares : 2 * shares], refs[-2], refs[-1]
    blocks, tall, block = mine[0].shape
    rank = tall // 2
    tiles = out_ref.shape[1] // LANES
    for b in range(blocks):
        here = slice(b * block, (b + 1) * block)
        total = mine[0][b, :rank, :].astype(jnp.float32)
        for part in mine[1:] + theirs:
            total += part[b, :rank, :].astype(jnp.float32)
        for k in range(shares):
            tile = lax.rem(mate_at(k, 1, groups, pair), tiles)
            up[b, :, pl.ds(pl.multiple_of(tile * LANES, LANES), LANES)] = mine[k][b, rank:, :]
        delta = lax.dot_general(
            total.astype(jnp.bfloat16), up[b], (((0,), (0,)), ((), ())), preferred_element_type=jnp.float32
        )
        out_ref[here, :] = (base_a[here, :] + base_b[here, :] + delta).astype(out_ref.dtype)


def final(mine, theirs, base, groups, pair, dtype):
    blocks, tall, _ = mine[0].shape
    return pl.pallas_call(
        functools.partial(final_kernel, groups, pair),
        in_specs=[VMEM] * (2 + 2 * len(mine)),
        out_specs=VMEM,
        out_shape=jax.ShapeDtypeStruct(base[0].shape, dtype),
        scratch_shapes=[pltpu.VMEM((blocks, tall // 2, base[0].shape[1]), mine[0].dtype)],
        compiler_params=ROOM,
        name="final",
    )(*base, *mine, *theirs)


def body(tokens, base_key, adapter_down, adapter_up, adapter_ids, owner_slot, lengths):
    groups, ring, pair = lax.axis_size("groups"), lax.axis_size("ring"), lax.axis_size("pair")
    sides = lax.axis_size("tensor")
    shares = groups * pair
    rows = tokens.shape[0]
    blocks = lengths.shape[0]

    def across(x):
        return lax.ppermute(x, "tensor", [(i, (i + 1) % sides) for i in range(sides)])

    def along(x, step):
        return lax.ppermute(x, "ring", [(a, (a + step) % ring) for a in range(ring)])

    def first_hops(x):
        return {0: x, ring - 1: along(x, 1), **({1: along(x, -1)} if ring > 2 else {})}

    def in_plane(x, kg, ky):
        pairs = []
        for a in range(groups):
            for b in range(pair):
                pairs.append((a * pair + b, (a + kg) % groups * pair + (b + ky) % pair))
        return lax.ppermute(x, PLANE, pairs)

    def more_hops(held, way, *after):
        for k in range(2, ring // 2 + 1):
            if 2 * k < ring or way % 2 == 0:
                if k == 2:
                    held[ring - 1] = hand_on(held[ring - 1], held[1], *after)
                held[ring - k] = along(held[ring - k + 1], 1)
            if 2 * k < ring or way % 2 == 1:
                if k == 2:
                    held[1] = hand_on(held[1], held[ring - 1], *after)
                held[k] = along(held[k - 1], -1)
        return [held[k] for k in range(ring)]

    packed = pack(jnp.swapaxes(adapter_down, 1, 2), adapter_up, shares, pair)
    slabs = spread(tokens, lengths, adapter_ids.reshape(-1), groups, pair)
    swapped = [
        lax.ppermute(packed[pair - w], "pair", [(a, (a - w) % pair) for a in range(pair)]) for w in range(1, pair)
    ]
    firsts = [first_hops(piece) for piece in [packed[0]] + swapped]
    toks = [slabs[0]] + [in_plane(slabs[k], k // pair, k % pair) for k in range(1, shares)]

    base_mine, base_out, flag = base_halves(tokens, base_key, sides, lengths)
    pieces = [
        more_hops(held, way, flag)
        for way, held in enumerate(firsts)
    ]

    flat = [piece for way in pieces for piece in way]
    late = [flat.pop((pair - 1) * ring + ring // 2)] if ring % 2 == 0 else []
    held = collect(flat)
    *parts, ready = rank_parts(owner_slot, toks[1:], held, late, ring, pair, rows, blocks)
    own_part = rank_parts(owner_slot, toks[:1], held, late, ring, pair, rows, blocks)[0]
    mine = [own_part] + [in_plane(parts[k - 1], -(k // pair), -(k % pair)) for k in range(1, shares)]
    theirs = [across(part) for part in mine]
    base_in = across(hand_on(base_out, ready))
    return final(mine, theirs, [base_mine, base_in], groups, pair, tokens.dtype)


def solution(mesh):
    groups, dp, sides = (mesh.shape[name] for name in ("groups", "dp", "tensor"))
    pair = 2 if dp % 2 == 0 else 1
    cut = Mesh(mesh.devices.reshape(groups, dp // pair, pair, sides), ("groups", "ring", "pair", "tensor"))
    stored = ("ring", "pair")
    placed = (
        P(WHOLE, "tensor"),
        P("tensor", None),
        P(stored, "tensor", None),
        P(stored, None, "tensor"),
        P(WHOLE, None),
        P(),
        P(WHOLE),
    )
    return jax.shard_map(body, mesh=cut, in_specs=placed, out_specs=P(WHOLE, "tensor"), check_vma=False)
```

```python
import functools

import jax
import jax.numpy as jnp
from jax import lax
from jax.experimental import pallas as pl
from jax.experimental.pallas import tpu as pltpu
from jax.sharding import Mesh
from jax.sharding import PartitionSpec as P

LANES = 128
ANY = pl.BlockSpec(memory_space=pl.ANY)
SMEM = pl.BlockSpec(memory_space=pltpu.SMEM)
VMEM = pl.BlockSpec(memory_space=pltpu.VMEM)
HBM = pl.BlockSpec(memory_space=pltpu.HBM)
ROOM = pltpu.CompilerParams(vmem_limit_bytes=32 * 1024 * 1024)
FULL = pltpu.CompilerParams(vmem_limit_bytes=60 * 1024 * 1024)
PLANE = ("groups", "pair")
WHOLE = ("groups", "ring", "pair")


def hand_kernel(*refs):
    pass


def hand_on(x, *after):
    return pl.pallas_call(
        hand_kernel,
        in_specs=[ANY] * (1 + len(after)),
        out_specs=ANY,
        out_shape=jax.ShapeDtypeStruct(x.shape, x.dtype),
        input_output_aliases={0: 0},
        compiler_params=FULL,
        name="hand",
    )(x, *after)


def pack_kernel(down, up, *refs):
    outs, sems = refs[:-1], refs[-1]
    feats = outs[0].shape[2] - LANES
    copies = []
    for way, out in enumerate(outs):
        share = lax.axis_index("groups") * len(outs) + lax.rem(lax.axis_index("pair") + way, len(outs))
        start = pl.multiple_of(share * feats, LANES)
        tile = pl.multiple_of(lax.rem(share, up.shape[2] // LANES) * LANES, LANES)
        copies.append(pltpu.make_async_copy(down.at[:, :, pl.ds(start, feats)], out.at[:, :, :feats], sems.at[way, 0]))
        copies.append(pltpu.make_async_copy(up.at[:, :, pl.ds(tile, LANES)], out.at[:, :, feats:], sems.at[way, 1]))
    for copy in copies:
        copy.start()
    for copy in copies:
        copy.wait()


def pack(down, up, shares, ways):
    adapters, rank, feats = down.shape
    shape = jax.ShapeDtypeStruct((adapters, rank, feats // shares + LANES), down.dtype)
    return pl.pallas_call(
        pack_kernel,
        in_specs=[HBM, HBM],
        out_specs=[VMEM] * ways,
        out_shape=[shape] * ways,
        scratch_shapes=[pltpu.SemaphoreType.DMA((ways, 2))],
        compiler_params=FULL,
        name="pack",
    )(down, up)


def mate_at(k, sign, groups, pair):
    kg, ky = k // pair, k % pair
    g = lax.rem(lax.axis_index("groups") + sign * kg + groups, groups)
    y = lax.rem(lax.axis_index("pair") + sign * ky + pair, pair)
    return g * pair + y


def spread_kernel(groups, pair, lengths, ids, tok, *refs):
    held, in_sems, out_sems = refs[-3:]
    outs = refs[:-3]
    blocks = lengths.shape[0]
    shares, tall, step = held.shape
    rows = tok.shape[0]
    block = rows // blocks
    mates = [pl.multiple_of(mate_at(k, 1, groups, pair) * step, LANES) for k in range(shares)]
    order = list(range(1, shares)) + [0]

    def read(k, b):
        here = pl.ds(b * block, block)
        return pltpu.make_async_copy(tok.at[here, pl.ds(mates[k], step)], held.at[k, here, :], in_sems.at[k, b])

    for k in order:
        for b in range(blocks):
            read(k, b).start()
    lane = lax.broadcasted_iota(jnp.int32, (tall - rows, step), 1)
    named = jnp.zeros((tall - rows, step), jnp.float32)
    for b in range(blocks):
        named = jnp.where(lane == b, ids[b].astype(jnp.float32), named)
    named = named.astype(held.dtype)
    writes = []

    def write(k, b):
        here = pl.ds(b * block, block if b < blocks else tall - rows)
        writes.append(pltpu.make_async_copy(held.at[k, here, :], outs[k].at[here, :], out_sems.at[k, b]))
        writes[-1].start()

    for k in order:
        held[k, rows:, :] = named
        write(k, blocks)
        for b in range(blocks):
            read(k, b).wait()

            @pl.when(lengths[b] < block)
            def _():
                here = slice(b * block, (b + 1) * block)
                row = lax.broadcasted_iota(jnp.int32, (block, step), 0)
                part = held[k, here, :]
                held[k, here, :] = jnp.where(row < lengths[b], part, jnp.zeros_like(part))

            write(k, b)
    for one in writes:
        one.wait()


def spread(tokens, lengths, ids, groups, pair):
    rows, feats = tokens.shape
    shares = groups * pair
    shape = (rows + 16, feats // shares)
    return pl.pallas_call(
        functools.partial(spread_kernel, groups, pair),
        in_specs=[SMEM, SMEM, ANY],
        out_specs=[ANY] * shares,
        out_shape=[jax.ShapeDtypeStruct(shape, tokens.dtype)] * shares,
        scratch_shapes=[
            pltpu.VMEM((shares,) + shape, tokens.dtype),
            pltpu.SemaphoreType.DMA((shares, lengths.shape[0])),
            pltpu.SemaphoreType.DMA((shares, lengths.shape[0] + 1)),
        ],
        compiler_params=FULL,
        name="spread",
    )(lengths, ids, tokens)


def base_kernel(sides, lengths, tok, key, mine, other, flag_ref, tok_held, key_held, total, tok_sems, key_sems):
    depth, rows = key.shape[0], tok.shape[0]
    chunk = depth // key_sems.shape[0]
    steps = tok_sems.shape[0]
    step = depth // steps

    def key_copy(i):
        here = pl.ds(i * chunk, chunk)
        return pltpu.make_async_copy(key.at[here, :], key_held.at[here, :], key_sems.at[i])

    def tok_copy(i, b):
        here = pl.ds(i * step, step)
        some = pl.ds(b * (rows // tok_sems.shape[1]), rows // tok_sems.shape[1])
        return pltpu.make_async_copy(tok.at[some, here], tok_held.at[some, here], tok_sems.at[i, b])

    flag_ref[...] = jnp.zeros_like(flag_ref)
    for i in range(steps):
        for b in range(tok_sems.shape[1]):
            tok_copy(i, b).start()
        for j in range(step // chunk):
            key_copy(i * (step // chunk) + j).start()
    for i in range(steps):
        for b in range(tok_sems.shape[1]):
            tok_copy(i, b).wait()
        for j in range(step // chunk):
            key_copy(i * (step // chunk) + j).wait()
        here = slice(i * step, (i + 1) * step)
        part = jnp.dot(tok_held[:, here], key_held[here, :], preferred_element_type=jnp.float32)
        if i == 0:
            total[...] = part
        else:
            total[...] += part
    blocks = lengths.shape[0]
    wide = mine.shape[1]
    block = rows // blocks
    row = lax.broadcasted_iota(jnp.int32, (block, wide), 0)
    t = lax.axis_index("tensor")
    for out, side in ((mine, t), (other, lax.rem(t + 1, sides))):
        columns = pl.ds(pl.multiple_of(side * wide, LANES), wide)
        for b in range(blocks):
            here = slice(b * block, (b + 1) * block)
            out[here, :] = jnp.where(row < lengths[b], total[here, columns], 0.0)


def base_halves(tokens, base_key, sides, lengths):
    rows, depth = tokens.shape
    features = base_key.shape[1]
    half = jax.ShapeDtypeStruct((rows, features // sides), jnp.float32)
    steps, chunks = depth // 1024, depth // 256
    return pl.pallas_call(
        functools.partial(base_kernel, sides),
        in_specs=[SMEM, ANY, ANY],
        out_specs=[VMEM] * 3,
        out_shape=[half, half, jax.ShapeDtypeStruct((8, LANES), jnp.float32)],
        scratch_shapes=[
            pltpu.VMEM(tokens.shape, tokens.dtype),
            pltpu.VMEM(base_key.shape, base_key.dtype),
            pltpu.VMEM((rows, features), jnp.float32),
            pltpu.SemaphoreType.DMA((steps, lengths.shape[0])),
            pltpu.SemaphoreType.DMA((chunks,)),
        ],
        cost_estimate=pl.CostEstimate(flops=0, bytes_accessed=0, transcendentals=0),
        compiler_params=FULL,
        name="base",
    )(lengths, tokens, base_key)


def collect_kernel(*refs):
    sems, held, pieces = refs[-1], refs[-2], refs[:-2]
    copies, start = [], 0
    for j, piece in enumerate(pieces):
        copies.append(pltpu.make_async_copy(piece, held.at[pl.ds(start, piece.shape[0])], sems.at[j]))
        start += piece.shape[0]
    for copy in copies:
        copy.start()
    for copy in copies:
        copy.wait()


def collect(pieces):
    count = sum(piece.shape[0] for piece in pieces)
    return pl.pallas_call(
        collect_kernel,
        in_specs=[ANY] * len(pieces),
        out_specs=VMEM,
        out_shape=jax.ShapeDtypeStruct((count,) + pieces[0].shape[1:], pieces[0].dtype),
        scratch_shapes=[pltpu.SemaphoreType.DMA((len(pieces),))],
        compiler_params=ROOM,
        name="collect",
    )(*pieces)


def rank_kernel(ring, pair, rows, count, lates, owner, held, *refs):
    late, toks, outs, flag = refs[:lates], refs[lates : lates + count], refs[-1 - count : -1], refs[-1]
    flag[...] = jnp.zeros_like(flag)
    rank = held.shape[1]
    per = owner.shape[0] // (ring * pair)
    blocks, _, block = outs[0].shape
    feats = toks[0].shape[1]
    z, y = lax.axis_index("ring"), lax.axis_index("pair")
    lane = lax.broadcasted_iota(jnp.int32, (16, LANES), 1)
    row = lax.broadcasted_iota(jnp.int32, (16, LANES), 0)
    ids = []
    for tok in toks:
        named = tok[rows:, :LANES].astype(jnp.float32)
        ids += [jnp.sum(jnp.where((lane == b) & (row == 0), named, 0.0)).astype(jnp.int32) for b in range(blocks)]
    for i, one in enumerate(ids):
        slot = owner[one]
        chip = slot // per
        local = lax.rem(slot, per)
        away = lax.rem(chip // pair - z + ring, ring)
        way = lax.rem(lax.rem(chip, pair) - y + pair, pair)
        if late:
            half = ring // 2
            near = jnp.where(away == half, 0, away - jnp.where(away > half, 1, 0))
            piece = held[(way * (ring - 1) + near) * per + local]
            for w in range(pair):
                piece = jnp.where((away == half) & (way == w), late[w][local], piece)
        else:
            piece = held[(way * ring + away) * per + local]
        k, b = i // blocks, i % blocks
        part = lax.dot_general(
            piece[:, :feats],
            toks[k][b * block : (b + 1) * block, :],
            (((1,), (1,)), ((), ())),
            preferred_element_type=jnp.float32,
        )
        outs[k][b, :rank, :] = part.astype(outs[k].dtype)
        outs[k][b, rank:, :] = piece[:, feats:]


def rank_parts(owner, toks, held, late, ring, pair, rows, blocks, after=()):
    count, rank = len(toks), held.shape[1]
    return pl.pallas_call(
        functools.partial(rank_kernel, ring, pair, rows, count, len(late)),
        in_specs=[SMEM, VMEM] + [VMEM] * (len(late) + count) + [ANY] * len(after),
        out_specs=[VMEM] * (count + 1),
        out_shape=[jax.ShapeDtypeStruct((blocks, 2 * rank, rows // blocks), held.dtype)] * count
        + [jax.ShapeDtypeStruct((8, LANES), jnp.float32)],
        cost_estimate=pl.CostEstimate(flops=0, bytes_accessed=0, transcendentals=0),
        compiler_params=ROOM,
        name="rank",
    )(owner, held, *late, *toks, *after)


def final_kernel(groups, pair, base_a, base_b, *refs):
    shares = groups * pair
    mine, theirs, out_ref, up = refs[:shares], refs[shares : 2 * shares], refs[-2], refs[-1]
    blocks, tall, block = mine[0].shape
    rank = tall // 2
    tiles = out_ref.shape[1] // LANES
    for b in range(blocks):
        here = slice(b * block, (b + 1) * block)
        total = mine[0][b, :rank, :].astype(jnp.float32)
        for part in mine[1:] + theirs:
            total += part[b, :rank, :].astype(jnp.float32)
        for k in range(shares):
            tile = lax.rem(mate_at(k, 1, groups, pair), tiles)
            up[b, :, pl.ds(pl.multiple_of(tile * LANES, LANES), LANES)] = mine[k][b, rank:, :]
        delta = lax.dot_general(
            total.astype(jnp.bfloat16), up[b], (((0,), (0,)), ((), ())), preferred_element_type=jnp.float32
        )
        out_ref[here, :] = (base_a[here, :] + base_b[here, :] + delta).astype(out_ref.dtype)


def final(mine, theirs, base, groups, pair, dtype):
    blocks, tall, _ = mine[0].shape
    return pl.pallas_call(
        functools.partial(final_kernel, groups, pair),
        in_specs=[VMEM] * (2 + 2 * len(mine)),
        out_specs=VMEM,
        out_shape=jax.ShapeDtypeStruct(base[0].shape, dtype),
        scratch_shapes=[pltpu.VMEM((blocks, tall // 2, base[0].shape[1]), mine[0].dtype)],
        compiler_params=ROOM,
        name="final",
    )(*base, *mine, *theirs)


def body(tokens, base_key, adapter_down, adapter_up, adapter_ids, owner_slot, lengths):
    groups, ring, pair = lax.axis_size("groups"), lax.axis_size("ring"), lax.axis_size("pair")
    sides = lax.axis_size("tensor")
    shares = groups * pair
    rows = tokens.shape[0]
    blocks = lengths.shape[0]

    def across(x):
        return lax.ppermute(x, "tensor", [(i, (i + 1) % sides) for i in range(sides)])

    def along(x, step):
        return lax.ppermute(x, "ring", [(a, (a + step) % ring) for a in range(ring)])

    def first_hops(x):
        return {0: x, ring - 1: along(x, 1), **({1: along(x, -1)} if ring > 2 else {})}

    def in_plane(x, kg, ky):
        pairs = []
        for a in range(groups):
            for b in range(pair):
                pairs.append((a * pair + b, (a + kg) % groups * pair + (b + ky) % pair))
        return lax.ppermute(x, PLANE, pairs)

    def more_hops(held, way, *after):
        for k in range(2, ring // 2 + 1):
            if 2 * k < ring or way % 2 == 0:
                if k == 2:
                    held[ring - 1] = hand_on(held[ring - 1], held[1], *after)
                held[ring - k] = along(held[ring - k + 1], 1)
            if 2 * k < ring or way % 2 == 1:
                if k == 2:
                    held[1] = hand_on(held[1], held[ring - 1], *after)
                held[k] = along(held[k - 1], -1)
        return [held[k] for k in range(ring)]

    packed = pack(jnp.swapaxes(adapter_down, 1, 2), adapter_up, shares, pair)
    slabs = spread(tokens, lengths, adapter_ids.reshape(-1), groups, pair)
    swapped = [
        lax.ppermute(packed[pair - w], "pair", [(a, (a - w) % pair) for a in range(pair)]) for w in range(1, pair)
    ]
    firsts = [first_hops(piece) for piece in [packed[0]] + swapped]
    toks = [slabs[0]] * shares
    for k in reversed(range(1, shares)):
        toks[k] = in_plane(slabs[k], k // pair, k % pair)

    base_mine, base_out, flag = base_halves(tokens, base_key, sides, lengths)
    pieces = [
        more_hops(held, way, flag)
        for way, held in enumerate(firsts)
    ]

    halfway = ring // 2 if ring % 2 == 0 else ring
    held = collect([piece for way in pieces for away, piece in enumerate(way) if away != halfway])
    late = [way[halfway] for way in pieces] if halfway < ring else []
    first = [0] + list(reversed(range(2, shares)))
    *parts, ready = rank_parts(owner_slot, [toks[k] for k in first], held, late, ring, pair, rows, blocks)
    mine = [parts[0]] * shares
    for k, part in zip(first[1:], parts[1:]):
        mine[k] = in_plane(part, -(k // pair), -(k % pair))
    last = rank_parts(owner_slot, toks[1:2], held, late, ring, pair, rows, blocks, mine[2:])[0]
    mine[1] = in_plane(last, 0, -1)
    theirs = [across(part) for part in mine]
    base_in = across(hand_on(base_out, ready))
    return final(mine, theirs, [base_mine, base_in], groups, pair, tokens.dtype)


def solution(mesh):
    groups, dp, sides = (mesh.shape[name] for name in ("groups", "dp", "tensor"))
    pair = 2 if dp % 2 == 0 else 1
    cut = Mesh(mesh.devices.reshape(groups, dp // pair, pair, sides), ("groups", "ring", "pair", "tensor"))
    stored = ("ring", "pair")
    placed = (
        P(WHOLE, "tensor"),
        P("tensor", None),
        P(stored, "tensor", None),
        P(stored, None, "tensor"),
        P(WHOLE, None),
        P(),
        P(WHOLE),
    )
    return jax.shard_map(body, mesh=cut, in_specs=placed, out_specs=P(WHOLE, "tensor"), check_vma=False)
```

```python
import functools

import jax
import jax.numpy as jnp
from jax import lax
from jax.experimental import pallas as pl
from jax.experimental.pallas import tpu as pltpu
from jax.sharding import Mesh
from jax.sharding import PartitionSpec as P

LANES = 128
ANY = pl.BlockSpec(memory_space=pl.ANY)
SMEM = pl.BlockSpec(memory_space=pltpu.SMEM)
VMEM = pl.BlockSpec(memory_space=pltpu.VMEM)
HBM = pl.BlockSpec(memory_space=pltpu.HBM)
ROOM = pltpu.CompilerParams(vmem_limit_bytes=32 * 1024 * 1024)
FULL = pltpu.CompilerParams(vmem_limit_bytes=60 * 1024 * 1024)
PLANE = ("groups", "pair")
WHOLE = ("groups", "ring", "pair")


def hand_kernel(*refs):
    pass


def hand_on(x, *after):
    return pl.pallas_call(
        hand_kernel,
        in_specs=[ANY] * (1 + len(after)),
        out_specs=ANY,
        out_shape=jax.ShapeDtypeStruct(x.shape, x.dtype),
        input_output_aliases={0: 0},
        compiler_params=FULL,
        name="hand",
    )(x, *after)


def pack_kernel(down, up, *refs):
    outs, sems = refs[:-1], refs[-1]
    feats = outs[0].shape[2] - LANES
    copies = []
    for way, out in enumerate(outs):
        share = lax.axis_index("groups") * len(outs) + lax.rem(lax.axis_index("pair") + way, len(outs))
        start = pl.multiple_of(share * feats, LANES)
        tile = pl.multiple_of(lax.rem(share, up.shape[2] // LANES) * LANES, LANES)
        copies.append(pltpu.make_async_copy(down.at[:, :, pl.ds(start, feats)], out.at[:, :, :feats], sems.at[way, 0]))
        copies.append(pltpu.make_async_copy(up.at[:, :, pl.ds(tile, LANES)], out.at[:, :, feats:], sems.at[way, 1]))
    for copy in copies:
        copy.start()
    for copy in copies:
        copy.wait()


def pack(down, up, shares, ways):
    adapters, rank, feats = down.shape
    shape = jax.ShapeDtypeStruct((adapters, rank, feats // shares + LANES), down.dtype)
    return pl.pallas_call(
        pack_kernel,
        in_specs=[HBM, HBM],
        out_specs=[VMEM] * ways,
        out_shape=[shape] * ways,
        scratch_shapes=[pltpu.SemaphoreType.DMA((ways, 2))],
        compiler_params=FULL,
        name="pack",
    )(down, up)


def mate_at(k, sign, groups, pair):
    kg, ky = k // pair, k % pair
    g = lax.rem(lax.axis_index("groups") + sign * kg + groups, groups)
    y = lax.rem(lax.axis_index("pair") + sign * ky + pair, pair)
    return g * pair + y


def spread_kernel(groups, pair, lengths, ids, tok, *refs):
    held, in_sems, out_sems = refs[-3:]
    outs = refs[:-3]
    blocks = lengths.shape[0]
    shares, tall, step = held.shape
    rows = tok.shape[0]
    block = rows // blocks
    mates = [pl.multiple_of(mate_at(k, 1, groups, pair) * step, LANES) for k in range(shares)]
    order = list(range(1, shares)) + [0]

    def read(k, b):
        here = pl.ds(b * block, block)
        return pltpu.make_async_copy(tok.at[here, pl.ds(mates[k], step)], held.at[k, here, :], in_sems.at[k, b])

    for k in order:
        for b in range(blocks):
            read(k, b).start()
    lane = lax.broadcasted_iota(jnp.int32, (tall - rows, step), 1)
    named = jnp.zeros((tall - rows, step), jnp.float32)
    for b in range(blocks):
        named = jnp.where(lane == b, ids[b].astype(jnp.float32), named)
    named = named.astype(held.dtype)
    writes = []

    def write(k, b):
        here = pl.ds(b * block, block if b < blocks else tall - rows)
        writes.append(pltpu.make_async_copy(held.at[k, here, :], outs[k].at[here, :], out_sems.at[k, b]))
        writes[-1].start()

    for k in order:
        held[k, rows:, :] = named
        write(k, blocks)
        for b in range(blocks):
            read(k, b).wait()

            @pl.when(lengths[b] < block)
            def _():
                here = slice(b * block, (b + 1) * block)
                row = lax.broadcasted_iota(jnp.int32, (block, step), 0)
                part = held[k, here, :]
                held[k, here, :] = jnp.where(row < lengths[b], part, jnp.zeros_like(part))

            write(k, b)
    for one in writes:
        one.wait()


def spread(tokens, lengths, ids, groups, pair):
    rows, feats = tokens.shape
    shares = groups * pair
    shape = (rows + 16, feats // shares)
    return pl.pallas_call(
        functools.partial(spread_kernel, groups, pair),
        in_specs=[SMEM, SMEM, ANY],
        out_specs=[ANY] * shares,
        out_shape=[jax.ShapeDtypeStruct(shape, tokens.dtype)] * shares,
        scratch_shapes=[
            pltpu.VMEM((shares,) + shape, tokens.dtype),
            pltpu.SemaphoreType.DMA((shares, lengths.shape[0])),
            pltpu.SemaphoreType.DMA((shares, lengths.shape[0] + 1)),
        ],
        compiler_params=FULL,
        name="spread",
    )(lengths, ids, tokens)


def base_kernel(sides, lengths, tok, key, mine, other, flag_ref, tok_held, key_held, total, tok_sems, key_sems):
    depth, rows = key.shape[0], tok.shape[0]
    chunk = depth // key_sems.shape[0]
    steps = tok_sems.shape[0]
    step = depth // steps

    def key_copy(i):
        here = pl.ds(i * chunk, chunk)
        return pltpu.make_async_copy(key.at[here, :], key_held.at[here, :], key_sems.at[i])

    def tok_copy(i, b):
        here = pl.ds(i * step, step)
        some = pl.ds(b * (rows // tok_sems.shape[1]), rows // tok_sems.shape[1])
        return pltpu.make_async_copy(tok.at[some, here], tok_held.at[some, here], tok_sems.at[i, b])

    flag_ref[...] = jnp.zeros_like(flag_ref)
    for i in range(steps):
        for b in range(tok_sems.shape[1]):
            tok_copy(i, b).start()
        for j in range(step // chunk):
            key_copy(i * (step // chunk) + j).start()
    for i in range(steps):
        for b in range(tok_sems.shape[1]):
            tok_copy(i, b).wait()
        for j in range(step // chunk):
            key_copy(i * (step // chunk) + j).wait()
        here = slice(i * step, (i + 1) * step)
        part = jnp.dot(tok_held[:, here], key_held[here, :], preferred_element_type=jnp.float32)
        if i == 0:
            total[...] = part
        else:
            total[...] += part
    blocks = lengths.shape[0]
    wide = mine.shape[1]
    block = rows // blocks
    row = lax.broadcasted_iota(jnp.int32, (block, wide), 0)
    t = lax.axis_index("tensor")
    for out, side in ((mine, t), (other, lax.rem(t + 1, sides))):
        columns = pl.ds(pl.multiple_of(side * wide, LANES), wide)
        for b in range(blocks):
            here = slice(b * block, (b + 1) * block)
            out[here, :] = jnp.where(row < lengths[b], total[here, columns], 0.0)


def base_halves(tokens, base_key, sides, lengths):
    rows, depth = tokens.shape
    features = base_key.shape[1]
    half = jax.ShapeDtypeStruct((rows, features // sides), jnp.float32)
    steps, chunks = depth // 1024, depth // 256
    return pl.pallas_call(
        functools.partial(base_kernel, sides),
        in_specs=[SMEM, ANY, ANY],
        out_specs=[VMEM] * 3,
        out_shape=[half, half, jax.ShapeDtypeStruct((8, LANES), jnp.float32)],
        scratch_shapes=[
            pltpu.VMEM(tokens.shape, tokens.dtype),
            pltpu.VMEM(base_key.shape, base_key.dtype),
            pltpu.VMEM((rows, features), jnp.float32),
            pltpu.SemaphoreType.DMA((steps, lengths.shape[0])),
            pltpu.SemaphoreType.DMA((chunks,)),
        ],
        cost_estimate=pl.CostEstimate(flops=0, bytes_accessed=0, transcendentals=0),
        compiler_params=FULL,
        name="base",
    )(lengths, tokens, base_key)


def collect_kernel(*refs):
    sems, held, pieces = refs[-1], refs[-2], refs[:-2]
    copies, start = [], 0
    for j, piece in enumerate(pieces):
        copies.append(pltpu.make_async_copy(piece, held.at[pl.ds(start, piece.shape[0])], sems.at[j]))
        start += piece.shape[0]
    for copy in copies:
        copy.start()
    for copy in copies:
        copy.wait()


def collect(pieces):
    count = sum(piece.shape[0] for piece in pieces)
    return pl.pallas_call(
        collect_kernel,
        in_specs=[ANY] * len(pieces),
        out_specs=VMEM,
        out_shape=jax.ShapeDtypeStruct((count,) + pieces[0].shape[1:], pieces[0].dtype),
        scratch_shapes=[pltpu.SemaphoreType.DMA((len(pieces),))],
        compiler_params=ROOM,
        name="collect",
    )(*pieces)


def rank_kernel(ring, pair, rows, shares, owner, held, *refs):
    late, toks, outs = refs[: -2 * shares], refs[-2 * shares : -shares], refs[-shares:]
    rank = held.shape[1]
    per = owner.shape[0] // (ring * pair)
    blocks, _, block = outs[0].shape
    feats = toks[0].shape[1]
    z, y = lax.axis_index("ring"), lax.axis_index("pair")
    lane = lax.broadcasted_iota(jnp.int32, (16, LANES), 1)
    row = lax.broadcasted_iota(jnp.int32, (16, LANES), 0)
    ids = []
    for tok in toks:
        named = tok[rows:, :LANES].astype(jnp.float32)
        ids += [jnp.sum(jnp.where((lane == b) & (row == 0), named, 0.0)).astype(jnp.int32) for b in range(blocks)]
    for i, one in enumerate(ids):
        slot = owner[one]
        chip = slot // per
        local = lax.rem(slot, per)
        away = lax.rem(chip // pair - z + ring, ring)
        way = lax.rem(lax.rem(chip, pair) - y + pair, pair)
        if late:
            half = ring // 2
            near = jnp.where(away == half, 0, away - jnp.where(away > half, 1, 0))
            piece = held[(way * (ring - 1) + near) * per + local]
            for w in range(pair):
                piece = jnp.where((away == half) & (way == w), late[w][local], piece)
        else:
            piece = held[(way * ring + away) * per + local]
        k, b = i // blocks, i % blocks
        part = lax.dot_general(
            piece[:, :feats],
            toks[k][b * block : (b + 1) * block, :],
            (((1,), (1,)), ((), ())),
            preferred_element_type=jnp.float32,
        )
        outs[k][b, :rank, :] = part.astype(outs[k].dtype)
        outs[k][b, rank:, :] = piece[:, feats:]


def rank_parts(owner, toks, held, late, ring, pair, rows, blocks):
    shares, rank = len(toks), held.shape[1]
    return pl.pallas_call(
        functools.partial(rank_kernel, ring, pair, rows, shares),
        in_specs=[SMEM, VMEM] + [VMEM] * (len(late) + shares),
        out_specs=[VMEM] * shares,
        out_shape=[jax.ShapeDtypeStruct((blocks, 2 * rank, rows // blocks), held.dtype)] * shares,
        cost_estimate=pl.CostEstimate(flops=0, bytes_accessed=0, transcendentals=0),
        compiler_params=ROOM,
        name="rank",
    )(owner, held, *late, *toks)


def final_kernel(groups, pair, base_a, base_b, *refs):
    shares = groups * pair
    mine, theirs, out_ref, up = refs[:shares], refs[shares : 2 * shares], refs[-2], refs[-1]
    blocks, tall, block = mine[0].shape
    rank = tall // 2
    tiles = out_ref.shape[1] // LANES
    for b in range(blocks):
        here = slice(b * block, (b + 1) * block)
        total = mine[0][b, :rank, :].astype(jnp.float32)
        for part in mine[1:] + theirs:
            total += part[b, :rank, :].astype(jnp.float32)
        for k in range(shares):
            tile = lax.rem(mate_at(k, 1, groups, pair), tiles)
            up[b, :, pl.ds(pl.multiple_of(tile * LANES, LANES), LANES)] = mine[k][b, rank:, :]
        delta = lax.dot_general(
            total.astype(jnp.bfloat16), up[b], (((0,), (0,)), ((), ())), preferred_element_type=jnp.float32
        )
        out_ref[here, :] = (base_a[here, :] + base_b[here, :] + delta).astype(out_ref.dtype)


def final(mine, theirs, base, groups, pair, dtype):
    blocks, tall, _ = mine[0].shape
    return pl.pallas_call(
        functools.partial(final_kernel, groups, pair),
        in_specs=[VMEM] * (2 + 2 * len(mine)),
        out_specs=VMEM,
        out_shape=jax.ShapeDtypeStruct(base[0].shape, dtype),
        scratch_shapes=[pltpu.VMEM((blocks, tall // 2, base[0].shape[1]), mine[0].dtype)],
        compiler_params=ROOM,
        name="final",
    )(*base, *mine, *theirs)


def body(tokens, base_key, adapter_down, adapter_up, adapter_ids, owner_slot, lengths):
    groups, ring, pair = lax.axis_size("groups"), lax.axis_size("ring"), lax.axis_size("pair")
    sides = lax.axis_size("tensor")
    shares = groups * pair
    rows = tokens.shape[0]
    blocks = lengths.shape[0]

    def across(x):
        return lax.ppermute(x, "tensor", [(i, (i + 1) % sides) for i in range(sides)])

    def along(x, step):
        return lax.ppermute(x, "ring", [(a, (a + step) % ring) for a in range(ring)])

    def first_hops(x):
        return {0: x, ring - 1: along(x, 1), **({1: along(x, -1)} if ring > 2 else {})}

    def in_plane(x, kg, ky):
        pairs = []
        for a in range(groups):
            for b in range(pair):
                pairs.append((a * pair + b, (a + kg) % groups * pair + (b + ky) % pair))
        return lax.ppermute(x, PLANE, pairs)

    def more_hops(held, way, *after):
        for k in range(2, ring // 2 + 1):
            if 2 * k < ring or way % 2 == 0:
                if k == 2:
                    held[ring - 1] = hand_on(held[ring - 1], held[1], *after)
                held[ring - k] = along(held[ring - k + 1], 1)
            if 2 * k < ring or way % 2 == 1:
                if k == 2:
                    held[1] = hand_on(held[1], held[ring - 1], *after)
                held[k] = along(held[k - 1], -1)
        return [held[k] for k in range(ring)]

    packed = pack(jnp.swapaxes(adapter_down, 1, 2), adapter_up, shares, pair)
    slabs = spread(tokens, lengths, adapter_ids.reshape(-1), groups, pair)
    swapped = [
        lax.ppermute(packed[pair - w], "pair", [(a, (a - w) % pair) for a in range(pair)]) for w in range(1, pair)
    ]
    firsts = [first_hops(piece) for piece in [packed[0]] + swapped]
    toks = [slabs[0]] + [in_plane(slabs[k], k // pair, k % pair) for k in range(1, shares)]

    base_mine, base_out, flag = base_halves(tokens, base_key, sides, lengths)
    pieces = [
        more_hops(held, way, flag)
        for way, held in enumerate(firsts)
    ]

    halfway = ring // 2 if ring % 2 == 0 else ring
    held = collect([piece for way in pieces for away, piece in enumerate(way) if away != halfway])
    late = [way[halfway] for way in pieces] if halfway < ring else []
    parts = rank_parts(owner_slot, toks, held, late, ring, pair, rows, blocks)
    mine = [parts[0]] + [in_plane(parts[k], -(k // pair), -(k % pair)) for k in range(1, shares)]
    theirs = [across(part) for part in mine]
    base_in = across(base_out)
    return final(mine, theirs, [base_mine, base_in], groups, pair, tokens.dtype)


def solution(mesh):
    groups, dp, sides = (mesh.shape[name] for name in ("groups", "dp", "tensor"))
    pair = 2 if dp % 2 == 0 else 1
    cut = Mesh(mesh.devices.reshape(groups, dp // pair, pair, sides), ("groups", "ring", "pair", "tensor"))
    stored = ("ring", "pair")
    placed = (
        P(WHOLE, "tensor"),
        P("tensor", None),
        P(stored, "tensor", None),
        P(stored, None, "tensor"),
        P(WHOLE, None),
        P(),
        P(WHOLE),
    )
    return jax.shard_map(body, mesh=cut, in_specs=placed, out_specs=P(WHOLE, "tensor"), check_vma=False)
```

```python
import functools

import jax
import jax.numpy as jnp
from jax import lax
from jax.experimental import pallas as pl
from jax.experimental.pallas import tpu as pltpu
from jax.sharding import Mesh
from jax.sharding import PartitionSpec as P

LANES = 128
ANY = pl.BlockSpec(memory_space=pl.ANY)
SMEM = pl.BlockSpec(memory_space=pltpu.SMEM)
VMEM = pl.BlockSpec(memory_space=pltpu.VMEM)
HBM = pl.BlockSpec(memory_space=pltpu.HBM)
ROOM = pltpu.CompilerParams(vmem_limit_bytes=32 * 1024 * 1024)
FULL = pltpu.CompilerParams(vmem_limit_bytes=60 * 1024 * 1024)
PLANE = ("groups", "pair")
WHOLE = ("groups", "ring", "pair")


def hand_kernel(*refs):
    pass


def hand_on(x, *after, spec=ANY):
    return pl.pallas_call(
        hand_kernel,
        in_specs=[ANY] + [spec] * len(after),
        out_specs=ANY,
        out_shape=jax.ShapeDtypeStruct(x.shape, x.dtype),
        input_output_aliases={0: 0},
        compiler_params=FULL,
        name="hand",
    )(x, *after)


def pack_kernel(down, up, *refs):
    outs, sems = refs[:-1], refs[-1]
    feats = outs[0].shape[2] - LANES
    copies = []
    for way, out in enumerate(outs):
        share = lax.axis_index("groups") * len(outs) + lax.rem(lax.axis_index("pair") + way, len(outs))
        start = pl.multiple_of(share * feats, LANES)
        tile = pl.multiple_of(lax.rem(share, up.shape[2] // LANES) * LANES, LANES)
        copies.append(pltpu.make_async_copy(down.at[:, :, pl.ds(start, feats)], out.at[:, :, :feats], sems.at[way, 0]))
        copies.append(pltpu.make_async_copy(up.at[:, :, pl.ds(tile, LANES)], out.at[:, :, feats:], sems.at[way, 1]))
    for copy in copies:
        copy.start()
    for copy in copies:
        copy.wait()


def pack(down, up, shares, ways):
    adapters, rank, feats = down.shape
    shape = jax.ShapeDtypeStruct((adapters, rank, feats // shares + LANES), down.dtype)
    return pl.pallas_call(
        pack_kernel,
        in_specs=[HBM, HBM],
        out_specs=[VMEM] * ways,
        out_shape=[shape] * ways,
        scratch_shapes=[pltpu.SemaphoreType.DMA((ways, 2))],
        compiler_params=FULL,
        name="pack",
    )(down, up)


def mate_at(k, sign, groups, pair):
    kg, ky = k // pair, k % pair
    g = lax.rem(lax.axis_index("groups") + sign * kg + groups, groups)
    y = lax.rem(lax.axis_index("pair") + sign * ky + pair, pair)
    return g * pair + y


def named_rows(ids, shape):
    lane = lax.broadcasted_iota(jnp.int32, shape, 1)
    named = jnp.zeros(shape, jnp.float32)
    for b in range(ids.shape[0]):
        named = jnp.where(lane == b, ids[b].astype(jnp.float32), named)
    return named


def spread_kernel(groups, pair, lengths, ids, tok, *refs):
    held, in_sems, out_sems = refs[-3:]
    outs = refs[:-3]
    blocks = lengths.shape[0]
    sent, tall, step = held.shape
    shares = sent + 1
    rows = tok.shape[0]
    block = rows // blocks
    mates = [pl.multiple_of(mate_at(k, 1, groups, pair) * step, LANES) for k in range(shares)]
    order = list(range(1, shares))

    def read(k, b):
        here = pl.ds(b * block, block)
        return pltpu.make_async_copy(tok.at[here, pl.ds(mates[k], step)], held.at[k - 1, here, :], in_sems.at[k - 1, b])

    for k in order:
        for b in range(blocks):
            read(k, b).start()
    named = named_rows(ids, (tall - rows, step)).astype(held.dtype)
    writes = []

    def write(k, b):
        here = pl.ds(b * block, block if b < blocks else tall - rows)
        writes.append(pltpu.make_async_copy(held.at[k - 1, here, :], outs[k - 1].at[here, :], out_sems.at[k - 1, b]))
        writes[-1].start()

    for k in order:
        held[k - 1, rows:, :] = named
        write(k, blocks)
        for b in range(blocks):
            read(k, b).wait()

            @pl.when(lengths[b] < block)
            def _():
                here = slice(b * block, (b + 1) * block)
                row = lax.broadcasted_iota(jnp.int32, (block, step), 0)
                part = held[k - 1, here, :]
                held[k - 1, here, :] = jnp.where(row < lengths[b], part, jnp.zeros_like(part))

            write(k, b)
    for one in writes:
        one.wait()


def spread(tokens, lengths, ids, groups, pair):
    rows, feats = tokens.shape
    shares = groups * pair
    shape = (rows + 16, feats // shares)
    return pl.pallas_call(
        functools.partial(spread_kernel, groups, pair),
        in_specs=[SMEM, SMEM, ANY],
        out_specs=[ANY] * (shares - 1),
        out_shape=[jax.ShapeDtypeStruct(shape, tokens.dtype)] * (shares - 1),
        scratch_shapes=[
            pltpu.VMEM((shares - 1,) + shape, tokens.dtype),
            pltpu.SemaphoreType.DMA((shares - 1, lengths.shape[0])),
            pltpu.SemaphoreType.DMA((shares - 1, lengths.shape[0] + 1)),
        ],
        compiler_params=FULL,
        name="spread",
    )(lengths, ids, tokens)


def base_kernel(sides, groups, pair, lengths, ids, tok, key, mine, other, flag_ref, slab, tok_held, key_held, total, tok_sems, key_sems):
    depth, rows = key.shape[0], tok.shape[0]
    chunk = depth // key_sems.shape[0]
    steps = tok_sems.shape[0]
    step = depth // steps

    def key_copy(i):
        here = pl.ds(i * chunk, chunk)
        return pltpu.make_async_copy(key.at[here, :], key_held.at[here, :], key_sems.at[i])

    def tok_copy(i, b):
        here = pl.ds(i * step, step)
        some = pl.ds(b * (rows // tok_sems.shape[1]), rows // tok_sems.shape[1])
        return pltpu.make_async_copy(tok.at[some, here], tok_held.at[some, here], tok_sems.at[i, b])

    flag_ref[...] = jnp.zeros_like(flag_ref)
    for i in range(steps):
        for b in range(tok_sems.shape[1]):
            tok_copy(i, b).start()
        for j in range(step // chunk):
            key_copy(i * (step // chunk) + j).start()
    for i in range(steps):
        for b in range(tok_sems.shape[1]):
            tok_copy(i, b).wait()
        for j in range(step // chunk):
            key_copy(i * (step // chunk) + j).wait()
        here = slice(i * step, (i + 1) * step)
        part = jnp.dot(tok_held[:, here], key_held[here, :], preferred_element_type=jnp.float32)
        if i == 0:
            total[...] = part
        else:
            total[...] += part
    blocks = lengths.shape[0]
    wide = mine.shape[1]
    block = rows // blocks
    feats = slab.shape[1]
    own = pl.ds(pl.multiple_of(mate_at(0, 1, groups, pair) * feats, LANES), feats)
    row = lax.broadcasted_iota(jnp.int32, (block, feats), 0)
    for b in range(blocks):
        here = slice(b * block, (b + 1) * block)
        some = tok_held[here, own]
        slab[here, :] = jnp.where(row < lengths[b], some, jnp.zeros_like(some))
    slab[rows:, :] = named_rows(ids, (slab.shape[0] - rows, feats)).astype(slab.dtype)
    row = lax.broadcasted_iota(jnp.int32, (block, wide), 0)
    t = lax.axis_index("tensor")
    for out, side in ((mine, t), (other, lax.rem(t + 1, sides))):
        columns = pl.ds(pl.multiple_of(side * wide, LANES), wide)
        for b in range(blocks):
            here = slice(b * block, (b + 1) * block)
            out[here, :] = jnp.where(row < lengths[b], total[here, columns], 0.0)


def base_halves(tokens, base_key, sides, lengths, ids, groups, pair):
    rows, depth = tokens.shape
    features = base_key.shape[1]
    half = jax.ShapeDtypeStruct((rows, features // sides), jnp.float32)
    steps, chunks = depth // 1024, depth // 256
    return pl.pallas_call(
        functools.partial(base_kernel, sides, groups, pair),
        in_specs=[SMEM, SMEM, ANY, ANY],
        out_specs=[VMEM] * 4,
        out_shape=[
            half,
            half,
            jax.ShapeDtypeStruct((8, LANES), jnp.float32),
            jax.ShapeDtypeStruct((rows + 16, depth // (groups * pair)), tokens.dtype),
        ],
        scratch_shapes=[
            pltpu.VMEM(tokens.shape, tokens.dtype),
            pltpu.VMEM(base_key.shape, base_key.dtype),
            pltpu.VMEM((rows, features), jnp.float32),
            pltpu.SemaphoreType.DMA((steps, lengths.shape[0])),
            pltpu.SemaphoreType.DMA((chunks,)),
        ],
        cost_estimate=pl.CostEstimate(flops=0, bytes_accessed=0, transcendentals=0),
        compiler_params=FULL,
        name="base",
    )(lengths, ids, tokens, base_key)


def collect_kernel(*refs):
    sems, held, pieces = refs[-1], refs[-2], refs[:-2]
    copies, start = [], 0
    for j, piece in enumerate(pieces):
        copies.append(pltpu.make_async_copy(piece, held.at[pl.ds(start, piece.shape[0])], sems.at[j]))
        start += piece.shape[0]
    for copy in copies:
        copy.start()
    for copy in copies:
        copy.wait()


def collect(pieces):
    count = sum(piece.shape[0] for piece in pieces)
    return pl.pallas_call(
        collect_kernel,
        in_specs=[ANY] * len(pieces),
        out_specs=VMEM,
        out_shape=jax.ShapeDtypeStruct((count,) + pieces[0].shape[1:], pieces[0].dtype),
        scratch_shapes=[pltpu.SemaphoreType.DMA((len(pieces),))],
        compiler_params=ROOM,
        name="collect",
    )(*pieces)


def rank_kernel(ring, pair, rows, shares, owner, held, *refs):
    late, toks, outs = refs[: -1 - 2 * shares], refs[-1 - 2 * shares : -1 - shares], refs[-1 - shares : -1]
    flag = refs[-1]
    flag[...] = jnp.zeros_like(flag)
    rank = held.shape[1]
    per = owner.shape[0] // (ring * pair)
    blocks, _, block = outs[0].shape
    feats = toks[0].shape[1]
    z, y = lax.axis_index("ring"), lax.axis_index("pair")
    lane = lax.broadcasted_iota(jnp.int32, (16, LANES), 1)
    row = lax.broadcasted_iota(jnp.int32, (16, LANES), 0)
    ids = []
    for tok in toks:
        named = tok[rows:, :LANES].astype(jnp.float32)
        ids += [jnp.sum(jnp.where((lane == b) & (row == 0), named, 0.0)).astype(jnp.int32) for b in range(blocks)]
    for i, one in enumerate(ids):
        slot = owner[one]
        chip = slot // per
        local = lax.rem(slot, per)
        away = lax.rem(chip // pair - z + ring, ring)
        way = lax.rem(lax.rem(chip, pair) - y + pair, pair)
        if late:
            half = ring // 2
            near = jnp.where(away == half, 0, away - jnp.where(away > half, 1, 0))
            piece = held[(way * (ring - 1) + near) * per + local]
            for w in range(pair):
                piece = jnp.where((away == half) & (way == w), late[w][local], piece)
        else:
            piece = held[(way * ring + away) * per + local]
        k, b = i // blocks, i % blocks
        part = lax.dot_general(
            piece[:, :feats],
            toks[k][b * block : (b + 1) * block, :],
            (((1,), (1,)), ((), ())),
            preferred_element_type=jnp.float32,
        )
        outs[k][b, :rank, :] = part.astype(outs[k].dtype)
        outs[k][b, rank:, :] = piece[:, feats:]


def rank_parts(owner, toks, held, late, ring, pair, rows, blocks):
    shares, rank = len(toks), held.shape[1]
    return pl.pallas_call(
        functools.partial(rank_kernel, ring, pair, rows, shares),
        in_specs=[SMEM, VMEM] + [VMEM] * (len(late) + shares),
        out_specs=[VMEM] * (shares + 1),
        out_shape=[jax.ShapeDtypeStruct((blocks, 2 * rank, rows // blocks), held.dtype)] * shares
        + [jax.ShapeDtypeStruct((8, LANES), jnp.float32)],
        cost_estimate=pl.CostEstimate(flops=0, bytes_accessed=0, transcendentals=0),
        compiler_params=ROOM,
        name="rank",
    )(owner, held, *late, *toks)


def final_kernel(groups, pair, base_a, base_b, *refs):
    shares = groups * pair
    mine, theirs, out_ref, up = refs[:shares], refs[shares : 2 * shares], refs[-2], refs[-1]
    blocks, tall, block = mine[0].shape
    rank = tall // 2
    tiles = out_ref.shape[1] // LANES
    for b in range(blocks):
        here = slice(b * block, (b + 1) * block)
        total = mine[0][b, :rank, :].astype(jnp.float32)
        for part in mine[1:] + theirs:
            total += part[b, :rank, :].astype(jnp.float32)
        for k in range(shares):
            tile = lax.rem(mate_at(k, 1, groups, pair), tiles)
            up[b, :, pl.ds(pl.multiple_of(tile * LANES, LANES), LANES)] = mine[k][b, rank:, :]
        delta = lax.dot_general(
            total.astype(jnp.bfloat16), up[b], (((0,), (0,)), ((), ())), preferred_element_type=jnp.float32
        )
        out_ref[here, :] = (base_a[here, :] + base_b[here, :] + delta).astype(out_ref.dtype)


def final(mine, theirs, base, groups, pair, dtype):
    blocks, tall, _ = mine[0].shape
    return pl.pallas_call(
        functools.partial(final_kernel, groups, pair),
        in_specs=[VMEM] * (2 + 2 * len(mine)),
        out_specs=VMEM,
        out_shape=jax.ShapeDtypeStruct(base[0].shape, dtype),
        scratch_shapes=[pltpu.VMEM((blocks, tall // 2, base[0].shape[1]), mine[0].dtype)],
        compiler_params=ROOM,
        name="final",
    )(*base, *mine, *theirs)


def body(tokens, base_key, adapter_down, adapter_up, adapter_ids, owner_slot, lengths):
    groups, ring, pair = lax.axis_size("groups"), lax.axis_size("ring"), lax.axis_size("pair")
    sides = lax.axis_size("tensor")
    shares = groups * pair
    rows = tokens.shape[0]
    blocks = lengths.shape[0]

    def across(x):
        return lax.ppermute(x, "tensor", [(i, (i + 1) % sides) for i in range(sides)])

    def along(x, step):
        return lax.ppermute(x, "ring", [(a, (a + step) % ring) for a in range(ring)])

    def first_hops(x):
        return {0: x, ring - 1: along(x, 1), **({1: along(x, -1)} if ring > 2 else {})}

    def in_plane(x, kg, ky):
        pairs = []
        for a in range(groups):
            for b in range(pair):
                pairs.append((a * pair + b, (a + kg) % groups * pair + (b + ky) % pair))
        return lax.ppermute(x, PLANE, pairs)

    def more_hops(held, way, *after):
        for k in range(2, ring // 2 + 1):
            if 2 * k < ring or way % 2 == 0:
                if k == 2:
                    held[ring - 1] = hand_on(held[ring - 1], held[1], *after)
                held[ring - k] = along(held[ring - k + 1], 1)
            if 2 * k < ring or way % 2 == 1:
                if k == 2:
                    held[1] = hand_on(held[1], held[ring - 1], *after)
                held[k] = along(held[k - 1], -1)
        return [held[k] for k in range(ring)]

    packed = pack(jnp.swapaxes(adapter_down, 1, 2), adapter_up, shares, pair)
    ids = adapter_ids.reshape(-1)
    slabs = spread(tokens, lengths, ids, groups, pair)
    swapped = [
        lax.ppermute(packed[pair - w], "pair", [(a, (a - w) % pair) for a in range(pair)]) for w in range(1, pair)
    ]
    firsts = [first_hops(piece) for piece in [packed[0]] + swapped]
    toks = [in_plane(slabs[k - 1], k // pair, k % pair) for k in range(1, shares)]

    base_mine, base_out, flag, own_slab = base_halves(tokens, base_key, sides, lengths, ids, groups, pair)
    toks = [own_slab] + toks
    pieces = [
        more_hops(held, way, flag)
        for way, held in enumerate(firsts)
    ]

    halfway = ring // 2 if ring % 2 == 0 else ring
    held = collect([piece for way in pieces for away, piece in enumerate(way) if away != halfway])
    late = [way[halfway] for way in pieces] if halfway < ring else []
    *parts, ready = rank_parts(owner_slot, toks, held, late, ring, pair, rows, blocks)
    mine = [parts[0]] + [in_plane(parts[k], -(k // pair), -(k % pair)) for k in range(1, shares)]
    theirs = [across(part) for part in mine]
    base_in = across(hand_on(base_out, ready, spec=VMEM))
    return final(mine, theirs, [base_mine, base_in], groups, pair, tokens.dtype)


def solution(mesh):
    groups, dp, sides = (mesh.shape[name] for name in ("groups", "dp", "tensor"))
    pair = 2 if dp % 2 == 0 else 1
    cut = Mesh(mesh.devices.reshape(groups, dp // pair, pair, sides), ("groups", "ring", "pair", "tensor"))
    stored = ("ring", "pair")
    placed = (
        P(WHOLE, "tensor"),
        P("tensor", None),
        P(stored, "tensor", None),
        P(stored, None, "tensor"),
        P(WHOLE, None),
        P(),
        P(WHOLE),
    )
    return jax.shard_map(body, mesh=cut, in_specs=placed, out_specs=P(WHOLE, "tensor"), check_vma=False)
```

```python
import functools

import jax
import jax.numpy as jnp
from jax import lax
from jax.experimental import pallas as pl
from jax.experimental.pallas import tpu as pltpu
from jax.sharding import Mesh
from jax.sharding import PartitionSpec as P

LANES = 128
ANY = pl.BlockSpec(memory_space=pl.ANY)
SMEM = pl.BlockSpec(memory_space=pltpu.SMEM)
VMEM = pl.BlockSpec(memory_space=pltpu.VMEM)
HBM = pl.BlockSpec(memory_space=pltpu.HBM)
ROOM = pltpu.CompilerParams(vmem_limit_bytes=32 * 1024 * 1024)
FULL = pltpu.CompilerParams(vmem_limit_bytes=60 * 1024 * 1024)
PLANE = ("groups", "pair")
WHOLE = ("groups", "ring", "pair")


def hand_kernel(*refs):
    pass


def hand_on(x, *after):
    return pl.pallas_call(
        hand_kernel,
        in_specs=[ANY] * (1 + len(after)),
        out_specs=ANY,
        out_shape=jax.ShapeDtypeStruct(x.shape, x.dtype),
        input_output_aliases={0: 0},
        compiler_params=FULL,
        name="hand",
    )(x, *after)


def pack_kernel(down, up, *refs):
    outs, sems = refs[:-1], refs[-1]
    feats = outs[0].shape[2] - LANES
    copies = []
    for way, out in enumerate(outs):
        share = lax.axis_index("groups") * len(outs) + lax.rem(lax.axis_index("pair") + way, len(outs))
        start = pl.multiple_of(share * feats, LANES)
        tile = pl.multiple_of(lax.rem(share, up.shape[2] // LANES) * LANES, LANES)
        copies.append(pltpu.make_async_copy(down.at[:, :, pl.ds(start, feats)], out.at[:, :, :feats], sems.at[way, 0]))
        copies.append(pltpu.make_async_copy(up.at[:, :, pl.ds(tile, LANES)], out.at[:, :, feats:], sems.at[way, 1]))
    for copy in copies:
        copy.start()
    for copy in copies:
        copy.wait()


def pack(down, up, shares, ways):
    adapters, rank, feats = down.shape
    shape = jax.ShapeDtypeStruct((adapters, rank, feats // shares + LANES), down.dtype)
    return pl.pallas_call(
        pack_kernel,
        in_specs=[HBM, HBM],
        out_specs=[VMEM] * ways,
        out_shape=[shape] * ways,
        scratch_shapes=[pltpu.SemaphoreType.DMA((ways, 2))],
        compiler_params=FULL,
        name="pack",
    )(down, up)


def mate_at(k, sign, groups, pair):
    kg, ky = k // pair, k % pair
    g = lax.rem(lax.axis_index("groups") + sign * kg + groups, groups)
    y = lax.rem(lax.axis_index("pair") + sign * ky + pair, pair)
    return g * pair + y


def named_rows(ids, shape):
    lane = lax.broadcasted_iota(jnp.int32, shape, 1)
    named = jnp.zeros(shape, jnp.float32)
    for b in range(ids.shape[0]):
        named = jnp.where(lane == b, ids[b].astype(jnp.float32), named)
    return named


def spread_kernel(groups, pair, lengths, ids, tok, *refs):
    held, in_sems, out_sems = refs[-3:]
    outs = refs[:-3]
    blocks = lengths.shape[0]
    sent, tall, step = held.shape
    shares = sent + 1
    rows = tok.shape[0]
    block = rows // blocks
    mates = [pl.multiple_of(mate_at(k, 1, groups, pair) * step, LANES) for k in range(shares)]
    order = list(range(1, shares))

    def read(k, b):
        here = pl.ds(b * block, block)
        return pltpu.make_async_copy(tok.at[here, pl.ds(mates[k], step)], held.at[k - 1, here, :], in_sems.at[k - 1, b])

    for k in order:
        for b in range(blocks):
            read(k, b).start()
    named = named_rows(ids, (tall - rows, step)).astype(held.dtype)
    writes = []

    def write(k, b):
        here = pl.ds(b * block, block if b < blocks else tall - rows)
        writes.append(pltpu.make_async_copy(held.at[k - 1, here, :], outs[k - 1].at[here, :], out_sems.at[k - 1, b]))
        writes[-1].start()

    for k in order:
        held[k - 1, rows:, :] = named
        write(k, blocks)
        for b in range(blocks):
            read(k, b).wait()

            @pl.when(lengths[b] < block)
            def _():
                here = slice(b * block, (b + 1) * block)
                row = lax.broadcasted_iota(jnp.int32, (block, step), 0)
                part = held[k - 1, here, :]
                held[k - 1, here, :] = jnp.where(row < lengths[b], part, jnp.zeros_like(part))

            write(k, b)
    for one in writes:
        one.wait()


def spread(tokens, lengths, ids, groups, pair):
    rows, feats = tokens.shape
    shares = groups * pair
    shape = (rows + 16, feats // shares)
    return pl.pallas_call(
        functools.partial(spread_kernel, groups, pair),
        in_specs=[SMEM, SMEM, ANY],
        out_specs=[ANY] * (shares - 1),
        out_shape=[jax.ShapeDtypeStruct(shape, tokens.dtype)] * (shares - 1),
        scratch_shapes=[
            pltpu.VMEM((shares - 1,) + shape, tokens.dtype),
            pltpu.SemaphoreType.DMA((shares - 1, lengths.shape[0])),
            pltpu.SemaphoreType.DMA((shares - 1, lengths.shape[0] + 1)),
        ],
        compiler_params=FULL,
        name="spread",
    )(lengths, ids, tokens)


def base_kernel(sides, groups, pair, lengths, ids, tok, key, mine, other, flag_ref, slab, tok_held, key_held, total, tok_sems, key_sems):
    depth, rows = key.shape[0], tok.shape[0]
    chunk = depth // key_sems.shape[0]
    steps = tok_sems.shape[0]
    step = depth // steps

    def key_copy(i):
        here = pl.ds(i * chunk, chunk)
        return pltpu.make_async_copy(key.at[here, :], key_held.at[here, :], key_sems.at[i])

    def tok_copy(i, b):
        here = pl.ds(i * step, step)
        some = pl.ds(b * (rows // tok_sems.shape[1]), rows // tok_sems.shape[1])
        return pltpu.make_async_copy(tok.at[some, here], tok_held.at[some, here], tok_sems.at[i, b])

    flag_ref[...] = jnp.zeros_like(flag_ref)
    for i in range(steps):
        for b in range(tok_sems.shape[1]):
            tok_copy(i, b).start()
        for j in range(step // chunk):
            key_copy(i * (step // chunk) + j).start()
    for i in range(steps):
        for b in range(tok_sems.shape[1]):
            tok_copy(i, b).wait()
        for j in range(step // chunk):
            key_copy(i * (step // chunk) + j).wait()
        here = slice(i * step, (i + 1) * step)
        part = jnp.dot(tok_held[:, here], key_held[here, :], preferred_element_type=jnp.float32)
        if i == 0:
            total[...] = part
        else:
            total[...] += part
    blocks = lengths.shape[0]
    wide = mine.shape[1]
    block = rows // blocks
    feats = slab.shape[1]
    own = pl.ds(pl.multiple_of(mate_at(0, 1, groups, pair) * feats, LANES), feats)
    row = lax.broadcasted_iota(jnp.int32, (block, feats), 0)
    for b in range(blocks):
        here = slice(b * block, (b + 1) * block)
        some = tok_held[here, own]
        slab[here, :] = jnp.where(row < lengths[b], some, jnp.zeros_like(some))
    slab[rows:, :] = named_rows(ids, (slab.shape[0] - rows, feats)).astype(slab.dtype)
    row = lax.broadcasted_iota(jnp.int32, (block, wide), 0)
    t = lax.axis_index("tensor")
    for out, side in ((mine, t), (other, lax.rem(t + 1, sides))):
        columns = pl.ds(pl.multiple_of(side * wide, LANES), wide)
        for b in range(blocks):
            here = slice(b * block, (b + 1) * block)
            out[here, :] = jnp.where(row < lengths[b], total[here, columns], 0.0)


def base_halves(tokens, base_key, sides, lengths, ids, groups, pair):
    rows, depth = tokens.shape
    features = base_key.shape[1]
    half = jax.ShapeDtypeStruct((rows, features // sides), jnp.float32)
    steps, chunks = depth // 1024, depth // 256
    return pl.pallas_call(
        functools.partial(base_kernel, sides, groups, pair),
        in_specs=[SMEM, SMEM, ANY, ANY],
        out_specs=[VMEM] * 4,
        out_shape=[
            half,
            half,
            jax.ShapeDtypeStruct((8, LANES), jnp.float32),
            jax.ShapeDtypeStruct((rows + 16, depth // (groups * pair)), tokens.dtype),
        ],
        scratch_shapes=[
            pltpu.VMEM(tokens.shape, tokens.dtype),
            pltpu.VMEM(base_key.shape, base_key.dtype),
            pltpu.VMEM((rows, features), jnp.float32),
            pltpu.SemaphoreType.DMA((steps, lengths.shape[0])),
            pltpu.SemaphoreType.DMA((chunks,)),
        ],
        cost_estimate=pl.CostEstimate(flops=0, bytes_accessed=0, transcendentals=0),
        compiler_params=FULL,
        name="base",
    )(lengths, ids, tokens, base_key)


def collect_kernel(*refs):
    sems, held, pieces = refs[-1], refs[-2], refs[:-2]
    copies, start = [], 0
    for j, piece in enumerate(pieces):
        copies.append(pltpu.make_async_copy(piece, held.at[pl.ds(start, piece.shape[0])], sems.at[j]))
        start += piece.shape[0]
    for copy in copies:
        copy.start()
    for copy in copies:
        copy.wait()


def collect(pieces):
    count = sum(piece.shape[0] for piece in pieces)
    return pl.pallas_call(
        collect_kernel,
        in_specs=[ANY] * len(pieces),
        out_specs=VMEM,
        out_shape=jax.ShapeDtypeStruct((count,) + pieces[0].shape[1:], pieces[0].dtype),
        scratch_shapes=[pltpu.SemaphoreType.DMA((len(pieces),))],
        compiler_params=ROOM,
        name="collect",
    )(*pieces)


def rank_kernel(ring, pair, rows, shares, owner, held, *refs):
    late, toks, outs = refs[: -1 - 2 * shares], refs[-1 - 2 * shares : -1 - shares], refs[-1 - shares : -1]
    flag = refs[-1]
    flag[...] = jnp.zeros_like(flag)
    rank = held.shape[1]
    per = owner.shape[0] // (ring * pair)
    blocks, _, block = outs[0].shape
    feats = toks[0].shape[1]
    z, y = lax.axis_index("ring"), lax.axis_index("pair")
    lane = lax.broadcasted_iota(jnp.int32, (16, LANES), 1)
    row = lax.broadcasted_iota(jnp.int32, (16, LANES), 0)
    ids = []
    for tok in toks:
        named = tok[rows:, :LANES].astype(jnp.float32)
        ids += [jnp.sum(jnp.where((lane == b) & (row == 0), named, 0.0)).astype(jnp.int32) for b in range(blocks)]
    for i, one in enumerate(ids):
        slot = owner[one]
        chip = slot // per
        local = lax.rem(slot, per)
        away = lax.rem(chip // pair - z + ring, ring)
        way = lax.rem(lax.rem(chip, pair) - y + pair, pair)
        if late:
            half = ring // 2
            near = jnp.where(away == half, 0, away - jnp.where(away > half, 1, 0))
            piece = held[(way * (ring - 1) + near) * per + local]
            for w in range(pair):
                piece = jnp.where((away == half) & (way == w), late[w][local], piece)
        else:
            piece = held[(way * ring + away) * per + local]
        k, b = i // blocks, i % blocks
        part = lax.dot_general(
            piece[:, :feats],
            toks[k][b * block : (b + 1) * block, :],
            (((1,), (1,)), ((), ())),
            preferred_element_type=jnp.float32,
        )
        outs[k][b, :rank, :] = part.astype(outs[k].dtype)
        outs[k][b, rank:, :] = piece[:, feats:]


def rank_parts(owner, toks, held, late, ring, pair, rows, blocks):
    shares, rank = len(toks), held.shape[1]
    return pl.pallas_call(
        functools.partial(rank_kernel, ring, pair, rows, shares),
        in_specs=[SMEM, VMEM] + [VMEM] * (len(late) + shares),
        out_specs=[VMEM] * (shares + 1),
        out_shape=[jax.ShapeDtypeStruct((blocks, 2 * rank, rows // blocks), held.dtype)] * shares
        + [jax.ShapeDtypeStruct((8, LANES), jnp.float32)],
        cost_estimate=pl.CostEstimate(flops=0, bytes_accessed=0, transcendentals=0),
        compiler_params=ROOM,
        name="rank",
    )(owner, held, *late, *toks)


def final_kernel(groups, pair, base_a, base_b, *refs):
    shares = groups * pair
    mine, theirs, out_ref, up = refs[:shares], refs[shares : 2 * shares], refs[-2], refs[-1]
    blocks, tall, block = mine[0].shape
    rank = tall // 2
    tiles = out_ref.shape[1] // LANES
    for b in range(blocks):
        here = slice(b * block, (b + 1) * block)
        total = mine[0][b, :rank, :].astype(jnp.float32)
        for part in mine[1:] + theirs:
            total += part[b, :rank, :].astype(jnp.float32)
        for k in range(shares):
            tile = lax.rem(mate_at(k, 1, groups, pair), tiles)
            up[b, :, pl.ds(pl.multiple_of(tile * LANES, LANES), LANES)] = mine[k][b, rank:, :]
        delta = lax.dot_general(
            total.astype(jnp.bfloat16), up[b], (((0,), (0,)), ((), ())), preferred_element_type=jnp.float32
        )
        out_ref[here, :] = (base_a[here, :] + base_b[here, :] + delta).astype(out_ref.dtype)


def final(mine, theirs, base, groups, pair, dtype):
    blocks, tall, _ = mine[0].shape
    return pl.pallas_call(
        functools.partial(final_kernel, groups, pair),
        in_specs=[VMEM] * (2 + 2 * len(mine)),
        out_specs=VMEM,
        out_shape=jax.ShapeDtypeStruct(base[0].shape, dtype),
        scratch_shapes=[pltpu.VMEM((blocks, tall // 2, base[0].shape[1]), mine[0].dtype)],
        compiler_params=ROOM,
        name="final",
    )(*base, *mine, *theirs)


def body(tokens, base_key, adapter_down, adapter_up, adapter_ids, owner_slot, lengths):
    groups, ring, pair = lax.axis_size("groups"), lax.axis_size("ring"), lax.axis_size("pair")
    sides = lax.axis_size("tensor")
    shares = groups * pair
    rows = tokens.shape[0]
    blocks = lengths.shape[0]

    def across(x):
        return lax.ppermute(x, "tensor", [(i, (i + 1) % sides) for i in range(sides)])

    def along(x, step):
        return lax.ppermute(x, "ring", [(a, (a + step) % ring) for a in range(ring)])

    def first_hops(x):
        return {0: x, ring - 1: along(x, 1), **({1: along(x, -1)} if ring > 2 else {})}

    def in_plane(x, kg, ky):
        pairs = []
        for a in range(groups):
            for b in range(pair):
                pairs.append((a * pair + b, (a + kg) % groups * pair + (b + ky) % pair))
        return lax.ppermute(x, PLANE, pairs)

    def more_hops(held, way, *after):
        for k in range(2, ring // 2 + 1):
            if 2 * k < ring or way % 2 == 0:
                if k == 2:
                    held[ring - 1] = hand_on(held[ring - 1], held[1], *after)
                held[ring - k] = along(held[ring - k + 1], 1)
            if 2 * k < ring or way % 2 == 1:
                if k == 2:
                    held[1] = hand_on(held[1], held[ring - 1], *after)
                held[k] = along(held[k - 1], -1)
        return [held[k] for k in range(ring)]

    packed = pack(jnp.swapaxes(adapter_down, 1, 2), adapter_up, shares, pair)
    ids = adapter_ids.reshape(-1)
    slabs = spread(tokens, lengths, ids, groups, pair)
    swapped = [
        lax.ppermute(packed[pair - w], "pair", [(a, (a - w) % pair) for a in range(pair)]) for w in range(1, pair)
    ]
    firsts = [first_hops(piece) for piece in [packed[0]] + swapped]
    toks = [in_plane(slabs[k - 1], k // pair, k % pair) for k in range(1, shares)]

    base_mine, base_out, flag, own_slab = base_halves(tokens, base_key, sides, lengths, ids, groups, pair)
    toks = [own_slab] + toks
    pieces = [
        more_hops(held, way, flag)
        for way, held in enumerate(firsts)
    ]

    halfway = ring // 2 if ring % 2 == 0 else ring
    held = collect([piece for way in pieces for away, piece in enumerate(way) if away != halfway])
    late = [way[halfway] for way in pieces] if halfway < ring else []
    *parts, ready = rank_parts(owner_slot, toks, held, late, ring, pair, rows, blocks)
    mine = [parts[0]] + [in_plane(parts[k], -(k // pair), -(k % pair)) for k in range(1, shares)]
    theirs = [across(part) for part in mine]
    base_in = across(hand_on(base_out, ready))
    return final(mine, theirs, [base_mine, base_in], groups, pair, tokens.dtype)


def solution(mesh):
    groups, dp, sides = (mesh.shape[name] for name in ("groups", "dp", "tensor"))
    pair = 2 if dp % 2 == 0 else 1
    cut = Mesh(mesh.devices.reshape(groups, dp // pair, pair, sides), ("groups", "ring", "pair", "tensor"))
    stored = ("ring", "pair")
    placed = (
        P(WHOLE, "tensor"),
        P("tensor", None),
        P(stored, "tensor", None),
        P(stored, None, "tensor"),
        P(WHOLE, None),
        P(),
        P(WHOLE),
    )
    return jax.shard_map(body, mesh=cut, in_specs=placed, out_specs=P(WHOLE, "tensor"), check_vma=False)
```

```python
import functools

import jax
import jax.numpy as jnp
from jax import lax
from jax.experimental import pallas as pl
from jax.experimental.pallas import tpu as pltpu
from jax.sharding import Mesh
from jax.sharding import PartitionSpec as P

LANES = 128
ANY = pl.BlockSpec(memory_space=pl.ANY)
SMEM = pl.BlockSpec(memory_space=pltpu.SMEM)
VMEM = pl.BlockSpec(memory_space=pltpu.VMEM)
HBM = pl.BlockSpec(memory_space=pltpu.HBM)
ROOM = pltpu.CompilerParams(vmem_limit_bytes=32 * 1024 * 1024)
FULL = pltpu.CompilerParams(vmem_limit_bytes=60 * 1024 * 1024)
PLANE = ("groups", "pair")
WHOLE = ("groups", "ring", "pair")


def hand_kernel(*refs):
    pass


def hand_on(x, *after):
    return pl.pallas_call(
        hand_kernel,
        in_specs=[ANY] * (1 + len(after)),
        out_specs=ANY,
        out_shape=jax.ShapeDtypeStruct(x.shape, x.dtype),
        input_output_aliases={0: 0},
        compiler_params=FULL,
        name="hand",
    )(x, *after)


def pack_kernel(down, up, *refs):
    outs, sems = refs[:-1], refs[-1]
    feats = outs[0].shape[2] - LANES
    copies = []
    for way, out in enumerate(outs):
        share = lax.axis_index("groups") * len(outs) + lax.rem(lax.axis_index("pair") + way, len(outs))
        start = pl.multiple_of(share * feats, LANES)
        tile = pl.multiple_of(lax.rem(share, up.shape[2] // LANES) * LANES, LANES)
        copies.append(pltpu.make_async_copy(down.at[:, :, pl.ds(start, feats)], out.at[:, :, :feats], sems.at[way, 0]))
        copies.append(pltpu.make_async_copy(up.at[:, :, pl.ds(tile, LANES)], out.at[:, :, feats:], sems.at[way, 1]))
    for copy in copies:
        copy.start()
    for copy in copies:
        copy.wait()


def pack(down, up, shares, ways):
    adapters, rank, feats = down.shape
    shape = jax.ShapeDtypeStruct((adapters, rank, feats // shares + LANES), down.dtype)
    return pl.pallas_call(
        pack_kernel,
        in_specs=[HBM, HBM],
        out_specs=[VMEM] * ways,
        out_shape=[shape] * ways,
        scratch_shapes=[pltpu.SemaphoreType.DMA((ways, 2))],
        compiler_params=FULL,
        name="pack",
    )(down, up)


def mate_at(k, sign, groups, pair):
    kg, ky = k // pair, k % pair
    g = lax.rem(lax.axis_index("groups") + sign * kg + groups, groups)
    y = lax.rem(lax.axis_index("pair") + sign * ky + pair, pair)
    return g * pair + y


def named_rows(ids, shape):
    lane = lax.broadcasted_iota(jnp.int32, shape, 1)
    named = jnp.zeros(shape, jnp.float32)
    for b in range(ids.shape[0]):
        named = jnp.where(lane == b, ids[b].astype(jnp.float32), named)
    return named


def spread_kernel(groups, pair, lengths, ids, tok, *refs):
    held, in_sems, out_sems = refs[-3:]
    outs = refs[:-3]
    blocks = lengths.shape[0]
    sent, tall, step = held.shape
    shares = sent + 1
    rows = tok.shape[0]
    block = rows // blocks
    mates = [pl.multiple_of(mate_at(k, 1, groups, pair) * step, LANES) for k in range(shares)]
    order = list(range(1, shares))

    def read(k, b):
        here = pl.ds(b * block, block)
        return pltpu.make_async_copy(tok.at[here, pl.ds(mates[k], step)], held.at[k - 1, here, :], in_sems.at[k - 1, b])

    for k in order:
        for b in range(blocks):
            read(k, b).start()
    named = named_rows(ids, (tall - rows, step)).astype(held.dtype)
    writes = []

    def write(k, b):
        here = pl.ds(b * block, block if b < blocks else tall - rows)
        writes.append(pltpu.make_async_copy(held.at[k - 1, here, :], outs[k - 1].at[here, :], out_sems.at[k - 1, b]))
        writes[-1].start()

    for k in order:
        held[k - 1, rows:, :] = named
        write(k, blocks)
        for b in range(blocks):
            read(k, b).wait()

            @pl.when(lengths[b] < block)
            def _():
                here = slice(b * block, (b + 1) * block)
                row = lax.broadcasted_iota(jnp.int32, (block, step), 0)
                part = held[k - 1, here, :]
                held[k - 1, here, :] = jnp.where(row < lengths[b], part, jnp.zeros_like(part))

            write(k, b)
    for one in writes:
        one.wait()


def spread(tokens, lengths, ids, groups, pair):
    rows, feats = tokens.shape
    shares = groups * pair
    shape = (rows + 16, feats // shares)
    return pl.pallas_call(
        functools.partial(spread_kernel, groups, pair),
        in_specs=[SMEM, SMEM, ANY],
        out_specs=[ANY] * (shares - 1),
        out_shape=[jax.ShapeDtypeStruct(shape, tokens.dtype)] * (shares - 1),
        scratch_shapes=[
            pltpu.VMEM((shares - 1,) + shape, tokens.dtype),
            pltpu.SemaphoreType.DMA((shares - 1, lengths.shape[0])),
            pltpu.SemaphoreType.DMA((shares - 1, lengths.shape[0] + 1)),
        ],
        compiler_params=FULL,
        name="spread",
    )(lengths, ids, tokens)


def base_kernel(sides, groups, pair, lengths, ids, tok, key, mine, other, flag_ref, slab, tok_held, key_held, total, tok_sems, key_sems):
    depth, rows = key.shape[0], tok.shape[0]
    chunk = depth // key_sems.shape[0]
    steps = tok_sems.shape[0]
    step = depth // steps

    def key_copy(i):
        here = pl.ds(i * chunk, chunk)
        return pltpu.make_async_copy(key.at[here, :], key_held.at[here, :], key_sems.at[i])

    def tok_copy(i, b):
        here = pl.ds(i * step, step)
        some = pl.ds(b * (rows // tok_sems.shape[1]), rows // tok_sems.shape[1])
        return pltpu.make_async_copy(tok.at[some, here], tok_held.at[some, here], tok_sems.at[i, b])

    flag_ref[...] = jnp.zeros_like(flag_ref)
    for i in range(steps):
        for b in range(tok_sems.shape[1]):
            tok_copy(i, b).start()
        for j in range(step // chunk):
            key_copy(i * (step // chunk) + j).start()
    for i in range(steps):
        for b in range(tok_sems.shape[1]):
            tok_copy(i, b).wait()
        for j in range(step // chunk):
            key_copy(i * (step // chunk) + j).wait()
        here = slice(i * step, (i + 1) * step)
        part = jnp.dot(tok_held[:, here], key_held[here, :], preferred_element_type=jnp.float32)
        if i == 0:
            total[...] = part
        else:
            total[...] += part
    blocks = lengths.shape[0]
    wide = mine.shape[1]
    block = rows // blocks
    feats = slab.shape[1]
    own = pl.ds(pl.multiple_of(mate_at(0, 1, groups, pair) * feats, LANES), feats)
    row = lax.broadcasted_iota(jnp.int32, (block, feats), 0)
    for b in range(blocks):
        here = slice(b * block, (b + 1) * block)
        some = tok_held[here, own]
        slab[here, :] = jnp.where(row < lengths[b], some, jnp.zeros_like(some))
    slab[rows:, :] = named_rows(ids, (slab.shape[0] - rows, feats)).astype(slab.dtype)
    row = lax.broadcasted_iota(jnp.int32, (block, wide), 0)
    t = lax.axis_index("tensor")
    for out, side in ((mine, t), (other, lax.rem(t + 1, sides))):
        columns = pl.ds(pl.multiple_of(side * wide, LANES), wide)
        for b in range(blocks):
            here = slice(b * block, (b + 1) * block)
            out[here, :] = jnp.where(row < lengths[b], total[here, columns], 0.0)


def base_halves(tokens, base_key, sides, lengths, ids, groups, pair):
    rows, depth = tokens.shape
    features = base_key.shape[1]
    half = jax.ShapeDtypeStruct((rows, features // sides), jnp.float32)
    steps, chunks = depth // 1024, depth // 256
    return pl.pallas_call(
        functools.partial(base_kernel, sides, groups, pair),
        in_specs=[SMEM, SMEM, ANY, ANY],
        out_specs=[VMEM] * 4,
        out_shape=[
            half,
            half,
            jax.ShapeDtypeStruct((8, LANES), jnp.float32),
            jax.ShapeDtypeStruct((rows + 16, depth // (groups * pair)), tokens.dtype),
        ],
        scratch_shapes=[
            pltpu.VMEM(tokens.shape, tokens.dtype),
            pltpu.VMEM(base_key.shape, base_key.dtype),
            pltpu.VMEM((rows, features), jnp.float32),
            pltpu.SemaphoreType.DMA((steps, lengths.shape[0])),
            pltpu.SemaphoreType.DMA((chunks,)),
        ],
        cost_estimate=pl.CostEstimate(flops=0, bytes_accessed=0, transcendentals=0),
        compiler_params=FULL,
        name="base",
    )(lengths, ids, tokens, base_key)


def collect_kernel(*refs):
    sems, held, pieces = refs[-1], refs[-2], refs[:-2]
    copies, start = [], 0
    for j, piece in enumerate(pieces):
        copies.append(pltpu.make_async_copy(piece, held.at[pl.ds(start, piece.shape[0])], sems.at[j]))
        start += piece.shape[0]
    for copy in copies:
        copy.start()
    for copy in copies:
        copy.wait()


def collect(pieces):
    count = sum(piece.shape[0] for piece in pieces)
    return pl.pallas_call(
        collect_kernel,
        in_specs=[ANY] * len(pieces),
        out_specs=VMEM,
        out_shape=jax.ShapeDtypeStruct((count,) + pieces[0].shape[1:], pieces[0].dtype),
        scratch_shapes=[pltpu.SemaphoreType.DMA((len(pieces),))],
        compiler_params=ROOM,
        name="collect",
    )(*pieces)


def rank_kernel(ring, pair, rows, shares, owner, held, *refs):
    late, toks, outs = refs[: -1 - 2 * shares], refs[-1 - 2 * shares : -1 - shares], refs[-1 - shares : -1]
    flag = refs[-1]
    flag[...] = jnp.zeros_like(flag)
    rank = held.shape[1]
    per = owner.shape[0] // (ring * pair)
    blocks, _, block = outs[0].shape
    feats = toks[0].shape[1]
    z, y = lax.axis_index("ring"), lax.axis_index("pair")
    lane = lax.broadcasted_iota(jnp.int32, (16, LANES), 1)
    row = lax.broadcasted_iota(jnp.int32, (16, LANES), 0)
    ids = []
    for tok in toks:
        named = tok[rows:, :LANES].astype(jnp.float32)
        ids += [jnp.sum(jnp.where((lane == b) & (row == 0), named, 0.0)).astype(jnp.int32) for b in range(blocks)]
    for i, one in enumerate(ids):
        slot = owner[one]
        chip = slot // per
        local = lax.rem(slot, per)
        away = lax.rem(chip // pair - z + ring, ring)
        way = lax.rem(lax.rem(chip, pair) - y + pair, pair)
        if late:
            half = ring // 2
            near = jnp.where(away == half, 0, away - jnp.where(away > half, 1, 0))
            piece = held[(way * (ring - 1) + near) * per + local]
            for w in range(pair):
                piece = jnp.where((away == half) & (way == w), late[w][local], piece)
        else:
            piece = held[(way * ring + away) * per + local]
        k, b = i // blocks, i % blocks
        part = lax.dot_general(
            piece[:, :feats],
            toks[k][b * block : (b + 1) * block, :],
            (((1,), (1,)), ((), ())),
            preferred_element_type=jnp.float32,
        )
        outs[k][b, :rank, :] = part.astype(outs[k].dtype)
        outs[k][b, rank:, :] = piece[:, feats:]


def rank_parts(owner, toks, held, late, ring, pair, rows, blocks):
    shares, rank = len(toks), held.shape[1]
    return pl.pallas_call(
        functools.partial(rank_kernel, ring, pair, rows, shares),
        in_specs=[SMEM, VMEM] + [VMEM] * (len(late) + shares),
        out_specs=[VMEM] * (shares + 1),
        out_shape=[jax.ShapeDtypeStruct((blocks, 2 * rank, rows // blocks), held.dtype)] * shares
        + [jax.ShapeDtypeStruct((8, LANES), jnp.float32)],
        cost_estimate=pl.CostEstimate(flops=0, bytes_accessed=0, transcendentals=0),
        compiler_params=ROOM,
        name="rank",
    )(owner, held, *late, *toks)


def final_kernel(groups, pair, base_a, base_b, *refs):
    shares = groups * pair
    mine, theirs, out_ref, up = refs[:shares], refs[shares : 2 * shares], refs[-2], refs[-1]
    blocks, tall, block = mine[0].shape
    rank = tall // 2
    tiles = out_ref.shape[1] // LANES
    for b in range(blocks):
        here = slice(b * block, (b + 1) * block)
        total = mine[0][b, :rank, :].astype(jnp.float32)
        for part in mine[1:] + theirs:
            total += part[b, :rank, :].astype(jnp.float32)
        for k in range(shares):
            tile = lax.rem(mate_at(k, 1, groups, pair), tiles)
            up[b, :, pl.ds(pl.multiple_of(tile * LANES, LANES), LANES)] = mine[k][b, rank:, :]
        delta = lax.dot_general(
            total.astype(jnp.bfloat16), up[b], (((0,), (0,)), ((), ())), preferred_element_type=jnp.float32
        )
        out_ref[here, :] = (base_a[here, :] + base_b[here, :] + delta).astype(out_ref.dtype)


def final(mine, theirs, base, groups, pair, dtype):
    blocks, tall, _ = mine[0].shape
    return pl.pallas_call(
        functools.partial(final_kernel, groups, pair),
        in_specs=[VMEM] * (2 + 2 * len(mine)),
        out_specs=VMEM,
        out_shape=jax.ShapeDtypeStruct(base[0].shape, dtype),
        scratch_shapes=[pltpu.VMEM((blocks, tall // 2, base[0].shape[1]), mine[0].dtype)],
        compiler_params=ROOM,
        name="final",
    )(*base, *mine, *theirs)


def body(tokens, base_key, adapter_down, adapter_up, adapter_ids, owner_slot, lengths):
    groups, ring, pair = lax.axis_size("groups"), lax.axis_size("ring"), lax.axis_size("pair")
    sides = lax.axis_size("tensor")
    shares = groups * pair
    rows = tokens.shape[0]
    blocks = lengths.shape[0]

    def across(x):
        return lax.ppermute(x, "tensor", [(i, (i + 1) % sides) for i in range(sides)])

    def along(x, step):
        return lax.ppermute(x, "ring", [(a, (a + step) % ring) for a in range(ring)])

    def first_hops(x):
        return {0: x, ring - 1: along(x, 1), **({1: along(x, -1)} if ring > 2 else {})}

    def in_plane(x, kg, ky):
        pairs = []
        for a in range(groups):
            for b in range(pair):
                pairs.append((a * pair + b, (a + kg) % groups * pair + (b + ky) % pair))
        return lax.ppermute(x, PLANE, pairs)

    def more_hops(held, way, *after):
        for k in range(2, ring // 2 + 1):
            if 2 * k < ring or way % 2 == 0:
                if k == 2:
                    held[ring - 1] = hand_on(held[ring - 1], held[1], *after)
                held[ring - k] = along(held[ring - k + 1], 1)
            if 2 * k < ring or way % 2 == 1:
                if k == 2:
                    held[1] = hand_on(held[1], held[ring - 1], *after)
                held[k] = along(held[k - 1], -1)
        return [held[k] for k in range(ring)]

    packed = pack(jnp.swapaxes(adapter_down, 1, 2), adapter_up, shares, pair)
    ids = adapter_ids.reshape(-1)
    slabs = spread(tokens, lengths, ids, groups, pair)
    swapped = [
        lax.ppermute(packed[pair - w], "pair", [(a, (a - w) % pair) for a in range(pair)]) for w in range(1, pair)
    ]
    firsts = [first_hops(piece) for piece in [packed[0]] + swapped]
    toks = [in_plane(slabs[k - 1], k // pair, k % pair) for k in reversed(range(1, shares))][::-1]

    base_mine, base_out, flag, own_slab = base_halves(tokens, base_key, sides, lengths, ids, groups, pair)
    toks = [own_slab] + toks
    pieces = [
        more_hops(held, way, flag)
        for way, held in enumerate(firsts)
    ]

    halfway = ring // 2 if ring % 2 == 0 else ring
    held = collect([piece for way in pieces for away, piece in enumerate(way) if away != halfway])
    late = [way[halfway] for way in pieces] if halfway < ring else []
    *parts, ready = rank_parts(owner_slot, toks, held, late, ring, pair, rows, blocks)
    mine = [parts[0]] + [in_plane(parts[k], -(k // pair), -(k % pair)) for k in range(1, shares)]
    theirs = [across(part) for part in mine]
    base_in = across(hand_on(base_out, ready))
    return final(mine, theirs, [base_mine, base_in], groups, pair, tokens.dtype)


def solution(mesh):
    groups, dp, sides = (mesh.shape[name] for name in ("groups", "dp", "tensor"))
    pair = 2 if dp % 2 == 0 else 1
    cut = Mesh(mesh.devices.reshape(groups, dp // pair, pair, sides), ("groups", "ring", "pair", "tensor"))
    stored = ("ring", "pair")
    placed = (
        P(WHOLE, "tensor"),
        P("tensor", None),
        P(stored, "tensor", None),
        P(stored, None, "tensor"),
        P(WHOLE, None),
        P(),
        P(WHOLE),
    )
    return jax.shard_map(body, mesh=cut, in_specs=placed, out_specs=P(WHOLE, "tensor"), check_vma=False)
```

```python
import functools

import jax
import jax.numpy as jnp
from jax import lax
from jax.experimental import pallas as pl
from jax.experimental.pallas import tpu as pltpu
from jax.sharding import Mesh
from jax.sharding import PartitionSpec as P

LANES = 128
ANY = pl.BlockSpec(memory_space=pl.ANY)
SMEM = pl.BlockSpec(memory_space=pltpu.SMEM)
VMEM = pl.BlockSpec(memory_space=pltpu.VMEM)
HBM = pl.BlockSpec(memory_space=pltpu.HBM)
ROOM = pltpu.CompilerParams(vmem_limit_bytes=32 * 1024 * 1024)
FULL = pltpu.CompilerParams(vmem_limit_bytes=60 * 1024 * 1024)
PLANE = ("groups", "pair")
WHOLE = ("groups", "ring", "pair")


def hand_kernel(*refs):
    pass


def hand_on(x, *after):
    return pl.pallas_call(
        hand_kernel,
        in_specs=[ANY] * (1 + len(after)),
        out_specs=ANY,
        out_shape=jax.ShapeDtypeStruct(x.shape, x.dtype),
        input_output_aliases={0: 0},
        compiler_params=FULL,
        name="hand",
    )(x, *after)


def pack_kernel(down, up, *refs):
    outs, sems = refs[:-1], refs[-1]
    feats = outs[0].shape[2] - LANES
    copies = []
    for way, out in enumerate(outs):
        share = lax.axis_index("groups") * len(outs) + lax.rem(lax.axis_index("pair") + way, len(outs))
        start = pl.multiple_of(share * feats, LANES)
        tile = pl.multiple_of(lax.rem(share, up.shape[2] // LANES) * LANES, LANES)
        copies.append(pltpu.make_async_copy(down.at[:, :, pl.ds(start, feats)], out.at[:, :, :feats], sems.at[way, 0]))
        copies.append(pltpu.make_async_copy(up.at[:, :, pl.ds(tile, LANES)], out.at[:, :, feats:], sems.at[way, 1]))
    for copy in copies:
        copy.start()
    for copy in copies:
        copy.wait()


def pack(down, up, shares, ways):
    adapters, rank, feats = down.shape
    shape = jax.ShapeDtypeStruct((adapters, rank, feats // shares + LANES), down.dtype)
    return pl.pallas_call(
        pack_kernel,
        in_specs=[HBM, HBM],
        out_specs=[VMEM] * ways,
        out_shape=[shape] * ways,
        scratch_shapes=[pltpu.SemaphoreType.DMA((ways, 2))],
        compiler_params=FULL,
        name="pack",
    )(down, up)


def mate_at(k, sign, groups, pair):
    kg, ky = k // pair, k % pair
    g = lax.rem(lax.axis_index("groups") + sign * kg + groups, groups)
    y = lax.rem(lax.axis_index("pair") + sign * ky + pair, pair)
    return g * pair + y


def named_rows(ids, shape):
    lane = lax.broadcasted_iota(jnp.int32, shape, 1)
    named = jnp.zeros(shape, jnp.float32)
    for b in range(ids.shape[0]):
        named = jnp.where(lane == b, ids[b].astype(jnp.float32), named)
    return named


def spread_kernel(groups, pair, lengths, ids, tok, *refs):
    held, in_sems, out_sems = refs[-3:]
    outs = refs[:-3]
    blocks = lengths.shape[0]
    sent, tall, step = held.shape
    shares = sent + 1
    rows = tok.shape[0]
    block = rows // blocks
    mates = [pl.multiple_of(mate_at(k, 1, groups, pair) * step, LANES) for k in range(shares)]
    order = list(range(1, shares))

    def read(k, b):
        here = pl.ds(b * block, block)
        return pltpu.make_async_copy(tok.at[here, pl.ds(mates[k], step)], held.at[k - 1, here, :], in_sems.at[k - 1, b])

    for k in order:
        for b in range(blocks):
            read(k, b).start()
    named = named_rows(ids, (tall - rows, step)).astype(held.dtype)
    writes = []

    def write(k, b):
        here = pl.ds(b * block, block if b < blocks else tall - rows)
        writes.append(pltpu.make_async_copy(held.at[k - 1, here, :], outs[k - 1].at[here, :], out_sems.at[k - 1, b]))
        writes[-1].start()

    for k in order:
        held[k - 1, rows:, :] = named
        write(k, blocks)
        for b in range(blocks):
            read(k, b).wait()

            @pl.when(lengths[b] < block)
            def _():
                here = slice(b * block, (b + 1) * block)
                row = lax.broadcasted_iota(jnp.int32, (block, step), 0)
                part = held[k - 1, here, :]
                held[k - 1, here, :] = jnp.where(row < lengths[b], part, jnp.zeros_like(part))

            write(k, b)
    for one in writes:
        one.wait()


def spread(tokens, lengths, ids, groups, pair):
    rows, feats = tokens.shape
    shares = groups * pair
    shape = (rows + 16, feats // shares)
    return pl.pallas_call(
        functools.partial(spread_kernel, groups, pair),
        in_specs=[SMEM, SMEM, ANY],
        out_specs=[ANY] * (shares - 1),
        out_shape=[jax.ShapeDtypeStruct(shape, tokens.dtype)] * (shares - 1),
        scratch_shapes=[
            pltpu.VMEM((shares - 1,) + shape, tokens.dtype),
            pltpu.SemaphoreType.DMA((shares - 1, lengths.shape[0])),
            pltpu.SemaphoreType.DMA((shares - 1, lengths.shape[0] + 1)),
        ],
        compiler_params=FULL,
        name="spread",
    )(lengths, ids, tokens)


def base_kernel(sides, groups, pair, lengths, ids, tok, key, mine, other, flag_ref, slab, tok_held, key_held, total, tok_sems, key_sems):
    depth, rows = key.shape[0], tok.shape[0]
    chunk = depth // key_sems.shape[0]
    steps = tok_sems.shape[0]
    step = depth // steps

    def key_copy(i):
        here = pl.ds(i * chunk, chunk)
        return pltpu.make_async_copy(key.at[here, :], key_held.at[here, :], key_sems.at[i])

    def tok_copy(i, b):
        here = pl.ds(i * step, step)
        some = pl.ds(b * (rows // tok_sems.shape[1]), rows // tok_sems.shape[1])
        return pltpu.make_async_copy(tok.at[some, here], tok_held.at[some, here], tok_sems.at[i, b])

    flag_ref[...] = jnp.zeros_like(flag_ref)
    for i in range(steps):
        for b in range(tok_sems.shape[1]):
            tok_copy(i, b).start()
        for j in range(step // chunk):
            key_copy(i * (step // chunk) + j).start()
    for i in range(steps):
        for b in range(tok_sems.shape[1]):
            tok_copy(i, b).wait()
        for j in range(step // chunk):
            key_copy(i * (step // chunk) + j).wait()
        here = slice(i * step, (i + 1) * step)
        part = jnp.dot(tok_held[:, here], key_held[here, :], preferred_element_type=jnp.float32)
        if i == 0:
            total[...] = part
        else:
            total[...] += part
    blocks = lengths.shape[0]
    wide = mine.shape[1]
    block = rows // blocks
    feats = slab.shape[1]
    own = pl.ds(pl.multiple_of(mate_at(0, 1, groups, pair) * feats, LANES), feats)
    row = lax.broadcasted_iota(jnp.int32, (block, feats), 0)
    for b in range(blocks):
        here = slice(b * block, (b + 1) * block)
        some = tok_held[here, own]
        slab[here, :] = jnp.where(row < lengths[b], some, jnp.zeros_like(some))
    slab[rows:, :] = named_rows(ids, (slab.shape[0] - rows, feats)).astype(slab.dtype)
    row = lax.broadcasted_iota(jnp.int32, (block, wide), 0)
    t = lax.axis_index("tensor")
    for out, side in ((mine, t), (other, lax.rem(t + 1, sides))):
        columns = pl.ds(pl.multiple_of(side * wide, LANES), wide)
        for b in range(blocks):
            here = slice(b * block, (b + 1) * block)
            out[here, :] = jnp.where(row < lengths[b], total[here, columns], 0.0)


def base_halves(tokens, base_key, sides, lengths, ids, groups, pair):
    rows, depth = tokens.shape
    features = base_key.shape[1]
    half = jax.ShapeDtypeStruct((rows, features // sides), jnp.float32)
    steps, chunks = depth // 1024, depth // 256
    return pl.pallas_call(
        functools.partial(base_kernel, sides, groups, pair),
        in_specs=[SMEM, SMEM, ANY, ANY],
        out_specs=[VMEM] * 4,
        out_shape=[
            half,
            half,
            jax.ShapeDtypeStruct((8, LANES), jnp.float32),
            jax.ShapeDtypeStruct((rows + 16, depth // (groups * pair)), tokens.dtype),
        ],
        scratch_shapes=[
            pltpu.VMEM(tokens.shape, tokens.dtype),
            pltpu.VMEM(base_key.shape, base_key.dtype),
            pltpu.VMEM((rows, features), jnp.float32),
            pltpu.SemaphoreType.DMA((steps, lengths.shape[0])),
            pltpu.SemaphoreType.DMA((chunks,)),
        ],
        cost_estimate=pl.CostEstimate(flops=0, bytes_accessed=0, transcendentals=0),
        compiler_params=FULL,
        name="base",
    )(lengths, ids, tokens, base_key)


def collect_kernel(*refs):
    sems, held, pieces = refs[-1], refs[-2], refs[:-2]
    copies, start = [], 0
    for j, piece in enumerate(pieces):
        copies.append(pltpu.make_async_copy(piece, held.at[pl.ds(start, piece.shape[0])], sems.at[j]))
        start += piece.shape[0]
    for copy in copies:
        copy.start()
    for copy in copies:
        copy.wait()


def collect(pieces):
    count = sum(piece.shape[0] for piece in pieces)
    return pl.pallas_call(
        collect_kernel,
        in_specs=[ANY] * len(pieces),
        out_specs=VMEM,
        out_shape=jax.ShapeDtypeStruct((count,) + pieces[0].shape[1:], pieces[0].dtype),
        scratch_shapes=[pltpu.SemaphoreType.DMA((len(pieces),))],
        compiler_params=ROOM,
        name="collect",
    )(*pieces)


def rank_kernel(ring, pair, rows, shares, owner, held, *refs):
    late, toks, outs = refs[: -1 - 2 * shares], refs[-1 - 2 * shares : -1 - shares], refs[-1 - shares : -1]
    flag = refs[-1]
    flag[...] = jnp.zeros_like(flag)
    rank = held.shape[1]
    per = owner.shape[0] // (ring * pair)
    blocks, _, block = outs[0].shape
    feats = toks[0].shape[1]
    z, y = lax.axis_index("ring"), lax.axis_index("pair")
    lane = lax.broadcasted_iota(jnp.int32, (16, LANES), 1)
    row = lax.broadcasted_iota(jnp.int32, (16, LANES), 0)
    ids = []
    for tok in toks:
        named = tok[rows:, :LANES].astype(jnp.float32)
        ids += [jnp.sum(jnp.where((lane == b) & (row == 0), named, 0.0)).astype(jnp.int32) for b in range(blocks)]
    for i, one in enumerate(ids):
        slot = owner[one]
        chip = slot // per
        local = lax.rem(slot, per)
        away = lax.rem(chip // pair - z + ring, ring)
        way = lax.rem(lax.rem(chip, pair) - y + pair, pair)
        if late:
            half = ring // 2
            near = jnp.where(away == half, 0, away - jnp.where(away > half, 1, 0))
            piece = held[(way * (ring - 1) + near) * per + local]
            piece = jnp.where(away == half, late[0][way * per + local], piece)
        else:
            piece = held[(way * ring + away) * per + local]
        k, b = i // blocks, i % blocks
        part = lax.dot_general(
            piece[:, :feats],
            toks[k][b * block : (b + 1) * block, :],
            (((1,), (1,)), ((), ())),
            preferred_element_type=jnp.float32,
        )
        outs[k][b, :rank, :] = part.astype(outs[k].dtype)
        outs[k][b, rank:, :] = piece[:, feats:]


def rank_parts(owner, toks, held, late, ring, pair, rows, blocks):
    shares, rank = len(toks), held.shape[1]
    return pl.pallas_call(
        functools.partial(rank_kernel, ring, pair, rows, shares),
        in_specs=[SMEM, VMEM] + [VMEM] * (len(late) + shares),
        out_specs=[VMEM] * (shares + 1),
        out_shape=[jax.ShapeDtypeStruct((blocks, 2 * rank, rows // blocks), held.dtype)] * shares
        + [jax.ShapeDtypeStruct((8, LANES), jnp.float32)],
        cost_estimate=pl.CostEstimate(flops=0, bytes_accessed=0, transcendentals=0),
        compiler_params=ROOM,
        name="rank",
    )(owner, held, *late, *toks)


def final_kernel(groups, pair, base_a, base_b, *refs):
    shares = groups * pair
    mine, theirs, out_ref, up = refs[:shares], refs[shares : 2 * shares], refs[-2], refs[-1]
    blocks, tall, block = mine[0].shape
    rank = tall // 2
    tiles = out_ref.shape[1] // LANES
    for b in range(blocks):
        here = slice(b * block, (b + 1) * block)
        total = mine[0][b, :rank, :].astype(jnp.float32)
        for part in mine[1:] + theirs:
            total += part[b, :rank, :].astype(jnp.float32)
        for k in range(shares):
            tile = lax.rem(mate_at(k, 1, groups, pair), tiles)
            up[b, :, pl.ds(pl.multiple_of(tile * LANES, LANES), LANES)] = mine[k][b, rank:, :]
        delta = lax.dot_general(
            total.astype(jnp.bfloat16), up[b], (((0,), (0,)), ((), ())), preferred_element_type=jnp.float32
        )
        out_ref[here, :] = (base_a[here, :] + base_b[here, :] + delta).astype(out_ref.dtype)


def final(mine, theirs, base, groups, pair, dtype):
    blocks, tall, _ = mine[0].shape
    return pl.pallas_call(
        functools.partial(final_kernel, groups, pair),
        in_specs=[VMEM] * (2 + 2 * len(mine)),
        out_specs=VMEM,
        out_shape=jax.ShapeDtypeStruct(base[0].shape, dtype),
        scratch_shapes=[pltpu.VMEM((blocks, tall // 2, base[0].shape[1]), mine[0].dtype)],
        compiler_params=ROOM,
        name="final",
    )(*base, *mine, *theirs)


def body(tokens, base_key, adapter_down, adapter_up, adapter_ids, owner_slot, lengths):
    groups, ring, pair = lax.axis_size("groups"), lax.axis_size("ring"), lax.axis_size("pair")
    sides = lax.axis_size("tensor")
    shares = groups * pair
    rows = tokens.shape[0]
    blocks = lengths.shape[0]

    def across(x):
        return lax.ppermute(x, "tensor", [(i, (i + 1) % sides) for i in range(sides)])

    def along(x, step):
        return lax.ppermute(x, "ring", [(a, (a + step) % ring) for a in range(ring)])

    def first_hops(x):
        return {0: x, ring - 1: along(x, 1), **({1: along(x, -1)} if ring > 2 else {})}

    def in_plane(x, kg, ky):
        pairs = []
        for a in range(groups):
            for b in range(pair):
                pairs.append((a * pair + b, (a + kg) % groups * pair + (b + ky) % pair))
        return lax.ppermute(x, PLANE, pairs)

    def more_hops(held, way, *after):
        for k in range(2, ring // 2 + 1):
            if 2 * k < ring or way % 2 == 0:
                if k == 2:
                    held[ring - 1] = hand_on(held[ring - 1], held[1], *after)
                held[ring - k] = along(held[ring - k + 1], 1)
            if 2 * k < ring or way % 2 == 1:
                if k == 2:
                    held[1] = hand_on(held[1], held[ring - 1], *after)
                held[k] = along(held[k - 1], -1)
        return [held[k] for k in range(ring)]

    packed = pack(jnp.swapaxes(adapter_down, 1, 2), adapter_up, shares, pair)
    ids = adapter_ids.reshape(-1)
    slabs = spread(tokens, lengths, ids, groups, pair)
    swapped = [
        lax.ppermute(packed[pair - w], "pair", [(a, (a - w) % pair) for a in range(pair)]) for w in range(1, pair)
    ]
    firsts = [first_hops(piece) for piece in [packed[0]] + swapped]
    toks = [in_plane(slabs[k - 1], k // pair, k % pair) for k in range(1, shares)]

    base_mine, base_out, flag, own_slab = base_halves(tokens, base_key, sides, lengths, ids, groups, pair)
    toks = [own_slab] + toks
    pieces = [
        more_hops(held, way, flag)
        for way, held in enumerate(firsts)
    ]

    halfway = ring // 2 if ring % 2 == 0 else ring
    held = collect([piece for way in pieces for away, piece in enumerate(way) if away != halfway])
    late = [collect([way[halfway] for way in pieces])] if halfway < ring else []
    *parts, ready = rank_parts(owner_slot, toks, held, late, ring, pair, rows, blocks)
    mine = [parts[0]] + [in_plane(parts[k], -(k // pair), -(k % pair)) for k in range(1, shares)]
    theirs = [across(part) for part in mine]
    base_in = across(hand_on(base_out, ready))
    return final(mine, theirs, [base_mine, base_in], groups, pair, tokens.dtype)


def solution(mesh):
    groups, dp, sides = (mesh.shape[name] for name in ("groups", "dp", "tensor"))
    pair = 2 if dp % 2 == 0 else 1
    cut = Mesh(mesh.devices.reshape(groups, dp // pair, pair, sides), ("groups", "ring", "pair", "tensor"))
    stored = ("ring", "pair")
    placed = (
        P(WHOLE, "tensor"),
        P("tensor", None),
        P(stored, "tensor", None),
        P(stored, None, "tensor"),
        P(WHOLE, None),
        P(),
        P(WHOLE),
    )
    return jax.shard_map(body, mesh=cut, in_specs=placed, out_specs=P(WHOLE, "tensor"), check_vma=False)
```

```python
import functools

import jax
import jax.numpy as jnp
from jax import lax
from jax.experimental import pallas as pl
from jax.experimental.pallas import tpu as pltpu
from jax.sharding import Mesh
from jax.sharding import PartitionSpec as P

LANES = 128
ANY = pl.BlockSpec(memory_space=pl.ANY)
SMEM = pl.BlockSpec(memory_space=pltpu.SMEM)
VMEM = pl.BlockSpec(memory_space=pltpu.VMEM)
HBM = pl.BlockSpec(memory_space=pltpu.HBM)
ROOM = pltpu.CompilerParams(vmem_limit_bytes=32 * 1024 * 1024)
FULL = pltpu.CompilerParams(vmem_limit_bytes=60 * 1024 * 1024)
PLANE = ("groups", "pair")
WHOLE = ("groups", "ring", "pair")


def hand_kernel(*refs):
    pass


def hand_on(x, *after):
    return pl.pallas_call(
        hand_kernel,
        in_specs=[ANY] * (1 + len(after)),
        out_specs=ANY,
        out_shape=jax.ShapeDtypeStruct(x.shape, x.dtype),
        input_output_aliases={0: 0},
        compiler_params=FULL,
        name="hand",
    )(x, *after)


def pack_kernel(down, up, *refs):
    outs, sems = refs[:-1], refs[-1]
    feats = outs[0].shape[2] - LANES
    copies = []
    for way, out in enumerate(outs):
        share = lax.axis_index("groups") * len(outs) + lax.rem(lax.axis_index("pair") + way, len(outs))
        start = pl.multiple_of(share * feats, LANES)
        tile = pl.multiple_of(lax.rem(share, up.shape[2] // LANES) * LANES, LANES)
        half = down.shape[1] // 2
        for a in range(down.shape[0]):
            for h in range(2):
                rows, sem = pl.ds(h * half, half), sems.at[way, a, h]
                to = out.at[a, rows, :]
                copies.append(pltpu.make_async_copy(down.at[a, rows, pl.ds(start, feats)], to.at[:, :feats], sem.at[0]))
                copies.append(pltpu.make_async_copy(up.at[a, rows, pl.ds(tile, LANES)], to.at[:, feats:], sem.at[1]))
    for copy in copies:
        copy.start()
    for copy in copies:
        copy.wait()


def pack(down, up, shares, ways):
    adapters, rank, feats = down.shape
    shape = jax.ShapeDtypeStruct((adapters, rank, feats // shares + LANES), down.dtype)
    return pl.pallas_call(
        pack_kernel,
        in_specs=[HBM, HBM],
        out_specs=[VMEM] * ways,
        out_shape=[shape] * ways,
        scratch_shapes=[pltpu.SemaphoreType.DMA((ways, adapters, 2, 2))],
        compiler_params=FULL,
        name="pack",
    )(down, up)


def mate_at(k, sign, groups, pair):
    kg, ky = k // pair, k % pair
    g = lax.rem(lax.axis_index("groups") + sign * kg + groups, groups)
    y = lax.rem(lax.axis_index("pair") + sign * ky + pair, pair)
    return g * pair + y


def named_rows(ids, shape):
    lane = lax.broadcasted_iota(jnp.int32, shape, 1)
    named = jnp.zeros(shape, jnp.float32)
    for b in range(ids.shape[0]):
        named = jnp.where(lane == b, ids[b].astype(jnp.float32), named)
    return named


def spread_kernel(groups, pair, lengths, ids, tok, *refs):
    held, in_sems, out_sems = refs[-3:]
    outs = refs[:-3]
    blocks = lengths.shape[0]
    sent, tall, step = held.shape
    shares = sent + 1
    rows = tok.shape[0]
    block = rows // blocks
    mates = [pl.multiple_of(mate_at(k, 1, groups, pair) * step, LANES) for k in range(shares)]
    order = list(range(1, shares))

    def read(k, b):
        here = pl.ds(b * block, block)
        return pltpu.make_async_copy(tok.at[here, pl.ds(mates[k], step)], held.at[k - 1, here, :], in_sems.at[k - 1, b])

    for k in order:
        for b in range(blocks):
            read(k, b).start()
    named = named_rows(ids, (tall - rows, step)).astype(held.dtype)
    writes = []

    def write(k, b):
        here = pl.ds(b * block, block if b < blocks else tall - rows)
        writes.append(pltpu.make_async_copy(held.at[k - 1, here, :], outs[k - 1].at[here, :], out_sems.at[k - 1, b]))
        writes[-1].start()

    for k in order:
        held[k - 1, rows:, :] = named
        write(k, blocks)
        for b in range(blocks):
            read(k, b).wait()

            @pl.when(lengths[b] < block)
            def _():
                here = slice(b * block, (b + 1) * block)
                row = lax.broadcasted_iota(jnp.int32, (block, step), 0)
                part = held[k - 1, here, :]
                held[k - 1, here, :] = jnp.where(row < lengths[b], part, jnp.zeros_like(part))

            write(k, b)
    for one in writes:
        one.wait()


def spread(tokens, lengths, ids, groups, pair):
    rows, feats = tokens.shape
    shares = groups * pair
    shape = (rows + 16, feats // shares)
    return pl.pallas_call(
        functools.partial(spread_kernel, groups, pair),
        in_specs=[SMEM, SMEM, ANY],
        out_specs=[ANY] * (shares - 1),
        out_shape=[jax.ShapeDtypeStruct(shape, tokens.dtype)] * (shares - 1),
        scratch_shapes=[
            pltpu.VMEM((shares - 1,) + shape, tokens.dtype),
            pltpu.SemaphoreType.DMA((shares - 1, lengths.shape[0])),
            pltpu.SemaphoreType.DMA((shares - 1, lengths.shape[0] + 1)),
        ],
        compiler_params=FULL,
        name="spread",
    )(lengths, ids, tokens)


def base_kernel(sides, groups, pair, lengths, ids, tok, key, mine, other, flag_ref, slab, tok_held, key_held, total, tok_sems, key_sems):
    depth, rows = key.shape[0], tok.shape[0]
    chunk = depth // key_sems.shape[0]
    steps = tok_sems.shape[0]
    step = depth // steps

    def key_copy(i):
        here = pl.ds(i * chunk, chunk)
        return pltpu.make_async_copy(key.at[here, :], key_held.at[here, :], key_sems.at[i])

    def tok_copy(i, b):
        here = pl.ds(i * step, step)
        some = pl.ds(b * (rows // tok_sems.shape[1]), rows // tok_sems.shape[1])
        return pltpu.make_async_copy(tok.at[some, here], tok_held.at[some, here], tok_sems.at[i, b])

    flag_ref[...] = jnp.zeros_like(flag_ref)
    for i in range(steps):
        for b in range(tok_sems.shape[1]):
            tok_copy(i, b).start()
        for j in range(step // chunk):
            key_copy(i * (step // chunk) + j).start()
    for i in range(steps):
        for b in range(tok_sems.shape[1]):
            tok_copy(i, b).wait()
        for j in range(step // chunk):
            key_copy(i * (step // chunk) + j).wait()
        here = slice(i * step, (i + 1) * step)
        part = jnp.dot(tok_held[:, here], key_held[here, :], preferred_element_type=jnp.float32)
        if i == 0:
            total[...] = part
        else:
            total[...] += part
    blocks = lengths.shape[0]
    wide = mine.shape[1]
    block = rows // blocks
    feats = slab.shape[1]
    own = pl.ds(pl.multiple_of(mate_at(0, 1, groups, pair) * feats, LANES), feats)
    row = lax.broadcasted_iota(jnp.int32, (block, feats), 0)
    for b in range(blocks):
        here = slice(b * block, (b + 1) * block)
        some = tok_held[here, own]
        slab[here, :] = jnp.where(row < lengths[b], some, jnp.zeros_like(some))
    slab[rows:, :] = named_rows(ids, (slab.shape[0] - rows, feats)).astype(slab.dtype)
    row = lax.broadcasted_iota(jnp.int32, (block, wide), 0)
    t = lax.axis_index("tensor")
    for out, side in ((mine, t), (other, lax.rem(t + 1, sides))):
        columns = pl.ds(pl.multiple_of(side * wide, LANES), wide)
        for b in range(blocks):
            here = slice(b * block, (b + 1) * block)
            out[here, :] = jnp.where(row < lengths[b], total[here, columns], 0.0)


def base_halves(tokens, base_key, sides, lengths, ids, groups, pair):
    rows, depth = tokens.shape
    features = base_key.shape[1]
    half = jax.ShapeDtypeStruct((rows, features // sides), jnp.float32)
    steps, chunks = depth // 1024, depth // 256
    return pl.pallas_call(
        functools.partial(base_kernel, sides, groups, pair),
        in_specs=[SMEM, SMEM, ANY, ANY],
        out_specs=[VMEM] * 4,
        out_shape=[
            half,
            half,
            jax.ShapeDtypeStruct((8, LANES), jnp.float32),
            jax.ShapeDtypeStruct((rows + 16, depth // (groups * pair)), tokens.dtype),
        ],
        scratch_shapes=[
            pltpu.VMEM(tokens.shape, tokens.dtype),
            pltpu.VMEM(base_key.shape, base_key.dtype),
            pltpu.VMEM((rows, features), jnp.float32),
            pltpu.SemaphoreType.DMA((steps, lengths.shape[0])),
            pltpu.SemaphoreType.DMA((chunks,)),
        ],
        cost_estimate=pl.CostEstimate(flops=0, bytes_accessed=0, transcendentals=0),
        compiler_params=FULL,
        name="base",
    )(lengths, ids, tokens, base_key)


def collect_kernel(*refs):
    sems, held, pieces = refs[-1], refs[-2], refs[:-2]
    copies, start = [], 0
    for j, piece in enumerate(pieces):
        copies.append(pltpu.make_async_copy(piece, held.at[pl.ds(start, piece.shape[0])], sems.at[j]))
        start += piece.shape[0]
    for copy in copies:
        copy.start()
    for copy in copies:
        copy.wait()


def collect(pieces):
    count = sum(piece.shape[0] for piece in pieces)
    return pl.pallas_call(
        collect_kernel,
        in_specs=[ANY] * len(pieces),
        out_specs=VMEM,
        out_shape=jax.ShapeDtypeStruct((count,) + pieces[0].shape[1:], pieces[0].dtype),
        scratch_shapes=[pltpu.SemaphoreType.DMA((len(pieces),))],
        compiler_params=ROOM,
        name="collect",
    )(*pieces)


def rank_kernel(ring, pair, rows, shares, owner, held, *refs):
    late, toks, outs = refs[: -1 - 2 * shares], refs[-1 - 2 * shares : -1 - shares], refs[-1 - shares : -1]
    flag = refs[-1]
    flag[...] = jnp.zeros_like(flag)
    rank = held.shape[1]
    per = owner.shape[0] // (ring * pair)
    blocks, _, block = outs[0].shape
    feats = toks[0].shape[1]
    z, y = lax.axis_index("ring"), lax.axis_index("pair")
    lane = lax.broadcasted_iota(jnp.int32, (16, LANES), 1)
    row = lax.broadcasted_iota(jnp.int32, (16, LANES), 0)
    ids = []
    for tok in toks:
        named = tok[rows:, :LANES].astype(jnp.float32)
        ids += [jnp.sum(jnp.where((lane == b) & (row == 0), named, 0.0)).astype(jnp.int32) for b in range(blocks)]
    for i, one in enumerate(ids):
        slot = owner[one]
        chip = slot // per
        local = lax.rem(slot, per)
        away = lax.rem(chip // pair - z + ring, ring)
        way = lax.rem(lax.rem(chip, pair) - y + pair, pair)
        if late:
            half = ring // 2
            near = jnp.where(away == half, 0, away - jnp.where(away > half, 1, 0))
            piece = held[(way * (ring - 1) + near) * per + local]
            for w in range(pair):
                piece = jnp.where((away == half) & (way == w), late[w][local], piece)
        else:
            piece = held[(way * ring + away) * per + local]
        k, b = i // blocks, i % blocks
        part = lax.dot_general(
            piece[:, :feats],
            toks[k][b * block : (b + 1) * block, :],
            (((1,), (1,)), ((), ())),
            preferred_element_type=jnp.float32,
        )
        outs[k][b, :rank, :] = part.astype(outs[k].dtype)
        outs[k][b, rank:, :] = piece[:, feats:]


def rank_parts(owner, toks, held, late, ring, pair, rows, blocks):
    shares, rank = len(toks), held.shape[1]
    return pl.pallas_call(
        functools.partial(rank_kernel, ring, pair, rows, shares),
        in_specs=[SMEM, VMEM] + [VMEM] * (len(late) + shares),
        out_specs=[VMEM] * (shares + 1),
        out_shape=[jax.ShapeDtypeStruct((blocks, 2 * rank, rows // blocks), held.dtype)] * shares
        + [jax.ShapeDtypeStruct((8, LANES), jnp.float32)],
        cost_estimate=pl.CostEstimate(flops=0, bytes_accessed=0, transcendentals=0),
        compiler_params=ROOM,
        name="rank",
    )(owner, held, *late, *toks)


def final_kernel(groups, pair, base_a, base_b, *refs):
    shares = groups * pair
    mine, theirs, out_ref, up = refs[:shares], refs[shares : 2 * shares], refs[-2], refs[-1]
    blocks, tall, block = mine[0].shape
    rank = tall // 2
    tiles = out_ref.shape[1] // LANES
    for b in range(blocks):
        here = slice(b * block, (b + 1) * block)
        total = mine[0][b, :rank, :].astype(jnp.float32)
        for part in mine[1:] + theirs:
            total += part[b, :rank, :].astype(jnp.float32)
        for k in range(shares):
            tile = lax.rem(mate_at(k, 1, groups, pair), tiles)
            up[b, :, pl.ds(pl.multiple_of(tile * LANES, LANES), LANES)] = mine[k][b, rank:, :]
        delta = lax.dot_general(
            total.astype(jnp.bfloat16), up[b], (((0,), (0,)), ((), ())), preferred_element_type=jnp.float32
        )
        out_ref[here, :] = (base_a[here, :] + base_b[here, :] + delta).astype(out_ref.dtype)


def final(mine, theirs, base, groups, pair, dtype):
    blocks, tall, _ = mine[0].shape
    return pl.pallas_call(
        functools.partial(final_kernel, groups, pair),
        in_specs=[VMEM] * (2 + 2 * len(mine)),
        out_specs=VMEM,
        out_shape=jax.ShapeDtypeStruct(base[0].shape, dtype),
        scratch_shapes=[pltpu.VMEM((blocks, tall // 2, base[0].shape[1]), mine[0].dtype)],
        compiler_params=ROOM,
        name="final",
    )(*base, *mine, *theirs)


def body(tokens, base_key, adapter_down, adapter_up, adapter_ids, owner_slot, lengths):
    groups, ring, pair = lax.axis_size("groups"), lax.axis_size("ring"), lax.axis_size("pair")
    sides = lax.axis_size("tensor")
    shares = groups * pair
    rows = tokens.shape[0]
    blocks = lengths.shape[0]

    def across(x):
        return lax.ppermute(x, "tensor", [(i, (i + 1) % sides) for i in range(sides)])

    def along(x, step):
        return lax.ppermute(x, "ring", [(a, (a + step) % ring) for a in range(ring)])

    def first_hops(x):
        return {0: x, ring - 1: along(x, 1), **({1: along(x, -1)} if ring > 2 else {})}

    def in_plane(x, kg, ky):
        pairs = []
        for a in range(groups):
            for b in range(pair):
                pairs.append((a * pair + b, (a + kg) % groups * pair + (b + ky) % pair))
        return lax.ppermute(x, PLANE, pairs)

    def more_hops(held, way, *after):
        for k in range(2, ring // 2 + 1):
            if 2 * k < ring or way % 2 == 0:
                if k == 2:
                    held[ring - 1] = hand_on(held[ring - 1], held[1], *after)
                held[ring - k] = along(held[ring - k + 1], 1)
            if 2 * k < ring or way % 2 == 1:
                if k == 2:
                    held[1] = hand_on(held[1], held[ring - 1], *after)
                held[k] = along(held[k - 1], -1)
        return [held[k] for k in range(ring)]

    packed = pack(jnp.swapaxes(adapter_down, 1, 2), adapter_up, shares, pair)
    ids = adapter_ids.reshape(-1)
    slabs = spread(tokens, lengths, ids, groups, pair)
    swapped = [
        lax.ppermute(packed[pair - w], "pair", [(a, (a - w) % pair) for a in range(pair)]) for w in range(1, pair)
    ]
    firsts = [first_hops(piece) for piece in [packed[0]] + swapped]
    toks = [in_plane(slabs[k - 1], k // pair, k % pair) for k in range(1, shares)]

    base_mine, base_out, flag, own_slab = base_halves(tokens, base_key, sides, lengths, ids, groups, pair)
    toks = [own_slab] + toks
    pieces = [
        more_hops(held, way, flag)
        for way, held in enumerate(firsts)
    ]

    halfway = ring // 2 if ring % 2 == 0 else ring
    held = collect([piece for way in pieces for away, piece in enumerate(way) if away != halfway])
    late = [way[halfway] for way in pieces] if halfway < ring else []
    *parts, ready = rank_parts(owner_slot, toks, held, late, ring, pair, rows, blocks)
    mine = [parts[0]] + [in_plane(parts[k], -(k // pair), -(k % pair)) for k in range(1, shares)]
    theirs = [across(part) for part in mine]
    base_in = across(hand_on(base_out, ready))
    return final(mine, theirs, [base_mine, base_in], groups, pair, tokens.dtype)


def solution(mesh):
    groups, dp, sides = (mesh.shape[name] for name in ("groups", "dp", "tensor"))
    pair = 2 if dp % 2 == 0 else 1
    cut = Mesh(mesh.devices.reshape(groups, dp // pair, pair, sides), ("groups", "ring", "pair", "tensor"))
    stored = ("ring", "pair")
    placed = (
        P(WHOLE, "tensor"),
        P("tensor", None),
        P(stored, "tensor", None),
        P(stored, None, "tensor"),
        P(WHOLE, None),
        P(),
        P(WHOLE),
    )
    return jax.shard_map(body, mesh=cut, in_specs=placed, out_specs=P(WHOLE, "tensor"), check_vma=False)
```
